32 devices in a mesh: seq: 4 (over y, x), fsdp: 8 (over z, core).
Axes of the slice: x: 2, y: 2, z: 4, core: 2. Of those that a mesh axis runs over, the one named last changes fastest.
Arguments:
- tokens: bfloat16 [2, 8, 2048, 640], P(None, 'fsdp', 'seq'), may hold values from -6 to 6
- document_lengths: int32 [2, 8, 2], P(None, 'fsdp'), may hold values from 0 to 2048, as said below
- cotangent: bfloat16 [2, 8, 2048, 640], P(None, 'fsdp', 'seq'), may hold values from -6 to 6
- attention_gain: bfloat16 [640], P('fsdp'), may hold values from 0.5 to 1.5
- query_projection: bfloat16 [640, 1024], P('fsdp'), may hold values from -0.25 to 0.25
- narrowing_factor: bfloat16 [640, 256], P('fsdp'), may hold values from -0.25 to 0.25
- widening_factor: bfloat16 [256, 1024], P('fsdp'), may hold values from -0.1875 to 0.1875
- key_value_projection: bfloat16 [640, 512], P('fsdp'), may hold values from -0.25 to 0.25
- output_projection: bfloat16 [1024, 640], P('fsdp'), may hold values from -3 to 3
- feedforward_gain: bfloat16 [640], P('fsdp'), may hold values from 0.5 to 1.5
- gate_projection: bfloat16 [640, 2048], P('fsdp'), may hold values from -0.25 to 0.25
- up_projection: bfloat16 [640, 2048], P('fsdp'), may hold values from -0.25 to 0.25
- down_projection: bfloat16 [2048, 640], P('fsdp'), may hold values from -0.125 to 0.125
Outputs:
- output: bfloat16 [2, 8, 2048, 640], P(None, 'fsdp', 'seq')
- input_grad: float32 [2, 8, 2048, 640], P(None, 'fsdp', 'seq')
- attn_gain_grad: float32 [640], P('fsdp')
- query_weight_grad: float32 [640, 1024], P('fsdp')
- lora_down_grad: float32 [640, 256], P('fsdp')
- lora_up_grad: float32 [256, 1024], P('fsdp')
- key_value_weight_grad: float32 [640, 512], P('fsdp')
- out_weight_grad: float32 [1024, 640], P('fsdp')
- ffn_gain_grad: float32 [640], P('fsdp')
- gate_weight_grad: float32 [640, 2048], P('fsdp')
- up_weight_grad: float32 [640, 2048], P('fsdp')
- down_weight_grad: float32 [2048, 640], P('fsdp')
The draws below stay inside these ranges and needn't reach their ends.
Inputs may be any that keep to these rules, and one draw needn't show every extreme that they name: document_lengths[m, g] lists the lengths of the documents packed one after another from the first token of group g in micro-batch m; unused slots hold 0 and come after the used ones; tokens past the last document are padding. In micro-batches of even index one document covers all but at most 256 tokens of its group, and in at least one group the whole group; in micro-batches of odd index the documents fill the group, none longer than 2048.
All inputs are finite; a program needn't handle non-finite values.
Results may differ from the reference program's by a relative error of at most 0.023.
Values may be sent and summed in bfloat16 or wider, within the bound.
No kernel may reach another device: no remote copies, remote signals or barrier semaphores. Data moves between devices by JAX's collectives and lax.ppermute only.
A program may use at most 128 MiB of HBM per device.

```python
import math
import jax
import jax.numpy as jnp
from jax import lax

EMBED_SIZE = 640
ASKER_COUNT = 4
CHANNEL_SIZE = 256
FF = 2048
FACTOR_INNER_DIM = 256
ROWS = 512
MB = 2
SHORT = 2048
GROUP = 2048
GROUPS = 8
DOCS = 2


def draw_document_lengths(key, part):
    key = jax.random.fold_in(key, 17)
    first, second, third = jax.random.split(key, 3)
    drawn = jax.random.randint(first, (MB, GROUPS, DOCS), 3 * SHORT // 4, SHORT + 1, dtype=jnp.int32)
    ends = jnp.cumsum(drawn, axis=-1, dtype=jnp.int32)
    room = jnp.maximum(GROUP - (ends - drawn), 0)
    packed = jnp.minimum(drawn, room)
    margin = jax.random.randint(second, (MB, GROUPS), 0, ROWS // 2 + 1, dtype=jnp.int32)
    chosen = jax.random.randint(third, (MB, 1), 0, GROUPS, dtype=jnp.int32)
    margin = jnp.where(jnp.arange(GROUPS, dtype=jnp.int32)[None, :] == chosen, 0, margin)
    single = jnp.where(jnp.arange(DOCS, dtype=jnp.int32)[None, None, :] == 0, (GROUP - margin)[:, :, None], 0)
    longer = (jnp.arange(MB, dtype=jnp.int32) % 2 == 0)[:, None, None]
    return jnp.where(longer, single, packed).astype(jnp.int32)


def level_of(stream_key, shape, pieces, least, high):
    def one(dim, blocks):
        draws = jax.random.uniform(jax.random.fold_in(jax.random.fold_in(stream_key, 6), dim), (blocks,), jnp.float32, least / len(pieces), high / len(pieces))
        return jnp.repeat(jnp.exp(draws), shape[dim] // blocks).reshape((-1,) + (1,) * (len(shape) - dim - 1))

    factor_of = one(*pieces[0])
    for cut in pieces[1:]:
        factor_of = factor_of * one(*cut)
    return factor_of


def scatter_about(own_key, extent, scale, reach, cuts=(), held_as=jnp.bfloat16):
    array = jax.random.normal(own_key, extent, jnp.float32) * scale
    if len(cuts) > 0:
        array = level_of(own_key, extent, cuts, -0.22, 0.18) * array
    return jnp.clip(array, min=-reach, max=reach).astype(held_as)


def setup_inputs(seed: int = 0) -> dict:
    seeds = jax.random.split(jax.random.key(seed), 14)
    tokens = scatter_about(seeds[0], (MB, GROUPS, GROUP, EMBED_SIZE), 1.0, 6.0, ((1, 8), (2, 4)))
    document_lengths = draw_document_lengths(jax.random.fold_in(seeds[13], 71), 0)
    cotangent = scatter_about(seeds[2], (MB, GROUPS, GROUP, EMBED_SIZE), 1.0, 6.0, ((1, 8), (2, 4)))
    attention_gain = jnp.clip(1.0 + 0.1 * jax.random.normal(seeds[3], (EMBED_SIZE,), jnp.float32), 0.5, 1.5).astype(jnp.bfloat16)
    query_projection = scatter_about(seeds[4], (EMBED_SIZE, ASKER_COUNT * CHANNEL_SIZE), EMBED_SIZE ** -0.5, 0.25, ((0, 8),))
    narrowing_factor = scatter_about(seeds[5], (EMBED_SIZE, FACTOR_INNER_DIM), EMBED_SIZE ** -0.5, 0.25, ((0, 8),))
    widening_factor = scatter_about(seeds[6], (FACTOR_INNER_DIM, ASKER_COUNT * CHANNEL_SIZE), (4 * FACTOR_INNER_DIM) ** -0.5, 0.1875, ((0, 8),))
    key_value_projection = scatter_about(seeds[7], (EMBED_SIZE, 2 * CHANNEL_SIZE), EMBED_SIZE ** -0.5, 0.25, ((0, 8),))
    output_projection = scatter_about(seeds[8], (ASKER_COUNT * CHANNEL_SIZE, EMBED_SIZE), 4 ** -0.5, 3.0, ((0, 8),))
    feedforward_gain = jnp.clip(1.0 + 0.1 * jax.random.normal(seeds[9], (EMBED_SIZE,), jnp.float32), 0.5, 1.5).astype(jnp.bfloat16)
    gate_projection = scatter_about(seeds[10], (EMBED_SIZE, FF), EMBED_SIZE ** -0.5, 0.25, ((0, 8),))
    up_projection = scatter_about(seeds[11], (EMBED_SIZE, FF), EMBED_SIZE ** -0.5, 0.25, ((0, 8),))
    down_projection = scatter_about(seeds[12], (FF, EMBED_SIZE), FF ** -0.5, 0.125, ((0, 8),))
    return {"tokens": tokens, "document_lengths": document_lengths, "cotangent": cotangent, "attention_gain": attention_gain, "query_projection": query_projection, "narrowing_factor": narrowing_factor, "widening_factor": widening_factor, "key_value_projection": key_value_projection, "output_projection": output_projection, "feedforward_gain": feedforward_gain, "gate_projection": gate_projection, "up_projection": up_projection, "down_projection": down_projection}


@jax.custom_vjp
def low_precision(v):
    return lax.optimization_barrier(v.astype(jnp.bfloat16)).astype(jnp.float32)

@jax.custom_vjp
def low_precision_backward(v):
    return v

def low_keep(v):
    return (low_precision(v), None)

def low_pass(kept, grad):
    return (grad,)

def back_keep(v):
    return (v, None)

def back_low(kept, grad):
    return (low_precision(grad),)
low_precision.defvjp(low_keep, low_pass)
low_precision_backward.defvjp(back_keep, back_low)
EPSILON = 1e-06
MASKED = -1e+30
THETA = 10000.0

def matrix_product(left, right):
    return jnp.dot(left, right, preferred_element_type=jnp.float32, precision=lax.Precision.HIGHEST)

def norm_rows(value_rows, gain):
    return value_rows * lax.rsqrt(lax.optimization_barrier(jnp.mean(value_rows * value_rows, axis=-1, keepdims=True)) + EPSILON) * gain

def doc_layout(lengths, loop_index):
    lengths = lengths.astype(jnp.int32)
    ends = jnp.cumsum(lengths, dtype=jnp.int32).astype(jnp.int32)
    starts = ends - lengths
    number = lax.optimization_barrier(jnp.sum((loop_index[:, None] >= ends[None, :]).astype(jnp.int32), axis=1, dtype=jnp.int32)).astype(jnp.int32)
    live = loop_index < ends[-1]
    match = number[:, None] == jnp.arange(lengths.shape[0], dtype=jnp.int32)[None, :]
    begin = lax.optimization_barrier(jnp.sum(jnp.where(match, starts[None, :], 0), axis=1, dtype=jnp.int32)).astype(jnp.int32)
    token_position = jnp.where(live, loop_index - begin, 0).astype(jnp.int32)
    token_label = jnp.where(live, number, lengths.shape[0] + loop_index).astype(jnp.int32)
    return (token_label, token_position)

def rotate(value_rows, token_position):
    half = value_rows.shape[-1] // 2
    freqs = THETA ** (-(jnp.arange(half, dtype=jnp.float32) * 2.0 / value_rows.shape[-1]))
    angles = token_position.astype(jnp.float32)[:, None] * freqs[None, :]
    if value_rows.ndim == 3:
        angles = angles[:, None, :]
    cosine = jnp.cos(angles)
    sine = jnp.sin(angles)
    first = value_rows[..., :half]
    second = value_rows[..., half:]
    return jnp.concatenate([first * cosine - second * sine, second * cosine + first * sine], axis=-1)

def layer_number(value_rows, attention_gain, query_projection, narrowing_factor, widening_factor, key_value_projection, output_projection, feedforward_gain, gate_projection, up_projection, down_projection, token_label, token_position, loop_index):
    normalized_rows = low_precision(norm_rows(value_rows, attention_gain))
    adapter_middle = low_precision_backward(low_precision(matrix_product(normalized_rows, narrowing_factor)))
    query_rows = low_precision_backward(matrix_product(normalized_rows, query_projection) + matrix_product(adapter_middle, widening_factor))
    query_rows = low_precision(rotate(query_rows.reshape(GROUP, ASKER_COUNT, CHANNEL_SIZE), token_position))
    pair = low_precision_backward(matrix_product(normalized_rows, key_value_projection))
    keys = low_precision(rotate(pair[:, :CHANNEL_SIZE], token_position))
    vals = low_precision(pair[:, CHANNEL_SIZE:])
    width = math.gcd(GROUP, 512)

    def attend(item):
        block_query, block_label, block_index = item
        scores = jnp.einsum('qhd,kd->hqk', block_query, keys, precision=lax.Precision.HIGHEST) * CHANNEL_SIZE ** (-0.5)
        scores = low_precision_backward(scores)
        mask = (block_label[:, None] == token_label[None, :]) & (loop_index[None, :] <= block_index[:, None])
        scores = jnp.where(mask[None], scores, MASKED)
        peak = lax.optimization_barrier(jnp.max(scores, axis=-1, keepdims=True))
        weights = jnp.exp(scores - peak)
        weights = low_precision(weights / lax.optimization_barrier(jnp.sum(weights, axis=-1, keepdims=True)))
        return jnp.einsum('hqk,kd->qhd', weights, vals, precision=lax.Precision.HIGHEST)
    mixed = lax.map(jax.checkpoint(attend), (query_rows.reshape(GROUP // width, width, ASKER_COUNT, CHANNEL_SIZE), token_label.reshape(GROUP // width, width), loop_index.reshape(GROUP // width, width)))
    mixed = low_precision_backward(low_precision(mixed.reshape(GROUP, ASKER_COUNT * CHANNEL_SIZE)))
    middle = value_rows + low_precision_backward(matrix_product(mixed, output_projection))
    normed_ffn = low_precision(norm_rows(middle, feedforward_gain))
    gate = low_precision_backward(matrix_product(normed_ffn, gate_projection))
    lift = low_precision_backward(matrix_product(normed_ffn, up_projection))
    hidden = low_precision(jax.nn.gelu(gate, approximate=True) * lift)
    return middle + matrix_product(hidden, down_projection)

def reference(tokens, document_lengths, cotangent, attention_gain, query_projection, narrowing_factor, widening_factor, key_value_projection, output_projection, feedforward_gain, gate_projection, up_projection, down_projection):
    parameter_tree = (attention_gain.astype(jnp.float32), query_projection.astype(jnp.float32), narrowing_factor.astype(jnp.float32), widening_factor.astype(jnp.float32), key_value_projection.astype(jnp.float32), output_projection.astype(jnp.float32), feedforward_gain.astype(jnp.float32), gate_projection.astype(jnp.float32), up_projection.astype(jnp.float32), down_projection.astype(jnp.float32))
    flat_tokens = tokens.reshape(MB * GROUPS, GROUP, EMBED_SIZE)
    flat_grads = cotangent.reshape(MB * GROUPS, GROUP, EMBED_SIZE)
    flat_lengths = document_lengths.reshape(MB * GROUPS, DOCS)
    loop_index = jnp.arange(GROUP, dtype=jnp.int32)

    def one_group(sums, item):
        value_rows, grad_out, lengths = item
        token_label, token_position = doc_layout(lengths, loop_index)

        def forward(value_rows, first, second, third, fourth, fifth, sixth, seventh, eighth, ninth, tenth):
            return layer_number(value_rows, first, second, third, fourth, fifth, sixth, seventh, eighth, ninth, tenth, token_label, token_position, loop_index)
        result, pull = jax.vjp(forward, value_rows.astype(jnp.float32), parameter_tree[0], parameter_tree[1], parameter_tree[2], parameter_tree[3], parameter_tree[4], parameter_tree[5], parameter_tree[6], parameter_tree[7], parameter_tree[8], parameter_tree[9])
        grads = pull(grad_out.astype(jnp.float32))
        sums = tuple((total + grad for total, grad in zip(sums, grads[1:])))
        return (sums, (result.astype(jnp.bfloat16), grads[0]))
    zeros = tuple((jnp.zeros(param.shape, jnp.float32) for param in parameter_tree))
    sums, (outputs, input_grads) = lax.scan(one_group, zeros, (flat_tokens, flat_grads, flat_lengths))
    return (outputs.reshape(MB, GROUPS, GROUP, EMBED_SIZE), input_grads.reshape(MB, GROUPS, GROUP, EMBED_SIZE), sums[0], sums[1], sums[2], sums[3], sums[4], sums[5], sums[6], sums[7], sums[8], sums[9])
```

```python
import functools
import math

import jax
import jax.numpy as jnp
from jax import lax
from jax.experimental import pallas as pl
from jax.experimental.pallas import tpu as pltpu
from jax.sharding import PartitionSpec as P

EPSILON = 1e-06
THETA = 10000.0
F32 = jnp.float32
BF16 = jnp.bfloat16
GELU_C = math.sqrt(2.0 / math.pi)
GELU_A = 0.044715
LOWEST = -1e30
VMEM_LIMIT = 60 * 1024 * 1024


def mm(left, right):
    return lax.dot_general(left, right, (((1,), (0,)), ((), ())), preferred_element_type=F32)


def mm_nt(left, right):
    return lax.dot_general(left, right, (((1,), (1,)), ((), ())), preferred_element_type=F32)


def full(shape):
    return pl.BlockSpec(shape, lambda i: (0,) * len(shape))


def rows_of(tile, cols):
    return pl.BlockSpec((tile, cols), lambda i: (i, 0))


def params(**more):
    return pltpu.CompilerParams(vmem_limit_bytes=VMEM_LIMIT, **more)


def cost(flops, bytes_accessed, transcendentals=0):
    return pl.CostEstimate(
        flops=int(flops), bytes_accessed=int(bytes_accessed), transcendentals=int(transcendentals)
    )


def project_kernel(x_ref, gain_ref, cos_ref, sin_ref, wq_ref, wn_ref, ww_ref, wkv_ref,
                   normed_ref, lora_ref, q_ref, kv_ref, *, head_dim, scale):
    half = head_dim // 2
    x = x_ref[...].astype(F32)
    inv = lax.rsqrt(jnp.mean(x * x, axis=-1, keepdims=True) + EPSILON)
    normed = (x * inv * gain_ref[...]).astype(BF16)
    normed_ref[...] = normed
    cos, sin = cos_ref[...], sin_ref[...]
    pair = mm(normed, wkv_ref[...])
    a, b = pair[:, :half], pair[:, half:head_dim]
    kv_ref[:, :half] = (a * cos - b * sin).astype(BF16)
    kv_ref[:, half:head_dim] = (b * cos + a * sin).astype(BF16)
    kv_ref[:, head_dim:] = pair[:, head_dim:].astype(BF16)
    mid = mm(normed, wn_ref[...]).astype(BF16)
    lora_ref[...] = mid
    query = mm(normed, wq_ref[...]) + mm(mid, ww_ref[...])
    for h in range(query.shape[1] // head_dim):
        c = h * head_dim
        a, b = query[:, c : c + half], query[:, c + half : c + head_dim]
        q_ref[:, c : c + half] = ((a * cos - b * sin) * scale).astype(BF16)
        q_ref[:, c + half : c + head_dim] = ((b * cos + a * sin) * scale).astype(BF16)


def project(x, gain, cos, sin, wq, wn, ww, wkv, head_dim, scale):
    rows, width = x.shape
    tile = math.gcd(rows, 256)
    q_cols, mid, kv_cols = wq.shape[1], wn.shape[1], wkv.shape[1]
    return pl.pallas_call(
        functools.partial(project_kernel, head_dim=head_dim, scale=scale),
        grid=(rows // tile,),
        in_specs=[rows_of(tile, width), full(gain.shape), rows_of(tile, head_dim // 2),
                  rows_of(tile, head_dim // 2), full(wq.shape), full(wn.shape),
                  full(ww.shape), full(wkv.shape)],
        out_specs=[rows_of(tile, width), rows_of(tile, mid), rows_of(tile, q_cols),
                   rows_of(tile, kv_cols)],
        out_shape=[jax.ShapeDtypeStruct((rows, width), BF16),
                   jax.ShapeDtypeStruct((rows, mid), BF16),
                   jax.ShapeDtypeStruct((rows, q_cols), BF16),
                   jax.ShapeDtypeStruct((rows, kv_cols), BF16)],
        compiler_params=params(),
        cost_estimate=cost(2 * rows * (width * (q_cols + mid + kv_cols) + mid * q_cols), 8e6),
        name="project",
    )(x, gain, cos, sin, wq, wn, ww, wkv)


def attend_kernel(info_ref, low_ref, q_ref, kv_ref, o_ref, lse_ref, vt_ref, acc_ref,
                  *, head_dim, tile, block):
    heads = q_ref.shape[1] // head_dim
    base = info_ref[0]
    last = info_ref[1]

    def flip(kb, carry):
        at = pl.ds(pl.multiple_of(kb * block, block), block)
        vt_ref[:, at] = kv_ref[at, head_dim:].T
        return carry

    lax.fori_loop(info_ref[2], last, flip, 0)
    for t in range(q_ref.shape[0] // tile):
        q_rows = slice(t * tile, (t + 1) * tile)
        low = low_ref[:, q_rows]
        high = base + t * tile + lax.broadcasted_iota(jnp.int32, (1, tile), 1)
        acc_ref[...] = jnp.zeros_like(acc_ref)

        def visit(kb, carry):
            at = pl.ds(pl.multiple_of(kb * block, block), block)
            keys = kv_ref[at, :head_dim]
            vt = vt_ref[:, at]
            index = kb * block + lax.broadcasted_iota(jnp.int32, (block, tile), 0)
            mask = (index >= low) & (index <= high)
            out = []
            for h in range(heads):
                peak, total = carry[h]
                s = mm_nt(keys, q_ref[q_rows, h * head_dim : (h + 1) * head_dim])
                s = jnp.where(mask, s, -jnp.inf)
                new_peak = jnp.maximum(peak, jnp.max(s, axis=0, keepdims=True))
                factor = jnp.exp(peak - new_peak)
                p = jnp.exp(s - new_peak)
                total = total * factor + jnp.sum(p, axis=0, keepdims=True)
                acc_ref[h] = acc_ref[h] * factor + mm(vt, p.astype(BF16))
                out.append((new_peak, total))
            return tuple(out)

        start = tuple(
            (jnp.full((1, tile), LOWEST, F32), jnp.zeros((1, tile), F32)) for _ in range(heads)
        )
        stats = lax.fori_loop(info_ref[2 + t], (base + (t + 1) * tile + block - 1) // block,
                              visit, start)
        for h in range(heads):
            peak, total = stats[h]
            o_ref[q_rows, h * head_dim : (h + 1) * head_dim] = (acc_ref[h] / total).T.astype(BF16)
            lse_ref[h : h + 1, q_rows] = peak + jnp.log(total)


def attend(info, low, q, kv, head_dim, tile, block):
    rows, q_cols = q.shape
    heads = q_cols // head_dim
    vmem = pl.BlockSpec(memory_space=pltpu.VMEM)
    return pl.pallas_call(
        functools.partial(attend_kernel, head_dim=head_dim, tile=tile, block=block),
        in_specs=[pl.BlockSpec(memory_space=pltpu.SMEM), vmem, vmem, vmem],
        out_specs=[vmem, vmem],
        out_shape=[jax.ShapeDtypeStruct((rows, q_cols), BF16),
                   jax.ShapeDtypeStruct((heads, rows), F32)],
        scratch_shapes=[pltpu.VMEM((head_dim, kv.shape[0]), BF16),
                        pltpu.VMEM((heads, head_dim, tile), F32)],
        compiler_params=params(),
        cost_estimate=cost(4 * rows * kv.shape[0] * q_cols, 6e6, rows * kv.shape[0] * heads),
        name="attend",
    )(info, low, q, kv)


def middle_kernel(x_ref, attn_ref, g_ref, gain_ref, wo_ref, wg_ref, wu_ref, wd_ref,
                  out_ref, mid_grad_ref, branch_ref, attn_grad_ref, delta_ref, low_ref,
                  hidden_ref, gate_grad_ref, lift_grad_ref, gain_grad_ref,
                  *, head_dim, chunk):
    @pl.when(pl.program_id(0) == 0)
    def _():
        gain_grad_ref[...] = jnp.zeros_like(gain_grad_ref)

    gain = gain_ref[...]
    attn = attn_ref[...]
    middle = x_ref[...].astype(F32) + mm(attn, wo_ref[...])
    inv = lax.rsqrt(jnp.mean(middle * middle, axis=-1, keepdims=True) + EPSILON)
    unit = middle * inv
    low = (unit * gain).astype(BF16)
    low_ref[...] = low
    grad = g_ref[...]
    result = middle
    back = jnp.zeros_like(middle)
    for c in range(wg_ref.shape[1] // chunk):
        at = slice(c * chunk, (c + 1) * chunk)
        gate = mm(low, wg_ref[:, at])
        lift = mm(low, wu_ref[:, at])
        square = gate * gate
        bend = jnp.tanh(GELU_C * gate * (1.0 + GELU_A * square))
        cdf = 0.5 * (1.0 + bend)
        gelu = gate * cdf
        hidden = (gelu * lift).astype(BF16)
        hidden_ref[:, at] = hidden
        result = result + mm(hidden, wd_ref[at, :])
        hidden_grad = mm_nt(grad, wd_ref[at, :])
        slope = cdf + (0.5 * GELU_C) * gate * (1.0 - bend * bend) * (1.0 + 3.0 * GELU_A * square)
        gate_grad = (hidden_grad * lift * slope).astype(BF16)
        lift_grad = (hidden_grad * gelu).astype(BF16)
        gate_grad_ref[:, at] = gate_grad
        lift_grad_ref[:, at] = lift_grad
        back = back + mm_nt(gate_grad, wg_ref[:, at]) + mm_nt(lift_grad, wu_ref[:, at])
    out_ref[...] = result.astype(BF16)
    gain_grad_ref[...] += jnp.sum(unit * back, axis=0, keepdims=True)
    scaled = back * gain
    mid_grad = grad.astype(F32) + inv * (
        scaled - unit * jnp.mean(unit * scaled, axis=-1, keepdims=True)
    )
    mid_grad_ref[...] = mid_grad
    branch = mid_grad.astype(BF16)
    branch_ref[...] = branch
    attn_grad = mm_nt(branch, wo_ref[...]).astype(BF16)
    attn_grad_ref[...] = attn_grad
    product = attn_grad.astype(F32) * attn.astype(F32)
    half = head_dim // 2
    for h in range(attn.shape[1] // head_dim):
        c = h * head_dim
        folded = product[:, c : c + half] + product[:, c + half : c + head_dim]
        delta_ref[h : h + 1, :] = jnp.sum(folded.T, axis=0, keepdims=True)


def middle_part(x, attn, grad, gain, wo, wg, wu, wd, head_dim):
    rows, width = x.shape
    q_cols, hidden = attn.shape[1], wg.shape[1]
    heads = q_cols // head_dim
    tile = math.gcd(rows, 256)
    return pl.pallas_call(
        functools.partial(middle_kernel, head_dim=head_dim, chunk=512),
        grid=(rows // tile,),
        in_specs=[rows_of(tile, width), rows_of(tile, q_cols), rows_of(tile, width),
                  full(gain.shape), full(wo.shape), full(wg.shape), full(wu.shape), full(wd.shape)],
        out_specs=[rows_of(tile, width), rows_of(tile, width), rows_of(tile, width),
                   rows_of(tile, q_cols), pl.BlockSpec((heads, tile), lambda i: (0, i)),
                   rows_of(tile, width), rows_of(tile, hidden), rows_of(tile, hidden),
                   rows_of(tile, hidden), full((1, width))],
        out_shape=[jax.ShapeDtypeStruct((rows, width), BF16),
                   jax.ShapeDtypeStruct((rows, width), F32),
                   jax.ShapeDtypeStruct((rows, width), BF16),
                   jax.ShapeDtypeStruct((rows, q_cols), BF16),
                   jax.ShapeDtypeStruct((heads, rows), F32),
                   jax.ShapeDtypeStruct((rows, width), BF16),
                   jax.ShapeDtypeStruct((rows, hidden), BF16),
                   jax.ShapeDtypeStruct((rows, hidden), BF16),
                   jax.ShapeDtypeStruct((rows, hidden), BF16),
                   jax.ShapeDtypeStruct((1, width), F32)],
        compiler_params=params(),
        cost_estimate=cost(4 * rows * width * (q_cols + 3 * hidden), 40e6, rows * hidden),
        name="middle",
    )(x, attn, grad, gain, wo, wg, wu, wd)


def attend_back_kernel(info_ref, low_ref, lse_ref, delta_ref, q_ref, do_ref, kv_ref, cos_ref,
                       sin_ref, dq_ref, dkv_ref, kt_ref, acc_ref, *, head_dim, tile, block, scale):
    heads = q_ref.shape[1] // head_dim
    half = head_dim // 2
    base = info_ref[0]
    last = info_ref[1]
    tiles = q_ref.shape[0] // tile
    acc_ref[...] = jnp.zeros_like(acc_ref)
    dkv_ref[...] = jnp.zeros_like(dkv_ref)

    def visit(kb, carry):
        at = pl.ds(pl.multiple_of(kb * block, block), block)
        keys = kv_ref[at, :head_dim]
        vals = kv_ref[at, head_dim:]
        kt_ref[...] = keys.T
        dkv_ref[at, :] = jnp.zeros((block, 2 * head_dim), F32)
        for t in range(tiles):
            q_rows = slice(t * tile, (t + 1) * tile)

            @pl.when((kb >= info_ref[2 + t]) & (kb * block < base + (t + 1) * tile))
            def _():
                low = low_ref[:, q_rows]
                high = base + t * tile + lax.broadcasted_iota(jnp.int32, (1, tile), 1)
                index = kb * block + lax.broadcasted_iota(jnp.int32, (block, tile), 0)
                mask = (index >= low) & (index <= high)
                dk = jnp.zeros((block, head_dim), F32)
                dv = jnp.zeros((block, head_dim), F32)
                for h in range(heads):
                    cols = slice(h * head_dim, (h + 1) * head_dim)
                    q = q_ref[q_rows, cols]
                    do = do_ref[q_rows, cols]
                    s = mm_nt(keys, q)
                    p = jnp.where(mask, jnp.exp(s - lse_ref[h : h + 1, q_rows]), 0.0)
                    dv = dv + mm(p.astype(BF16), do)
                    ds = (p * (mm_nt(vals, do) - delta_ref[h : h + 1, q_rows])).astype(BF16)
                    dk = dk + mm(ds, q)
                    acc_ref[h, :, q_rows] += mm(kt_ref[...], ds)
                dkv_ref[at, :head_dim] += dk
                dkv_ref[at, head_dim:] += dv

        return carry

    lax.fori_loop(info_ref[2], last, visit, 0)
    cos, sin = cos_ref[...], sin_ref[...]
    for h in range(heads):
        c = h * head_dim
        dq = acc_ref[h].T * scale
        a, b = dq[:, :half], dq[:, half:]
        dq_ref[:, c : c + half] = (a * cos + b * sin).astype(BF16)
        dq_ref[:, c + half : c + head_dim] = (b * cos - a * sin).astype(BF16)


def attend_back(info, low, lse, delta, q, do, kv, cos, sin, head_dim, tile, block, scale):
    rows, q_cols = q.shape
    heads = q_cols // head_dim
    vmem = pl.BlockSpec(memory_space=pltpu.VMEM)
    return pl.pallas_call(
        functools.partial(attend_back_kernel, head_dim=head_dim, tile=tile, block=block,
                          scale=scale),
        in_specs=[pl.BlockSpec(memory_space=pltpu.SMEM)] + [vmem] * 8,
        out_specs=[vmem, vmem],
        out_shape=[jax.ShapeDtypeStruct((rows, q_cols), BF16),
                   jax.ShapeDtypeStruct(kv.shape, F32)],
        scratch_shapes=[pltpu.VMEM((head_dim, block), BF16),
                        pltpu.VMEM((heads, head_dim, rows), F32)],
        compiler_params=params(),
        cost_estimate=cost(10 * rows * kv.shape[0] * q_cols, 12e6, rows * kv.shape[0] * heads),
        name="attend_back",
    )(info, low, lse, delta, q, do, kv, cos, sin)


def project_back_kernel(x_ref, gain_ref, cos_ref, sin_ref, wq_ref, wn_ref, ww_ref, wkv_ref,
                        dq_ref, dkv_ref, mid_grad_ref,
                        lora_grad_ref, pair_grad_ref, in_grad_ref, gain_grad_ref, *, head_dim):
    @pl.when(pl.program_id(0) == 0)
    def _():
        gain_grad_ref[...] = jnp.zeros_like(gain_grad_ref)

    half = head_dim // 2
    gain = gain_ref[...]
    cos, sin = cos_ref[...], sin_ref[...]
    dq = dq_ref[...]
    lora_grad = mm_nt(dq, ww_ref[...]).astype(BF16)
    lora_grad_ref[...] = lora_grad
    a, b = dkv_ref[:, :half].astype(F32), dkv_ref[:, half:head_dim].astype(F32)
    pair_grad_ref[:, :half] = (a * cos + b * sin).astype(BF16)
    pair_grad_ref[:, half:head_dim] = (b * cos - a * sin).astype(BF16)
    pair_grad_ref[:, head_dim:] = dkv_ref[:, head_dim:].astype(BF16)
    back = (mm_nt(dq, wq_ref[...]) + mm_nt(lora_grad, wn_ref[...])
            + mm_nt(pair_grad_ref[...], wkv_ref[...]))
    x = x_ref[...].astype(F32)
    inv = lax.rsqrt(jnp.mean(x * x, axis=-1, keepdims=True) + EPSILON)
    unit = x * inv
    gain_grad_ref[...] += jnp.sum(unit * back, axis=0, keepdims=True)
    scaled = back * gain
    in_grad_ref[...] = mid_grad_ref[...] + inv * (
        scaled - unit * jnp.mean(unit * scaled, axis=-1, keepdims=True)
    )


def project_back(x, gain, cos, sin, wq, wn, ww, wkv, dq, dkv, mid_grad, head_dim):
    rows, width = x.shape
    tile = math.gcd(rows, 256)
    q_cols, mid, kv_cols = wq.shape[1], wn.shape[1], wkv.shape[1]
    return pl.pallas_call(
        functools.partial(project_back_kernel, head_dim=head_dim),
        grid=(rows // tile,),
        in_specs=[rows_of(tile, width), full(gain.shape), rows_of(tile, head_dim // 2),
                  rows_of(tile, head_dim // 2), full(wq.shape), full(wn.shape),
                  full(ww.shape), full(wkv.shape), rows_of(tile, q_cols),
                  rows_of(tile, kv_cols), rows_of(tile, width)],
        out_specs=[rows_of(tile, mid), rows_of(tile, kv_cols), rows_of(tile, width),
                   full((1, width))],
        out_shape=[jax.ShapeDtypeStruct((rows, mid), BF16),
                   jax.ShapeDtypeStruct((rows, kv_cols), BF16),
                   jax.ShapeDtypeStruct((rows, width), F32),
                   jax.ShapeDtypeStruct((1, width), F32)],
        compiler_params=params(),
        cost_estimate=cost(2 * rows * (width * (q_cols + mid + kv_cols) + mid * q_cols), 12e6),
        name="project_back",
    )(x, gain, cos, sin, wq, wn, ww, wkv, dq, dkv, mid_grad)


def weight_grad_kernel(x_ref, y_ref, out_ref, xt_ref):
    @pl.when(pl.program_id(0) == 0)
    def _():
        xt_ref[...] = x_ref[...].T

    out_ref[...] = mm(xt_ref[...], y_ref[...]).astype(BF16)


def weight_grad(x, y, tile=256):
    rows, width = x.shape
    cols = y.shape[1]
    tile = math.gcd(cols, tile)
    return pl.pallas_call(
        weight_grad_kernel,
        grid=(cols // tile,),
        in_specs=[full(x.shape), pl.BlockSpec((rows, tile), lambda i: (0, i))],
        out_specs=pl.BlockSpec((width, tile), lambda i: (0, i)),
        out_shape=jax.ShapeDtypeStruct((width, cols), BF16),
        scratch_shapes=[pltpu.VMEM((width, rows), BF16)],
        compiler_params=params(),
        cost_estimate=cost(2 * rows * width * cols, 2 * (rows * width + rows * cols + width * cols)),
        name="weight_grad",
    )(x, y)


def layout(lengths, index):
    ends = jnp.cumsum(lengths, dtype=jnp.int32)
    starts = ends - lengths
    number = jnp.sum((index[:, None] >= ends[None, :]).astype(jnp.int32), axis=1, dtype=jnp.int32)
    live = index < ends[-1]
    match = number[:, None] == jnp.arange(lengths.shape[0], dtype=jnp.int32)[None, :]
    begin = jnp.sum(jnp.where(match, starts[None, :], 0), axis=1, dtype=jnp.int32)
    return jnp.where(live, begin, index), jnp.where(live, index - begin, 0)


def local(tokens, document_lengths, cotangent, attention_gain, query_projection, narrowing_factor,
          widening_factor, key_value_projection, output_projection, feedforward_gain,
          gate_projection, up_projection, down_projection):
    batches, _, rows, width = tokens.shape
    head_dim = key_value_projection.shape[1] // 2
    q_cols = query_projection.shape[1]
    scale = head_dim ** (-0.5)
    parts = lax.axis_size("fsdp")
    place = lax.axis_index("seq")
    tile = math.gcd(rows, 256)
    block = math.gcd(rows, 512)

    def gather(x):
        return lax.all_gather(x, "fsdp", axis=0, tiled=True)

    piece = width // parts
    mid = narrowing_factor.shape[1]
    gains = jnp.stack([attention_gain, feedforward_gain], axis=1)
    first = gather(jnp.concatenate(
        [query_projection, key_value_projection, narrowing_factor,
         jnp.pad(gains, ((0, 0), (0, 126)))], axis=1))
    ww = gather(widening_factor)
    gate_up = gather(jnp.concatenate([gate_projection, up_projection], axis=1))
    wo = gather(output_projection)
    wd = gather(down_projection)
    kv_cols = 2 * head_dim
    hidden = gate_projection.shape[1]
    wq = first[:, :q_cols]
    wkv = first[:, q_cols : q_cols + kv_cols]
    wn = first[:, q_cols + kv_cols : q_cols + kv_cols + mid]
    gain_one = first[:, q_cols + kv_cols + mid].astype(F32)[None, :]
    gain_two = first[:, q_cols + kv_cols + mid + 1].astype(F32)[None, :]
    wg, wu = gate_up[:, :hidden], gate_up[:, hidden:]

    index = place * rows + jnp.arange(rows, dtype=jnp.int32)
    lows, positions = [], []
    for m in range(batches):
        low, position = layout(document_lengths[m, 0], index)
        lows.append(low)
        positions.append(position)
    position = jnp.concatenate(positions).astype(F32)
    half = head_dim // 2
    freqs = THETA ** (-(jnp.arange(half, dtype=F32) * 2.0 / head_dim))
    angles = position[:, None] * freqs[None, :]
    cos, sin = jnp.cos(angles), jnp.sin(angles)
    infos = []
    for m in range(batches):
        marks = [place * rows, ((place + 1) * rows + block - 1) // block]
        marks += [lows[m][t * tile] // block for t in range(rows // tile)]
        infos.append(jnp.stack(marks).astype(jnp.int32))

    x = tokens.reshape(batches * rows, width)
    grad = cotangent.reshape(batches * rows, width)
    normed, lora_mid, q, kv = project(x, gain_one, cos, sin, wq, wn, ww, wkv, head_dim, scale)
    kv_all, attended, lses = [], [], []
    for m in range(batches):
        at = slice(m * rows, (m + 1) * rows)
        kv_all.append(lax.all_gather(kv[at], "seq", axis=0, tiled=True))
    for m in range(batches):
        at = slice(m * rows, (m + 1) * rows)
        o, lse = attend(infos[m], lows[m][None, :], q[at], kv_all[m], head_dim, tile, block)
        attended.append(o)
        lses.append(lse)
    attended = jnp.concatenate(attended)
    (output, mid_grad, branch, attn_grad, delta, ffn_low, hidden_low, gate_grad, lift_grad,
     gain_two_grad) = middle_part(x, attended, grad, gain_two, wo, wg, wu, wd, head_dim)
    down_grad = weight_grad(grad, hidden_low)
    gate_w_grad = weight_grad(ffn_low, gate_grad)
    lift_w_grad = weight_grad(ffn_low, lift_grad)
    out_grad = weight_grad(branch, attended)
    dqs, dkvs = [], []
    for m in range(batches):
        at = slice(m * rows, (m + 1) * rows)
        dq, dkv = attend_back(infos[m], lows[m][None, :], lses[m], delta[:, at], q[at],
                              attn_grad[at], kv_all[m], cos[at], sin[at], head_dim, tile, block,
                              scale)
        dqs.append(dq)
        dkvs.append(lax.psum_scatter(dkv.astype(BF16), "seq", scatter_dimension=0, tiled=True))
    dq = jnp.concatenate(dqs)
    dkv = jnp.concatenate(dkvs)
    lora_grad, pair_grad, in_grad, gain_one_grad = project_back(
        x, gain_one, cos, sin, wq, wn, ww, wkv, dq, dkv, mid_grad, head_dim)
    query_grad = weight_grad(normed, dq)
    pair_w_grad = weight_grad(normed, pair_grad)
    narrow_grad = weight_grad(normed, lora_grad)
    widen_grad = weight_grad(lora_mid, dq)

    def scatter(x, dim=0):
        part = lax.psum_scatter(x.astype(BF16), "fsdp", scatter_dimension=dim, tiled=True)
        return part

    gain_pair = jnp.concatenate([gain_one_grad, gain_two_grad], axis=0)
    sums = [
        scatter(jnp.concatenate([query_grad, narrow_grad, pair_w_grad, gate_w_grad, lift_w_grad,
                                 jnp.pad(gain_pair.T.astype(BF16), ((0, 0), (0, 126)))], axis=1)),
        scatter(widen_grad),
        scatter(jnp.concatenate([down_grad.reshape(width, parts, -1),
                                 out_grad.reshape(width, parts, -1)], axis=2)
                .reshape(width, -1).T),
    ]
    sums = lax.psum(tuple(sums), "seq")
    wide, widen, turned = sums
    wide = wide.astype(F32)
    turned = turned.astype(F32)
    cuts = [0]
    for n in (q_cols, mid, kv_cols, hidden, hidden):
        cuts.append(cuts[-1] + n)
    pieces = [wide[:, cuts[i] : cuts[i + 1]] for i in range(5)]
    shard = hidden // parts
    return (
        output.reshape(batches, 1, rows, width),
        in_grad.reshape(batches, 1, rows, width),
        wide[:, cuts[5]],
        pieces[0],
        pieces[1],
        widen.astype(F32),
        pieces[2],
        turned[shard:],
        wide[:, cuts[5] + 1],
        pieces[3],
        pieces[4],
        turned[:shard],
    )


def solution(mesh):
    rows = P(None, "fsdp", "seq", None)
    vector, matrix = P("fsdp"), P("fsdp", None)
    in_specs = (rows, P(None, "fsdp", None), rows, vector) + (matrix,) * 5 + (vector,) + (matrix,) * 3
    out_specs = (rows, rows, vector) + (matrix,) * 5 + (vector,) + (matrix,) * 3
    return jax.shard_map(local, mesh=mesh, in_specs=in_specs, out_specs=out_specs, check_vma=False)
```

```python
import functools
import math

import jax
import jax.numpy as jnp
from jax import lax
from jax.experimental import pallas as pl
from jax.experimental.pallas import tpu as pltpu
from jax.sharding import PartitionSpec as P

EPSILON = 1e-06
THETA = 10000.0
F32 = jnp.float32
BF16 = jnp.bfloat16
GELU_C = math.sqrt(2.0 / math.pi)
GELU_A = 0.044715
LOWEST = -1e30
VMEM_LIMIT = 60 * 1024 * 1024
ANY = pl.BlockSpec(memory_space=pl.ANY)
VMEM = pl.BlockSpec(memory_space=pltpu.VMEM)
SMEM = pl.BlockSpec(memory_space=pltpu.SMEM)


def mm(left, right):
    return lax.dot_general(left, right, (((1,), (0,)), ((), ())), preferred_element_type=F32)


def mm_nt(left, right):
    return lax.dot_general(left, right, (((1,), (1,)), ((), ())), preferred_element_type=F32)


def full(shape):
    return pl.BlockSpec(shape, lambda i: (0,) * len(shape))


def rows_of(tile, cols):
    return pl.BlockSpec((tile, cols), lambda i: (i, 0))


def params(**more):
    return pltpu.CompilerParams(vmem_limit_bytes=VMEM_LIMIT, **more)


def cost(flops, bytes_accessed, transcendentals=0):
    return pl.CostEstimate(
        flops=int(flops), bytes_accessed=int(bytes_accessed), transcendentals=int(transcendentals)
    )


def like(shape, dtype):
    return jax.ShapeDtypeStruct(tuple(shape), dtype)


def swap(x, axis, by):
    return lax.ppermute(x, axis, [(i, i ^ by) for i in range(lax.axis_size(axis))])


def skipping(kernel, first, count):
    return lambda *refs: kernel(*refs[:first], *refs[first + count :])


def tree(values):
    while len(values) > 1:
        values = [values[i] + values[i + 1] for i in range(0, len(values), 2)]
    return values[0]


def add_kernel(*refs, count, groups):
    for out, group in zip(refs[count:], groups):
        values = [refs[i][...] if k is None else refs[i][k] for i, k in group]
        out[...] = tree([v.astype(F32) for v in values]).astype(out.dtype)


def add(arrays, groups, later=(), dtype=BF16):
    shapes = [arrays[g[0][0]].shape if g[0][1] is None else arrays[g[0][0]].shape[1:]
              for g in groups]
    count = len(arrays)
    later = list(later)
    return list(pl.pallas_call(
        skipping(functools.partial(add_kernel, count=count, groups=groups), count, len(later)),
        in_specs=[VMEM] * count + [ANY] * len(later),
        out_specs=[VMEM] * len(groups),
        out_shape=[like(s, dtype) for s in shapes],
        compiler_params=params(),
        cost_estimate=cost(0, sum(2 * a.size for a in arrays)),
        name="add",
    )(*arrays, *later))


class Whole:
    def __init__(self, array):
        self.arrays = [array]
        self.shape = array.shape
        self.count = 1

    def copies(self, where, refs, dst):
        return [(refs[0], dst)]


class Shards:
    def __init__(self, x):
        parts = lax.axis_size("fsdp")
        got = {0: x}
        for r in range(2, parts, 2):
            got[r] = swap(x, "fsdp", r)
        self.last = [got[r] for r in range(2, parts, 2)]
        for r in range(0, parts, 2):
            got[r + 1] = swap(got[r], "fsdp", 1)
        self.arrays = [got[r] for r in range(parts)]
        self.rows = x.shape[0]
        self.shape = (parts * x.shape[0], x.shape[1])
        self.count = parts

    def copies(self, where, refs, dst):
        out = []
        for r, ref in enumerate(refs):
            at = pl.multiple_of((where[0] ^ r) * self.rows, self.rows)
            out.append((ref, dst.at[pl.ds(at, self.rows), :]))
        return out


class Tiled:
    def __init__(self, gate_up, *tall):
        parts, span = lax.axis_size("fsdp"), lax.axis_size("seq")
        q = lax.axis_index("seq")
        piece = gate_up.shape[0]
        part = gate_up.shape[1] // span
        self.piece, self.part, self.parts, self.span = piece, part, parts, span
        self.heights = [t.shape[0] // span for t in tall]
        stack = jnp.concatenate([lax.dynamic_slice_in_dim(t, q * n, n, 0)
                                 for t, n in zip(tall, self.heights)])
        self.up, self.across = stack.shape[0] // 16, stack.shape[1] // 128
        stack = stack.reshape(self.up, 16, self.across, 128).transpose(2, 1, 0, 3)
        stack = stack.reshape(piece, self.up * 128)
        mine = lax.dynamic_slice_in_dim(gate_up, q * part, part, 1)
        packed = jnp.concatenate([mine, stack], axis=1)
        self.array = lax.all_gather(packed, ("seq", "fsdp"), axis=0, tiled=True)
        self.shape = (parts * piece, gate_up.shape[1])
        self.shapes = [(parts * t.shape[0], t.shape[1]) for t in tall]
        self.scratch = (span, parts * piece, self.up * 128)

    def copies(self, ref, dst, rest):
        out = []
        height = self.parts * self.piece
        for s in range(self.span):
            rows = pl.ds(s * height, height)
            out.append((ref.at[rows, pl.ds(0, self.part)],
                        dst.at[:, pl.ds(s * self.part, self.part)]))
            out.append((ref.at[rows, pl.ds(self.part, self.up * 128)], rest.at[s]))
        return out

    def unfold(self, rest, dsts):
        starts, tops = [], 0
        for n in self.heights:
            starts.append(tops)
            tops += n // 16

        def shard(d, carry):
            for s in range(self.span):
                for n, first, dst in zip(self.heights, starts, dsts):
                    for i in range(n // 16):
                        at = pl.ds(pl.multiple_of(d * n * self.span + s * n + i * 16, 16), 16)
                        for j in range(self.across):
                            row = pl.ds(pl.multiple_of(d * self.piece + 16 * j, 16), 16)
                            col = (first + i) * 128
                            dst[at, j * 128 : (j + 1) * 128] = rest[s, row, col : col + 128]
            return carry

        lax.fori_loop(0, self.parts, shard, 0)


def carry_out(copies, sem):
    made = [pltpu.make_async_copy(src, dst, sem.at[i]) for i, (src, dst) in enumerate(copies)]
    for c in made:
        c.start()
    for c in made:
        c.wait()


def project_kv_kernel(*refs, held, head_dim, mid_rows):
    where, x_ref, cos_ref, sin_ref = refs[:4]
    pieces = refs[4 : 4 + len(held.arrays)]
    normed_ref, kv_ref, w_ref, gains_ref, sem = refs[4 + len(held.arrays) :]
    kv_cols = 2 * head_dim

    @pl.when(pl.program_id(0) == 0)
    def _():
        carry_out(held.copies(where, pieces, w_ref), sem)
        gains_ref[...] = w_ref[:, kv_cols:].astype(F32).T[:8]

    half = head_dim // 2
    x = x_ref[...].astype(F32)
    inv = lax.rsqrt(jnp.mean(x * x, axis=-1, keepdims=True) + EPSILON)
    normed = (x * inv * gains_ref[0:1, :]).astype(BF16)
    normed_ref[...] = normed
    cos, sin = cos_ref[...], sin_ref[...]
    pair = mm(normed, w_ref[:, :kv_cols])
    a, b = pair[:, :half], pair[:, half:head_dim]
    kv_ref[:, :half] = (a * cos - b * sin).astype(BF16)
    kv_ref[:, half:head_dim] = (b * cos + a * sin).astype(BF16)
    kv_ref[:, head_dim:] = pair[:, head_dim:].astype(BF16)


def project_kv(where, x, cos, sin, held, head_dim):
    rows, width = x.shape
    tile = math.gcd(rows, 256)
    half = head_dim // 2
    return pl.pallas_call(
        functools.partial(project_kv_kernel, held=held, head_dim=head_dim, mid_rows=0),
        grid=(rows // tile,),
        in_specs=[SMEM, rows_of(tile, width), rows_of(tile, half), rows_of(tile, half)]
        + [ANY] * len(held.arrays),
        out_specs=[rows_of(tile, width), rows_of(tile, 2 * head_dim), full(held.shape),
                   full((8, width))],
        out_shape=[like((rows, width), BF16), like((rows, 2 * head_dim), BF16),
                   like(held.shape, BF16), like((8, width), F32)],
        scratch_shapes=[pltpu.SemaphoreType.DMA((held.count,))],
        compiler_params=params(),
        cost_estimate=cost(4 * rows * width * head_dim, 6e6),
        name="project_kv",
    )(where, x, cos, sin, *held.arrays)


def project_q_kernel(*refs, held, head_dim, q_cols, mid, scale):
    where, normed_ref, cos_ref, sin_ref = refs[:4]
    pieces = refs[4 : 4 + len(held.arrays)]
    lora_ref, q_ref, w_ref, ww_ref, sem = refs[4 + len(held.arrays) :]
    half = head_dim // 2
    fold = (held.shape[1] - q_cols - mid)
    parts = q_cols // fold

    @pl.when(pl.program_id(0) == 0)
    def _():
        carry_out(held.copies(where, pieces, w_ref), sem)
        shards = held.shape[0] // held.rows if hasattr(held, "rows") else 0
        count = mid // shards
        for d in range(shards):
            for j in range(parts):
                ww_ref[d * count : (d + 1) * count, j * fold : (j + 1) * fold] = w_ref[
                    d * held.rows + j * count : d * held.rows + (j + 1) * count, q_cols + mid :]

    normed = normed_ref[...]
    cos, sin = cos_ref[...], sin_ref[...]
    low = mm(normed, w_ref[:, q_cols : q_cols + mid]).astype(BF16)
    lora_ref[...] = low
    query = mm(normed, w_ref[:, :q_cols]) + mm(low, ww_ref[...])
    for h in range(q_cols // head_dim):
        c = h * head_dim
        a, b = query[:, c : c + half], query[:, c + half : c + head_dim]
        q_ref[:, c : c + half] = ((a * cos - b * sin) * scale).astype(BF16)
        q_ref[:, c + half : c + head_dim] = ((b * cos + a * sin) * scale).astype(BF16)


def project_q(where, normed, cos, sin, held, head_dim, q_cols, mid, scale):
    rows, width = normed.shape
    tile = math.gcd(rows, 256)
    half = head_dim // 2
    return pl.pallas_call(
        functools.partial(project_q_kernel, held=held, head_dim=head_dim, q_cols=q_cols, mid=mid,
                          scale=scale),
        grid=(rows // tile,),
        in_specs=[SMEM, rows_of(tile, width), rows_of(tile, half), rows_of(tile, half)]
        + [ANY] * len(held.arrays),
        out_specs=[rows_of(tile, mid), rows_of(tile, q_cols), full(held.shape),
                   full((mid, q_cols))],
        out_shape=[like((rows, mid), BF16), like((rows, q_cols), BF16), like(held.shape, BF16),
                   like((mid, q_cols), BF16)],
        scratch_shapes=[pltpu.SemaphoreType.DMA((held.count,))],
        compiler_params=params(),
        cost_estimate=cost(2 * rows * (width * (q_cols + mid) + mid * q_cols), 8e6),
        name="project_q",
    )(where, normed, cos, sin, *held.arrays)


def attend_kernel(*refs, head_dim, tile, block, span):
    info_ref, low_ref, q_ref = refs[:3]
    kvs = refs[3 : 3 + span]
    o_ref, lse_ref, kv_ref, vt_ref, acc_ref, sem = refs[-6:]
    heads = q_ref.shape[1] // head_dim
    rows = q_ref.shape[0]
    base, last, place = info_ref[0], info_ref[1], info_ref[2]

    def copy(s):
        at = pl.multiple_of((place ^ s) * rows, rows)
        return pltpu.make_async_copy(kvs[s], kv_ref.at[pl.ds(at, rows), :], sem.at[s])

    for s in range(span):
        pl.when((place ^ s) <= place)(lambda s=s: copy(s).start())
    for s in range(span):
        pl.when((place ^ s) <= place)(lambda s=s: copy(s).wait())

    def flip(kb, carry):
        at = pl.ds(pl.multiple_of(kb * block, block), block)
        vt_ref[:, at] = kv_ref[at, head_dim:].T
        return carry

    lax.fori_loop(info_ref[3], last, flip, 0)
    for t in range(rows // tile):
        q_rows = slice(t * tile, (t + 1) * tile)
        low = low_ref[:, q_rows]
        high = base + t * tile + lax.broadcasted_iota(jnp.int32, (1, tile), 1)
        acc_ref[...] = jnp.zeros_like(acc_ref)

        def visit(kb, carry):
            at = pl.ds(pl.multiple_of(kb * block, block), block)
            keys = kv_ref[at, :head_dim]
            vt = vt_ref[:, at]
            index = kb * block + lax.broadcasted_iota(jnp.int32, (block, tile), 0)
            mask = (index >= low) & (index <= high)
            out = []
            for h in range(heads):
                peak, total = carry[h]
                s = mm_nt(keys, q_ref[q_rows, h * head_dim : (h + 1) * head_dim])
                s = jnp.where(mask, s, -jnp.inf)
                new_peak = jnp.maximum(peak, jnp.max(s, axis=0, keepdims=True))
                factor = jnp.exp(peak - new_peak)
                p = jnp.exp(s - new_peak)
                total = total * factor + jnp.sum(p, axis=0, keepdims=True)
                acc_ref[h] = acc_ref[h] * factor + mm(vt, p.astype(BF16))
                out.append((new_peak, total))
            return tuple(out)

        start = tuple(
            (jnp.full((1, tile), LOWEST, F32), jnp.zeros((1, tile), F32)) for _ in range(heads)
        )
        stats = lax.fori_loop(info_ref[3 + t], (base + (t + 1) * tile + block - 1) // block,
                              visit, start)
        for h in range(heads):
            peak, total = stats[h]
            o_ref[q_rows, h * head_dim : (h + 1) * head_dim] = (acc_ref[h] / total).T.astype(BF16)
            lse_ref[h : h + 1, q_rows] = peak + jnp.log(total)


def attend(info, low, q, kvs, head_dim, tile, block, m, batches, before=None):
    q_cols = q.shape[1]
    rows = q.shape[0] // batches
    heads = q_cols // head_dim
    span = len(kvs)
    group = span * rows
    here = pl.BlockSpec((rows, q_cols), lambda i: (m, 0))
    more = [] if before is None else [before]
    return pl.pallas_call(
        functools.partial(attend_kernel, head_dim=head_dim, tile=tile, block=block, span=span),
        grid=(1,),
        in_specs=[SMEM, VMEM, here] + [ANY] * (span + len(more)),
        out_specs=[here, VMEM, VMEM],
        out_shape=[like(q.shape, BF16), like((heads, rows), F32),
                   like((group, 2 * head_dim), BF16)],
        scratch_shapes=[pltpu.VMEM((head_dim, group), BF16),
                        pltpu.VMEM((heads, head_dim, tile), F32),
                        pltpu.SemaphoreType.DMA((span,))],
        input_output_aliases={3 + span: 0} if more else {},
        compiler_params=params(),
        cost_estimate=cost(4 * rows * group * q_cols, 6e6, rows * group * heads),
        name="attend",
    )(info, low, q, *kvs, *more)


def middle_kernel(*refs, held, head_dim, chunk):
    x_ref, attn_ref, g_ref, gains_ref = refs[:4]
    if held is None:
        w_ref, wd_ref, wo_ref = refs[4:7]
    else:
        w_ref, wd_ref, wo_ref, rest_ref, sem = refs[-5:]
    (out_ref, mid_grad_ref, branch_ref, attn_grad_ref, delta_ref, low_ref, hidden_ref, grads_ref,
     gain_grad_ref) = refs[5:14] if held is not None else refs[7:16]

    @pl.when(pl.program_id(0) == 0)
    def _():
        if held is not None:
            carry_out(held.copies(refs[4], w_ref, rest_ref), sem)
            held.unfold(rest_ref, [wd_ref, wo_ref])
        gain_grad_ref[...] = jnp.zeros_like(gain_grad_ref)

    gain = gains_ref[1:2, :]
    attn = attn_ref[...]
    middle = x_ref[...].astype(F32) + mm(attn, wo_ref[...])
    inv = lax.rsqrt(jnp.mean(middle * middle, axis=-1, keepdims=True) + EPSILON)
    unit = middle * inv
    low = (unit * gain).astype(BF16)
    low_ref[...] = low
    grad = g_ref[...]
    result = middle
    back = jnp.zeros_like(middle)
    wide = wd_ref.shape[0]
    for c in range(wide // chunk):
        at = slice(c * chunk, (c + 1) * chunk)
        to = slice(wide + c * chunk, wide + (c + 1) * chunk)
        gate = mm(low, w_ref[:, at])
        lift = mm(low, w_ref[:, to])
        square = gate * gate
        bend = jnp.tanh(GELU_C * gate * (1.0 + GELU_A * square))
        cdf = 0.5 * (1.0 + bend)
        gelu = gate * cdf
        hidden = (gelu * lift).astype(BF16)
        hidden_ref[:, at] = hidden
        result = result + mm(hidden, wd_ref[at, :])
        hidden_grad = mm_nt(grad, wd_ref[at, :])
        slope = cdf + (0.5 * GELU_C) * gate * (1.0 - bend * bend) * (1.0 + 3.0 * GELU_A * square)
        gate_grad = (hidden_grad * lift * slope).astype(BF16)
        lift_grad = (hidden_grad * gelu).astype(BF16)
        grads_ref[:, at] = gate_grad
        grads_ref[:, to] = lift_grad
        back = back + mm_nt(gate_grad, w_ref[:, at]) + mm_nt(lift_grad, w_ref[:, to])
    out_ref[...] = result.astype(BF16)
    gain_grad_ref[...] += jnp.sum(unit * back, axis=0, keepdims=True)
    scaled = back * gain
    mid_grad = grad.astype(F32) + inv * (
        scaled - unit * jnp.mean(unit * scaled, axis=-1, keepdims=True)
    )
    mid_grad_ref[...] = mid_grad
    branch = mid_grad.astype(BF16)
    branch_ref[...] = branch
    attn_grad = mm_nt(branch, wo_ref[...]).astype(BF16)
    attn_grad_ref[...] = attn_grad
    product = attn_grad.astype(F32) * attn.astype(F32)
    half = head_dim // 2
    for h in range(attn.shape[1] // head_dim):
        c = h * head_dim
        folded = product[:, c : c + half] + product[:, c + half : c + head_dim]
        delta_ref[h : h + 1, :] = jnp.sum(folded.T, axis=0, keepdims=True)


def middle_part(x, attn, grad, gains, held, weights, head_dim):
    rows, width = x.shape
    q_cols = attn.shape[1]
    hidden = (weights[0].shape if held is None else held.shape)[1] // 2
    heads = q_cols // head_dim
    tile = math.gcd(rows, 256)
    if held is None:
        more, specs, scratch = weights, [full(w.shape) for w in weights], []
    else:
        more, specs = [held.array], [ANY]
        scratch = [pltpu.VMEM(held.shape, BF16)] + [pltpu.VMEM(s, BF16) for s in held.shapes]
        scratch += [pltpu.VMEM(held.scratch, BF16), pltpu.SemaphoreType.DMA((2 * held.span,))]
    return pl.pallas_call(
        functools.partial(middle_kernel, held=held, head_dim=head_dim, chunk=512),
        grid=(rows // tile,),
        in_specs=[rows_of(tile, width), rows_of(tile, q_cols), rows_of(tile, width),
                  full(gains.shape)] + specs,
        out_specs=[rows_of(tile, width), rows_of(tile, width), rows_of(tile, width),
                   rows_of(tile, q_cols), pl.BlockSpec((heads, tile), lambda i: (0, i)),
                   rows_of(tile, width), rows_of(tile, hidden), rows_of(tile, 2 * hidden),
                   full((1, width))],
        out_shape=[like((rows, width), BF16), like((rows, width), F32), like((rows, width), BF16),
                   like((rows, q_cols), BF16), like((heads, rows), F32),
                   like((rows, width), BF16), like((rows, hidden), BF16),
                   like((rows, 2 * hidden), BF16), like((1, width), F32)],
        scratch_shapes=scratch,
        compiler_params=params(),
        cost_estimate=cost(4 * rows * width * (q_cols + 3 * hidden), 40e6, rows * hidden),
        name="middle",
    )(x, attn, grad, gains, *more)


def attend_back_kernel(*refs, head_dim, tile, block, scale):
    info_ref, low_ref, lse_ref, delta_ref, q_ref, do_ref, kv_ref, cos_ref, sin_ref = refs[:9]
    span = kv_ref.shape[0] // q_ref.shape[0]
    sends = refs[-3 - (span - 1) : -3]
    dq_ref, own_ref = refs[-3 - span - 1 : -3 - span + 1]
    dkv_ref, kt_ref, acc_ref = refs[-3:]
    heads = q_ref.shape[1] // head_dim
    half = head_dim // 2
    rows = q_ref.shape[0]
    base, last, place = info_ref[0], info_ref[1], info_ref[2]
    tiles = rows // tile
    acc_ref[...] = jnp.zeros_like(acc_ref)
    dkv_ref[...] = jnp.zeros_like(dkv_ref)

    def visit(kb, carry):
        at = pl.ds(pl.multiple_of(kb * block, block), block)
        keys = kv_ref[at, :head_dim]
        vals = kv_ref[at, head_dim:]
        kt_ref[...] = keys.T
        for t in range(tiles):
            q_rows = slice(t * tile, (t + 1) * tile)

            @pl.when((kb >= info_ref[3 + t]) & (kb * block < base + (t + 1) * tile))
            def _():
                low = low_ref[:, q_rows]
                high = base + t * tile + lax.broadcasted_iota(jnp.int32, (1, tile), 1)
                index = kb * block + lax.broadcasted_iota(jnp.int32, (block, tile), 0)
                mask = (index >= low) & (index <= high)
                dk = jnp.zeros((block, head_dim), F32)
                dv = jnp.zeros((block, head_dim), F32)
                for h in range(heads):
                    cols = slice(h * head_dim, (h + 1) * head_dim)
                    q = q_ref[q_rows, cols]
                    do = do_ref[q_rows, cols]
                    s = mm_nt(keys, q)
                    p = jnp.where(mask, jnp.exp(s - lse_ref[h : h + 1, q_rows]), 0.0)
                    dv = dv + mm(p.astype(BF16), do)
                    ds = (p * (mm_nt(vals, do) - delta_ref[h : h + 1, q_rows])).astype(BF16)
                    dk = dk + mm(ds, q)
                    acc_ref[h, :, q_rows] += mm(kt_ref[...], ds)
                dkv_ref[at, :head_dim] += dk
                dkv_ref[at, head_dim:] += dv

        return carry

    lax.fori_loop(info_ref[3], last, visit, 0)
    cos, sin = cos_ref[...], sin_ref[...]
    for h in range(heads):
        c = h * head_dim
        dq = acc_ref[h].T * scale
        a, b = dq[:, :half], dq[:, half:]
        dq_ref[:, c : c + half] = (a * cos + b * sin).astype(BF16)
        dq_ref[:, c + half : c + head_dim] = (b * cos - a * sin).astype(BF16)
    own_ref[...] = dkv_ref[pl.ds(pl.multiple_of(place * rows, rows), rows), :]
    for s, send_ref in enumerate(sends, 1):
        at = pl.multiple_of((place ^ s) * rows, rows)
        send_ref[...] = dkv_ref[pl.ds(at, rows), :].astype(BF16)


def attend_back(info, low, lse, delta, q, do, kv, cos, sin, head_dim, tile, block, scale, m,
                batches, before, later):
    q_cols = q.shape[1]
    rows = q.shape[0] // batches
    heads = q_cols // head_dim
    span = kv.shape[0] // rows
    half = head_dim // 2
    here = pl.BlockSpec((rows, q_cols), lambda i: (m, 0))
    angle = pl.BlockSpec((rows, half), lambda i: (m, 0))
    more = ([] if before is None else [before]) + later
    return pl.pallas_call(
        functools.partial(attend_back_kernel, head_dim=head_dim, tile=tile, block=block,
                          scale=scale),
        grid=(1,),
        in_specs=[SMEM, VMEM, VMEM, pl.BlockSpec((heads, rows), lambda i: (0, m)), here, here,
                  VMEM, angle, angle] + [ANY] * len(more),
        out_specs=[here] + [VMEM] * span,
        out_shape=[like(q.shape, BF16), like((rows, 2 * head_dim), F32)]
        + [like((rows, 2 * head_dim), BF16)] * (span - 1),
        scratch_shapes=[pltpu.VMEM(kv.shape, F32), pltpu.VMEM((head_dim, block), BF16),
                        pltpu.VMEM((heads, head_dim, rows), F32)],
        input_output_aliases={} if before is None else {9: 0},
        compiler_params=params(),
        cost_estimate=cost(10 * rows * kv.shape[0] * q_cols, 12e6, rows * kv.shape[0] * heads),
        name="attend_back",
    )(info, low, lse, delta, q, do, kv, cos, sin, *more)


def query_back_kernel(dq_ref, w_ref, ww_ref, lora_grad_ref, back_ref, *, q_cols, mid):
    dq = dq_ref[...]
    lora_grad = mm_nt(dq, ww_ref[...]).astype(BF16)
    lora_grad_ref[...] = lora_grad
    back_ref[...] = (mm_nt(dq, w_ref[:, :q_cols])
                     + mm_nt(lora_grad, w_ref[:, q_cols : q_cols + mid]))


def query_back(dq, w, ww, later=()):
    rows, q_cols = dq.shape
    mid, width = ww.shape[0], w.shape[0]
    tile = math.gcd(rows, 256)
    return pl.pallas_call(
        skipping(functools.partial(query_back_kernel, q_cols=q_cols, mid=mid), 3, len(later)),
        grid=(rows // tile,),
        in_specs=[rows_of(tile, q_cols), full(w.shape), full(ww.shape)] + [ANY] * len(later),
        out_specs=[rows_of(tile, mid), rows_of(tile, width)],
        out_shape=[like((rows, mid), BF16), like((rows, width), F32)],
        compiler_params=params(),
        cost_estimate=cost(2 * rows * (width * (q_cols + mid) + mid * q_cols), 9e6),
        name="query_back",
    )(dq, w, ww, *later)


def pair_back_kernel(*refs, head_dim, others):
    x_ref, gains_ref, cos_ref, sin_ref, w_ref, back_ref, mid_grad_ref, own_ref = refs[:8]
    pair_grad_ref, in_grad_ref, gain_grad_ref = refs[-3:]

    @pl.when(pl.program_id(0) == 0)
    def _():
        gain_grad_ref[...] = jnp.zeros_like(gain_grad_ref)

    half = head_dim // 2
    gain = gains_ref[0:1, :]
    cos, sin = cos_ref[...], sin_ref[...]
    dkv = own_ref[...]
    for ref in refs[8 : 8 + others]:
        dkv = dkv + ref[...].astype(F32)
    a, b = dkv[:, :half], dkv[:, half:head_dim]
    pair_grad_ref[:, :half] = (a * cos + b * sin).astype(BF16)
    pair_grad_ref[:, half:head_dim] = (b * cos - a * sin).astype(BF16)
    pair_grad_ref[:, head_dim:] = dkv[:, head_dim:].astype(BF16)
    back = back_ref[...] + mm_nt(pair_grad_ref[...], w_ref[:, : 2 * head_dim])
    x = x_ref[...].astype(F32)
    inv = lax.rsqrt(jnp.mean(x * x, axis=-1, keepdims=True) + EPSILON)
    unit = x * inv
    gain_grad_ref[...] += jnp.sum(unit * back, axis=0, keepdims=True)
    scaled = back * gain
    in_grad_ref[...] = mid_grad_ref[...] + inv * (
        scaled - unit * jnp.mean(unit * scaled, axis=-1, keepdims=True)
    )


def pair_back(x, gains, cos, sin, w, own, others, back, mid_grad, head_dim, m, batches, before=None,
              later=()):
    width = x.shape[1]
    rows = x.shape[0] // batches
    tile = math.gcd(rows, 256)
    half, cols = head_dim // 2, 2 * head_dim
    count = rows // tile

    def here(n):
        return pl.BlockSpec((tile, n), lambda i: (m * count + i, 0))

    more = ([] if before is None else [before]) + list(later)
    return pl.pallas_call(
        functools.partial(pair_back_kernel, head_dim=head_dim, others=len(others)),
        grid=(count,),
        in_specs=[here(width), full(gains.shape), here(half), here(half), full(w.shape),
                  here(width), here(width)] + [rows_of(tile, cols)] * (1 + len(others))
        + [ANY] * len(more),
        out_specs=[rows_of(tile, cols), here(width), full((1, width))],
        out_shape=[like((rows, cols), BF16), like(x.shape, F32), like((1, width), F32)],
        input_output_aliases={} if before is None else {8 + len(others): 1},
        compiler_params=params(),
        cost_estimate=cost(2 * rows * width * cols, 7e6),
        name="pair_back",
    )(x, gains, cos, sin, w, back, mid_grad, own, *others, *more)


def weight_grad_kernel(x_ref, y_ref, out_ref, xt_ref):
    @pl.when(pl.program_id(0) == 0)
    def _():
        xt_ref[...] = x_ref[...].T

    out_ref[...] = mm(xt_ref[...], y_ref[...]).astype(BF16)


def weight_grad(x, y, tile=256, later=()):
    rows, width = x.shape
    cols = y.shape[1]
    tile = math.gcd(cols, tile)
    return pl.pallas_call(
        skipping(weight_grad_kernel, 2, len(later)),
        grid=(cols // tile,),
        in_specs=[full(x.shape), pl.BlockSpec((rows, tile), lambda i: (0, i))] + [ANY] * len(later),
        out_specs=pl.BlockSpec((width, tile), lambda i: (0, i)),
        out_shape=like((width, cols), BF16),
        scratch_shapes=[pltpu.VMEM((width, rows), BF16)],
        compiler_params=params(),
        cost_estimate=cost(2 * rows * width * cols, 2 * (rows * width + rows * cols + width * cols)),
        name="weight_grad",
    )(x, y, *later)


def turn(x_ref, flat_ref, xt_ref, me, parts):
    flat_ref[...] = x_ref[...].T
    piece = flat_ref.shape[0] // parts
    for r in range(parts):
        at = pl.multiple_of((me ^ r) * piece, piece)
        to = (r % 2) * (parts // 2) + r // 2
        xt_ref[to * piece : (to + 1) * piece, :] = flat_ref[pl.ds(at, piece), :]


def column_grads_kernel(where, g_ref, b_ref, hidden_ref, attn_ref, keep_ref, send_ref, gt_ref,
                        bt_ref, *, piece):
    r = pl.program_id(0)

    @pl.when(r == 0)
    def _():
        gt_ref[...] = g_ref[...].T
        bt_ref[...] = b_ref[...].T

    down = mm(gt_ref[...], hidden_ref[...]).astype(BF16)
    out = mm(bt_ref[...], attn_ref[...]).astype(BF16)

    def put(ref):
        span = ref.shape[0]
        per = down.shape[0] // piece // span
        n, k = down.shape[1], out.shape[1]
        for s in range(span):
            to = s ^ where[1]
            for i in range(per):
                at = slice((s * per + i) * piece, (s * per + i + 1) * piece)
                ref[to, 0, :, i * n : (i + 1) * n] = down[at]
                ref[to, 0, :, per * n + i * k : per * n + (i + 1) * k] = out[at]

    pl.when(r % 2 == 0)(lambda: put(keep_ref))
    pl.when(r % 2 == 1)(lambda: put(send_ref))


def column_grads(where, grad, hidden, branch, attn, parts, span):
    rows, width = grad.shape
    piece = width // parts
    n, k = hidden.shape[1] // parts, attn.shape[1] // parts
    cols = (n + k) * (parts // span)
    block = pl.BlockSpec((span, 1, piece, cols), lambda r, where: (0, r // 2, 0, 0))
    shape = like((span, parts // 2, piece, cols), BF16)
    whole = pl.BlockSpec((rows, width), lambda r, where: (0, 0))
    return pl.pallas_call(
        functools.partial(column_grads_kernel, piece=piece),
        grid_spec=pltpu.PrefetchScalarGridSpec(
            num_scalar_prefetch=1,
            grid=(parts,),
            in_specs=[whole, whole,
                      pl.BlockSpec((rows, n), lambda r, where: (0, where[0] ^ r)),
                      pl.BlockSpec((rows, k), lambda r, where: (0, where[0] ^ r))],
            out_specs=[block, block],
            scratch_shapes=[pltpu.VMEM((width, rows), BF16)] * 2,
        ),
        out_shape=[shape, shape],
        compiler_params=params(),
        cost_estimate=cost(2 * rows * width * cols * span, 16e6),
        name="column_grads",
    )(where, grad, branch, hidden, attn)


def query_grads_kernel(normed_ref, lora_ref, dq_ref, lora_grad_ref, out_ref, xt_ref, xt2_ref,
                       *, parts, fold):
    xt_ref[...] = normed_ref[...].T
    xt2_ref[...] = lora_ref[...].T
    piece, count = xt_ref.shape[0] // parts, xt2_ref.shape[0] // parts
    q_cols, mid = dq_ref.shape[1], lora_grad_ref.shape[1]
    step = math.gcd(q_cols, 512)
    for c in range(0, q_cols, step):
        out_ref[:, c : c + step] = mm(xt_ref[...], dq_ref[:, c : c + step]).astype(BF16)
    out_ref[:, q_cols : q_cols + mid] = mm(xt_ref[...], lora_grad_ref[...]).astype(BF16)
    for j in range(q_cols // fold):
        out = mm(xt2_ref[...], dq_ref[:, j * fold : (j + 1) * fold]).astype(BF16)
        for d in range(parts):
            at = d * piece + j * count
            out_ref[at : at + count, q_cols + mid :] = out[d * count : (d + 1) * count]
    rest = (q_cols // fold) * count
    for d in range(parts):
        out_ref[d * piece + rest : (d + 1) * piece, q_cols + mid :] = jnp.zeros(
            (piece - rest, fold), BF16)


def query_grads(normed, lora_mid, dq, lora_grad, parts, fold):
    rows, width = normed.shape
    mid, q_cols = lora_mid.shape[1], dq.shape[1]
    return pl.pallas_call(
        functools.partial(query_grads_kernel, parts=parts, fold=fold),
        in_specs=[VMEM] * 4,
        out_specs=VMEM,
        out_shape=like((width, q_cols + mid + fold), BF16),
        scratch_shapes=[pltpu.VMEM((width, rows), BF16), pltpu.VMEM((mid, rows), BF16)],
        compiler_params=params(),
        cost_estimate=cost(2 * rows * (width * (q_cols + mid) + mid * q_cols), 10e6),
        name="query_grads",
    )(normed, lora_mid, dq, lora_grad)


def pair_grads_kernel(where, normed_ref, *refs, parts, batches):
    pairs, ones = refs[:batches], refs[batches : 2 * batches]
    two_ref = refs[2 * batches]
    outs, (flat_ref, xt_ref, gain_ref) = refs[2 * batches + 1 : -3], refs[-3:]
    send_ref, keeps = outs[0], outs[1:]
    turn(normed_ref, flat_ref, xt_ref, where[0], parts)
    width = flat_ref.shape[0]
    piece, half, cols = width // parts, parts // 2, pairs[0].shape[1]
    pair = jnp.concatenate([p[...] for p in pairs])
    out = mm(xt_ref[...], pair).astype(BF16)
    pad = jnp.zeros((126, width), F32)
    one = ones[0][...]
    for ref in ones[1:]:
        one = one + ref[...]
    gain_ref[...] = jnp.concatenate([one, two_ref[...], pad], axis=0).T.astype(BF16)
    for k in range(half):
        keeps[k][:, :cols] = out[k * piece : (k + 1) * piece]
        send_ref[k, :, :cols] = out[(half + k) * piece : (half + k + 1) * piece]
        at = pl.multiple_of((where[0] ^ (2 * k)) * piece, piece)
        keeps[k][:, cols:] = gain_ref[pl.ds(at, piece), :]
        at = pl.multiple_of((where[0] ^ (2 * k + 1)) * piece, piece)
        send_ref[k, :, cols:] = gain_ref[pl.ds(at, piece), :]


def pair_grads(where, normed, pairs, ones, two, parts):
    rows, width = normed.shape
    cols = pairs[0].shape[1]
    piece = width // parts
    batches = len(pairs)
    return pl.pallas_call(
        functools.partial(pair_grads_kernel, parts=parts, batches=batches),
        in_specs=[SMEM] + [VMEM] * (2 + 2 * batches),
        out_specs=[VMEM] * (1 + parts // 2),
        out_shape=[like((parts // 2, piece, cols + 128), BF16)]
        + [like((piece, cols + 128), BF16)] * (parts // 2),
        scratch_shapes=[pltpu.VMEM((width, rows), BF16)] * 2 + [pltpu.VMEM((width, 128), BF16)],
        compiler_params=params(),
        cost_estimate=cost(2 * rows * width * cols, 4e6),
        name="pair_grads",
    )(where, normed, *pairs, *ones, two)


def sum_owned(send, keeps):
    got = swap(send, "fsdp", 1)
    count = len(keeps)
    shards = add([*keeps, got], [[(k, None), (count, k)] for k in range(count)])
    there = [shards[0]] + [swap(a, "fsdp", 2 * k) for k, a in enumerate(shards) if k > 0]
    return add(there, [[(i, None) for i in range(count)]])[0]


class QuarterSum:
    def __init__(self, keep, send):
        self.keep, self.got = keep, swap(send, "fsdp", 1)

    def cores(self, *later):
        self.parts = add([self.keep, self.got],
                         [[(0, s), (1, s)] for s in range(self.keep.shape[0])], later)
        self.there = [self.parts[0]] + [
            swap(a, "seq", s) for s, a in enumerate(self.parts) if s > 0]
        return self

    def chips(self, *later):
        count, span = self.keep.shape[1], len(self.there)
        self.shards = add(self.there, [[(s, k) for s in range(span)] for k in range(count)], later)
        self.here = [self.shards[0]] + [
            swap(a, "fsdp", 2 * k) for k, a in enumerate(self.shards) if k > 0]
        return self

    def total(self, *later):
        return add(self.here, [[(k, None) for k in range(len(self.here))]], later)[0]


def cut_kernel(where, x_ref, *outs):
    part = outs[0].shape[1]
    for s, out in enumerate(outs):
        at = pl.multiple_of((where[1] ^ s) * part, part)
        out[...] = x_ref[:, pl.ds(at, part)]


def sum_parts(where, x, later=()):
    span = lax.axis_size("seq")
    rows, part = x.shape[0], x.shape[1] // span
    cut = pl.pallas_call(
        skipping(cut_kernel, 2, len(later)),
        in_specs=[SMEM, VMEM] + [ANY] * len(later),
        out_specs=[VMEM] * span,
        out_shape=[like((rows, part), x.dtype)] * span,
        compiler_params=params(),
        cost_estimate=cost(0, 4 * x.size),
        name="cut",
    )(where, x, *later)
    there = [cut[0]] + [swap(cut[s], "seq", s) for s in range(1, span)]
    return add(there, [[(s, None) for s in range(span)]])[0]


def lay_kernel(where, *refs, n, k):
    span = (len(refs) - 6) // 2
    parts, columns = refs[:span], refs[span : 2 * span]
    gate_ref, up_ref, down_ref, out_ref, tall_ref, tall2_ref = refs[-6:]
    piece = parts[0].shape[0]
    half = span // 2
    wide = parts[0].shape[1]
    per = columns[0].shape[1] // (n + k)
    for s in range(span):
        ref, col_ref = parts[s], columns[s]
        q = where[1] ^ s
        for i, out in enumerate((gate_ref, up_ref)):
            @pl.when(q // half == i)
            def _():
                at = pl.multiple_of((q % half) * wide, wide)
                out[:, pl.ds(at, wide)] = ref[...].astype(F32)
        for i in range(per):
            at = pl.ds(pl.multiple_of((q * per + i) * piece, piece), piece)
            tall_ref[at, :] = col_ref[:, i * n : (i + 1) * n].astype(F32)
            first = per * n + i * k
            tall2_ref[at, :] = col_ref[:, first : first + k].astype(F32)
    down_ref[...] = tall_ref[...].T
    out_ref[...] = tall2_ref[...].T


def lay(where, parts, columns, hidden, n, k, later=()):
    piece = parts[0].shape[0]
    width = piece * lax.axis_size("fsdp")
    return pl.pallas_call(
        skipping(functools.partial(lay_kernel, n=n, k=k), 1 + 2 * len(parts), len(later)),
        in_specs=[SMEM] + [VMEM] * (2 * len(parts)) + [ANY] * len(later),
        out_specs=[VMEM] * 4,
        out_shape=[like((piece, hidden), F32)] * 2 + [like((n, width), F32), like((k, width), F32)],
        scratch_shapes=[pltpu.VMEM((width, n), F32), pltpu.VMEM((width, k), F32)],
        compiler_params=params(),
        cost_estimate=cost(0, 6e6),
        name="lay",
    )(where, *parts, *columns, *later)


def layout(lengths, index):
    ends = jnp.cumsum(lengths, dtype=jnp.int32)
    starts = ends - lengths
    number = jnp.sum((index[:, None] >= ends[None, :]).astype(jnp.int32), axis=1, dtype=jnp.int32)
    live = index < ends[-1]
    match = number[:, None] == jnp.arange(lengths.shape[0], dtype=jnp.int32)[None, :]
    begin = jnp.sum(jnp.where(match, starts[None, :], 0), axis=1, dtype=jnp.int32)
    return jnp.where(live, begin, index), jnp.where(live, index - begin, 0)


def local(tokens, document_lengths, cotangent, attention_gain, query_projection, narrowing_factor,
          widening_factor, key_value_projection, output_projection, feedforward_gain,
          gate_projection, up_projection, down_projection):
    batches, _, rows, width = tokens.shape
    head_dim = key_value_projection.shape[1] // 2
    q_cols = query_projection.shape[1]
    mid = narrowing_factor.shape[1]
    hidden = gate_projection.shape[1]
    kv_cols = 2 * head_dim
    scale = head_dim ** (-0.5)
    parts, span = lax.axis_size("fsdp"), lax.axis_size("seq")
    place = lax.axis_index("seq")
    tile = math.gcd(rows, 256)
    block = math.gcd(rows, 512)
    where = jnp.stack([lax.axis_index("fsdp"), place]).astype(jnp.int32)
    piece = width // parts
    direct = piece % 16 == 0
    fold = 512
    folds = q_cols // fold

    first = jnp.concatenate(
        [key_value_projection,
         jnp.pad(jnp.stack([attention_gain, feedforward_gain], axis=1), ((0, 0), (0, 126)))],
        axis=1)
    turned = jnp.concatenate([widening_factor[:, j * fold : (j + 1) * fold] for j in range(folds)])
    turned = jnp.pad(turned, ((0, piece - turned.shape[0]), (0, 0)))
    second = jnp.concatenate([query_projection, narrowing_factor, turned], axis=1)
    gate_up = jnp.concatenate([gate_projection, up_projection], axis=1)
    if direct:
        held, weights = Tiled(gate_up, down_projection, output_projection), None
        first = Shards(first)
        second = Shards(second)
    else:
        def gather(x):
            return lax.all_gather(x, "fsdp", axis=0, tiled=True)

        first, second = Whole(gather(first)), Whole(gather(second))
        second.rows = piece
        held = None
        weights = [gather(gate_up), gather(down_projection), gather(output_projection)]

    index = place * rows + jnp.arange(rows, dtype=jnp.int32)
    lows, positions = [], []
    for m in range(batches):
        low, position = layout(document_lengths[m, 0], index)
        lows.append(low)
        positions.append(position)
    position = jnp.concatenate(positions).astype(F32)
    half = head_dim // 2
    freqs = THETA ** (-(jnp.arange(half, dtype=F32) * 2.0 / head_dim))
    angles = position[:, None] * freqs[None, :]
    cos, sin = jnp.cos(angles), jnp.sin(angles)
    infos = []
    for m in range(batches):
        marks = [place * rows, ((place + 1) * rows + block - 1) // block, place]
        marks += [lows[m][t * tile] // block for t in range(rows // tile)]
        infos.append(jnp.stack(marks).astype(jnp.int32))

    x = tokens.reshape(batches * rows, width)
    grad = cotangent.reshape(batches * rows, width)
    normed, kv, w_pair, gains = project_kv(where, x, cos, sin, first, head_dim)
    cuts = [slice(m * rows, (m + 1) * rows) for m in range(batches)]
    kvs = []
    for at in cuts:
        kvs.append([kv[at]] + [swap(kv[at], "seq", s) for s in range(1, span)])
    lora_mid, q, w_query, ww = project_q(where, normed, cos, sin, second, head_dim, q_cols, mid,
                                         scale)
    attended, lses, groups = None, [], []
    for m in range(batches):
        attended, lse, group = attend(infos[m], lows[m][None, :], q, kvs[m], head_dim, tile, block,
                                      m, batches, attended)
        lses.append(lse)
        groups.append(group)
    (output, mid_grad, branch, attn_grad, delta, ffn_low, hidden_low, lift_grads,
     gain_two_grad) = middle_part(x, attended, grad, gains, held, weights, head_dim)

    if direct:
        columns = QuarterSum(*column_grads(where, grad, hidden_low, branch, attended, parts, span))
        lifts = weight_grad(ffn_low, lift_grads, 512, [columns.keep])
        columns.cores(lifts)
        lifts_sum = lax.psum_scatter(lifts, "fsdp", scatter_dimension=0, tiled=True)
    dq, owns, others = None, [], []
    for m in range(batches):
        later = []
        if direct and m == 0:
            later = columns.parts + [lifts]
        if direct and m == 1:
            later = columns.chips(dq).shards
        dq, own, *sends = attend_back(infos[m], lows[m][None, :], lses[m], delta, q, attn_grad,
                                      groups[m], cos, sin, head_dim, tile, block, scale, m, batches,
                                      dq, later)
        owns.append(own)
        others.append([swap(a, "seq", s) for s, a in enumerate(sends, 1)])
    later = []
    if direct:
        columns_sum = columns.total(dq)
        later = others[0] + [columns_sum]
    lora_grad, back = query_back(dq, w_query, ww, later)
    later = [], []
    if direct:
        queries = query_grads(normed, lora_mid, dq, lora_grad, parts, fold)
        queries_sum = lax.psum_scatter(queries, "fsdp", scatter_dimension=0, tiled=True)
        lifts_part = sum_parts(where, lifts_sum, [lora_grad])
        later = [queries], [lifts_part]
    in_grad, pairs, ones = None, [], []
    for m in range(batches):
        pair, in_grad, one = pair_back(x, gains, cos, sin, w_pair, owns[m], others[m], back,
                                       mid_grad, head_dim, m, batches, in_grad, later[m])
        pairs.append(pair)
        ones.append(one)
    if direct:
        send, *keeps = pair_grads(where, normed, pairs, ones, gain_two_grad, parts)
        pairs_sum = sum_owned(send, keeps)

        def share(x):
            return [x] + [swap(x, "seq", s) for s in range(1, span)]

        gate_grad, up_grad, down_grad, out_grad = lay(
            where, share(lifts_part), share(columns_sum), hidden, hidden // parts, q_cols // parts,
            [send])
        mine = jnp.concatenate([queries_sum, pairs_sum], axis=1)
        last = add(share(mine), [[(s, None) for s in range(span)]], dtype=F32)[0]
        query_grad = last[:, :q_cols]
        narrow_grad = last[:, q_cols : q_cols + mid]
        count = mid // parts
        widen_grad = jnp.concatenate(
            [last[j * count : (j + 1) * count, q_cols + mid : q_cols + mid + fold]
             for j in range(folds)], axis=1)
        first = q_cols + mid + fold
        key_value_grad = last[:, first : first + kv_cols]
        gain_one_grad = last[:, first + kv_cols]
        gain_two_grad = last[:, first + kv_cols + 1]
    else:
        def scatter(x):
            part = lax.psum_scatter(x.astype(BF16), "fsdp", scatter_dimension=0, tiled=True)
            return lax.psum(part, "seq").astype(F32)

        pair_grad = jnp.concatenate(pairs)
        gain_one_grad = sum(ones)
        down_grad = scatter(weight_grad(grad, hidden_low).T)
        out_grad = scatter(weight_grad(branch, attended).T)
        lift_w = scatter(weight_grad(ffn_low, lift_grads))
        gate_grad, up_grad = lift_w[:, :hidden], lift_w[:, hidden:]
        query_grad = scatter(weight_grad(normed, dq))
        narrow_grad = scatter(weight_grad(normed, lora_grad))
        widen_grad = scatter(weight_grad(lora_mid, dq))
        key_value_grad = scatter(weight_grad(normed, pair_grad))
        gains_grad = scatter(jnp.concatenate([gain_one_grad, gain_two_grad]).T)
        gain_one_grad, gain_two_grad = gains_grad[:, 0], gains_grad[:, 1]
    return (output.reshape(batches, 1, rows, width), in_grad.reshape(batches, 1, rows, width),
            gain_one_grad, query_grad, narrow_grad, widen_grad, key_value_grad, out_grad,
            gain_two_grad, gate_grad, up_grad, down_grad)


def solution(mesh):
    rows = P(None, "fsdp", "seq", None)
    vector, matrix = P("fsdp"), P("fsdp", None)
    in_specs = (rows, P(None, "fsdp", None), rows, vector) + (matrix,) * 5 + (vector,) + (matrix,) * 3
    out_specs = (rows, rows, vector) + (matrix,) * 5 + (vector,) + (matrix,) * 3
    return jax.shard_map(local, mesh=mesh, in_specs=in_specs, out_specs=out_specs, check_vma=False)
```

```python
import functools
import math

import jax
import jax.numpy as jnp
from jax import lax
from jax.experimental import pallas as pl
from jax.experimental.pallas import tpu as pltpu
from jax.sharding import PartitionSpec as P

EPSILON = 1e-06
THETA = 10000.0
F32 = jnp.float32
BF16 = jnp.bfloat16
GELU_C = math.sqrt(2.0 / math.pi)
GELU_A = 0.044715
LOWEST = -1e30
VMEM_LIMIT = 60 * 1024 * 1024
ANY = pl.BlockSpec(memory_space=pl.ANY)
VMEM = pl.BlockSpec(memory_space=pltpu.VMEM)
SMEM = pl.BlockSpec(memory_space=pltpu.SMEM)


def mm(left, right):
    return lax.dot_general(left, right, (((1,), (0,)), ((), ())), preferred_element_type=F32)


def mm_nt(left, right):
    return lax.dot_general(left, right, (((1,), (1,)), ((), ())), preferred_element_type=F32)


def full(shape):
    return pl.BlockSpec(shape, lambda i: (0,) * len(shape))


def rows_of(tile, cols):
    return pl.BlockSpec((tile, cols), lambda i: (i, 0))


def params(**more):
    return pltpu.CompilerParams(vmem_limit_bytes=VMEM_LIMIT, **more)


def cost(flops, bytes_accessed, transcendentals=0):
    return pl.CostEstimate(
        flops=int(flops), bytes_accessed=int(bytes_accessed), transcendentals=int(transcendentals)
    )


def took(us):
    return cost(us * 1.1e9, 1)


LONG = 10**12


def like(shape, dtype):
    return jax.ShapeDtypeStruct(tuple(shape), dtype)


def swap(x, axis, by):
    return lax.ppermute(x, axis, [(i, i ^ by) for i in range(lax.axis_size(axis))])


def skipping(kernel, first, count):
    return lambda *refs: kernel(*refs[:first], *refs[first + count :])


def tree(values):
    while len(values) > 1:
        values = [values[i] + values[i + 1] for i in range(0, len(values), 2)]
    return values[0]


def add_kernel(*refs, count, groups):
    for out, group in zip(refs[count:], groups):
        values = [refs[i][...] if k is None else refs[i][k] for i, k in group]
        out[...] = tree([v.astype(F32) for v in values]).astype(out.dtype)


def add(arrays, groups, later=(), dtype=BF16):
    shapes = [arrays[g[0][0]].shape if g[0][1] is None else arrays[g[0][0]].shape[1:]
              for g in groups]
    count = len(arrays)
    later = list(later)
    return list(pl.pallas_call(
        skipping(functools.partial(add_kernel, count=count, groups=groups), count, len(later)),
        in_specs=[VMEM] * count + [ANY] * len(later),
        out_specs=[VMEM] * len(groups),
        out_shape=[like(s, dtype) for s in shapes],
        compiler_params=params(),
        cost_estimate=took(3.5),
        name="add",
    )(*arrays, *later))


class Whole:
    def __init__(self, array):
        self.arrays = [array]
        self.shape = array.shape
        self.count = 1

    def copies(self, where, refs, dst):
        return [(refs[0], dst)]


class Shards:
    def __init__(self, x, relay=False):
        parts = lax.axis_size("fsdp")
        got = {0: x}
        for r in range(2, parts, 2):
            low = r & -r
            near = relay and r != low
            got[r] = swap(got[r - low], "fsdp", low) if near else swap(x, "fsdp", r)
        for r in range(0, parts, 2):
            got[r + 1] = swap(got[r], "fsdp", 1)
        self.arrays = [got[r] for r in range(parts)]
        self.rows = x.shape[0]
        self.shape = (parts * x.shape[0], x.shape[1])
        self.count = parts

    def copies(self, where, refs, dst):
        out = []
        for r, ref in enumerate(refs):
            at = pl.multiple_of((where[0] ^ r) * self.rows, self.rows)
            out.append((ref, dst.at[pl.ds(at, self.rows), :]))
        return out


def pack_pair_kernel(kv_ref, one_ref, two_ref, out_ref):
    piece, kv_cols = kv_ref.shape
    out_ref[:, :kv_cols] = kv_ref[...]
    pad = jnp.zeros((126, piece), F32)
    gains = jnp.concatenate([one_ref[...].astype(F32), two_ref[...].astype(F32), pad], axis=0)
    out_ref[:, kv_cols:] = gains.T.astype(BF16)


def pack_pair(kv, one, two):
    piece = kv.shape[0]
    return pl.pallas_call(
        pack_pair_kernel,
        in_specs=[VMEM] * 3,
        out_specs=VMEM,
        out_shape=like((piece, kv.shape[1] + 128), BF16),
        compiler_params=params(),
        cost_estimate=took(1.6),
        name="pack_pair",
    )(kv, one.reshape(1, piece), two.reshape(1, piece))


def pack_kernel(where, gate_ref, up_ref, down_ref, out_ref, third_ref, *, span):
    piece = gate_ref.shape[0]
    hidden = gate_ref.shape[1]
    part = 2 * hidden // span
    for s in range(span):
        ref, at = (gate_ref, s * part) if s * part < hidden else (up_ref, s * part - hidden)

        @pl.when(where[1] == s)
        def _():
            third_ref[:, :part] = ref[:, at : at + part]

    col = part
    for ref in (down_ref, out_ref):
        n = ref.shape[0] // span
        for i in range(n // 16):
            row = pl.ds(pl.multiple_of(where[1] * n + 16 * i, 16), 16)
            for j in range(ref.shape[1] // 128):
                third_ref[16 * j : 16 * j + 16, col : col + 128] = ref[row, j * 128 : (j + 1) * 128]
            col += 128


def pack(where, gate, up, down, out, span, later):
    piece = gate.shape[0]
    third = (gate.shape[1] * 2 * piece + (down.shape[0] + out.shape[0]) * down.shape[1]) // span
    return pl.pallas_call(
        skipping(functools.partial(pack_kernel, span=span), 5, len(later)),
        in_specs=[SMEM] + [VMEM] * 4 + [ANY] * len(later),
        out_specs=VMEM,
        out_shape=like((piece, third // piece), BF16),
        compiler_params=params(),
        cost_estimate=took(2),
        name="pack",
    )(where, gate, up, down, out, *later)


def pack_query_kernel(q_ref, narrow_ref, widen_ref, out_ref, *, fold):
    q_cols, mid, count = q_ref.shape[1], narrow_ref.shape[1], widen_ref.shape[0]
    out_ref[:, :q_cols] = q_ref[...]
    out_ref[:, q_cols : q_cols + mid] = narrow_ref[...]
    folds = q_cols // fold
    for j in range(folds):
        out_ref[j * count : (j + 1) * count, q_cols + mid :] = widen_ref[
            :, j * fold : (j + 1) * fold]
    rest = out_ref.shape[0] - folds * count
    out_ref[folds * count :, q_cols + mid :] = jnp.zeros((rest, fold), BF16)


def pack_query(q, narrow, widen, fold, later):
    return pl.pallas_call(
        skipping(functools.partial(pack_query_kernel, fold=fold), 3, len(later)),
        in_specs=[VMEM] * 3 + [ANY] * len(later),
        out_specs=VMEM,
        out_shape=like((q.shape[0], q.shape[1] + narrow.shape[1] + fold), BF16),
        compiler_params=params(),
        cost_estimate=took(1.7),
        name="pack_query",
    )(q, narrow, widen, *later)


class Tiled:
    def __init__(self, packed, gate_up, *tall):
        parts, span = lax.axis_size("fsdp"), lax.axis_size("seq")
        piece = packed.shape[0]
        self.piece, self.part, self.parts, self.span = piece, gate_up // span, parts, span
        self.heights = [t.shape[0] // span for t in tall]
        self.up, self.across = sum(self.heights) // 16, tall[0].shape[1] // 128
        self.array = lax.all_gather(packed, ("seq", "fsdp"), axis=0, tiled=True)
        self.shape = (parts * piece, gate_up)
        self.shapes = [(parts * t.shape[0], t.shape[1]) for t in tall]
        self.scratch = (span, parts * piece, self.up * 128)

    def copies(self, ref, dst, rest):
        height = self.parts * self.piece
        rows = [pl.ds(s * height, height) for s in range(self.span)]
        return [(ref.at[at, pl.ds(self.part, self.up * 128)], rest.at[s])
                for s, at in enumerate(rows)] + [
            (ref.at[at, pl.ds(0, self.part)], dst.at[:, pl.ds(s * self.part, self.part)])
            for s, at in enumerate(rows)]

    def unfold(self, rest, dsts):
        starts, tops = [], 0
        for n in self.heights:
            starts.append(tops)
            tops += n // 16

        def shard(d, carry):
            for s in range(self.span):
                for n, first, dst in zip(self.heights, starts, dsts):
                    for i in range(n // 16):
                        at = pl.ds(pl.multiple_of(d * n * self.span + s * n + i * 16, 16), 16)
                        for j in range(self.across):
                            row = pl.ds(pl.multiple_of(d * self.piece + 16 * j, 16), 16)
                            col = (first + i) * 128
                            dst[at, j * 128 : (j + 1) * 128] = rest[s, row, col : col + 128]
            return carry

        lax.fori_loop(0, self.parts, shard, 0)


def carry_out(copies, sem):
    made = [pltpu.make_async_copy(src, dst, sem.at[i]) for i, (src, dst) in enumerate(copies)]
    for c in made:
        c.start()
    for c in made:
        c.wait()


def normalize(x_ref, gains_ref):
    x = x_ref[...].astype(F32)
    inv = lax.rsqrt(jnp.mean(x * x, axis=-1, keepdims=True) + EPSILON)
    return (x * inv * gains_ref[0:1, :]).astype(BF16)


def put_pair(kv_ref, pair, cos, sin, head_dim):
    half = head_dim // 2
    a, b = pair[:, :half], pair[:, half:head_dim]
    kv_ref[:, :half] = (a * cos - b * sin).astype(BF16)
    kv_ref[:, half:head_dim] = (b * cos + a * sin).astype(BF16)
    kv_ref[:, head_dim:] = pair[:, head_dim:].astype(BF16)


def project_kv_kernel(*refs, held, head_dim):
    where, x_ref, cos_ref, sin_ref = refs[:4]
    pieces = refs[4 : 4 + len(held.arrays)]
    normed_ref, kv_ref, w_ref, gains_ref, sem = refs[4 + len(held.arrays) :]
    kv_cols = 2 * head_dim

    @pl.when(pl.program_id(0) == 0)
    def _():
        carry_out(held.copies(where, pieces, w_ref), sem)
        gains_ref[...] = w_ref[:, kv_cols:].astype(F32).T[:8]

    normed = normalize(x_ref, gains_ref)
    normed_ref[...] = normed
    put_pair(kv_ref, mm(normed, w_ref[:, :kv_cols]), cos_ref[...], sin_ref[...], head_dim)


def project_kv(where, x, cos, sin, held, head_dim):
    rows, width = x.shape
    tile = math.gcd(rows, 512)
    half = head_dim // 2
    return pl.pallas_call(
        functools.partial(project_kv_kernel, held=held, head_dim=head_dim),
        grid=(rows // tile,),
        in_specs=[SMEM, rows_of(tile, width), rows_of(tile, half), rows_of(tile, half)]
        + [ANY] * len(held.arrays),
        out_specs=[rows_of(tile, width), rows_of(tile, 2 * head_dim), full(held.shape),
                   full((8, width))],
        out_shape=[like((rows, width), BF16), like((rows, 2 * head_dim), BF16),
                   like(held.shape, BF16), like((8, width), F32)],
        scratch_shapes=[pltpu.SemaphoreType.DMA((held.count,))],
        compiler_params=params(),
        cost_estimate=took(5),
        name="project_kv",
    )(where, x, cos, sin, *held.arrays)


def project_q_kernel(*refs, held, head_dim, q_cols, mid, scale):
    where, normed_ref, cos_ref, sin_ref = refs[:4]
    pieces = refs[4 : 4 + len(held.arrays)]
    lora_ref, q_ref, w_ref, ww_ref, sem = refs[4 + len(held.arrays) :]
    half = head_dim // 2
    fold = held.shape[1] - q_cols - mid
    parts = q_cols // fold

    @pl.when(pl.program_id(0) == 0)
    def _():
        carry_out(held.copies(where, pieces, w_ref), sem)
        shards = held.shape[0] // held.rows
        count = mid // shards
        for d in range(shards):
            for j in range(parts):
                ww_ref[d * count : (d + 1) * count, j * fold : (j + 1) * fold] = w_ref[
                    d * held.rows + j * count : d * held.rows + (j + 1) * count, q_cols + mid :]

    normed = normed_ref[...]
    cos, sin = cos_ref[...], sin_ref[...]
    low = mm(normed, w_ref[:, q_cols : q_cols + mid]).astype(BF16)
    lora_ref[...] = low
    query = mm(normed, w_ref[:, :q_cols]) + mm(low, ww_ref[...])
    for h in range(q_cols // head_dim):
        c = h * head_dim
        a, b = query[:, c : c + half], query[:, c + half : c + head_dim]
        q_ref[:, c : c + half] = ((a * cos - b * sin) * scale).astype(BF16)
        q_ref[:, c + half : c + head_dim] = ((b * cos + a * sin) * scale).astype(BF16)


def project_q(where, normed, cos, sin, held, head_dim, q_cols, mid, scale, later):
    rows, width = normed.shape
    tile = math.gcd(rows, 256)
    half = head_dim // 2
    count = 4 + len(held.arrays)
    return pl.pallas_call(
        skipping(functools.partial(project_q_kernel, held=held, head_dim=head_dim, q_cols=q_cols,
                                   mid=mid, scale=scale), count, len(later)),
        grid=(rows // tile,),
        in_specs=[SMEM, rows_of(tile, width), rows_of(tile, half), rows_of(tile, half)]
        + [ANY] * (len(held.arrays) + len(later)),
        out_specs=[rows_of(tile, mid), rows_of(tile, q_cols), full(held.shape),
                   full((mid, q_cols))],
        out_shape=[like((rows, mid), BF16), like((rows, q_cols), BF16), like(held.shape, BF16),
                   like((mid, q_cols), BF16)],
        scratch_shapes=[pltpu.SemaphoreType.DMA((held.count,))],
        compiler_params=params(),
        cost_estimate=took(8.5),
        name="project_q",
    )(where, normed, cos, sin, *held.arrays, *later)


def attend_kernel(*refs, head_dim, tile, block, span):
    where, lengths_ref, q_ref = refs[:3]
    kvs = refs[3 : 3 + span]
    o_ref, lse_ref, kv_ref, vt_ref, acc_ref, sem = refs[-6:]
    heads = q_ref.shape[1] // head_dim
    rows = q_ref.shape[0]
    m = pl.program_id(0)
    place = where[1]
    base = place * rows
    lengths = [lengths_ref[m, d] for d in range(lengths_ref.shape[1])]

    def first(t):
        return lax.div(begin_of(base + t * tile, lengths), block)

    def copy(n, s):
        at = pl.multiple_of((place ^ s) * rows, rows)
        return pltpu.make_async_copy(kvs[s].at[pl.ds(n * rows, rows)],
                                     kv_ref.at[n, pl.ds(at, rows), :], sem.at[n, s])

    @pl.when(m == 0)
    def _():
        for n in range(kv_ref.shape[0]):
            for s in range(span):
                pl.when((place ^ s) <= place)(lambda n=n, s=s: copy(n, s).start())

    for n in range(kv_ref.shape[0]):
        for s in range(span):
            pl.when((m == n) & ((place ^ s) <= place))(lambda n=n, s=s: copy(n, s).wait())

    def flip(kb, carry):
        at = pl.ds(pl.multiple_of(kb * block, block), block)
        vt_ref[:, at] = kv_ref[m, at, head_dim:].T
        return carry

    lax.fori_loop(first(0), lax.div(base + rows + block - 1, block), flip, 0)
    for t in range(rows // tile):
        q_rows = slice(t * tile, (t + 1) * tile)
        high = base + t * tile + lax.broadcasted_iota(jnp.int32, (1, tile), 1)
        low = begin_of(high, lengths)
        acc_ref[...] = jnp.zeros_like(acc_ref)

        def visit(kb, carry):
            at = pl.ds(pl.multiple_of(kb * block, block), block)
            keys = kv_ref[m, at, :head_dim]
            vt = vt_ref[:, at]
            index = kb * block + lax.broadcasted_iota(jnp.int32, (block, tile), 0)
            mask = (index >= low) & (index <= high)
            out = []
            for h in range(heads):
                peak, total = carry[h]
                s = mm_nt(keys, q_ref[q_rows, h * head_dim : (h + 1) * head_dim])
                s = jnp.where(mask, s, -jnp.inf)
                new_peak = jnp.maximum(peak, jnp.max(s, axis=0, keepdims=True))
                factor = jnp.exp(peak - new_peak)
                p = jnp.exp(s - new_peak)
                total = total * factor + jnp.sum(p, axis=0, keepdims=True)
                acc_ref[h] = acc_ref[h] * factor + mm(vt, p.astype(BF16))
                out.append((new_peak, total))
            return tuple(out)

        start = tuple(
            (jnp.full((1, tile), LOWEST, F32), jnp.zeros((1, tile), F32)) for _ in range(heads)
        )
        stats = lax.fori_loop(first(t), lax.div(base + (t + 1) * tile + block - 1, block), visit,
                              start)
        for h in range(heads):
            peak, total = stats[h]
            o_ref[q_rows, h * head_dim : (h + 1) * head_dim] = (acc_ref[h] / total).T.astype(BF16)
            lse_ref[0, h : h + 1, q_rows] = peak + jnp.log(total)


def attend(where, lengths, q, kvs, head_dim, tile, block):
    total, q_cols = q.shape
    batches = lengths.shape[0]
    rows = total // batches
    heads = q_cols // head_dim
    span = len(kvs)
    group = span * rows
    return pl.pallas_call(
        functools.partial(attend_kernel, head_dim=head_dim, tile=tile, block=block, span=span),
        grid=(batches,),
        in_specs=[SMEM, SMEM, rows_of(rows, q_cols)] + [ANY] * span,
        out_specs=[rows_of(rows, q_cols), pl.BlockSpec((1, heads, rows), lambda i: (i, 0, 0))],
        out_shape=[like(q.shape, BF16), like((batches, heads, rows), F32)],
        scratch_shapes=[pltpu.VMEM((batches, group, 2 * head_dim), BF16),
                        pltpu.VMEM((head_dim, group), BF16),
                        pltpu.VMEM((heads, head_dim, tile), F32),
                        pltpu.SemaphoreType.DMA((batches, span))],
        compiler_params=params(),
        cost_estimate=took(18),
        name="attend",
    )(where, lengths, q, *kvs)


def middle_kernel(*refs, held, head_dim, chunk):
    x_ref, attn_ref, g_ref, gains_ref = refs[:4]
    if held is None:
        w_ref, wd_ref, wo_ref = refs[4:7]
    else:
        w_ref, wd_ref, wo_ref, rest_ref, sem = refs[-5:]
    (out_ref, mid_grad_ref, branch_ref, attn_grad_ref, delta_ref, low_ref, hidden_ref, grads_ref,
     gain_grad_ref) = refs[5:14] if held is not None else refs[7:16]

    @pl.when(pl.program_id(0) == 0)
    def _():
        if held is not None:
            f = Fetch(held.copies(refs[4], w_ref, rest_ref), sem)
            f.wait(*range(held.span))
            held.unfold(rest_ref, [wd_ref, wo_ref])
            f.wait(*range(held.span, 2 * held.span))
        gain_grad_ref[...] = jnp.zeros_like(gain_grad_ref)

    gain = gains_ref[1:2, :]
    attn = attn_ref[...]
    middle = x_ref[...].astype(F32) + mm(attn, wo_ref[...])
    inv = lax.rsqrt(jnp.mean(middle * middle, axis=-1, keepdims=True) + EPSILON)
    unit = middle * inv
    low = (unit * gain).astype(BF16)
    low_ref[...] = low
    grad = g_ref[...]
    result = middle
    back = jnp.zeros_like(middle)
    wide = wd_ref.shape[0]
    for c in range(wide // chunk):
        at = slice(c * chunk, (c + 1) * chunk)
        to = slice(wide + c * chunk, wide + (c + 1) * chunk)
        gate = mm(low, w_ref[:, at])
        lift = mm(low, w_ref[:, to])
        square = gate * gate
        bend = jnp.tanh(GELU_C * gate * (1.0 + GELU_A * square))
        cdf = 0.5 * (1.0 + bend)
        gelu = gate * cdf
        hidden = (gelu * lift).astype(BF16)
        hidden_ref[:, at] = hidden
        result = result + mm(hidden, wd_ref[at, :])
        hidden_grad = mm_nt(grad, wd_ref[at, :])
        slope = cdf + (0.5 * GELU_C) * gate * (1.0 - bend * bend) * (1.0 + 3.0 * GELU_A * square)
        gate_grad = (hidden_grad * lift * slope).astype(BF16)
        lift_grad = (hidden_grad * gelu).astype(BF16)
        grads_ref[:, at] = gate_grad
        grads_ref[:, to] = lift_grad
        back = back + mm_nt(gate_grad, w_ref[:, at]) + mm_nt(lift_grad, w_ref[:, to])
    out_ref[...] = result.astype(BF16)
    gain_grad_ref[...] += jnp.sum(unit * back, axis=0, keepdims=True)
    scaled = back * gain
    mid_grad = grad.astype(F32) + inv * (
        scaled - unit * jnp.mean(unit * scaled, axis=-1, keepdims=True)
    )
    mid_grad_ref[...] = mid_grad
    branch = mid_grad.astype(BF16)
    branch_ref[...] = branch
    attn_grad = mm_nt(branch, wo_ref[...]).astype(BF16)
    attn_grad_ref[...] = attn_grad
    product = attn_grad.astype(F32) * attn.astype(F32)
    half = head_dim // 2
    for h in range(attn.shape[1] // head_dim):
        c = h * head_dim
        folded = product[:, c : c + half] + product[:, c + half : c + head_dim]
        delta_ref[h : h + 1, :] = jnp.sum(folded.T, axis=0, keepdims=True)


def middle_part(x, attn, grad, gains, held, weights, head_dim):
    rows, width = x.shape
    q_cols = attn.shape[1]
    hidden = (weights[0].shape if held is None else held.shape)[1] // 2
    heads = q_cols // head_dim
    tile = math.gcd(rows, 512)
    if held is None:
        more, specs, scratch = weights, [full(w.shape) for w in weights], []
    else:
        more, specs = [held.array], [ANY]
        scratch = [pltpu.VMEM(held.shape, BF16)] + [pltpu.VMEM(s, BF16) for s in held.shapes]
        scratch += [pltpu.VMEM(held.scratch, BF16), pltpu.SemaphoreType.DMA((2 * held.span,))]
    return pl.pallas_call(
        functools.partial(middle_kernel, held=held, head_dim=head_dim, chunk=512),
        grid=(rows // tile,),
        in_specs=[rows_of(tile, width), rows_of(tile, q_cols), rows_of(tile, width),
                  full(gains.shape)] + specs,
        out_specs=[rows_of(tile, width), rows_of(tile, width), rows_of(tile, width),
                   rows_of(tile, q_cols), pl.BlockSpec((heads, tile), lambda i: (0, i)),
                   rows_of(tile, width), rows_of(tile, hidden), rows_of(tile, 2 * hidden),
                   full((1, width))],
        out_shape=[like((rows, width), BF16), like((rows, width), F32), like((rows, width), BF16),
                   like((rows, q_cols), BF16), like((heads, rows), F32),
                   like((rows, width), BF16), like((rows, hidden), BF16),
                   like((rows, 2 * hidden), BF16), like((1, width), F32)],
        scratch_shapes=scratch,
        compiler_params=params(),
        cost_estimate=took(39),
        name="middle",
    )(x, attn, grad, gains, *more)


def attend_back_kernel(*refs, head_dim, tile, block, scale, m, span):
    where, lengths_ref, lse_ref, delta_ref, q_ref, do_ref, cos_ref, sin_ref = refs[:8]
    kvs = refs[8 : 8 + span]
    kv_ref, dkv_ref, kt_ref, acc_ref, sem = refs[-5:]
    sends = refs[-5 - (span - 1) : -5]
    dq_ref, own_ref = refs[-5 - span - 1 : -5 - span + 1]
    heads = q_ref.shape[1] // head_dim
    half = head_dim // 2
    rows = q_ref.shape[0]
    place = where[1]
    base = place * rows
    lengths = [lengths_ref[m, d] for d in range(lengths_ref.shape[1])]
    tiles = rows // tile
    firsts = [lax.div(begin_of(base + t * tile, lengths), block) for t in range(tiles)]

    def copy(s):
        at = pl.multiple_of((place ^ s) * rows, rows)
        return pltpu.make_async_copy(kvs[s].at[pl.ds(m * rows, rows)],
                                     kv_ref.at[pl.ds(at, rows), :], sem.at[s])

    for s in range(span):
        pl.when((place ^ s) <= place)(lambda s=s: copy(s).start())
    acc_ref[...] = jnp.zeros_like(acc_ref)
    dkv_ref[...] = jnp.zeros_like(dkv_ref)
    for s in range(span):
        pl.when((place ^ s) <= place)(lambda s=s: copy(s).wait())

    def visit(kb, carry):
        at = pl.ds(pl.multiple_of(kb * block, block), block)
        keys = kv_ref[at, :head_dim]
        vals = kv_ref[at, head_dim:]
        kt_ref[...] = keys.T
        for t in range(tiles):
            q_rows = slice(t * tile, (t + 1) * tile)

            @pl.when((kb >= firsts[t]) & (kb * block < base + (t + 1) * tile))
            def _():
                high = base + t * tile + lax.broadcasted_iota(jnp.int32, (1, tile), 1)
                low = begin_of(high, lengths)
                index = kb * block + lax.broadcasted_iota(jnp.int32, (block, tile), 0)
                mask = (index >= low) & (index <= high)
                dk = jnp.zeros((block, head_dim), F32)
                dv = jnp.zeros((block, head_dim), F32)
                for h in range(heads):
                    cols = slice(h * head_dim, (h + 1) * head_dim)
                    q = q_ref[q_rows, cols]
                    do = do_ref[q_rows, cols]
                    s = mm_nt(keys, q)
                    p = jnp.where(mask, jnp.exp(s - lse_ref[0, h : h + 1, q_rows]), 0.0)
                    dv = dv + mm(p.astype(BF16), do)
                    ds = (p * (mm_nt(vals, do) - delta_ref[h : h + 1, q_rows])).astype(BF16)
                    dk = dk + mm(ds, q)
                    acc_ref[h, :, q_rows] += mm(kt_ref[...], ds)
                dkv_ref[at, :head_dim] += dk
                dkv_ref[at, head_dim:] += dv

        return carry

    lax.fori_loop(firsts[0], lax.div(base + rows + block - 1, block), visit, 0)
    cos, sin = cos_ref[...], sin_ref[...]
    for h in range(heads):
        c = h * head_dim
        dq = acc_ref[h].T * scale
        a, b = dq[:, :half], dq[:, half:]
        dq_ref[:, c : c + half] = (a * cos + b * sin).astype(BF16)
        dq_ref[:, c + half : c + head_dim] = (b * cos - a * sin).astype(BF16)
    own_ref[...] = dkv_ref[pl.ds(pl.multiple_of(place * rows, rows), rows), :]
    for s, send_ref in enumerate(sends, 1):
        at = pl.multiple_of((place ^ s) * rows, rows)
        send_ref[...] = dkv_ref[pl.ds(at, rows), :].astype(BF16)


def attend_back(where, lengths, lse, delta, q, do, kvs, cos, sin, head_dim, tile, block, scale, m,
                before, later):
    q_cols = q.shape[1]
    rows = q.shape[0] // lengths.shape[0]
    heads = q_cols // head_dim
    span = len(kvs)
    group = span * rows
    half = head_dim // 2
    here = pl.BlockSpec((rows, q_cols), lambda i: (m, 0))
    angle = pl.BlockSpec((rows, half), lambda i: (m, 0))
    more = ([] if before is None else [before]) + later
    return pl.pallas_call(
        functools.partial(attend_back_kernel, head_dim=head_dim, tile=tile, block=block,
                          scale=scale, m=m, span=span),
        grid=(1,),
        in_specs=[SMEM, SMEM, pl.BlockSpec((1, heads, rows), lambda i: (m, 0, 0)),
                  pl.BlockSpec((heads, rows), lambda i: (0, m)), here, here, angle, angle]
        + [ANY] * (span + len(more)),
        out_specs=[here] + [VMEM] * span,
        out_shape=[like(q.shape, BF16), like((rows, 2 * head_dim), F32)]
        + [like((rows, 2 * head_dim), BF16)] * (span - 1),
        scratch_shapes=[pltpu.VMEM((group, 2 * head_dim), BF16),
                        pltpu.VMEM((group, 2 * head_dim), F32), pltpu.VMEM((head_dim, block), BF16),
                        pltpu.VMEM((heads, head_dim, rows), F32),
                        pltpu.SemaphoreType.DMA((span,))],
        input_output_aliases={} if before is None else {8 + span: 0},
        compiler_params=params(),
        cost_estimate=took(20),
        name="attend_back",
    )(where, lengths, lse, delta, q, do, cos, sin, *kvs, *more)


def query_back_kernel(dq_ref, w_ref, ww_ref, lora_grad_ref, back_ref, *, q_cols, mid):
    dq = dq_ref[...]
    lora_grad = mm_nt(dq, ww_ref[...]).astype(BF16)
    lora_grad_ref[...] = lora_grad
    back_ref[...] = (mm_nt(dq, w_ref[:, :q_cols])
                     + mm_nt(lora_grad, w_ref[:, q_cols : q_cols + mid]))


def query_back(dq, w, ww, later=()):
    rows, q_cols = dq.shape
    mid, width = ww.shape[0], w.shape[0]
    tile = math.gcd(rows, 256)
    return pl.pallas_call(
        skipping(functools.partial(query_back_kernel, q_cols=q_cols, mid=mid), 3, len(later)),
        grid=(rows // tile,),
        in_specs=[rows_of(tile, q_cols), full(w.shape), full(ww.shape)] + [ANY] * len(later),
        out_specs=[rows_of(tile, mid), rows_of(tile, width)],
        out_shape=[like((rows, mid), BF16), like((rows, width), F32)],
        compiler_params=params(),
        cost_estimate=cost(2 * rows * (width * (q_cols + mid) + mid * q_cols), 9e6),
        name="query_back",
    )(dq, w, ww, *later)


def pair_back_kernel(*refs, head_dim, others):
    x_ref, gains_ref, cos_ref, sin_ref, w_ref, back_ref, mid_grad_ref, own_ref = refs[:8]
    pair_grad_ref, in_grad_ref, gain_grad_ref = refs[-3:]

    @pl.when(pl.program_id(0) == 0)
    def _():
        gain_grad_ref[...] = jnp.zeros_like(gain_grad_ref)

    half = head_dim // 2
    gain = gains_ref[0:1, :]
    cos, sin = cos_ref[...], sin_ref[...]
    dkv = own_ref[...]
    for ref in refs[8 : 8 + others]:
        dkv = dkv + ref[...].astype(F32)
    a, b = dkv[:, :half], dkv[:, half:head_dim]
    pair_grad_ref[:, :half] = (a * cos + b * sin).astype(BF16)
    pair_grad_ref[:, half:head_dim] = (b * cos - a * sin).astype(BF16)
    pair_grad_ref[:, head_dim:] = dkv[:, head_dim:].astype(BF16)
    back = back_ref[...] + mm_nt(pair_grad_ref[...], w_ref[:, : 2 * head_dim])
    x = x_ref[...].astype(F32)
    inv = lax.rsqrt(jnp.mean(x * x, axis=-1, keepdims=True) + EPSILON)
    unit = x * inv
    gain_grad_ref[...] += jnp.sum(unit * back, axis=0, keepdims=True)
    scaled = back * gain
    in_grad_ref[...] = mid_grad_ref[...] + inv * (
        scaled - unit * jnp.mean(unit * scaled, axis=-1, keepdims=True)
    )


def pair_back(x, gains, cos, sin, w, own, others, back, mid_grad, head_dim, m, batches, before=None,
              later=()):
    width = x.shape[1]
    rows = x.shape[0] // batches
    tile = math.gcd(rows, 256)
    half, cols = head_dim // 2, 2 * head_dim
    count = rows // tile

    def here(n):
        return pl.BlockSpec((tile, n), lambda i: (m * count + i, 0))

    more = ([] if before is None else [before]) + list(later)
    return pl.pallas_call(
        functools.partial(pair_back_kernel, head_dim=head_dim, others=len(others)),
        grid=(count,),
        in_specs=[here(width), full(gains.shape), here(half), here(half), full(w.shape),
                  here(width), here(width)] + [rows_of(tile, cols)] * (1 + len(others))
        + [ANY] * len(more),
        out_specs=[rows_of(tile, cols), here(width), full((1, width))],
        out_shape=[like((rows, cols), BF16), like(x.shape, F32), like((1, width), F32)],
        input_output_aliases={} if before is None else {8 + len(others): 1},
        compiler_params=params(),
        cost_estimate=cost(2 * rows * width * cols, 7e6),
        name="pair_back",
    )(x, gains, cos, sin, w, back, mid_grad, own, *others, *more)


def weight_grad_kernel(x_ref, y_ref, out_ref, xt_ref):
    @pl.when(pl.program_id(0) == 0)
    def _():
        xt_ref[...] = x_ref[...].T

    out_ref[...] = mm(xt_ref[...], y_ref[...]).astype(BF16)


def weight_grad(x, y, tile=256, later=()):
    rows, width = x.shape
    cols = y.shape[1]
    tile = math.gcd(cols, tile)
    return pl.pallas_call(
        skipping(weight_grad_kernel, 2, len(later)),
        grid=(cols // tile,),
        in_specs=[full(x.shape), pl.BlockSpec((rows, tile), lambda i: (0, i))] + [ANY] * len(later),
        out_specs=pl.BlockSpec((width, tile), lambda i: (0, i)),
        out_shape=like((width, cols), BF16),
        scratch_shapes=[pltpu.VMEM((width, rows), BF16)],
        compiler_params=params(),
        cost_estimate=took(10.3),
        name="weight_grad",
    )(x, y, *later)


def turn(x_ref, flat_ref, xt_ref, me, parts):
    flat_ref[...] = x_ref[...].T
    piece = flat_ref.shape[0] // parts
    for r in range(parts):
        at = pl.multiple_of((me ^ r) * piece, piece)
        to = (r % 2) * (parts // 2) + r // 2
        xt_ref[to * piece : (to + 1) * piece, :] = flat_ref[pl.ds(at, piece), :]


def column_grads_kernel(where, g_in, hidden_in, b_in, attn_in, keep_ref, send_ref, g_ref, hidden_ref,
                        b_ref, attn_ref, sem, *, parts):
    f = Fetch([(g_in, g_ref), (hidden_in, hidden_ref), (b_in, b_ref), (attn_in, attn_ref)], sem)
    span, _, piece, _ = keep_ref.shape
    per = parts // span
    col = 0
    for pair, x_ref, y_ref in (((0, 1), g_ref, hidden_ref), ((2, 3), b_ref, attn_ref)):
        n = y_ref.shape[1] // parts
        f.wait(pair[0])
        turned = x_ref[...].T
        f.wait(pair[1])
        for r in range(parts):
            at = pl.multiple_of((where[0] ^ r) * n, n)
            out = mm(turned, y_ref[:, pl.ds(at, n)]).astype(BF16)
            ref = send_ref if r % 2 else keep_ref
            for s in range(span):
                for i in range(per):
                    ref[s ^ where[1], r // 2, :, col + i * n : col + (i + 1) * n] = out[
                        (s * per + i) * piece : (s * per + i + 1) * piece]
        col += per * n


def column_grads(where, grad, hidden, branch, attn, parts, span):
    rows, width = grad.shape
    piece = width // parts
    cols = (hidden.shape[1] + attn.shape[1]) // span
    shape = like((span, parts // 2, piece, cols), BF16)
    arrays = (grad, hidden, branch, attn)
    return pl.pallas_call(
        functools.partial(column_grads_kernel, parts=parts),
        in_specs=[SMEM] + [ANY] * 4,
        out_specs=[VMEM] * 2,
        out_shape=[shape, shape],
        scratch_shapes=[pltpu.VMEM(a.shape, BF16) for a in arrays]
        + [pltpu.SemaphoreType.DMA((4,))],
        compiler_params=params(),
        cost_estimate=took(9),
        name="column_grads",
    )(where, *arrays)


class Fetch:
    def __init__(self, pairs, sem):
        self.copies = [pltpu.make_async_copy(a, b, sem.at[i]) for i, (a, b) in enumerate(pairs)]
        for c in self.copies:
            c.start()

    def wait(self, *which):
        for i in which:
            self.copies[i].wait()


def unrotate(dkv, cos, sin, head_dim):
    half = head_dim // 2
    a, b = dkv[:, :half], dkv[:, half:head_dim]
    return jnp.concatenate([a * cos + b * sin, b * cos - a * sin, dkv[:, head_dim:]],
                           axis=1).astype(BF16)


def norm_back(x, gain, back, rest):
    inv = lax.rsqrt(jnp.mean(x * x, axis=-1, keepdims=True) + EPSILON)
    unit = x * inv
    scaled = back * gain
    return (rest + inv * (scaled - unit * jnp.mean(unit * scaled, axis=-1, keepdims=True)),
            jnp.sum(unit * back, axis=0, keepdims=True))


def fold_rows(out_ref, value, first, parts, piece, fold, j):
    count = value.shape[0] // parts
    for d in range(parts):
        at = d * piece + j * count
        out_ref[at : at + count, first : first + fold] = value[d * count : (d + 1) * count]


def query_side_kernel(*refs, head_dim, parts, fold, others):
    (dq_in, ww_in, w_in, normed_in, lora_in, own_in, wp_in, x_in, mg_in, gains_ref, cos_ref,
     sin_ref, keep_ref, got_ref) = refs[:14]
    others_in = refs[14 : 14 + others]
    (queries_ref, back_ref, pair_ref, in_grad_ref, one_ref, near_ref, far_ref,
     dq, ww, w, normed, lora, own, wp, x, mg, there, hold, sem) = refs[14 + others :]
    rows = x.shape[0]
    f = Fetch([(dq_in, dq), (ww_in, ww), (w_in, w), (normed_in, normed), (lora_in, lora),
               (own_in, own), (wp_in, wp), (x_in.at[pl.ds(0, rows)], x),
               (mg_in.at[pl.ds(0, rows)], mg)]
              + [(r, there.at[i]) for i, r in enumerate(others_in)], sem)
    near_ref[...] = (keep_ref[0].astype(F32) + got_ref[0].astype(F32)).astype(BF16)
    far_ref[...] = (keep_ref[1].astype(F32) + got_ref[1].astype(F32)).astype(BF16)
    q_cols, mid = dq.shape[1], lora.shape[1]
    f.wait(0, 1, 2)
    lora_grad = mm_nt(dq[...], ww[...]).astype(BF16)
    for m in range(dq.shape[0] // rows):
        at = slice(m * rows, (m + 1) * rows)
        back = mm_nt(dq[at, :], w[:, :q_cols]) + mm_nt(lora_grad[at], w[:, q_cols : q_cols + mid])
        if m == 0:
            hold[...] = back
        else:
            back_ref[(m - 1) * rows : m * rows] = back
    f.wait(3, 4)
    step = math.gcd(q_cols, 512)
    turned = normed[...].T
    for c in range(0, q_cols, step):
        queries_ref[:, c : c + step] = mm(turned, dq[:, c : c + step]).astype(BF16)
    queries_ref[:, q_cols : q_cols + mid] = mm(turned, lora_grad).astype(BF16)
    piece, count = normed.shape[1] // parts, mid // parts
    turned = lora[...].T
    for j in range(q_cols // fold):
        out = mm(turned, dq[:, j * fold : (j + 1) * fold]).astype(BF16)
        fold_rows(queries_ref, out, q_cols + mid, parts, piece, fold, j)
    rest = (q_cols // fold) * count
    for d in range(parts):
        queries_ref[d * piece + rest : (d + 1) * piece, q_cols + mid :] = jnp.zeros(
            (piece - rest, fold), BF16)
    f.wait(*range(5, 9 + others))
    dkv = own[...]
    for i in range(others):
        dkv = dkv + there[i].astype(F32)
    pair = unrotate(dkv, cos_ref[...], sin_ref[...], head_dim)
    pair_ref[...] = pair
    back = hold[...] + mm_nt(pair, wp[:, : 2 * head_dim])
    in_grad_ref[...], one_ref[...] = norm_back(x[...].astype(F32), gains_ref[0:1, :], back, mg[...])


def query_side(dq, ww, w, normed, lora_mid, own, others, w_pair, x, mid_grad, gains, cos, sin,
               keep, got, head_dim, parts, fold, batches, later):
    total, q_cols = dq.shape
    rows = total // batches
    width, mid = normed.shape[1], lora_mid.shape[1]
    half, cols = head_dim // 2, 2 * head_dim
    angle = pl.BlockSpec((rows, half), lambda i: (0, 0))
    n = len(others)
    return pl.pallas_call(
        skipping(functools.partial(query_side_kernel, head_dim=head_dim, parts=parts, fold=fold,
                                   others=n), 14 + n, len(later)),
        grid=(1,),
        in_specs=[ANY] * 9 + [VMEM, angle, angle, VMEM, VMEM] + [ANY] * (n + len(later)),
        out_specs=[VMEM] * 3 + [pl.BlockSpec((rows, width), lambda i: (0, 0))] + [VMEM] * 3,
        out_shape=[like((width, q_cols + mid + fold), BF16), like((total - rows, width), F32),
                   like((rows, cols), BF16), like((total, width), F32), like((1, width), F32)]
        + [like(keep.shape[1:], BF16)] * 2,
        scratch_shapes=[pltpu.VMEM(dq.shape, BF16), pltpu.VMEM(ww.shape, BF16),
                        pltpu.VMEM(w.shape, BF16), pltpu.VMEM(normed.shape, BF16),
                        pltpu.VMEM(lora_mid.shape, BF16), pltpu.VMEM((rows, cols), F32),
                        pltpu.VMEM(w_pair.shape, BF16), pltpu.VMEM((rows, width), BF16),
                        pltpu.VMEM((rows, width), F32), pltpu.VMEM((n, rows, cols), BF16),
                        pltpu.VMEM((rows, width), F32), pltpu.SemaphoreType.DMA((9 + n,))],
        compiler_params=params(),
        cost_estimate=cost(LONG, 20e6),
        name="query_side",
    )(dq, ww, w, normed, lora_mid, own, w_pair, x, mid_grad, gains, cos, sin, keep, got, *others,
      *later)


def pair_side_kernel(*refs, head_dim, parts, others):
    (where, own_in, wp_in, back_in, x_in, mg_in, normed_in, first_in, gains_ref, cos_ref, sin_ref,
     one_ref, two_ref) = refs[:13]
    others_in = refs[13 : 13 + others]
    outs = refs[14 + others :]
    in_grad_ref, send_ref = outs[:2]
    keeps = outs[2 : 2 + parts // 2]
    (own, wp, back, x, mg, normed, pair_ref, there, flat_ref, xt_ref, gain_ref,
     sem) = outs[2 + parts // 2 :]
    rows = x.shape[0]
    f = Fetch([(normed_in, normed), (own_in, own)]
              + [(r, there.at[i]) for i, r in enumerate(others_in)]
              + [(first_in, pair_ref.at[pl.ds(0, rows)]), (wp_in, wp), (back_in, back),
                 (x_in.at[pl.ds(rows, rows)], x), (mg_in.at[pl.ds(rows, rows)], mg)], sem)
    f.wait(0)
    turn(normed, flat_ref, xt_ref, where[0], parts)
    f.wait(*range(1, 2 + others))
    dkv = own[...]
    for i in range(others):
        dkv = dkv + there[i].astype(F32)
    pair = unrotate(dkv, cos_ref[...], sin_ref[...], head_dim)
    pair_ref[rows:, :] = pair
    f.wait(*range(2 + others, 7 + others))
    grads = back[...] + mm_nt(pair, wp[:, : 2 * head_dim])
    in_grad_ref[...], one = norm_back(x[...].astype(F32), gains_ref[0:1, :], grads, mg[...])
    width = flat_ref.shape[0]
    piece, half, cols = width // parts, parts // 2, 2 * head_dim
    out = mm(xt_ref[...], pair_ref[...]).astype(BF16)
    pad = jnp.zeros((126, width), F32)
    gain_ref[...] = jnp.concatenate([one + one_ref[...], two_ref[...], pad], axis=0).T.astype(BF16)
    for k in range(half):
        keeps[k][:, :cols] = out[k * piece : (k + 1) * piece]
        send_ref[k, :, :cols] = out[(half + k) * piece : (half + k + 1) * piece]
        at = pl.multiple_of((where[0] ^ (2 * k)) * piece, piece)
        keeps[k][:, cols:] = gain_ref[pl.ds(at, piece), :]
        at = pl.multiple_of((where[0] ^ (2 * k + 1)) * piece, piece)
        send_ref[k, :, cols:] = gain_ref[pl.ds(at, piece), :]


def pair_side(where, own, others, w_pair, back, x, mid_grad, normed, first, gains, cos, sin, one,
              two, in_grad, head_dim, parts):
    total, width = normed.shape
    rows = total // 2
    half, cols = head_dim // 2, 2 * head_dim
    piece = width // parts
    angle = pl.BlockSpec((rows, half), lambda i: (1, 0))
    n = len(others)
    return pl.pallas_call(
        functools.partial(pair_side_kernel, head_dim=head_dim, parts=parts, others=n),
        grid=(1,),
        in_specs=[SMEM] + [ANY] * 7 + [VMEM, angle, angle, VMEM, VMEM] + [ANY] * (n + 1),
        out_specs=[pl.BlockSpec((rows, width), lambda i: (1, 0))] + [VMEM] * (1 + parts // 2),
        out_shape=[like((total, width), F32), like((parts // 2, piece, cols + 128), BF16)]
        + [like((piece, cols + 128), BF16)] * (parts // 2),
        scratch_shapes=[pltpu.VMEM((rows, cols), F32), pltpu.VMEM(w_pair.shape, BF16),
                        pltpu.VMEM((rows, width), F32), pltpu.VMEM((rows, width), BF16),
                        pltpu.VMEM((rows, width), F32), pltpu.VMEM(normed.shape, BF16),
                        pltpu.VMEM((total, cols), BF16), pltpu.VMEM((n, rows, cols), BF16),
                        pltpu.VMEM((width, total), BF16), pltpu.VMEM((width, total), BF16),
                        pltpu.VMEM((width, 128), BF16), pltpu.SemaphoreType.DMA((7 + n,))],
        input_output_aliases={13 + n: 0},
        compiler_params=params(),
        cost_estimate=cost(LONG, 12e6),
        name="pair_side",
    )(where, own, w_pair, back, x, mid_grad, normed, first, gains, cos, sin, one, two, *others,
      in_grad)


def join_kernel(left_ref, *refs):
    out_ref = refs[-1]
    n = left_ref.shape[1]
    out_ref[:, :n] = left_ref[...]
    out_ref[:, n:] = tree([r[...].astype(F32) for r in refs[:-1]]).astype(BF16)


def join(left, parts, later=()):
    rows, n = left.shape
    count = 1 + len(parts)
    return pl.pallas_call(
        skipping(join_kernel, count, len(later)),
        in_specs=[VMEM] * count + [ANY] * len(later),
        out_specs=VMEM,
        out_shape=like((rows, n + parts[0].shape[1]), BF16),
        compiler_params=params(),
        cost_estimate=took(2),
        name="join",
    )(left, *parts, *later)


def finish_kernel(*refs, mid, q_cols, cols, fold):
    parts, outs = refs[:-6], refs[-6:]
    query_ref, narrow_ref, widen_ref, kv_ref, one_ref, two_ref = outs
    total = tree([p[...].astype(F32) for p in parts])
    query_ref[...] = total[:, :q_cols]
    narrow_ref[...] = total[:, q_cols : q_cols + mid]
    first = q_cols + mid
    count = widen_ref.shape[0]
    for j in range(q_cols // fold):
        widen_ref[:, j * fold : (j + 1) * fold] = total[j * count : (j + 1) * count,
                                                        first : first + fold]
    first += fold
    kv_ref[...] = total[:, first : first + cols]
    gains = total[:, first + cols :].T
    one_ref[...] = gains[0:1]
    two_ref[...] = gains[1:2]


def finish(parts, q_cols, mid, count, cols, fold):
    piece = parts[0].shape[0]
    return pl.pallas_call(
        functools.partial(finish_kernel, q_cols=q_cols, mid=mid, cols=cols, fold=fold),
        in_specs=[VMEM] * len(parts),
        out_specs=[VMEM] * 6,
        out_shape=[like((piece, q_cols), F32), like((piece, mid), F32), like((count, q_cols), F32),
                   like((piece, cols), F32), like((1, piece), F32), like((1, piece), F32)],
        compiler_params=params(),
        cost_estimate=took(2.5),
        name="finish",
    )(*parts)


def swap_cores(keeps, send, later=()):
    got, count = swap(send, "fsdp", 1), len(keeps)
    return add([*keeps, got], [[(k, None), (count, k)] for k in range(count)], later)


def pairs_kernel(*refs):
    parts, (keep_ref, send_ref) = refs[:-2], refs[-2:]
    for i in range(2):
        for k, ref in ((2 * i, keep_ref), (2 * i + 1, send_ref)):
            ref[i] = tree([p[k].astype(F32) for p in parts]).astype(BF16)


def sum_pairs(parts, later=()):
    count, shape = len(parts), like((2,) + parts[0].shape[1:], BF16)
    return pl.pallas_call(
        skipping(pairs_kernel, count, len(later)),
        in_specs=[VMEM] * count + [ANY] * len(later),
        out_specs=[VMEM] * 2,
        out_shape=[shape] * 2,
        compiler_params=params(),
        cost_estimate=took(2.4),
        name="sum_pairs",
    )(*parts, *later)


def cut_kernel(where, x_ref, *outs):
    part = outs[0].shape[1]
    for s, out in enumerate(outs):
        at = pl.multiple_of((where[1] ^ s) * part, part)
        out[...] = x_ref[:, pl.ds(at, part)]


def cut_parts(where, x, later=()):
    span = lax.axis_size("seq")
    rows, part = x.shape[0], x.shape[1] // span
    cut = pl.pallas_call(
        skipping(cut_kernel, 2, len(later)),
        in_specs=[SMEM, VMEM] + [ANY] * len(later),
        out_specs=[VMEM] * span,
        out_shape=[like((rows, part), x.dtype)] * span,
        compiler_params=params(),
        cost_estimate=took(2),
        name="cut",
    )(where, x, *later)
    return cut


def halves_kernel(*refs):
    out_ref = refs[-1]
    n = refs[0].shape[1]
    out_ref[:, :n] = tree([r[...].astype(F32) for r in refs[:-3]]).astype(BF16)
    out_ref[:, n:] = tree([r[...].astype(F32) for r in refs[-3:-1]]).astype(BF16)


def halves(left, right, later=()):
    count = len(left) + 2
    shape = (left[0].shape[0], left[0].shape[1] + right[0].shape[1])
    return pl.pallas_call(
        skipping(halves_kernel, count, len(later)),
        in_specs=[VMEM] * count + [ANY] * len(later),
        out_specs=VMEM,
        out_shape=like(shape, BF16),
        compiler_params=params(),
        cost_estimate=cost(LONG, 2e6),
        name="halves",
    )(*left, *right, *later)


def lay_kernel(where, *refs, n, k):
    parts = refs[:-6]
    span = len(parts)
    gate_ref, up_ref, down_ref, out_ref, tall_ref, tall2_ref = refs[-6:]
    piece = parts[0].shape[0]
    half = span // 2
    wide = gate_ref.shape[1] // half
    per = (parts[0].shape[1] - wide) // (n + k)
    for s, ref in enumerate(parts):
        q = where[1] ^ s
        for i, out in enumerate((gate_ref, up_ref)):
            @pl.when(q // half == i)
            def _():
                at = pl.multiple_of((q % half) * wide, wide)
                out[:, pl.ds(at, wide)] = ref[:, :wide].astype(F32)
        for i in range(per):
            at = pl.ds(pl.multiple_of((q * per + i) * piece, piece), piece)
            first = wide + i * n
            tall_ref[at, :] = ref[:, first : first + n].astype(F32)
            first = wide + per * n + i * k
            tall2_ref[at, :] = ref[:, first : first + k].astype(F32)
    down_ref[...] = tall_ref[...].T
    out_ref[...] = tall2_ref[...].T


def lay(where, parts, hidden, n, k, later=()):
    piece = parts[0].shape[0]
    width = piece * lax.axis_size("fsdp")
    return pl.pallas_call(
        skipping(functools.partial(lay_kernel, n=n, k=k), 1 + len(parts), len(later)),
        in_specs=[SMEM] + [VMEM] * len(parts) + [ANY] * len(later),
        out_specs=[VMEM] * 4,
        out_shape=[like((piece, hidden), F32)] * 2 + [like((n, width), F32), like((k, width), F32)],
        scratch_shapes=[pltpu.VMEM((width, n), F32), pltpu.VMEM((width, k), F32)],
        compiler_params=params(),
        cost_estimate=took(3),
        name="lay",
    )(where, *parts, *later)


def begin_of(index, lengths):
    ends = [lengths[0]]
    for n in lengths[1:]:
        ends.append(ends[-1] + n)
    begin = index
    for d in reversed(range(len(lengths))):
        begin = jnp.where(index < ends[d], ends[d] - lengths[d], begin)
    return begin


def local(tokens, document_lengths, cotangent, attention_gain, query_projection, narrowing_factor,
          widening_factor, key_value_projection, output_projection, feedforward_gain,
          gate_projection, up_projection, down_projection):
    batches, _, rows, width = tokens.shape
    head_dim = key_value_projection.shape[1] // 2
    q_cols = query_projection.shape[1]
    mid = narrowing_factor.shape[1]
    hidden = gate_projection.shape[1]
    kv_cols = 2 * head_dim
    scale = head_dim ** (-0.5)
    parts, span = lax.axis_size("fsdp"), lax.axis_size("seq")
    place = lax.axis_index("seq")
    tile = block = math.gcd(rows, 512)
    where = jnp.stack([lax.axis_index("fsdp"), place]).astype(jnp.int32)
    piece = width // parts
    direct = piece % 16 == 0
    fold = 512
    folds = q_cols // fold

    lengths = document_lengths[:, 0]
    half = head_dim // 2
    index = place * rows + lax.broadcasted_iota(jnp.int32, (batches, rows, half), 1)
    begin = begin_of(index, [lengths[:, d][:, None, None] for d in range(lengths.shape[1])])
    freqs = THETA ** (-(lax.broadcasted_iota(jnp.int32, (1, half), 1).astype(F32) * 2.0 / head_dim))
    angles = ((index - begin).astype(F32) * freqs).reshape(batches * rows, half)
    cos, sin = jnp.cos(angles), jnp.sin(angles)

    if direct:
        first = Shards(pack_pair(key_value_projection, attention_gain, feedforward_gain))
        third = pack(where, gate_projection, up_projection, down_projection, output_projection,
                     span, [cos, sin] + first.arrays[2::2])
        held = Tiled(third, 2 * hidden, down_projection, output_projection)
        weights = None
    else:
        def gather(x):
            return lax.all_gather(x, "fsdp", axis=0, tiled=True)

        first = jnp.concatenate(
            [key_value_projection,
             jnp.pad(jnp.stack([attention_gain, feedforward_gain], axis=1), ((0, 0), (0, 126)))],
            axis=1)
        turned = jnp.concatenate(
            [widening_factor[:, j * fold : (j + 1) * fold] for j in range(folds)])
        turned = jnp.pad(turned, ((0, piece - turned.shape[0]), (0, 0)))
        second = jnp.concatenate([query_projection, narrowing_factor, turned], axis=1)
        first, second = Whole(gather(first)), Whole(gather(second))
        second.rows = piece
        held = None
        weights = [gather(jnp.concatenate([gate_projection, up_projection], axis=1)),
                   gather(down_projection), gather(output_projection)]

    x = tokens.reshape(batches * rows, width)
    grad = cotangent.reshape(batches * rows, width)
    normed, kv, w_pair, gains = project_kv(where, x, cos, sin, first, head_dim)
    kvs = [kv] + [swap(kv, "seq", s) for s in range(1, span)]
    if direct:
        second = Shards(pack_query(query_projection, narrowing_factor, widening_factor, fold,
                                   [kv]), True)
    lora_mid, q, w_query, ww = project_q(where, normed, cos, sin, second, head_dim, q_cols, mid,
                                         scale, kvs[1:])
    attended, lse = attend(where, lengths, q, kvs, head_dim, tile, block)
    (output, mid_grad, branch, attn_grad, delta, ffn_low, hidden_low, lift_grads,
     gain_two_grad) = middle_part(x, attended, grad, gains, held, weights, head_dim)

    if direct:
        keep, send = column_grads(where, grad, hidden_low, branch, attended, parts, span)
        got = swap(send, "fsdp", 1)
        lifts = weight_grad(ffn_low, lift_grads, 1024, [keep])
        lifts_sum = lax.psum_scatter(lifts, "fsdp", scatter_dimension=0, tiled=True)
        columns = add([keep, got], [[(0, s), (1, s)] for s in range(span)], [lifts])
        there = [columns[0]] + [swap(a, "seq", s) for s, a in enumerate(columns) if s > 0]
    dq, owns, others = None, [], []
    for m in range(batches):
        later = []
        if direct and m == 0:
            later = columns
        if direct and m == 1:
            keep, send = sum_pairs(there, [dq])
            got = swap(send, "fsdp", 2)
            later = [keep]
        dq, own, *sends = attend_back(where, lengths, lse, delta, q, attn_grad, kvs, cos, sin,
                                      head_dim, tile, block, scale, m, dq, later)
        owns.append(own)
        others.append([swap(a, "seq", s) for s, a in enumerate(sends, 1)])
    if direct:
        queries, back, pair, in_grad, one, near, far = query_side(
            dq, ww, w_query, normed, lora_mid, owns[0], others[0], w_pair, x, mid_grad, gains, cos,
            sin, keep, got, head_dim, parts, fold, batches, [lifts_sum])
        queries_sum = lax.psum_scatter(queries, "fsdp", scatter_dimension=0, tiled=True)
        in_grad, send, *keeps = pair_side(where, owns[1], others[1], w_pair, back, x, mid_grad,
                                          normed, pair, gains, cos, sin, one, gain_two_grad,
                                          in_grad, head_dim, parts)

        def share(x):
            return [x] + [swap(x, "seq", s) for s in range(1, span)]

        lifts_cut = cut_parts(where, lifts_sum, others[1])
        lifts_parts = [lifts_cut[0]] + [swap(lifts_cut[s], "seq", s) for s in range(1, span)]
        mine = halves(lifts_parts, [near, swap(far, "fsdp", 4)], [send])
        laid = share(mine)
        shards = swap_cores(keeps, send, [mine])
        mine = join(queries_sum, [shards[0]] + [
            swap(a, "fsdp", 2 * k) for k, a in enumerate(shards) if k > 0])
        last = share(mine)
        gate_grad, up_grad, down_grad, out_grad = lay(
            where, laid, hidden, hidden // parts, q_cols // parts, [mine])
        query_grad, narrow_grad, widen_grad, key_value_grad, one, two = finish(
            last, q_cols, mid, mid // parts, kv_cols, fold)
        gain_one_grad, gain_two_grad = one.reshape(piece), two.reshape(piece)
    else:
        lora_grad, back = query_back(dq, w_query, ww)
        in_grad, pairs, ones = None, [], []
        for m in range(batches):
            pair, in_grad, one = pair_back(x, gains, cos, sin, w_pair, owns[m], others[m], back,
                                           mid_grad, head_dim, m, batches, in_grad)
            pairs.append(pair)
            ones.append(one)

        def scatter(x):
            part = lax.psum_scatter(x.astype(BF16), "fsdp", scatter_dimension=0, tiled=True)
            return lax.psum(part, "seq").astype(F32)

        pair_grad = jnp.concatenate(pairs)
        gain_one_grad = sum(ones)
        down_grad = scatter(weight_grad(grad, hidden_low).T)
        out_grad = scatter(weight_grad(branch, attended).T)
        lift_w = scatter(weight_grad(ffn_low, lift_grads))
        gate_grad, up_grad = lift_w[:, :hidden], lift_w[:, hidden:]
        query_grad = scatter(weight_grad(normed, dq))
        narrow_grad = scatter(weight_grad(normed, lora_grad))
        widen_grad = scatter(weight_grad(lora_mid, dq))
        key_value_grad = scatter(weight_grad(normed, pair_grad))
        gains_grad = scatter(jnp.concatenate([gain_one_grad, gain_two_grad]).T)
        gain_one_grad, gain_two_grad = gains_grad[:, 0], gains_grad[:, 1]
    return (output.reshape(batches, 1, rows, width), in_grad.reshape(batches, 1, rows, width),
            gain_one_grad, query_grad, narrow_grad, widen_grad, key_value_grad, out_grad,
            gain_two_grad, gate_grad, up_grad, down_grad)


def solution(mesh):
    rows = P(None, "fsdp", "seq", None)
    vector, matrix = P("fsdp"), P("fsdp", None)
    in_specs = (rows, P(None, "fsdp", None), rows, vector) + (matrix,) * 5 + (vector,) + (matrix,) * 3
    out_specs = (rows, rows, vector) + (matrix,) * 5 + (vector,) + (matrix,) * 3
    return jax.shard_map(local, mesh=mesh, in_specs=in_specs, out_specs=out_specs, check_vma=False)
```

```python
import functools
import math

import jax
import jax.numpy as jnp
from jax import lax
from jax.experimental import pallas as pl
from jax.experimental.pallas import tpu as pltpu
from jax.sharding import PartitionSpec as P

EPSILON = 1e-06
THETA = 10000.0
F32 = jnp.float32
BF16 = jnp.bfloat16
GELU_C = math.sqrt(2.0 / math.pi)
GELU_A = 0.044715
LOWEST = -1e30
VMEM_LIMIT = 60 * 1024 * 1024
ANY = pl.BlockSpec(memory_space=pl.ANY)
VMEM = pl.BlockSpec(memory_space=pltpu.VMEM)
SMEM = pl.BlockSpec(memory_space=pltpu.SMEM)


def mm(left, right):
    return lax.dot_general(left, right, (((1,), (0,)), ((), ())), preferred_element_type=F32)


def mm_nt(left, right):
    return lax.dot_general(left, right, (((1,), (1,)), ((), ())), preferred_element_type=F32)


def full(shape):
    return pl.BlockSpec(shape, lambda i: (0,) * len(shape))


def rows_of(tile, cols):
    return pl.BlockSpec((tile, cols), lambda i: (i, 0))


def params(**more):
    return pltpu.CompilerParams(vmem_limit_bytes=VMEM_LIMIT, **more)


def cost(flops, bytes_accessed, transcendentals=0):
    return pl.CostEstimate(
        flops=int(flops), bytes_accessed=int(bytes_accessed), transcendentals=int(transcendentals)
    )


def took(us):
    return cost(us * 1.1e9, 1)


LONG = 10**12


def like(shape, dtype):
    return jax.ShapeDtypeStruct(tuple(shape), dtype)


def swap(x, axis, by):
    return lax.ppermute(x, axis, [(i, i ^ by) for i in range(lax.axis_size(axis))])


def skipping(kernel, first, count):
    return lambda *refs: kernel(*refs[:first], *refs[first + count :])


def tree(values):
    while len(values) > 1:
        values = [values[i] + values[i + 1] for i in range(0, len(values), 2)]
    return values[0]


def add_kernel(*refs, count, groups):
    for out, group in zip(refs[count:], groups):
        values = [refs[i][...] if k is None else refs[i][k] for i, k in group]
        out[...] = tree([v.astype(F32) for v in values]).astype(out.dtype)


def add(arrays, groups, later=(), dtype=BF16):
    shapes = [arrays[g[0][0]].shape if g[0][1] is None else arrays[g[0][0]].shape[1:]
              for g in groups]
    count = len(arrays)
    later = list(later)
    return list(pl.pallas_call(
        skipping(functools.partial(add_kernel, count=count, groups=groups), count, len(later)),
        in_specs=[VMEM] * count + [ANY] * len(later),
        out_specs=[VMEM] * len(groups),
        out_shape=[like(s, dtype) for s in shapes],
        compiler_params=params(),
        cost_estimate=took(3.5),
        name="add",
    )(*arrays, *later))


class Whole:
    def __init__(self, array):
        self.arrays = [array]
        self.shape = array.shape
        self.count = 1

    def copies(self, where, refs, dst):
        return [(refs[0], dst)]


class Shards:
    def __init__(self, x, relay=False):
        parts = lax.axis_size("fsdp")
        got = {0: x}
        for r in range(2, parts, 2):
            low = r & -r
            near = relay and r != low
            got[r] = swap(got[r - low], "fsdp", low) if near else swap(x, "fsdp", r)
        for r in range(0, parts, 2):
            got[r + 1] = swap(got[r], "fsdp", 1)
        self.arrays = [got[r] for r in range(parts)]
        self.rows = x.shape[0]
        self.shape = (parts * x.shape[0], x.shape[1])
        self.count = parts

    def copies(self, where, refs, dst):
        out = []
        for r, ref in enumerate(refs):
            at = pl.multiple_of((where[0] ^ r) * self.rows, self.rows)
            out.append((ref, dst.at[pl.ds(at, self.rows), :]))
        return out


def pack_pair_kernel(kv_ref, one_ref, two_ref, out_ref):
    piece, kv_cols = kv_ref.shape
    out_ref[:, :kv_cols] = kv_ref[...]
    pad = jnp.zeros((126, piece), F32)
    gains = jnp.concatenate([one_ref[...].astype(F32), two_ref[...].astype(F32), pad], axis=0)
    out_ref[:, kv_cols:] = gains.T.astype(BF16)


def pack_pair(kv, one, two):
    piece = kv.shape[0]
    return pl.pallas_call(
        pack_pair_kernel,
        in_specs=[VMEM] * 3,
        out_specs=VMEM,
        out_shape=like((piece, kv.shape[1] + 128), BF16),
        compiler_params=params(),
        cost_estimate=took(1.6),
        name="pack_pair",
    )(kv, one.reshape(1, piece), two.reshape(1, piece))


def pack_kernel(where, gate_ref, up_ref, down_ref, out_ref, third_ref, *, span):
    piece = gate_ref.shape[0]
    hidden = gate_ref.shape[1]
    part = 2 * hidden // span
    for s in range(span):
        ref, at = (gate_ref, s * part) if s * part < hidden else (up_ref, s * part - hidden)

        @pl.when(where[1] == s)
        def _():
            third_ref[:, :part] = ref[:, at : at + part]

    col = part
    for ref in (down_ref, out_ref):
        n = ref.shape[0] // span
        for i in range(n // 16):
            row = pl.ds(pl.multiple_of(where[1] * n + 16 * i, 16), 16)
            for j in range(ref.shape[1] // 128):
                third_ref[16 * j : 16 * j + 16, col : col + 128] = ref[row, j * 128 : (j + 1) * 128]
            col += 128


def pack(where, gate, up, down, out, span, later):
    piece = gate.shape[0]
    third = (gate.shape[1] * 2 * piece + (down.shape[0] + out.shape[0]) * down.shape[1]) // span
    return pl.pallas_call(
        skipping(functools.partial(pack_kernel, span=span), 5, len(later)),
        in_specs=[SMEM] + [VMEM] * 4 + [ANY] * len(later),
        out_specs=VMEM,
        out_shape=like((piece, third // piece), BF16),
        compiler_params=params(),
        cost_estimate=took(2),
        name="pack",
    )(where, gate, up, down, out, *later)


def pack_query_kernel(q_ref, narrow_ref, widen_ref, out_ref, *, fold):
    q_cols, mid, count = q_ref.shape[1], narrow_ref.shape[1], widen_ref.shape[0]
    out_ref[:, :q_cols] = q_ref[...]
    out_ref[:, q_cols : q_cols + mid] = narrow_ref[...]
    folds = q_cols // fold
    for j in range(folds):
        out_ref[j * count : (j + 1) * count, q_cols + mid :] = widen_ref[
            :, j * fold : (j + 1) * fold]
    rest = out_ref.shape[0] - folds * count
    out_ref[folds * count :, q_cols + mid :] = jnp.zeros((rest, fold), BF16)


def pack_query(q, narrow, widen, fold, later):
    return pl.pallas_call(
        skipping(functools.partial(pack_query_kernel, fold=fold), 3, len(later)),
        in_specs=[VMEM] * 3 + [ANY] * len(later),
        out_specs=VMEM,
        out_shape=like((q.shape[0], q.shape[1] + narrow.shape[1] + fold), BF16),
        compiler_params=params(),
        cost_estimate=took(1.7),
        name="pack_query",
    )(q, narrow, widen, *later)


class Tiled:
    def __init__(self, packed, gate_up, *tall):
        parts, span = lax.axis_size("fsdp"), lax.axis_size("seq")
        piece = packed.shape[0]
        self.piece, self.part, self.parts, self.span = piece, gate_up // span, parts, span
        self.heights = [t.shape[0] // span for t in tall]
        self.up, self.across = sum(self.heights) // 16, tall[0].shape[1] // 128
        self.array = lax.all_gather(packed, ("seq", "fsdp"), axis=0, tiled=True)
        self.shape = (parts * piece, gate_up)
        self.shapes = [(parts * t.shape[0], t.shape[1]) for t in tall]
        self.scratch = (span, parts * piece, self.up * 128)

    def copies(self, ref, dst, rest):
        height = self.parts * self.piece
        rows = [pl.ds(s * height, height) for s in range(self.span)]
        return [(ref.at[at, pl.ds(self.part, self.up * 128)], rest.at[s])
                for s, at in enumerate(rows)] + [
            (ref.at[at, pl.ds(0, self.part)], dst.at[:, pl.ds(s * self.part, self.part)])
            for s, at in enumerate(rows)]

    def unfold(self, rest, dsts):
        starts, tops = [], 0
        for n in self.heights:
            starts.append(tops)
            tops += n // 16

        def shard(d, carry):
            for s in range(self.span):
                for n, first, dst in zip(self.heights, starts, dsts):
                    for i in range(n // 16):
                        at = pl.ds(pl.multiple_of(d * n * self.span + s * n + i * 16, 16), 16)
                        for j in range(self.across):
                            row = pl.ds(pl.multiple_of(d * self.piece + 16 * j, 16), 16)
                            col = (first + i) * 128
                            dst[at, j * 128 : (j + 1) * 128] = rest[s, row, col : col + 128]
            return carry

        lax.fori_loop(0, self.parts, shard, 0)


def carry_out(copies, sem):
    made = [pltpu.make_async_copy(src, dst, sem.at[i]) for i, (src, dst) in enumerate(copies)]
    for c in made:
        c.start()
    for c in made:
        c.wait()


def normalize(x_ref, gains_ref):
    x = x_ref[...].astype(F32)
    inv = lax.rsqrt(jnp.mean(x * x, axis=-1, keepdims=True) + EPSILON)
    return (x * inv * gains_ref[0:1, :]).astype(BF16)


def put_pair(kv_ref, pair, cos, sin, head_dim):
    half = head_dim // 2
    a, b = pair[:, :half], pair[:, half:head_dim]
    kv_ref[:, :half] = (a * cos - b * sin).astype(BF16)
    kv_ref[:, half:head_dim] = (b * cos + a * sin).astype(BF16)
    kv_ref[:, head_dim:] = pair[:, head_dim:].astype(BF16)


def project_kv_kernel(*refs, held, head_dim):
    where, x_ref, cos_ref, sin_ref = refs[:4]
    pieces = refs[4 : 4 + len(held.arrays)]
    normed_ref, kv_ref, w_ref, gains_ref, sem = refs[4 + len(held.arrays) :]
    kv_cols = 2 * head_dim

    @pl.when(pl.program_id(0) == 0)
    def _():
        carry_out(held.copies(where, pieces, w_ref), sem)
        gains_ref[...] = w_ref[:, kv_cols:].astype(F32).T[:8]

    normed = normalize(x_ref, gains_ref)
    normed_ref[...] = normed
    put_pair(kv_ref, mm(normed, w_ref[:, :kv_cols]), cos_ref[...], sin_ref[...], head_dim)


def project_kv(where, x, cos, sin, held, head_dim):
    rows, width = x.shape
    tile = math.gcd(rows, 512)
    half = head_dim // 2
    return pl.pallas_call(
        functools.partial(project_kv_kernel, held=held, head_dim=head_dim),
        grid=(rows // tile,),
        in_specs=[SMEM, rows_of(tile, width), rows_of(tile, half), rows_of(tile, half)]
        + [ANY] * len(held.arrays),
        out_specs=[rows_of(tile, width), rows_of(tile, 2 * head_dim), full(held.shape),
                   full((8, width))],
        out_shape=[like((rows, width), BF16), like((rows, 2 * head_dim), BF16),
                   like(held.shape, BF16), like((8, width), F32)],
        scratch_shapes=[pltpu.SemaphoreType.DMA((held.count,))],
        compiler_params=params(),
        cost_estimate=took(5),
        name="project_kv",
    )(where, x, cos, sin, *held.arrays)


def project_q_kernel(*refs, held, head_dim, q_cols, mid, scale):
    where, normed_ref, cos_ref, sin_ref = refs[:4]
    pieces = refs[4 : 4 + len(held.arrays)]
    lora_ref, q_ref, w_ref, ww_ref, sem = refs[4 + len(held.arrays) :]
    half = head_dim // 2
    fold = held.shape[1] - q_cols - mid
    parts = q_cols // fold

    @pl.when(pl.program_id(0) == 0)
    def _():
        carry_out(held.copies(where, pieces, w_ref), sem)
        shards = held.shape[0] // held.rows
        count = mid // shards
        for d in range(shards):
            for j in range(parts):
                ww_ref[d * count : (d + 1) * count, j * fold : (j + 1) * fold] = w_ref[
                    d * held.rows + j * count : d * held.rows + (j + 1) * count, q_cols + mid :]

    normed = normed_ref[...]
    cos, sin = cos_ref[...], sin_ref[...]
    low = mm(normed, w_ref[:, q_cols : q_cols + mid]).astype(BF16)
    lora_ref[...] = low
    query = mm(normed, w_ref[:, :q_cols]) + mm(low, ww_ref[...])
    for h in range(q_cols // head_dim):
        c = h * head_dim
        a, b = query[:, c : c + half], query[:, c + half : c + head_dim]
        q_ref[:, c : c + half] = ((a * cos - b * sin) * scale).astype(BF16)
        q_ref[:, c + half : c + head_dim] = ((b * cos + a * sin) * scale).astype(BF16)


def project_q(where, normed, cos, sin, held, head_dim, q_cols, mid, scale, later):
    rows, width = normed.shape
    tile = math.gcd(rows, 256)
    half = head_dim // 2
    count = 4 + len(held.arrays)
    return pl.pallas_call(
        skipping(functools.partial(project_q_kernel, held=held, head_dim=head_dim, q_cols=q_cols,
                                   mid=mid, scale=scale), count, len(later)),
        grid=(rows // tile,),
        in_specs=[SMEM, rows_of(tile, width), rows_of(tile, half), rows_of(tile, half)]
        + [ANY] * (len(held.arrays) + len(later)),
        out_specs=[rows_of(tile, mid), rows_of(tile, q_cols), full(held.shape),
                   full((mid, q_cols))],
        out_shape=[like((rows, mid), BF16), like((rows, q_cols), BF16), like(held.shape, BF16),
                   like((mid, q_cols), BF16)],
        scratch_shapes=[pltpu.SemaphoreType.DMA((held.count,))],
        compiler_params=params(),
        cost_estimate=cost(1, 1),
        name="project_q",
    )(where, normed, cos, sin, *held.arrays, *later)


class Group:
    def __init__(self, kv, batches):
        self.rows = kv.shape[0] // batches
        span = lax.axis_size("seq")
        self.span = span
        self.relay = span == 4 and batches == 2
        if self.relay:
            one, two = swap(kv, "seq", 1), swap(kv, "seq", 2)
            self.arrays = [kv, one, two, swap(one[: self.rows], "seq", 2),
                           swap(two[self.rows :], "seq", 1)]
        else:
            self.arrays = [kv] + [swap(kv, "seq", s) for s in range(1, span)]

    def at(self, n, s):
        return (3 + n, 0) if self.relay and s == 3 else (s, n * self.rows)

    def copy(self, refs, n, s, place, dst, sem):
        i, row = self.at(n, s)
        to = pl.multiple_of((place ^ s) * self.rows, self.rows)
        return pltpu.make_async_copy(refs[i].at[pl.ds(row, self.rows)],
                                     dst.at[pl.ds(to, self.rows), :], sem)


def attend_kernel(*refs, group, head_dim, tile, block):
    where, lengths_ref, q_ref = refs[:3]
    kvs = refs[3 : 3 + len(group.arrays)]
    span = group.span
    o_ref, lse_ref, kv_ref, vt_ref, acc_ref, sem = refs[-6:]
    heads = q_ref.shape[1] // head_dim
    rows = q_ref.shape[0]
    m = pl.program_id(0)
    place = where[1]
    base = place * rows
    lengths = [lengths_ref[m, d] for d in range(lengths_ref.shape[1])]

    def first(t):
        return lax.div(begin_of(base + t * tile, lengths), block)

    def copy(n, s):
        return group.copy(kvs, n, s, place, kv_ref.at[n], sem.at[n, s])

    @pl.when(m == 0)
    def _():
        for n in range(kv_ref.shape[0]):
            for s in range(span):
                pl.when((place ^ s) <= place)(lambda n=n, s=s: copy(n, s).start())

    for n in range(kv_ref.shape[0]):
        for s in range(span):
            pl.when((m == n) & ((place ^ s) <= place))(lambda n=n, s=s: copy(n, s).wait())

    def flip(kb, carry):
        at = pl.ds(pl.multiple_of(kb * block, block), block)
        vt_ref[:, at] = kv_ref[m, at, head_dim:].T
        return carry

    lax.fori_loop(first(0), lax.div(base + rows + block - 1, block), flip, 0)
    for t in range(rows // tile):
        q_rows = slice(t * tile, (t + 1) * tile)
        high = base + t * tile + lax.broadcasted_iota(jnp.int32, (1, tile), 1)
        low = begin_of(high, lengths)
        acc_ref[...] = jnp.zeros_like(acc_ref)

        def visit(kb, carry):
            at = pl.ds(pl.multiple_of(kb * block, block), block)
            keys = kv_ref[m, at, :head_dim]
            vt = vt_ref[:, at]
            index = kb * block + lax.broadcasted_iota(jnp.int32, (block, tile), 0)
            mask = (index >= low) & (index <= high)
            out = []
            for h in range(heads):
                peak, total = carry[h]
                s = mm_nt(keys, q_ref[q_rows, h * head_dim : (h + 1) * head_dim])
                s = jnp.where(mask, s, -jnp.inf)
                new_peak = jnp.maximum(peak, jnp.max(s, axis=0, keepdims=True))
                factor = jnp.exp(peak - new_peak)
                p = jnp.exp(s - new_peak)
                total = total * factor + jnp.sum(p, axis=0, keepdims=True)
                acc_ref[h] = acc_ref[h] * factor + mm(vt, p.astype(BF16))
                out.append((new_peak, total))
            return tuple(out)

        start = tuple(
            (jnp.full((1, tile), LOWEST, F32), jnp.zeros((1, tile), F32)) for _ in range(heads)
        )
        stats = lax.fori_loop(first(t), lax.div(base + (t + 1) * tile + block - 1, block), visit,
                              start)
        for h in range(heads):
            peak, total = stats[h]
            o_ref[q_rows, h * head_dim : (h + 1) * head_dim] = (acc_ref[h] / total).T.astype(BF16)
            lse_ref[0, h : h + 1, q_rows] = peak + jnp.log(total)


def attend(where, lengths, q, group, head_dim, tile, block):
    total, q_cols = q.shape
    batches = lengths.shape[0]
    rows = total // batches
    heads = q_cols // head_dim
    span = group.span
    return pl.pallas_call(
        functools.partial(attend_kernel, group=group, head_dim=head_dim, tile=tile, block=block),
        grid=(batches,),
        in_specs=[SMEM, SMEM, rows_of(rows, q_cols)] + [ANY] * len(group.arrays),
        out_specs=[rows_of(rows, q_cols), pl.BlockSpec((1, heads, rows), lambda i: (i, 0, 0))],
        out_shape=[like(q.shape, BF16), like((batches, heads, rows), F32)],
        scratch_shapes=[pltpu.VMEM((batches, span * rows, 2 * head_dim), BF16),
                        pltpu.VMEM((head_dim, span * rows), BF16),
                        pltpu.VMEM((heads, head_dim, tile), F32),
                        pltpu.SemaphoreType.DMA((batches, span))],
        compiler_params=params(),
        cost_estimate=took(18),
        name="attend",
    )(where, lengths, q, *group.arrays)


def middle_kernel(*refs, held, head_dim, chunk):
    x_ref, attn_ref, g_ref, gains_ref = refs[:4]
    if held is None:
        w_ref, wd_ref, wo_ref = refs[4:7]
    else:
        w_ref, wd_ref, wo_ref, rest_ref, sem = refs[-5:]
    (out_ref, mid_grad_ref, branch_ref, attn_grad_ref, delta_ref, low_ref, hidden_ref, grads_ref,
     gain_grad_ref) = refs[5:14] if held is not None else refs[7:16]

    @pl.when(pl.program_id(0) == 0)
    def _():
        if held is not None:
            f = Fetch(held.copies(refs[4], w_ref, rest_ref), sem)
            f.wait(*range(held.span))
            held.unfold(rest_ref, [wd_ref, wo_ref])
            f.wait(*range(held.span, 2 * held.span))
        gain_grad_ref[...] = jnp.zeros_like(gain_grad_ref)

    gain = gains_ref[1:2, :]
    attn = attn_ref[...]
    middle = x_ref[...].astype(F32) + mm(attn, wo_ref[...])
    inv = lax.rsqrt(jnp.mean(middle * middle, axis=-1, keepdims=True) + EPSILON)
    unit = middle * inv
    low = (unit * gain).astype(BF16)
    low_ref[...] = low
    grad = g_ref[...]
    result = middle
    back = jnp.zeros_like(middle)
    wide = wd_ref.shape[0]
    for c in range(wide // chunk):
        at = slice(c * chunk, (c + 1) * chunk)
        to = slice(wide + c * chunk, wide + (c + 1) * chunk)
        gate = mm(low, w_ref[:, at])
        lift = mm(low, w_ref[:, to])
        square = gate * gate
        bend = jnp.tanh(GELU_C * gate * (1.0 + GELU_A * square))
        cdf = 0.5 * (1.0 + bend)
        gelu = gate * cdf
        hidden = (gelu * lift).astype(BF16)
        hidden_ref[:, at] = hidden
        result = result + mm(hidden, wd_ref[at, :])
        hidden_grad = mm_nt(grad, wd_ref[at, :])
        slope = cdf + (0.5 * GELU_C) * gate * (1.0 - bend * bend) * (1.0 + 3.0 * GELU_A * square)
        gate_grad = (hidden_grad * lift * slope).astype(BF16)
        lift_grad = (hidden_grad * gelu).astype(BF16)
        grads_ref[:, at] = gate_grad
        grads_ref[:, to] = lift_grad
        back = back + mm_nt(gate_grad, w_ref[:, at]) + mm_nt(lift_grad, w_ref[:, to])
    out_ref[...] = result.astype(BF16)
    gain_grad_ref[...] += jnp.sum(unit * back, axis=0, keepdims=True)
    scaled = back * gain
    mid_grad = grad.astype(F32) + inv * (
        scaled - unit * jnp.mean(unit * scaled, axis=-1, keepdims=True)
    )
    mid_grad_ref[...] = mid_grad
    branch = mid_grad.astype(BF16)
    branch_ref[...] = branch
    attn_grad = mm_nt(branch, wo_ref[...]).astype(BF16)
    attn_grad_ref[...] = attn_grad
    product = attn_grad.astype(F32) * attn.astype(F32)
    half = head_dim // 2
    for h in range(attn.shape[1] // head_dim):
        c = h * head_dim
        folded = product[:, c : c + half] + product[:, c + half : c + head_dim]
        delta_ref[h : h + 1, :] = jnp.sum(folded.T, axis=0, keepdims=True)


def middle_part(x, attn, grad, gains, held, weights, head_dim):
    rows, width = x.shape
    q_cols = attn.shape[1]
    hidden = (weights[0].shape if held is None else held.shape)[1] // 2
    heads = q_cols // head_dim
    tile = math.gcd(rows, 512)
    if held is None:
        more, specs, scratch = weights, [full(w.shape) for w in weights], []
    else:
        more, specs = [held.array], [ANY]
        scratch = [pltpu.VMEM(held.shape, BF16)] + [pltpu.VMEM(s, BF16) for s in held.shapes]
        scratch += [pltpu.VMEM(held.scratch, BF16), pltpu.SemaphoreType.DMA((2 * held.span,))]
    return pl.pallas_call(
        functools.partial(middle_kernel, held=held, head_dim=head_dim, chunk=512),
        grid=(rows // tile,),
        in_specs=[rows_of(tile, width), rows_of(tile, q_cols), rows_of(tile, width),
                  full(gains.shape)] + specs,
        out_specs=[rows_of(tile, width), rows_of(tile, width), rows_of(tile, width),
                   rows_of(tile, q_cols), pl.BlockSpec((heads, tile), lambda i: (0, i)),
                   rows_of(tile, width), rows_of(tile, hidden), rows_of(tile, 2 * hidden),
                   full((1, width))],
        out_shape=[like((rows, width), BF16), like((rows, width), F32), like((rows, width), BF16),
                   like((rows, q_cols), BF16), like((heads, rows), F32),
                   like((rows, width), BF16), like((rows, hidden), BF16),
                   like((rows, 2 * hidden), BF16), like((1, width), F32)],
        scratch_shapes=scratch,
        compiler_params=params(),
        cost_estimate=took(39),
        name="middle",
    )(x, attn, grad, gains, *more)


def attend_back_kernel(*refs, group, head_dim, tile, block, scale, m):
    where, lengths_ref, lse_ref, delta_ref, q_ref, do_ref, cos_ref, sin_ref = refs[:8]
    kvs, span = refs[8 : 8 + len(group.arrays)], group.span
    kv_ref, dkv_ref, kt_ref, acc_ref, sem = refs[-5:]
    sends = refs[-5 - (span - 1) : -5]
    dq_ref, own_ref = refs[-5 - span - 1 : -5 - span + 1]
    heads = q_ref.shape[1] // head_dim
    half = head_dim // 2
    rows = q_ref.shape[0]
    place = where[1]
    base = place * rows
    lengths = [lengths_ref[m, d] for d in range(lengths_ref.shape[1])]
    tiles = rows // tile
    firsts = [lax.div(begin_of(base + t * tile, lengths), block) for t in range(tiles)]

    def copy(s):
        return group.copy(kvs, m, s, place, kv_ref, sem.at[s])

    for s in range(span):
        pl.when((place ^ s) <= place)(lambda s=s: copy(s).start())
    acc_ref[...] = jnp.zeros_like(acc_ref)
    dkv_ref[...] = jnp.zeros_like(dkv_ref)
    for s in range(span):
        pl.when((place ^ s) <= place)(lambda s=s: copy(s).wait())

    def visit(kb, carry):
        at = pl.ds(pl.multiple_of(kb * block, block), block)
        keys = kv_ref[at, :head_dim]
        vals = kv_ref[at, head_dim:]
        kt_ref[...] = keys.T
        for t in range(tiles):
            q_rows = slice(t * tile, (t + 1) * tile)

            @pl.when((kb >= firsts[t]) & (kb * block < base + (t + 1) * tile))
            def _():
                high = base + t * tile + lax.broadcasted_iota(jnp.int32, (1, tile), 1)
                low = begin_of(high, lengths)
                index = kb * block + lax.broadcasted_iota(jnp.int32, (block, tile), 0)
                mask = (index >= low) & (index <= high)
                dk = jnp.zeros((block, head_dim), F32)
                dv = jnp.zeros((block, head_dim), F32)
                for h in range(heads):
                    cols = slice(h * head_dim, (h + 1) * head_dim)
                    q = q_ref[q_rows, cols]
                    do = do_ref[q_rows, cols]
                    s = mm_nt(keys, q)
                    p = jnp.where(mask, jnp.exp(s - lse_ref[0, h : h + 1, q_rows]), 0.0)
                    dv = dv + mm(p.astype(BF16), do)
                    ds = (p * (mm_nt(vals, do) - delta_ref[h : h + 1, q_rows])).astype(BF16)
                    dk = dk + mm(ds, q)
                    acc_ref[h, :, q_rows] += mm(kt_ref[...], ds)
                dkv_ref[at, :head_dim] += dk
                dkv_ref[at, head_dim:] += dv

        return carry

    lax.fori_loop(firsts[0], lax.div(base + rows + block - 1, block), visit, 0)
    cos, sin = cos_ref[...], sin_ref[...]
    for h in range(heads):
        c = h * head_dim
        dq = acc_ref[h].T * scale
        a, b = dq[:, :half], dq[:, half:]
        dq_ref[:, c : c + half] = (a * cos + b * sin).astype(BF16)
        dq_ref[:, c + half : c + head_dim] = (b * cos - a * sin).astype(BF16)
    own_ref[...] = dkv_ref[pl.ds(pl.multiple_of(place * rows, rows), rows), :]
    for s, send_ref in enumerate(sends, 1):
        at = pl.multiple_of((place ^ s) * rows, rows)
        send_ref[...] = dkv_ref[pl.ds(at, rows), :].astype(BF16)


def attend_back(where, lengths, lse, delta, q, do, group, cos, sin, head_dim, tile, block, scale, m,
                before, later):
    q_cols = q.shape[1]
    rows = q.shape[0] // lengths.shape[0]
    heads = q_cols // head_dim
    span, n = group.span, len(group.arrays)
    tokens = span * rows
    half = head_dim // 2
    here = pl.BlockSpec((rows, q_cols), lambda i: (m, 0))
    angle = pl.BlockSpec((rows, half), lambda i: (m, 0))
    more = ([] if before is None else [before]) + later
    return pl.pallas_call(
        functools.partial(attend_back_kernel, group=group, head_dim=head_dim, tile=tile,
                          block=block, scale=scale, m=m),
        grid=(1,),
        in_specs=[SMEM, SMEM, pl.BlockSpec((1, heads, rows), lambda i: (m, 0, 0)),
                  pl.BlockSpec((heads, rows), lambda i: (0, m)), here, here, angle, angle]
        + [ANY] * (n + len(more)),
        out_specs=[here] + [VMEM] * span,
        out_shape=[like(q.shape, BF16), like((rows, 2 * head_dim), F32)]
        + [like((rows, 2 * head_dim), BF16)] * (span - 1),
        scratch_shapes=[pltpu.VMEM((tokens, 2 * head_dim), BF16),
                        pltpu.VMEM((tokens, 2 * head_dim), F32), pltpu.VMEM((head_dim, block), BF16),
                        pltpu.VMEM((heads, head_dim, rows), F32),
                        pltpu.SemaphoreType.DMA((span,))],
        input_output_aliases={} if before is None else {8 + n: 0},
        compiler_params=params(),
        cost_estimate=cost(LONG, 1),
        name="attend_back",
    )(where, lengths, lse, delta, q, do, cos, sin, *group.arrays, *more)


def query_back_kernel(dq_ref, w_ref, ww_ref, lora_grad_ref, back_ref, *, q_cols, mid):
    dq = dq_ref[...]
    lora_grad = mm_nt(dq, ww_ref[...]).astype(BF16)
    lora_grad_ref[...] = lora_grad
    back_ref[...] = (mm_nt(dq, w_ref[:, :q_cols])
                     + mm_nt(lora_grad, w_ref[:, q_cols : q_cols + mid]))


def query_back(dq, w, ww, later=()):
    rows, q_cols = dq.shape
    mid, width = ww.shape[0], w.shape[0]
    tile = math.gcd(rows, 256)
    return pl.pallas_call(
        skipping(functools.partial(query_back_kernel, q_cols=q_cols, mid=mid), 3, len(later)),
        grid=(rows // tile,),
        in_specs=[rows_of(tile, q_cols), full(w.shape), full(ww.shape)] + [ANY] * len(later),
        out_specs=[rows_of(tile, mid), rows_of(tile, width)],
        out_shape=[like((rows, mid), BF16), like((rows, width), F32)],
        compiler_params=params(),
        cost_estimate=cost(2 * rows * (width * (q_cols + mid) + mid * q_cols), 9e6),
        name="query_back",
    )(dq, w, ww, *later)


def pair_back_kernel(*refs, head_dim, others):
    x_ref, gains_ref, cos_ref, sin_ref, w_ref, back_ref, mid_grad_ref, own_ref = refs[:8]
    pair_grad_ref, in_grad_ref, gain_grad_ref = refs[-3:]

    @pl.when(pl.program_id(0) == 0)
    def _():
        gain_grad_ref[...] = jnp.zeros_like(gain_grad_ref)

    half = head_dim // 2
    gain = gains_ref[0:1, :]
    cos, sin = cos_ref[...], sin_ref[...]
    dkv = own_ref[...]
    for ref in refs[8 : 8 + others]:
        dkv = dkv + ref[...].astype(F32)
    a, b = dkv[:, :half], dkv[:, half:head_dim]
    pair_grad_ref[:, :half] = (a * cos + b * sin).astype(BF16)
    pair_grad_ref[:, half:head_dim] = (b * cos - a * sin).astype(BF16)
    pair_grad_ref[:, head_dim:] = dkv[:, head_dim:].astype(BF16)
    back = back_ref[...] + mm_nt(pair_grad_ref[...], w_ref[:, : 2 * head_dim])
    x = x_ref[...].astype(F32)
    inv = lax.rsqrt(jnp.mean(x * x, axis=-1, keepdims=True) + EPSILON)
    unit = x * inv
    gain_grad_ref[...] += jnp.sum(unit * back, axis=0, keepdims=True)
    scaled = back * gain
    in_grad_ref[...] = mid_grad_ref[...] + inv * (
        scaled - unit * jnp.mean(unit * scaled, axis=-1, keepdims=True)
    )


def pair_back(x, gains, cos, sin, w, own, others, back, mid_grad, head_dim, m, batches, before=None,
              later=()):
    width = x.shape[1]
    rows = x.shape[0] // batches
    tile = math.gcd(rows, 256)
    half, cols = head_dim // 2, 2 * head_dim
    count = rows // tile

    def here(n):
        return pl.BlockSpec((tile, n), lambda i: (m * count + i, 0))

    more = ([] if before is None else [before]) + list(later)
    return pl.pallas_call(
        functools.partial(pair_back_kernel, head_dim=head_dim, others=len(others)),
        grid=(count,),
        in_specs=[here(width), full(gains.shape), here(half), here(half), full(w.shape),
                  here(width), here(width)] + [rows_of(tile, cols)] * (1 + len(others))
        + [ANY] * len(more),
        out_specs=[rows_of(tile, cols), here(width), full((1, width))],
        out_shape=[like((rows, cols), BF16), like(x.shape, F32), like((1, width), F32)],
        input_output_aliases={} if before is None else {8 + len(others): 1},
        compiler_params=params(),
        cost_estimate=cost(2 * rows * width * cols, 7e6),
        name="pair_back",
    )(x, gains, cos, sin, w, back, mid_grad, own, *others, *more)


def weight_grad_kernel(x_ref, y_ref, out_ref, xt_ref):
    @pl.when(pl.program_id(0) == 0)
    def _():
        xt_ref[...] = x_ref[...].T

    out_ref[...] = mm(xt_ref[...], y_ref[...]).astype(BF16)


def weight_grad(x, y, tile=256, later=()):
    rows, width = x.shape
    cols = y.shape[1]
    tile = math.gcd(cols, tile)
    return pl.pallas_call(
        skipping(weight_grad_kernel, 2, len(later)),
        grid=(cols // tile,),
        in_specs=[full(x.shape), pl.BlockSpec((rows, tile), lambda i: (0, i))] + [ANY] * len(later),
        out_specs=pl.BlockSpec((width, tile), lambda i: (0, i)),
        out_shape=like((width, cols), BF16),
        scratch_shapes=[pltpu.VMEM((width, rows), BF16)],
        compiler_params=params(),
        cost_estimate=took(10.3),
        name="weight_grad",
    )(x, y, *later)


def turn(x_ref, flat_ref, xt_ref, me, parts):
    flat_ref[...] = x_ref[...].T
    piece = flat_ref.shape[0] // parts
    for r in range(parts):
        at = pl.multiple_of((me ^ r) * piece, piece)
        to = (r % 2) * (parts // 2) + r // 2
        xt_ref[to * piece : (to + 1) * piece, :] = flat_ref[pl.ds(at, piece), :]


def column_grads_kernel(where, g_in, hidden_in, b_in, attn_in, keep_ref, send_ref, g_ref, hidden_ref,
                        b_ref, attn_ref, sem, *, parts):
    f = Fetch([(g_in, g_ref), (hidden_in, hidden_ref), (b_in, b_ref), (attn_in, attn_ref)], sem)
    span, _, piece, _ = keep_ref.shape
    per = parts // span
    col = 0
    for pair, x_ref, y_ref in (((0, 1), g_ref, hidden_ref), ((2, 3), b_ref, attn_ref)):
        n = y_ref.shape[1] // parts
        f.wait(pair[0])
        turned = x_ref[...].T
        f.wait(pair[1])
        for r in range(parts):
            at = pl.multiple_of((where[0] ^ r) * n, n)
            out = mm(turned, y_ref[:, pl.ds(at, n)]).astype(BF16)
            ref = send_ref if r % 2 else keep_ref
            for s in range(span):
                for i in range(per):
                    ref[s ^ where[1], r // 2, :, col + i * n : col + (i + 1) * n] = out[
                        (s * per + i) * piece : (s * per + i + 1) * piece]
        col += per * n


def column_grads(where, grad, hidden, branch, attn, parts, span):
    rows, width = grad.shape
    piece = width // parts
    cols = (hidden.shape[1] + attn.shape[1]) // span
    shape = like((span, parts // 2, piece, cols), BF16)
    arrays = (grad, hidden, branch, attn)
    return pl.pallas_call(
        functools.partial(column_grads_kernel, parts=parts),
        in_specs=[SMEM] + [ANY] * 4,
        out_specs=[VMEM] * 2,
        out_shape=[shape, shape],
        scratch_shapes=[pltpu.VMEM(a.shape, BF16) for a in arrays]
        + [pltpu.SemaphoreType.DMA((4,))],
        compiler_params=params(),
        cost_estimate=took(9),
        name="column_grads",
    )(where, *arrays)


class Fetch:
    def __init__(self, pairs, sem):
        self.copies = [pltpu.make_async_copy(a, b, sem.at[i]) for i, (a, b) in enumerate(pairs)]
        for c in self.copies:
            c.start()

    def wait(self, *which):
        for i in which:
            self.copies[i].wait()


def unrotate(dkv, cos, sin, head_dim):
    half = head_dim // 2
    a, b = dkv[:, :half], dkv[:, half:head_dim]
    return jnp.concatenate([a * cos + b * sin, b * cos - a * sin, dkv[:, head_dim:]],
                           axis=1).astype(BF16)


def norm_back(x, gain, back, rest):
    inv = lax.rsqrt(jnp.mean(x * x, axis=-1, keepdims=True) + EPSILON)
    unit = x * inv
    scaled = back * gain
    return (rest + inv * (scaled - unit * jnp.mean(unit * scaled, axis=-1, keepdims=True)),
            jnp.sum(unit * back, axis=0, keepdims=True))


def fold_rows(out_ref, value, first, parts, piece, fold, j):
    count = value.shape[0] // parts
    for d in range(parts):
        at = d * piece + j * count
        out_ref[at : at + count, first : first + fold] = value[d * count : (d + 1) * count]


def query_side_kernel(dq_in, ww_in, normed_in, lora_in, queries_ref, lora_grad_ref, dq, ww, normed,
                      lora, sem, *, parts, fold):
    f = Fetch([(dq_in, dq), (ww_in, ww), (normed_in, normed), (lora_in, lora)], sem)
    q_cols, mid = dq.shape[1], lora.shape[1]
    f.wait(0, 1)
    lora_grad = mm_nt(dq[...], ww[...]).astype(BF16)
    lora_grad_ref[...] = lora_grad
    f.wait(2, 3)
    step = math.gcd(q_cols, 512)
    turned = normed[...].T
    for c in range(0, q_cols, step):
        queries_ref[:, c : c + step] = mm(turned, dq[:, c : c + step]).astype(BF16)
    queries_ref[:, q_cols : q_cols + mid] = mm(turned, lora_grad).astype(BF16)
    piece, count = normed.shape[1] // parts, mid // parts
    turned = lora[...].T
    for j in range(q_cols // fold):
        out = mm(turned, dq[:, j * fold : (j + 1) * fold]).astype(BF16)
        fold_rows(queries_ref, out, q_cols + mid, parts, piece, fold, j)
    rest = (q_cols // fold) * count
    for d in range(parts):
        queries_ref[d * piece + rest : (d + 1) * piece, q_cols + mid :] = jnp.zeros(
            (piece - rest, fold), BF16)


def query_side(dq, ww, normed, lora_mid, parts, fold, later):
    total, q_cols = dq.shape
    width, mid = normed.shape[1], lora_mid.shape[1]
    arrays = (dq, ww, normed, lora_mid)
    return pl.pallas_call(
        skipping(functools.partial(query_side_kernel, parts=parts, fold=fold), 4, len(later)),
        in_specs=[ANY] * (4 + len(later)),
        out_specs=[VMEM] * 2,
        out_shape=[like((width, q_cols + mid + fold), BF16), like((total, mid), BF16)],
        scratch_shapes=[pltpu.VMEM(a.shape, BF16) for a in arrays]
        + [pltpu.SemaphoreType.DMA((4,))],
        compiler_params=params(),
        cost_estimate=cost(LONG, 1),
        name="query_side",
    )(*arrays, *later)


def first_side_kernel(*refs, head_dim, others):
    (dq_in, w_in, lora_in, own_in, wp_in, x_in, mg_in, gains_ref, cos_ref, sin_ref, keep_ref,
     got_ref) = refs[:12]
    others_in = refs[12 : 12 + others]
    (back_ref, pair_ref, in_grad_ref, one_ref, near_ref, far_ref,
     dq, w, lora, own, wp, x, mg, there, hold, sem) = refs[12 + others :]
    rows = x.shape[0]
    f = Fetch([(dq_in, dq), (w_in, w), (lora_in, lora), (own_in, own), (wp_in, wp),
               (x_in.at[pl.ds(0, rows)], x), (mg_in.at[pl.ds(0, rows)], mg)]
              + [(r, there.at[i]) for i, r in enumerate(others_in)], sem)
    near_ref[...] = (keep_ref[0].astype(F32) + got_ref[0].astype(F32)).astype(BF16)
    far_ref[...] = (keep_ref[1].astype(F32) + got_ref[1].astype(F32)).astype(BF16)
    q_cols, mid = dq.shape[1], lora.shape[1]
    f.wait(0, 1, 2)
    for m in range(dq.shape[0] // rows):
        at = slice(m * rows, (m + 1) * rows)
        back = mm_nt(dq[at, :], w[:, :q_cols]) + mm_nt(lora[at, :], w[:, q_cols : q_cols + mid])
        if m == 0:
            hold[...] = back
        else:
            back_ref[(m - 1) * rows : m * rows] = back
    f.wait(*range(3, 7 + others))
    dkv = own[...]
    for i in range(others):
        dkv = dkv + there[i].astype(F32)
    pair = unrotate(dkv, cos_ref[...], sin_ref[...], head_dim)
    pair_ref[...] = pair
    back = hold[...] + mm_nt(pair, wp[:, : 2 * head_dim])
    in_grad_ref[...], one_ref[...] = norm_back(x[...].astype(F32), gains_ref[0:1, :], back, mg[...])


def first_side(dq, w, lora_grad, own, others, w_pair, x, mid_grad, gains, cos, sin, keep, got,
               head_dim, batches, later):
    total = dq.shape[0]
    rows = total // batches
    width, mid = x.shape[1], lora_grad.shape[1]
    half, cols = head_dim // 2, 2 * head_dim
    angle = pl.BlockSpec((rows, half), lambda i: (0, 0))
    n = len(others)
    return pl.pallas_call(
        skipping(functools.partial(first_side_kernel, head_dim=head_dim, others=n), 12 + n,
                 len(later)),
        grid=(1,),
        in_specs=[ANY] * 7 + [VMEM, angle, angle, VMEM, VMEM] + [ANY] * (n + len(later)),
        out_specs=[VMEM] * 2 + [pl.BlockSpec((rows, width), lambda i: (0, 0))] + [VMEM] * 3,
        out_shape=[like((total - rows, width), F32), like((rows, cols), BF16),
                   like((total, width), F32), like((1, width), F32)]
        + [like(keep.shape[1:], BF16)] * 2,
        scratch_shapes=[pltpu.VMEM(dq.shape, BF16), pltpu.VMEM(w.shape, BF16),
                        pltpu.VMEM(lora_grad.shape, BF16), pltpu.VMEM((rows, cols), F32),
                        pltpu.VMEM(w_pair.shape, BF16), pltpu.VMEM((rows, width), BF16),
                        pltpu.VMEM((rows, width), F32), pltpu.VMEM((n, rows, cols), BF16),
                        pltpu.VMEM((rows, width), F32), pltpu.SemaphoreType.DMA((7 + n,))],
        compiler_params=params(),
        cost_estimate=cost(1, 1),
        name="first_side",
    )(dq, w, lora_grad, own, w_pair, x, mid_grad, gains, cos, sin, keep, got, *others, *later)


def pair_side_kernel(*refs, head_dim, parts, others):
    (where, own_in, wp_in, back_in, x_in, mg_in, normed_in, first_in, gains_ref, cos_ref, sin_ref,
     one_ref, two_ref) = refs[:13]
    others_in = refs[13 : 13 + others]
    outs = refs[14 + others :]
    in_grad_ref, send_ref = outs[:2]
    keeps = outs[2 : 2 + parts // 2]
    (own, wp, back, x, mg, normed, pair_ref, there, flat_ref, xt_ref, gain_ref,
     sem) = outs[2 + parts // 2 :]
    rows = x.shape[0]
    f = Fetch([(normed_in, normed), (own_in, own)]
              + [(r, there.at[i]) for i, r in enumerate(others_in)]
              + [(first_in, pair_ref.at[pl.ds(0, rows)]), (wp_in, wp), (back_in, back),
                 (x_in.at[pl.ds(rows, rows)], x), (mg_in.at[pl.ds(rows, rows)], mg)], sem)
    f.wait(0)
    turn(normed, flat_ref, xt_ref, where[0], parts)
    f.wait(*range(1, 2 + others))
    dkv = own[...]
    for i in range(others):
        dkv = dkv + there[i].astype(F32)
    pair = unrotate(dkv, cos_ref[...], sin_ref[...], head_dim)
    pair_ref[rows:, :] = pair
    f.wait(*range(2 + others, 7 + others))
    grads = back[...] + mm_nt(pair, wp[:, : 2 * head_dim])
    in_grad_ref[...], one = norm_back(x[...].astype(F32), gains_ref[0:1, :], grads, mg[...])
    width = flat_ref.shape[0]
    piece, half, cols = width // parts, parts // 2, 2 * head_dim
    out = mm(xt_ref[...], pair_ref[...]).astype(BF16)
    pad = jnp.zeros((126, width), F32)
    gain_ref[...] = jnp.concatenate([one + one_ref[...], two_ref[...], pad], axis=0).T.astype(BF16)
    for k in range(half):
        keeps[k][:, :cols] = out[k * piece : (k + 1) * piece]
        send_ref[k, :, :cols] = out[(half + k) * piece : (half + k + 1) * piece]
        at = pl.multiple_of((where[0] ^ (2 * k)) * piece, piece)
        keeps[k][:, cols:] = gain_ref[pl.ds(at, piece), :]
        at = pl.multiple_of((where[0] ^ (2 * k + 1)) * piece, piece)
        send_ref[k, :, cols:] = gain_ref[pl.ds(at, piece), :]


def pair_side(where, own, others, w_pair, back, x, mid_grad, normed, first, gains, cos, sin, one,
              two, in_grad, head_dim, parts):
    total, width = normed.shape
    rows = total // 2
    half, cols = head_dim // 2, 2 * head_dim
    piece = width // parts
    angle = pl.BlockSpec((rows, half), lambda i: (1, 0))
    n = len(others)
    return pl.pallas_call(
        functools.partial(pair_side_kernel, head_dim=head_dim, parts=parts, others=n),
        grid=(1,),
        in_specs=[SMEM] + [ANY] * 7 + [VMEM, angle, angle, VMEM, VMEM] + [ANY] * (n + 1),
        out_specs=[pl.BlockSpec((rows, width), lambda i: (1, 0))] + [VMEM] * (1 + parts // 2),
        out_shape=[like((total, width), F32), like((parts // 2, piece, cols + 128), BF16)]
        + [like((piece, cols + 128), BF16)] * (parts // 2),
        scratch_shapes=[pltpu.VMEM((rows, cols), F32), pltpu.VMEM(w_pair.shape, BF16),
                        pltpu.VMEM((rows, width), F32), pltpu.VMEM((rows, width), BF16),
                        pltpu.VMEM((rows, width), F32), pltpu.VMEM(normed.shape, BF16),
                        pltpu.VMEM((total, cols), BF16), pltpu.VMEM((n, rows, cols), BF16),
                        pltpu.VMEM((width, total), BF16), pltpu.VMEM((width, total), BF16),
                        pltpu.VMEM((width, 128), BF16), pltpu.SemaphoreType.DMA((7 + n,))],
        input_output_aliases={13 + n: 0},
        compiler_params=params(),
        cost_estimate=cost(LONG, 12e6),
        name="pair_side",
    )(where, own, w_pair, back, x, mid_grad, normed, first, gains, cos, sin, one, two, *others,
      in_grad)


def join_kernel(left_ref, *refs):
    out_ref = refs[-1]
    n = left_ref.shape[1]
    out_ref[:, :n] = left_ref[...]
    out_ref[:, n:] = tree([r[...].astype(F32) for r in refs[:-1]]).astype(BF16)


def join(left, parts, later=()):
    rows, n = left.shape
    count = 1 + len(parts)
    return pl.pallas_call(
        skipping(join_kernel, count, len(later)),
        in_specs=[VMEM] * count + [ANY] * len(later),
        out_specs=VMEM,
        out_shape=like((rows, n + parts[0].shape[1]), BF16),
        compiler_params=params(),
        cost_estimate=took(2),
        name="join",
    )(left, *parts, *later)


def finish_kernel(*refs, mid, q_cols, cols, fold):
    parts, outs = refs[:-6], refs[-6:]
    query_ref, narrow_ref, widen_ref, kv_ref, one_ref, two_ref = outs
    total = tree([p[...].astype(F32) for p in parts])
    query_ref[...] = total[:, :q_cols]
    narrow_ref[...] = total[:, q_cols : q_cols + mid]
    first = q_cols + mid
    count = widen_ref.shape[0]
    for j in range(q_cols // fold):
        widen_ref[:, j * fold : (j + 1) * fold] = total[j * count : (j + 1) * count,
                                                        first : first + fold]
    first += fold
    kv_ref[...] = total[:, first : first + cols]
    gains = total[:, first + cols :].T
    one_ref[...] = gains[0:1]
    two_ref[...] = gains[1:2]


def finish(parts, q_cols, mid, count, cols, fold):
    piece = parts[0].shape[0]
    return pl.pallas_call(
        functools.partial(finish_kernel, q_cols=q_cols, mid=mid, cols=cols, fold=fold),
        in_specs=[VMEM] * len(parts),
        out_specs=[VMEM] * 6,
        out_shape=[like((piece, q_cols), F32), like((piece, mid), F32), like((count, q_cols), F32),
                   like((piece, cols), F32), like((1, piece), F32), like((1, piece), F32)],
        compiler_params=params(),
        cost_estimate=took(2.5),
        name="finish",
    )(*parts)


def swap_cores(keeps, send, later=()):
    got, count = swap(send, "fsdp", 1), len(keeps)
    return add([*keeps, got], [[(k, None), (count, k)] for k in range(count)], later)


def pairs_kernel(*refs):
    parts, (keep_ref, send_ref) = refs[:-2], refs[-2:]
    for i in range(2):
        for k, ref in ((2 * i, keep_ref), (2 * i + 1, send_ref)):
            ref[i] = tree([p[k].astype(F32) for p in parts]).astype(BF16)


def sum_pairs(parts, later=()):
    count, shape = len(parts), like((2,) + parts[0].shape[1:], BF16)
    return pl.pallas_call(
        skipping(pairs_kernel, count, len(later)),
        in_specs=[VMEM] * count + [ANY] * len(later),
        out_specs=[VMEM] * 2,
        out_shape=[shape] * 2,
        compiler_params=params(),
        cost_estimate=took(2.4),
        name="sum_pairs",
    )(*parts, *later)


def cut_kernel(where, x_ref, *outs):
    part = outs[0].shape[1]
    for s, out in enumerate(outs):
        at = pl.multiple_of((where[1] ^ s) * part, part)
        out[...] = x_ref[:, pl.ds(at, part)]


def cut_parts(where, x, later=()):
    span = lax.axis_size("seq")
    rows, part = x.shape[0], x.shape[1] // span
    cut = pl.pallas_call(
        skipping(cut_kernel, 2, len(later)),
        in_specs=[SMEM, VMEM] + [ANY] * len(later),
        out_specs=[VMEM] * span,
        out_shape=[like((rows, part), x.dtype)] * span,
        compiler_params=params(),
        cost_estimate=took(2),
        name="cut",
    )(where, x, *later)
    return cut


def halves_kernel(*refs):
    out_ref = refs[-1]
    n = refs[0].shape[1]
    out_ref[:, :n] = tree([r[...].astype(F32) for r in refs[:-3]]).astype(BF16)
    out_ref[:, n:] = tree([r[...].astype(F32) for r in refs[-3:-1]]).astype(BF16)


def halves(left, right, later=()):
    count = len(left) + 2
    shape = (left[0].shape[0], left[0].shape[1] + right[0].shape[1])
    return pl.pallas_call(
        skipping(halves_kernel, count, len(later)),
        in_specs=[VMEM] * count + [ANY] * len(later),
        out_specs=VMEM,
        out_shape=like(shape, BF16),
        compiler_params=params(),
        cost_estimate=cost(LONG, 2e6),
        name="halves",
    )(*left, *right, *later)


def lay_kernel(where, *refs, n, k):
    parts = refs[:-6]
    span = len(parts)
    gate_ref, up_ref, down_ref, out_ref, tall_ref, tall2_ref = refs[-6:]
    piece = parts[0].shape[0]
    half = span // 2
    wide = gate_ref.shape[1] // half
    per = (parts[0].shape[1] - wide) // (n + k)
    for s, ref in enumerate(parts):
        q = where[1] ^ s
        for i, out in enumerate((gate_ref, up_ref)):
            @pl.when(q // half == i)
            def _():
                at = pl.multiple_of((q % half) * wide, wide)
                out[:, pl.ds(at, wide)] = ref[:, :wide].astype(F32)
        for i in range(per):
            at = pl.ds(pl.multiple_of((q * per + i) * piece, piece), piece)
            first = wide + i * n
            tall_ref[at, :] = ref[:, first : first + n].astype(F32)
            first = wide + per * n + i * k
            tall2_ref[at, :] = ref[:, first : first + k].astype(F32)
    down_ref[...] = tall_ref[...].T
    out_ref[...] = tall2_ref[...].T


def lay(where, parts, hidden, n, k, later=()):
    piece = parts[0].shape[0]
    width = piece * lax.axis_size("fsdp")
    return pl.pallas_call(
        skipping(functools.partial(lay_kernel, n=n, k=k), 1 + len(parts), len(later)),
        in_specs=[SMEM] + [VMEM] * len(parts) + [ANY] * len(later),
        out_specs=[VMEM] * 4,
        out_shape=[like((piece, hidden), F32)] * 2 + [like((n, width), F32), like((k, width), F32)],
        scratch_shapes=[pltpu.VMEM((width, n), F32), pltpu.VMEM((width, k), F32)],
        compiler_params=params(),
        cost_estimate=took(3),
        name="lay",
    )(where, *parts, *later)


def begin_of(index, lengths):
    ends = [lengths[0]]
    for n in lengths[1:]:
        ends.append(ends[-1] + n)
    begin = index
    for d in reversed(range(len(lengths))):
        begin = jnp.where(index < ends[d], ends[d] - lengths[d], begin)
    return begin


def local(tokens, document_lengths, cotangent, attention_gain, query_projection, narrowing_factor,
          widening_factor, key_value_projection, output_projection, feedforward_gain,
          gate_projection, up_projection, down_projection):
    batches, _, rows, width = tokens.shape
    head_dim = key_value_projection.shape[1] // 2
    q_cols = query_projection.shape[1]
    mid = narrowing_factor.shape[1]
    hidden = gate_projection.shape[1]
    kv_cols = 2 * head_dim
    scale = head_dim ** (-0.5)
    parts, span = lax.axis_size("fsdp"), lax.axis_size("seq")
    place = lax.axis_index("seq")
    tile = block = math.gcd(rows, 512)
    where = jnp.stack([lax.axis_index("fsdp"), place]).astype(jnp.int32)
    piece = width // parts
    direct = piece % 16 == 0
    fold = 512
    folds = q_cols // fold

    lengths = document_lengths[:, 0]
    half = head_dim // 2
    index = place * rows + lax.broadcasted_iota(jnp.int32, (batches, rows, half), 1)
    begin = begin_of(index, [lengths[:, d][:, None, None] for d in range(lengths.shape[1])])
    freqs = THETA ** (-(lax.broadcasted_iota(jnp.int32, (1, half), 1).astype(F32) * 2.0 / head_dim))
    angles = ((index - begin).astype(F32) * freqs).reshape(batches * rows, half)
    cos, sin = jnp.cos(angles), jnp.sin(angles)

    if direct:
        first = Shards(pack_pair(key_value_projection, attention_gain, feedforward_gain))
        third = pack(where, gate_projection, up_projection, down_projection, output_projection,
                     span, [cos, sin, first.arrays[2], first.arrays[parts - 2]])
        held = Tiled(third, 2 * hidden, down_projection, output_projection)
        weights = None
    else:
        def gather(x):
            return lax.all_gather(x, "fsdp", axis=0, tiled=True)

        first = jnp.concatenate(
            [key_value_projection,
             jnp.pad(jnp.stack([attention_gain, feedforward_gain], axis=1), ((0, 0), (0, 126)))],
            axis=1)
        turned = jnp.concatenate(
            [widening_factor[:, j * fold : (j + 1) * fold] for j in range(folds)])
        turned = jnp.pad(turned, ((0, piece - turned.shape[0]), (0, 0)))
        second = jnp.concatenate([query_projection, narrowing_factor, turned], axis=1)
        first, second = Whole(gather(first)), Whole(gather(second))
        second.rows = piece
        held = None
        weights = [gather(jnp.concatenate([gate_projection, up_projection], axis=1)),
                   gather(down_projection), gather(output_projection)]

    x = tokens.reshape(batches * rows, width)
    grad = cotangent.reshape(batches * rows, width)
    normed, kv, w_pair, gains = project_kv(where, x, cos, sin, first, head_dim)
    kvs = Group(kv, batches)
    if direct:
        second = Shards(pack_query(query_projection, narrowing_factor, widening_factor, fold,
                                   [kv]), True)
    lora_mid, q, w_query, ww = project_q(where, normed, cos, sin, second, head_dim, q_cols, mid,
                                         scale, [])
    attended, lse = attend(where, lengths, q, kvs, head_dim, tile, block)
    (output, mid_grad, branch, attn_grad, delta, ffn_low, hidden_low, lift_grads,
     gain_two_grad) = middle_part(x, attended, grad, gains, held, weights, head_dim)

    if direct:
        keep, send = column_grads(where, grad, hidden_low, branch, attended, parts, span)
        got = swap(send, "fsdp", 1)
        lifts = weight_grad(ffn_low, lift_grads, 1024, [keep])
        lifts_sum = lax.psum_scatter(lifts, "fsdp", scatter_dimension=0, tiled=True)
        columns = add([keep, got], [[(0, s), (1, s)] for s in range(span)], [lifts])
        there = [columns[0]] + [swap(a, "seq", s) for s, a in enumerate(columns) if s > 0]
    dq, owns, others = None, [], []
    for m in range(batches):
        later = []
        if direct and m == 0:
            later = columns
        if direct and m == 1:
            keep, send = sum_pairs(there, [dq])
            got = swap(send, "fsdp", 2)
            later = [keep]
        dq, own, *sends = attend_back(where, lengths, lse, delta, q, attn_grad, kvs, cos, sin,
                                      head_dim, tile, block, scale, m, dq, later)
        owns.append(own)
        others.append([swap(a, "seq", s) for s, a in enumerate(sends, 1)])
    if direct:
        queries, lora_grad = query_side(dq, ww, normed, lora_mid, parts, fold, [])
        queries_sum = lax.psum_scatter(queries, "fsdp", scatter_dimension=0, tiled=True)
        back, pair, in_grad, one, near, far = first_side(
            dq, w_query, lora_grad, owns[0], others[0], w_pair, x, mid_grad, gains, cos, sin, keep,
            got, head_dim, batches, [queries, lifts_sum])
        in_grad, send, *keeps = pair_side(where, owns[1], others[1], w_pair, back, x, mid_grad,
                                          normed, pair, gains, cos, sin, one, gain_two_grad,
                                          in_grad, head_dim, parts)

        def share(x):
            return [x] + [swap(x, "seq", s) for s in range(1, span)]

        lifts_cut = cut_parts(where, lifts_sum, [pair])
        lifts_parts = [lifts_cut[0]] + [swap(lifts_cut[s], "seq", s) for s in range(1, span)]
        mine = halves(lifts_parts, [near, swap(far, "fsdp", 4)], [send])
        laid = share(mine)
        shards = swap_cores(keeps, send, [mine])
        mine = join(queries_sum, [shards[0]] + [
            swap(a, "fsdp", 2 * k) for k, a in enumerate(shards) if k > 0])
        last = share(mine)
        gate_grad, up_grad, down_grad, out_grad = lay(
            where, laid, hidden, hidden // parts, q_cols // parts, [mine])
        query_grad, narrow_grad, widen_grad, key_value_grad, one, two = finish(
            last, q_cols, mid, mid // parts, kv_cols, fold)
        gain_one_grad, gain_two_grad = one.reshape(piece), two.reshape(piece)
    else:
        lora_grad, back = query_back(dq, w_query, ww)
        in_grad, pairs, ones = None, [], []
        for m in range(batches):
            pair, in_grad, one = pair_back(x, gains, cos, sin, w_pair, owns[m], others[m], back,
                                           mid_grad, head_dim, m, batches, in_grad)
            pairs.append(pair)
            ones.append(one)

        def scatter(x):
            part = lax.psum_scatter(x.astype(BF16), "fsdp", scatter_dimension=0, tiled=True)
            return lax.psum(part, "seq").astype(F32)

        pair_grad = jnp.concatenate(pairs)
        gain_one_grad = sum(ones)
        down_grad = scatter(weight_grad(grad, hidden_low).T)
        out_grad = scatter(weight_grad(branch, attended).T)
        lift_w = scatter(weight_grad(ffn_low, lift_grads))
        gate_grad, up_grad = lift_w[:, :hidden], lift_w[:, hidden:]
        query_grad = scatter(weight_grad(normed, dq))
        narrow_grad = scatter(weight_grad(normed, lora_grad))
        widen_grad = scatter(weight_grad(lora_mid, dq))
        key_value_grad = scatter(weight_grad(normed, pair_grad))
        gains_grad = scatter(jnp.concatenate([gain_one_grad, gain_two_grad]).T)
        gain_one_grad, gain_two_grad = gains_grad[:, 0], gains_grad[:, 1]
    return (output.reshape(batches, 1, rows, width), in_grad.reshape(batches, 1, rows, width),
            gain_one_grad, query_grad, narrow_grad, widen_grad, key_value_grad, out_grad,
            gain_two_grad, gate_grad, up_grad, down_grad)


def solution(mesh):
    rows = P(None, "fsdp", "seq", None)
    vector, matrix = P("fsdp"), P("fsdp", None)
    in_specs = (rows, P(None, "fsdp", None), rows, vector) + (matrix,) * 5 + (vector,) + (matrix,) * 3
    out_specs = (rows, rows, vector) + (matrix,) * 5 + (vector,) + (matrix,) * 3
    return jax.shard_map(local, mesh=mesh, in_specs=in_specs, out_specs=out_specs, check_vma=False)
```

```python
import functools
import math

import jax
import jax.numpy as jnp
from jax import lax
from jax.experimental import pallas as pl
from jax.experimental.pallas import tpu as pltpu
from jax.sharding import PartitionSpec as P

EPSILON = 1e-06
THETA = 10000.0
F32 = jnp.float32
BF16 = jnp.bfloat16
GELU_C = math.sqrt(2.0 / math.pi)
GELU_A = 0.044715
LOWEST = -1e30
VMEM_LIMIT = 60 * 1024 * 1024
ANY = pl.BlockSpec(memory_space=pl.ANY)
VMEM = pl.BlockSpec(memory_space=pltpu.VMEM)
SMEM = pl.BlockSpec(memory_space=pltpu.SMEM)


def mm(left, right):
    return lax.dot_general(left, right, (((1,), (0,)), ((), ())), preferred_element_type=F32)


def mm_tn(left, right):
    return lax.dot_general(left, right, (((0,), (0,)), ((), ())), preferred_element_type=F32)


def mm_nt(left, right):
    return lax.dot_general(left, right, (((1,), (1,)), ((), ())), preferred_element_type=F32)


def full(shape):
    return pl.BlockSpec(shape, lambda i: (0,) * len(shape))


def rows_of(tile, cols):
    return pl.BlockSpec((tile, cols), lambda i: (i, 0))


def params(**more):
    return pltpu.CompilerParams(vmem_limit_bytes=VMEM_LIMIT, **more)


def cost(flops, bytes_accessed, transcendentals=0):
    return pl.CostEstimate(
        flops=int(flops), bytes_accessed=int(bytes_accessed), transcendentals=int(transcendentals)
    )


def took(us):
    return cost(us * 1.1e9, 1)


LONG = 10**12


def like(shape, dtype):
    return jax.ShapeDtypeStruct(tuple(shape), dtype)


def swap(x, axis, by):
    return lax.ppermute(x, axis, [(i, i ^ by) for i in range(lax.axis_size(axis))])


def exchange(arrays):
    got = {s: swap(arrays[s], "seq", s) for s in reversed(range(1, len(arrays)))}
    return [arrays[0]] + [got[s] for s in range(1, len(arrays))]


def skipping(kernel, first, count):
    return lambda *refs: kernel(*refs[:first], *refs[first + count :])


def tree(values):
    while len(values) > 1:
        values = [values[i] + values[i + 1] for i in range(0, len(values), 2)]
    return values[0]


class Fetch:
    def __init__(self, pairs, sem):
        self.copies = [pltpu.make_async_copy(a, b, sem.at[i]) for i, (a, b) in enumerate(pairs)]
        for c in self.copies:
            c.start()

    def wait(self, *which):
        for i in which:
            self.copies[i].wait()


def fetched(kernel, count):
    def run(*refs):
        held, sem = refs[-1 - count : -1], refs[-1]
        Fetch(list(zip(refs[:count], held)), sem).wait(*range(count))
        kernel(*held, *refs[count : -1 - count])

    return run


def room(arrays):
    return [pltpu.VMEM(a.shape, a.dtype) for a in arrays] + [
        pltpu.SemaphoreType.DMA((len(arrays),))]


def add_kernel(*refs, count, groups):
    for out, group in zip(refs[count:], groups):
        values = [refs[i][...] if k is None else refs[i][k] for i, k in group]
        out[...] = tree([v.astype(F32) for v in values]).astype(out.dtype)


def add(arrays, groups, later=()):
    shapes = [arrays[g[0][0]].shape if g[0][1] is None else arrays[g[0][0]].shape[1:]
              for g in groups]
    count = len(arrays)
    later = list(later)
    kernel = fetched(functools.partial(add_kernel, count=count, groups=groups), count)
    return list(pl.pallas_call(
        skipping(kernel, count, len(later)),
        in_specs=[ANY] * (count + len(later)),
        out_specs=[VMEM] * len(groups),
        out_shape=[like(s, BF16) for s in shapes],
        scratch_shapes=room(arrays),
        compiler_params=params(),
        cost_estimate=took(3.5),
        name="add",
    )(*arrays, *later))


class Whole:
    def __init__(self, array):
        self.arrays = [array]
        self.shape = array.shape
        self.count = 1

    def copies(self, where, refs, dst):
        return [(refs[0], dst)]


class Shards:
    def __init__(self, x, relay=False):
        parts = lax.axis_size("fsdp")
        got = {0: x}
        for r in range(2, parts, 2):
            low = r & -r
            near = relay and r != low
            got[r] = swap(got[r - low], "fsdp", low) if near else swap(x, "fsdp", r)
        for r in range(0, parts, 2):
            got[r + 1] = swap(got[r], "fsdp", 1)
        self.arrays = [got[r] for r in range(parts)]
        self.rows = x.shape[0]
        self.shape = (parts * x.shape[0], x.shape[1])
        self.count = parts

    def copies(self, where, refs, dst):
        out = []
        for r, ref in enumerate(refs):
            at = pl.multiple_of((where[0] ^ r) * self.rows, self.rows)
            out.append((ref, dst.at[pl.ds(at, self.rows), :]))
        return out


def pack_pair_kernel(kv_ref, one_ref, two_ref, out_ref):
    piece, kv_cols = kv_ref.shape
    out_ref[:, :kv_cols] = kv_ref[...]
    pad = jnp.zeros((126, piece), F32)
    gains = jnp.concatenate([one_ref[...].astype(F32), two_ref[...].astype(F32), pad], axis=0)
    out_ref[:, kv_cols:] = gains.T.astype(BF16)


def pack_pair(kv, one, two):
    piece = kv.shape[0]
    return pl.pallas_call(
        pack_pair_kernel,
        in_specs=[VMEM] * 3,
        out_specs=VMEM,
        out_shape=like((piece, kv.shape[1] + 128), BF16),
        compiler_params=params(),
        cost_estimate=took(1.6),
        name="pack_pair",
    )(kv, one.reshape(1, piece), two.reshape(1, piece))


def pack_kernel(where, gate_ref, up_ref, down_ref, out_ref, third_ref, *, span):
    piece = gate_ref.shape[0]
    hidden = gate_ref.shape[1]
    part = 2 * hidden // span
    for s in range(span):
        ref, at = (gate_ref, s * part) if s * part < hidden else (up_ref, s * part - hidden)

        @pl.when(where[1] == s)
        def _():
            third_ref[:, :part] = ref[:, at : at + part]

    col = part
    for ref in (down_ref, out_ref):
        n = ref.shape[0] // span
        for i in range(n // 16):
            row = pl.ds(pl.multiple_of(where[1] * n + 16 * i, 16), 16)
            for j in range(ref.shape[1] // 128):
                third_ref[16 * j : 16 * j + 16, col : col + 128] = ref[row, j * 128 : (j + 1) * 128]
            col += 128


def pack(where, gate, up, down, out, span, later):
    piece = gate.shape[0]
    third = (gate.shape[1] * 2 * piece + (down.shape[0] + out.shape[0]) * down.shape[1]) // span
    return pl.pallas_call(
        skipping(functools.partial(pack_kernel, span=span), 5, len(later)),
        in_specs=[SMEM] + [VMEM] * 4 + [ANY] * len(later),
        out_specs=VMEM,
        out_shape=like((piece, third // piece), BF16),
        compiler_params=params(),
        cost_estimate=took(2),
        name="pack",
    )(where, gate, up, down, out, *later)


def pack_query_kernel(q_ref, narrow_ref, widen_ref, out_ref, *, fold):
    q_cols, mid, count = q_ref.shape[1], narrow_ref.shape[1], widen_ref.shape[0]
    out_ref[:, :q_cols] = q_ref[...]
    out_ref[:, q_cols : q_cols + mid] = narrow_ref[...]
    folds = q_cols // fold
    for j in range(folds):
        out_ref[j * count : (j + 1) * count, q_cols + mid :] = widen_ref[
            :, j * fold : (j + 1) * fold]
    rest = out_ref.shape[0] - folds * count
    out_ref[folds * count :, q_cols + mid :] = jnp.zeros((rest, fold), BF16)


def pack_query(q, narrow, widen, fold, later):
    return pl.pallas_call(
        skipping(functools.partial(pack_query_kernel, fold=fold), 3, len(later)),
        in_specs=[VMEM] * 3 + [ANY] * len(later),
        out_specs=VMEM,
        out_shape=like((q.shape[0], q.shape[1] + narrow.shape[1] + fold), BF16),
        compiler_params=params(),
        cost_estimate=took(1.7),
        name="pack_query",
    )(q, narrow, widen, *later)


class Tiled:
    def __init__(self, packed, gate_up, *tall):
        parts, span = lax.axis_size("fsdp"), lax.axis_size("seq")
        piece = packed.shape[0]
        self.piece, self.part, self.parts, self.span = piece, gate_up // span, parts, span
        self.heights = [t.shape[0] // span for t in tall]
        self.up, self.across = sum(self.heights) // 16, tall[0].shape[1] // 128
        self.array = lax.all_gather(packed, ("seq", "fsdp"), axis=0, tiled=True)
        self.shape = (parts * piece, gate_up)
        self.shapes = [(parts * t.shape[0], t.shape[1]) for t in tall]
        self.scratch = (span, parts * piece, self.up * 128)

    def copies(self, ref, dst, rest):
        height = self.parts * self.piece
        rows = [pl.ds(s * height, height) for s in range(self.span)]
        return [(ref.at[at, pl.ds(self.part, self.up * 128)], rest.at[s])
                for s, at in enumerate(rows)] + [
            (ref.at[at, pl.ds(0, self.part)], dst.at[:, pl.ds(s * self.part, self.part)])
            for s, at in enumerate(rows)]

    def unfold(self, rest, dsts):
        starts, tops = [], 0
        for n in self.heights:
            starts.append(tops)
            tops += n // 16

        def shard(d, carry):
            for s in range(self.span):
                for n, first, dst in zip(self.heights, starts, dsts):
                    for i in range(n // 16):
                        at = pl.ds(pl.multiple_of(d * n * self.span + s * n + i * 16, 16), 16)
                        for j in range(self.across):
                            row = pl.ds(pl.multiple_of(d * self.piece + 16 * j, 16), 16)
                            col = (first + i) * 128
                            dst[at, j * 128 : (j + 1) * 128] = rest[s, row, col : col + 128]
            return carry

        lax.fori_loop(0, self.parts, shard, 0)


def carry_out(copies, sem):
    made = [pltpu.make_async_copy(src, dst, sem.at[i]) for i, (src, dst) in enumerate(copies)]
    for c in made:
        c.start()
    for c in made:
        c.wait()


def normalize(x_ref, gains_ref):
    x = x_ref[...].astype(F32)
    inv = lax.rsqrt(jnp.mean(x * x, axis=-1, keepdims=True) + EPSILON)
    return (x * inv * gains_ref[0:1, :]).astype(BF16)


def put_pair(kv_ref, pair, cos, sin, head_dim):
    half = head_dim // 2
    a, b = pair[:, :half], pair[:, half:head_dim]
    kv_ref[:, :half] = (a * cos - b * sin).astype(BF16)
    kv_ref[:, half:head_dim] = (b * cos + a * sin).astype(BF16)
    kv_ref[:, head_dim:] = pair[:, head_dim:].astype(BF16)


def project_kv_kernel(*refs, held, head_dim):
    where, x_ref, cos_ref, sin_ref = refs[:4]
    pieces = refs[4 : 4 + len(held.arrays)]
    normed_ref, kv_ref, w_ref, gains_ref, sem = refs[4 + len(held.arrays) :]
    kv_cols = 2 * head_dim

    @pl.when(pl.program_id(0) == 0)
    def _():
        carry_out(held.copies(where, pieces, w_ref), sem)
        gains_ref[...] = w_ref[:, kv_cols:].astype(F32).T[:8]

    normed = normalize(x_ref, gains_ref)
    normed_ref[...] = normed
    put_pair(kv_ref, mm(normed, w_ref[:, :kv_cols]), cos_ref[...], sin_ref[...], head_dim)


def project_kv(where, x, cos, sin, held, head_dim):
    rows, width = x.shape
    tile = math.gcd(rows, 512)
    half = head_dim // 2
    return pl.pallas_call(
        functools.partial(project_kv_kernel, held=held, head_dim=head_dim),
        grid=(rows // tile,),
        in_specs=[SMEM, rows_of(tile, width), rows_of(tile, half), rows_of(tile, half)]
        + [ANY] * len(held.arrays),
        out_specs=[rows_of(tile, width), rows_of(tile, 2 * head_dim), full(held.shape),
                   full((8, width))],
        out_shape=[like((rows, width), BF16), like((rows, 2 * head_dim), BF16),
                   like(held.shape, BF16), like((8, width), F32)],
        scratch_shapes=[pltpu.SemaphoreType.DMA((held.count,))],
        compiler_params=params(),
        cost_estimate=took(5),
        name="project_kv",
    )(where, x, cos, sin, *held.arrays)


def project_q_kernel(*refs, held, head_dim, q_cols, mid, scale):
    where, normed_ref, cos_ref, sin_ref = refs[:4]
    pieces = refs[4 : 4 + len(held.arrays)]
    lora_ref, q_ref, w_ref, ww_ref, sem = refs[4 + len(held.arrays) :]
    half = head_dim // 2
    fold = held.shape[1] - q_cols - mid
    parts = q_cols // fold

    @pl.when(pl.program_id(0) == 0)
    def _():
        carry_out(held.copies(where, pieces, w_ref), sem)
        shards = held.shape[0] // held.rows
        count = mid // shards
        for d in range(shards):
            for j in range(parts):
                ww_ref[d * count : (d + 1) * count, j * fold : (j + 1) * fold] = w_ref[
                    d * held.rows + j * count : d * held.rows + (j + 1) * count, q_cols + mid :]

    normed = normed_ref[...]
    cos, sin = cos_ref[...], sin_ref[...]
    low = mm(normed, w_ref[:, q_cols : q_cols + mid]).astype(BF16)
    lora_ref[...] = low
    query = mm(normed, w_ref[:, :q_cols]) + mm(low, ww_ref[...])
    for h in range(q_cols // head_dim):
        c = h * head_dim
        a, b = query[:, c : c + half], query[:, c + half : c + head_dim]
        q_ref[:, c : c + half] = ((a * cos - b * sin) * scale).astype(BF16)
        q_ref[:, c + half : c + head_dim] = ((b * cos + a * sin) * scale).astype(BF16)


def project_q(where, normed, cos, sin, held, head_dim, q_cols, mid, scale, later):
    rows, width = normed.shape
    tile = math.gcd(rows, 256)
    half = head_dim // 2
    count = 4 + len(held.arrays)
    return pl.pallas_call(
        skipping(functools.partial(project_q_kernel, held=held, head_dim=head_dim, q_cols=q_cols,
                                   mid=mid, scale=scale), count, len(later)),
        grid=(rows // tile,),
        in_specs=[SMEM, rows_of(tile, width), rows_of(tile, half), rows_of(tile, half)]
        + [ANY] * (len(held.arrays) + len(later)),
        out_specs=[rows_of(tile, mid), rows_of(tile, q_cols), full(held.shape),
                   full((mid, q_cols))],
        out_shape=[like((rows, mid), BF16), like((rows, q_cols), BF16), like(held.shape, BF16),
                   like((mid, q_cols), BF16)],
        scratch_shapes=[pltpu.SemaphoreType.DMA((held.count,))],
        compiler_params=params(),
        cost_estimate=cost(1, 1),
        name="project_q",
    )(where, normed, cos, sin, *held.arrays, *later)


class Group:
    def __init__(self, kv, batches):
        self.rows = kv.shape[0] // batches
        span = lax.axis_size("seq")
        self.span = span
        self.relay = span == 4 and batches == 2
        if self.relay:
            one, two = swap(kv, "seq", 1), swap(kv, "seq", 2)
            self.arrays = [kv, one, two, swap(one[: self.rows], "seq", 2),
                           swap(two[self.rows :], "seq", 1)]
        else:
            self.arrays = [kv] + [swap(kv, "seq", s) for s in range(1, span)]

    def at(self, n, s):
        return (3 + n, 0) if self.relay and s == 3 else (s, n * self.rows)

    def copy(self, refs, n, s, place, dst, sem):
        i, row = self.at(n, s)
        to = pl.multiple_of((place ^ s) * self.rows, self.rows)
        return pltpu.make_async_copy(refs[i].at[pl.ds(row, self.rows)],
                                     dst.at[pl.ds(to, self.rows), :], sem)


def attend_kernel(*refs, group, head_dim, tile, block):
    where, lengths_ref, q_ref = refs[:3]
    kvs = refs[3 : 3 + len(group.arrays)]
    span = group.span
    o_ref, lse_ref, kv_ref, vt_ref, acc_ref, sem = refs[-6:]
    heads = q_ref.shape[1] // head_dim
    rows = q_ref.shape[0]
    m = pl.program_id(0)
    place = where[1]
    base = place * rows
    lengths = [lengths_ref[m, d] for d in range(lengths_ref.shape[1])]

    def first(t):
        return lax.div(begin_of(base + t * tile, lengths), block)

    def copy(n, s):
        return group.copy(kvs, n, s, place, kv_ref.at[n], sem.at[n, s])

    @pl.when(m == 0)
    def _():
        for n in range(kv_ref.shape[0]):
            for s in range(span):
                pl.when((place ^ s) <= place)(lambda n=n, s=s: copy(n, s).start())

    for n in range(kv_ref.shape[0]):
        for s in range(span):
            pl.when((m == n) & ((place ^ s) <= place))(lambda n=n, s=s: copy(n, s).wait())

    def flip(kb, carry):
        at = pl.ds(pl.multiple_of(kb * block, block), block)
        vt_ref[:, at] = kv_ref[m, at, head_dim:].T
        return carry

    lax.fori_loop(first(0), lax.div(base + rows + block - 1, block), flip, 0)
    for t in range(rows // tile):
        q_rows = slice(t * tile, (t + 1) * tile)
        high = base + t * tile + lax.broadcasted_iota(jnp.int32, (1, tile), 1)
        low = begin_of(high, lengths)
        acc_ref[...] = jnp.zeros_like(acc_ref)

        def visit(kb, carry):
            at = pl.ds(pl.multiple_of(kb * block, block), block)
            keys = kv_ref[m, at, :head_dim]
            vt = vt_ref[:, at]
            index = kb * block + lax.broadcasted_iota(jnp.int32, (block, tile), 0)
            mask = (index >= low) & (index <= high)
            out = []
            for h in range(heads):
                peak, total = carry[h]
                s = mm_nt(keys, q_ref[q_rows, h * head_dim : (h + 1) * head_dim])
                s = jnp.where(mask, s, -jnp.inf)
                new_peak = jnp.maximum(peak, jnp.max(s, axis=0, keepdims=True))
                factor = jnp.exp(peak - new_peak)
                p = jnp.exp(s - new_peak)
                total = total * factor + jnp.sum(p, axis=0, keepdims=True)
                acc_ref[h] = acc_ref[h] * factor + mm(vt, p.astype(BF16))
                out.append((new_peak, total))
            return tuple(out)

        start = tuple(
            (jnp.full((1, tile), LOWEST, F32), jnp.zeros((1, tile), F32)) for _ in range(heads)
        )
        stats = lax.fori_loop(first(t), lax.div(base + (t + 1) * tile + block - 1, block), visit,
                              start)
        for h in range(heads):
            peak, total = stats[h]
            o_ref[q_rows, h * head_dim : (h + 1) * head_dim] = (acc_ref[h] / total).T.astype(BF16)
            lse_ref[0, h : h + 1, q_rows] = peak + jnp.log(total)


def attend(where, lengths, q, group, head_dim, tile, block):
    total, q_cols = q.shape
    batches = lengths.shape[0]
    rows = total // batches
    heads = q_cols // head_dim
    span = group.span
    return pl.pallas_call(
        functools.partial(attend_kernel, group=group, head_dim=head_dim, tile=tile, block=block),
        grid=(batches,),
        in_specs=[SMEM, SMEM, rows_of(rows, q_cols)] + [ANY] * len(group.arrays),
        out_specs=[rows_of(rows, q_cols), pl.BlockSpec((1, heads, rows), lambda i: (i, 0, 0))],
        out_shape=[like(q.shape, BF16), like((batches, heads, rows), F32)],
        scratch_shapes=[pltpu.VMEM((batches, span * rows, 2 * head_dim), BF16),
                        pltpu.VMEM((head_dim, span * rows), BF16),
                        pltpu.VMEM((heads, head_dim, tile), F32),
                        pltpu.SemaphoreType.DMA((batches, span))],
        compiler_params=params(),
        cost_estimate=took(18),
        name="attend",
    )(where, lengths, q, *group.arrays)


def middle_kernel(*refs, held, head_dim, chunk):
    x_ref, attn_ref, g_ref, gains_ref = refs[:4]
    if held is None:
        w_ref, wd_ref, wo_ref = refs[4:7]
    else:
        w_ref, wd_ref, wo_ref, rest_ref, sem = refs[-5:]
    (out_ref, mid_grad_ref, branch_ref, attn_grad_ref, delta_ref, low_ref, hidden_ref, grads_ref,
     gain_grad_ref) = refs[5:14] if held is not None else refs[7:16]

    @pl.when(pl.program_id(0) == 0)
    def _():
        if held is not None:
            f = Fetch(held.copies(refs[4], w_ref, rest_ref), sem)
            f.wait(*range(held.span))
            held.unfold(rest_ref, [wd_ref, wo_ref])
            f.wait(*range(held.span, 2 * held.span))
        gain_grad_ref[...] = jnp.zeros_like(gain_grad_ref)

    gain = gains_ref[1:2, :]
    attn = attn_ref[...]
    middle = x_ref[...].astype(F32) + mm(attn, wo_ref[...])
    inv = lax.rsqrt(jnp.mean(middle * middle, axis=-1, keepdims=True) + EPSILON)
    unit = middle * inv
    low = (unit * gain).astype(BF16)
    low_ref[...] = low
    grad = g_ref[...]
    result = middle
    back = jnp.zeros_like(middle)
    wide = wd_ref.shape[0]
    for c in range(wide // chunk):
        at = slice(c * chunk, (c + 1) * chunk)
        to = slice(wide + c * chunk, wide + (c + 1) * chunk)
        gate = mm(low, w_ref[:, at])
        lift = mm(low, w_ref[:, to])
        square = gate * gate
        bend = jnp.tanh(GELU_C * gate * (1.0 + GELU_A * square))
        cdf = 0.5 * (1.0 + bend)
        gelu = gate * cdf
        hidden = (gelu * lift).astype(BF16)
        hidden_ref[:, at] = hidden
        result = result + mm(hidden, wd_ref[at, :])
        hidden_grad = mm_nt(grad, wd_ref[at, :])
        slope = cdf + (0.5 * GELU_C) * gate * (1.0 - bend * bend) * (1.0 + 3.0 * GELU_A * square)
        gate_grad = (hidden_grad * lift * slope).astype(BF16)
        lift_grad = (hidden_grad * gelu).astype(BF16)
        grads_ref[:, at] = gate_grad
        grads_ref[:, to] = lift_grad
        back = back + mm_nt(gate_grad, w_ref[:, at]) + mm_nt(lift_grad, w_ref[:, to])
    out_ref[...] = result.astype(BF16)
    gain_grad_ref[...] += jnp.sum(unit * back, axis=0, keepdims=True)
    scaled = back * gain
    mid_grad = grad.astype(F32) + inv * (
        scaled - unit * jnp.mean(unit * scaled, axis=-1, keepdims=True)
    )
    mid_grad_ref[...] = mid_grad
    branch = mid_grad.astype(BF16)
    branch_ref[...] = branch
    attn_grad = mm_nt(branch, wo_ref[...]).astype(BF16)
    attn_grad_ref[...] = attn_grad
    product = attn_grad.astype(F32) * attn.astype(F32)
    half = head_dim // 2
    for h in range(attn.shape[1] // head_dim):
        c = h * head_dim
        folded = product[:, c : c + half] + product[:, c + half : c + head_dim]
        delta_ref[h : h + 1, :] = jnp.sum(folded.T, axis=0, keepdims=True)


def middle_part(x, attn, grad, gains, held, weights, head_dim):
    rows, width = x.shape
    q_cols = attn.shape[1]
    hidden = (weights[0].shape if held is None else held.shape)[1] // 2
    heads = q_cols // head_dim
    tile = math.gcd(rows, 512)
    if held is None:
        more, specs, scratch = weights, [full(w.shape) for w in weights], []
    else:
        more, specs = [held.array], [ANY]
        scratch = [pltpu.VMEM(held.shape, BF16)] + [pltpu.VMEM(s, BF16) for s in held.shapes]
        scratch += [pltpu.VMEM(held.scratch, BF16), pltpu.SemaphoreType.DMA((2 * held.span,))]
    return pl.pallas_call(
        functools.partial(middle_kernel, held=held, head_dim=head_dim, chunk=512),
        grid=(rows // tile,),
        in_specs=[rows_of(tile, width), rows_of(tile, q_cols), rows_of(tile, width),
                  full(gains.shape)] + specs,
        out_specs=[rows_of(tile, width), rows_of(tile, width), rows_of(tile, width),
                   rows_of(tile, q_cols), pl.BlockSpec((heads, tile), lambda i: (0, i)),
                   rows_of(tile, width), rows_of(tile, hidden), rows_of(tile, 2 * hidden),
                   full((1, width))],
        out_shape=[like((rows, width), BF16), like((rows, width), F32), like((rows, width), BF16),
                   like((rows, q_cols), BF16), like((heads, rows), F32),
                   like((rows, width), BF16), like((rows, hidden), BF16),
                   like((rows, 2 * hidden), BF16), like((1, width), F32)],
        scratch_shapes=scratch,
        compiler_params=params(),
        cost_estimate=took(39),
        name="middle",
    )(x, attn, grad, gains, *more)


def attend_back_kernel(*refs, group, head_dim, block, scale, m):
    where, lengths_ref, lse_ref, delta_ref, q_ref, do_ref, cos_ref, sin_ref = refs[:8]
    kvs, span = refs[8 : 8 + len(group.arrays)], group.span
    kv_ref, kt_ref, acc_ref, sem = refs[-4:]
    sends = refs[-4 - (span - 1) : -4]
    dq_ref, own_ref = refs[-4 - span - 1 : -4 - span + 1]
    heads = q_ref.shape[1] // head_dim
    half = head_dim // 2
    rows = q_ref.shape[0]
    place = where[1]
    base = place * rows
    lengths = [lengths_ref[m, d] for d in range(lengths_ref.shape[1])]

    def copy(s):
        return group.copy(kvs, m, s, place, kv_ref, sem.at[s])

    for s in range(span):
        pl.when((place ^ s) <= place)(lambda s=s: copy(s).start())
    acc_ref[...] = jnp.zeros_like(acc_ref)
    for s in range(span):
        pl.when((place ^ s) <= place)(lambda s=s: copy(s).wait())
    index = lax.broadcasted_iota(jnp.int32, (block, rows), 0)
    high = base + lax.broadcasted_iota(jnp.int32, (1, rows), 1)
    low = begin_of(high, lengths)
    count = rows // block

    def visit(kb, carry):
        at = pl.ds(pl.multiple_of(kb * block, block), block)
        keys = kv_ref[at, :head_dim]
        vals = kv_ref[at, head_dim:]
        kt_ref[...] = keys.T
        here = kb * block + index
        mask = (here >= low) & (here <= high)
        dk = jnp.zeros((block, head_dim), F32)
        dv = jnp.zeros((block, head_dim), F32)
        for h in range(heads):
            cols = slice(h * head_dim, (h + 1) * head_dim)
            q = q_ref[:, cols]
            do = do_ref[:, cols]
            s = mm_nt(keys, q)
            p = jnp.where(mask, jnp.exp(s - lse_ref[0, h : h + 1, :]), 0.0)
            dv = dv + mm(p.astype(BF16), do)
            ds = (p * (mm_nt(vals, do) - delta_ref[h : h + 1, :])).astype(BF16)
            dk = dk + mm(ds, q)
            acc_ref[h] += mm(kt_ref[...], ds)
        owner = lax.div(kb, count)
        to = pl.ds(pl.multiple_of((kb - owner * count) * block, block), block)

        def put(ref):
            ref[to, :head_dim] = dk.astype(ref.dtype)
            ref[to, head_dim:] = dv.astype(ref.dtype)

        pl.when(owner == place)(lambda: put(own_ref))
        for s, ref in enumerate(sends, 1):
            pl.when(owner == (place ^ s))(lambda ref=ref: put(ref))
        return carry

    begin = lax.div(begin_of(base, lengths), block)
    for s, ref in enumerate([own_ref, *sends]):
        @pl.when(((place ^ s) > place) | ((place ^ s) * count < begin))
        def _():
            ref[...] = jnp.zeros_like(ref)

    lax.fori_loop(begin, (place + 1) * count, visit, 0)
    cos, sin = cos_ref[...], sin_ref[...]
    for h in range(heads):
        c = h * head_dim
        dq = acc_ref[h].T * scale
        a, b = dq[:, :half], dq[:, half:]
        dq_ref[:, c : c + half] = (a * cos + b * sin).astype(BF16)
        dq_ref[:, c + half : c + head_dim] = (b * cos - a * sin).astype(BF16)


def attend_back(where, lengths, lse, delta, q, do, group, cos, sin, head_dim, block, scale, m,
                before, later):
    q_cols = q.shape[1]
    rows = q.shape[0] // lengths.shape[0]
    heads = q_cols // head_dim
    span, n = group.span, len(group.arrays)
    tokens = span * rows
    half = head_dim // 2
    here = pl.BlockSpec((rows, q_cols), lambda i: (m, 0))
    angle = pl.BlockSpec((rows, half), lambda i: (m, 0))
    more = ([] if before is None else [before]) + later
    return pl.pallas_call(
        functools.partial(attend_back_kernel, group=group, head_dim=head_dim, block=block,
                          scale=scale, m=m),
        grid=(1,),
        in_specs=[SMEM, SMEM, pl.BlockSpec((1, heads, rows), lambda i: (m, 0, 0)),
                  pl.BlockSpec((heads, rows), lambda i: (0, m)), here, here, angle, angle]
        + [ANY] * (n + len(more)),
        out_specs=[here] + [VMEM] * span,
        out_shape=[like(q.shape, BF16), like((rows, 2 * head_dim), F32)]
        + [like((rows, 2 * head_dim), BF16)] * (span - 1),
        scratch_shapes=[pltpu.VMEM((tokens, 2 * head_dim), BF16),
                        pltpu.VMEM((head_dim, block), BF16),
                        pltpu.VMEM((heads, head_dim, rows), F32),
                        pltpu.SemaphoreType.DMA((span,))],
        input_output_aliases={} if before is None else {8 + n: 0},
        compiler_params=params(),
        cost_estimate=cost(LONG, 1),
        name="attend_back",
    )(where, lengths, lse, delta, q, do, cos, sin, *group.arrays, *more)


def query_back_kernel(dq_ref, w_ref, ww_ref, lora_grad_ref, back_ref, *, q_cols, mid):
    dq = dq_ref[...]
    lora_grad = mm_nt(dq, ww_ref[...]).astype(BF16)
    lora_grad_ref[...] = lora_grad
    back_ref[...] = (mm_nt(dq, w_ref[:, :q_cols])
                     + mm_nt(lora_grad, w_ref[:, q_cols : q_cols + mid]))


def query_back(dq, w, ww, later=()):
    rows, q_cols = dq.shape
    mid, width = ww.shape[0], w.shape[0]
    tile = math.gcd(rows, 256)
    return pl.pallas_call(
        skipping(functools.partial(query_back_kernel, q_cols=q_cols, mid=mid), 3, len(later)),
        grid=(rows // tile,),
        in_specs=[rows_of(tile, q_cols), full(w.shape), full(ww.shape)] + [ANY] * len(later),
        out_specs=[rows_of(tile, mid), rows_of(tile, width)],
        out_shape=[like((rows, mid), BF16), like((rows, width), F32)],
        compiler_params=params(),
        cost_estimate=cost(2 * rows * (width * (q_cols + mid) + mid * q_cols), 9e6),
        name="query_back",
    )(dq, w, ww, *later)


def pair_back_kernel(*refs, head_dim, others):
    x_ref, gains_ref, cos_ref, sin_ref, w_ref, back_ref, mid_grad_ref, own_ref = refs[:8]
    pair_grad_ref, in_grad_ref, gain_grad_ref = refs[-3:]

    @pl.when(pl.program_id(0) == 0)
    def _():
        gain_grad_ref[...] = jnp.zeros_like(gain_grad_ref)

    half = head_dim // 2
    gain = gains_ref[0:1, :]
    cos, sin = cos_ref[...], sin_ref[...]
    dkv = own_ref[...]
    for ref in refs[8 : 8 + others]:
        dkv = dkv + ref[...].astype(F32)
    a, b = dkv[:, :half], dkv[:, half:head_dim]
    pair_grad_ref[:, :half] = (a * cos + b * sin).astype(BF16)
    pair_grad_ref[:, half:head_dim] = (b * cos - a * sin).astype(BF16)
    pair_grad_ref[:, head_dim:] = dkv[:, head_dim:].astype(BF16)
    back = back_ref[...] + mm_nt(pair_grad_ref[...], w_ref[:, : 2 * head_dim])
    x = x_ref[...].astype(F32)
    inv = lax.rsqrt(jnp.mean(x * x, axis=-1, keepdims=True) + EPSILON)
    unit = x * inv
    gain_grad_ref[...] += jnp.sum(unit * back, axis=0, keepdims=True)
    scaled = back * gain
    in_grad_ref[...] = mid_grad_ref[...] + inv * (
        scaled - unit * jnp.mean(unit * scaled, axis=-1, keepdims=True)
    )


def pair_back(x, gains, cos, sin, w, own, others, back, mid_grad, head_dim, m, batches, before=None,
              later=()):
    width = x.shape[1]
    rows = x.shape[0] // batches
    tile = math.gcd(rows, 256)
    half, cols = head_dim // 2, 2 * head_dim
    count = rows // tile

    def here(n):
        return pl.BlockSpec((tile, n), lambda i: (m * count + i, 0))

    more = ([] if before is None else [before]) + list(later)
    return pl.pallas_call(
        functools.partial(pair_back_kernel, head_dim=head_dim, others=len(others)),
        grid=(count,),
        in_specs=[here(width), full(gains.shape), here(half), here(half), full(w.shape),
                  here(width), here(width)] + [rows_of(tile, cols)] * (1 + len(others))
        + [ANY] * len(more),
        out_specs=[rows_of(tile, cols), here(width), full((1, width))],
        out_shape=[like((rows, cols), BF16), like(x.shape, F32), like((1, width), F32)],
        input_output_aliases={} if before is None else {8 + len(others): 1},
        compiler_params=params(),
        cost_estimate=cost(2 * rows * width * cols, 7e6),
        name="pair_back",
    )(x, gains, cos, sin, w, back, mid_grad, own, *others, *more)


def weight_grad_kernel(x_ref, y_ref, out_ref):
    out_ref[...] = mm_tn(x_ref[...], y_ref[...]).astype(BF16)


def weight_grad(x, y, tile=256, later=()):
    rows, width = x.shape
    cols = y.shape[1]
    tile = math.gcd(cols, tile)
    return pl.pallas_call(
        skipping(weight_grad_kernel, 2, len(later)),
        grid=(cols // tile,),
        in_specs=[full(x.shape), pl.BlockSpec((rows, tile), lambda i: (0, i))] + [ANY] * len(later),
        out_specs=pl.BlockSpec((width, tile), lambda i: (0, i)),
        out_shape=like((width, cols), BF16),
        compiler_params=params(),
        cost_estimate=took(10),
        name="weight_grad",
    )(x, y, *later)


def turn(x_ref, flat_ref, xt_ref, me, parts):
    flat_ref[...] = x_ref[...].T
    piece = flat_ref.shape[0] // parts
    for r in range(parts):
        at = pl.multiple_of((me ^ r) * piece, piece)
        to = (r % 2) * (parts // 2) + r // 2
        xt_ref[to * piece : (to + 1) * piece, :] = flat_ref[pl.ds(at, piece), :]


def column_grads_kernel(where, g_in, hidden_in, b_in, attn_in, keep_ref, send_ref, g_ref, hidden_ref,
                        b_ref, attn_ref, sem, *, parts):
    f = Fetch([(g_in, g_ref), (hidden_in, hidden_ref), (b_in, b_ref), (attn_in, attn_ref)], sem)
    span, _, piece, _ = keep_ref.shape
    per = parts // span
    col = 0
    for pair, x_ref, y_ref in (((0, 1), g_ref, hidden_ref), ((2, 3), b_ref, attn_ref)):
        n = y_ref.shape[1] // parts
        f.wait(pair[0])
        f.wait(pair[1])
        for r in range(parts):
            at = pl.multiple_of((where[0] ^ r) * n, n)
            out = mm_tn(x_ref[...], y_ref[:, pl.ds(at, n)]).astype(BF16)
            ref = send_ref if r % 2 else keep_ref
            for s in range(span):
                for i in range(per):
                    ref[s ^ where[1], r // 2, :, col + i * n : col + (i + 1) * n] = out[
                        (s * per + i) * piece : (s * per + i + 1) * piece]
        col += per * n


def column_grads(where, grad, hidden, branch, attn, parts, span):
    rows, width = grad.shape
    piece = width // parts
    cols = (hidden.shape[1] + attn.shape[1]) // span
    shape = like((span, parts // 2, piece, cols), BF16)
    arrays = (grad, hidden, branch, attn)
    return pl.pallas_call(
        functools.partial(column_grads_kernel, parts=parts),
        in_specs=[SMEM] + [ANY] * 4,
        out_specs=[VMEM] * 2,
        out_shape=[shape, shape],
        scratch_shapes=[pltpu.VMEM(a.shape, BF16) for a in arrays]
        + [pltpu.SemaphoreType.DMA((4,))],
        compiler_params=params(),
        cost_estimate=took(9),
        name="column_grads",
    )(where, *arrays)


def unrotate(dkv, cos, sin, head_dim):
    half = head_dim // 2
    a, b = dkv[:, :half], dkv[:, half:head_dim]
    return jnp.concatenate([a * cos + b * sin, b * cos - a * sin, dkv[:, head_dim:]],
                           axis=1).astype(BF16)


def norm_back(x, gain, back, rest):
    inv = lax.rsqrt(jnp.mean(x * x, axis=-1, keepdims=True) + EPSILON)
    unit = x * inv
    scaled = back * gain
    return (rest + inv * (scaled - unit * jnp.mean(unit * scaled, axis=-1, keepdims=True)),
            jnp.sum(unit * back, axis=0, keepdims=True))


def fold_rows(out_ref, value, first, parts, piece, fold, j):
    count = value.shape[0] // parts
    for d in range(parts):
        at = d * piece + j * count
        out_ref[at : at + count, first : first + fold] = value[d * count : (d + 1) * count]


def query_side_kernel(dq_in, ww_in, normed_in, lora_in, queries_ref, lora_grad_ref, dq, ww, normed,
                      lora, sem, *, parts, fold):
    f = Fetch([(dq_in, dq), (ww_in, ww), (normed_in, normed), (lora_in, lora)], sem)
    q_cols, mid = dq.shape[1], lora.shape[1]
    f.wait(0, 1)
    lora_grad = mm_nt(dq[...], ww[...]).astype(BF16)
    lora_grad_ref[...] = lora_grad
    f.wait(2, 3)
    step = math.gcd(q_cols, 512)
    turned = normed[...].T
    for c in range(0, q_cols, step):
        queries_ref[:, c : c + step] = mm(turned, dq[:, c : c + step]).astype(BF16)
    queries_ref[:, q_cols : q_cols + mid] = mm(turned, lora_grad).astype(BF16)
    piece, count = normed.shape[1] // parts, mid // parts
    turned = lora[...].T
    for j in range(q_cols // fold):
        out = mm(turned, dq[:, j * fold : (j + 1) * fold]).astype(BF16)
        fold_rows(queries_ref, out, q_cols + mid, parts, piece, fold, j)
    rest = (q_cols // fold) * count
    for d in range(parts):
        queries_ref[d * piece + rest : (d + 1) * piece, q_cols + mid :] = jnp.zeros(
            (piece - rest, fold), BF16)


def query_side(dq, ww, normed, lora_mid, parts, fold, later):
    total, q_cols = dq.shape
    width, mid = normed.shape[1], lora_mid.shape[1]
    arrays = (dq, ww, normed, lora_mid)
    return pl.pallas_call(
        skipping(functools.partial(query_side_kernel, parts=parts, fold=fold), 4, len(later)),
        in_specs=[ANY] * (4 + len(later)),
        out_specs=[VMEM] * 2,
        out_shape=[like((width, q_cols + mid + fold), BF16), like((total, mid), BF16)],
        scratch_shapes=[pltpu.VMEM(a.shape, BF16) for a in arrays]
        + [pltpu.SemaphoreType.DMA((4,))],
        compiler_params=params(),
        cost_estimate=cost(LONG, 1),
        name="query_side",
    )(*arrays, *later)


def first_side_kernel(*refs, head_dim, others):
    (dq_in, w_in, lora_in, own_in, wp_in, x_in, mg_in, gains_ref, cos_ref, sin_ref, keep_ref,
     got_ref) = refs[:12]
    others_in = refs[12 : 12 + others]
    (back_ref, pair_ref, in_grad_ref, one_ref, near_ref, far_ref,
     dq, w, lora, own, wp, x, mg, there, hold, sem) = refs[12 + others :]
    rows = x.shape[0]
    f = Fetch([(dq_in, dq), (w_in, w), (lora_in, lora), (own_in, own), (wp_in, wp),
               (x_in.at[pl.ds(0, rows)], x), (mg_in.at[pl.ds(0, rows)], mg)]
              + [(r, there.at[i]) for i, r in enumerate(others_in)], sem)
    near_ref[...] = (keep_ref[0].astype(F32) + got_ref[0].astype(F32)).astype(BF16)
    far_ref[...] = (keep_ref[1].astype(F32) + got_ref[1].astype(F32)).astype(BF16)
    q_cols, mid = dq.shape[1], lora.shape[1]
    f.wait(0, 1, 2)
    for m in range(dq.shape[0] // rows):
        at = slice(m * rows, (m + 1) * rows)
        back = mm_nt(dq[at, :], w[:, :q_cols]) + mm_nt(lora[at, :], w[:, q_cols : q_cols + mid])
        if m == 0:
            hold[...] = back
        else:
            back_ref[(m - 1) * rows : m * rows] = back
    f.wait(*range(3, 7 + others))
    dkv = own[...]
    for i in range(others):
        dkv = dkv + there[i].astype(F32)
    pair = unrotate(dkv, cos_ref[...], sin_ref[...], head_dim)
    pair_ref[...] = pair
    back = hold[...] + mm_nt(pair, wp[:, : 2 * head_dim])
    in_grad_ref[...], one_ref[...] = norm_back(x[...].astype(F32), gains_ref[0:1, :], back, mg[...])


def first_side(dq, w, lora_grad, own, others, w_pair, x, mid_grad, gains, cos, sin, keep, got,
               head_dim, batches, later):
    total = dq.shape[0]
    rows = total // batches
    width, mid = x.shape[1], lora_grad.shape[1]
    half, cols = head_dim // 2, 2 * head_dim
    angle = pl.BlockSpec((rows, half), lambda i: (0, 0))
    n = len(others)
    return pl.pallas_call(
        skipping(functools.partial(first_side_kernel, head_dim=head_dim, others=n), 12 + n,
                 len(later)),
        grid=(1,),
        in_specs=[ANY] * 7 + [VMEM, angle, angle, VMEM, VMEM] + [ANY] * (n + len(later)),
        out_specs=[VMEM] * 2 + [pl.BlockSpec((rows, width), lambda i: (0, 0))] + [VMEM] * 3,
        out_shape=[like((total - rows, width), F32), like((rows, cols), BF16),
                   like((total, width), F32), like((1, width), F32)]
        + [like(keep.shape[1:], BF16)] * 2,
        scratch_shapes=[pltpu.VMEM(dq.shape, BF16), pltpu.VMEM(w.shape, BF16),
                        pltpu.VMEM(lora_grad.shape, BF16), pltpu.VMEM((rows, cols), F32),
                        pltpu.VMEM(w_pair.shape, BF16), pltpu.VMEM((rows, width), BF16),
                        pltpu.VMEM((rows, width), F32), pltpu.VMEM((n, rows, cols), BF16),
                        pltpu.VMEM((rows, width), F32), pltpu.SemaphoreType.DMA((7 + n,))],
        compiler_params=params(),
        cost_estimate=cost(1, 1),
        name="first_side",
    )(dq, w, lora_grad, own, w_pair, x, mid_grad, gains, cos, sin, keep, got, *others, *later)


def pair_side_kernel(*refs, head_dim, parts, others):
    (where, own_in, wp_in, back_in, x_in, mg_in, normed_in, first_in, gains_ref, cos_ref, sin_ref,
     one_ref, two_ref) = refs[:13]
    others_in = refs[13 : 13 + others]
    outs = refs[14 + others :]
    in_grad_ref, send_ref = outs[:2]
    keeps = outs[2 : 2 + parts // 2]
    (own, wp, back, x, mg, normed, pair_ref, there, flat_ref, xt_ref, gain_ref,
     sem) = outs[2 + parts // 2 :]
    rows = x.shape[0]
    f = Fetch([(normed_in, normed), (own_in, own)]
              + [(r, there.at[i]) for i, r in enumerate(others_in)]
              + [(first_in, pair_ref.at[pl.ds(0, rows)]), (wp_in, wp), (back_in, back),
                 (x_in.at[pl.ds(rows, rows)], x), (mg_in.at[pl.ds(rows, rows)], mg)], sem)
    f.wait(0)
    turn(normed, flat_ref, xt_ref, where[0], parts)
    f.wait(*range(1, 2 + others))
    dkv = own[...]
    for i in range(others):
        dkv = dkv + there[i].astype(F32)
    pair = unrotate(dkv, cos_ref[...], sin_ref[...], head_dim)
    pair_ref[rows:, :] = pair
    f.wait(*range(2 + others, 7 + others))
    grads = back[...] + mm_nt(pair, wp[:, : 2 * head_dim])
    in_grad_ref[...], one = norm_back(x[...].astype(F32), gains_ref[0:1, :], grads, mg[...])
    width = flat_ref.shape[0]
    piece, half, cols = width // parts, parts // 2, 2 * head_dim
    out = mm(xt_ref[...], pair_ref[...]).astype(BF16)
    pad = jnp.zeros((126, width), F32)
    gain_ref[...] = jnp.concatenate([one + one_ref[...], two_ref[...], pad], axis=0).T.astype(BF16)
    for k in range(half):
        keeps[k][:, :cols] = out[k * piece : (k + 1) * piece]
        send_ref[k, :, :cols] = out[(half + k) * piece : (half + k + 1) * piece]
        at = pl.multiple_of((where[0] ^ (2 * k)) * piece, piece)
        keeps[k][:, cols:] = gain_ref[pl.ds(at, piece), :]
        at = pl.multiple_of((where[0] ^ (2 * k + 1)) * piece, piece)
        send_ref[k, :, cols:] = gain_ref[pl.ds(at, piece), :]


def pair_side(where, own, others, w_pair, back, x, mid_grad, normed, first, gains, cos, sin, one,
              two, in_grad, head_dim, parts):
    total, width = normed.shape
    rows = total // 2
    half, cols = head_dim // 2, 2 * head_dim
    piece = width // parts
    angle = pl.BlockSpec((rows, half), lambda i: (1, 0))
    n = len(others)
    return pl.pallas_call(
        functools.partial(pair_side_kernel, head_dim=head_dim, parts=parts, others=n),
        grid=(1,),
        in_specs=[SMEM] + [ANY] * 7 + [VMEM, angle, angle, VMEM, VMEM] + [ANY] * (n + 1),
        out_specs=[pl.BlockSpec((rows, width), lambda i: (1, 0))] + [VMEM] * (1 + parts // 2),
        out_shape=[like((total, width), F32), like((parts // 2, piece, cols + 128), BF16)]
        + [like((piece, cols + 128), BF16)] * (parts // 2),
        scratch_shapes=[pltpu.VMEM((rows, cols), F32), pltpu.VMEM(w_pair.shape, BF16),
                        pltpu.VMEM((rows, width), F32), pltpu.VMEM((rows, width), BF16),
                        pltpu.VMEM((rows, width), F32), pltpu.VMEM(normed.shape, BF16),
                        pltpu.VMEM((total, cols), BF16), pltpu.VMEM((n, rows, cols), BF16),
                        pltpu.VMEM((width, total), BF16), pltpu.VMEM((width, total), BF16),
                        pltpu.VMEM((width, 128), BF16), pltpu.SemaphoreType.DMA((7 + n,))],
        input_output_aliases={13 + n: 0},
        compiler_params=params(),
        cost_estimate=cost(LONG, 12e6),
        name="pair_side",
    )(where, own, w_pair, back, x, mid_grad, normed, first, gains, cos, sin, one, two, *others,
      in_grad)


def join_kernel(left_ref, *refs):
    out_ref = refs[-1]
    n = left_ref.shape[1]
    out_ref[:, :n] = left_ref[...]
    out_ref[:, n:] = tree([r[...].astype(F32) for r in refs[:-1]]).astype(BF16)


def join(left, parts):
    rows, n = left.shape
    arrays = [left, *parts]
    return pl.pallas_call(
        fetched(join_kernel, len(arrays)),
        in_specs=[ANY] * len(arrays),
        out_specs=VMEM,
        out_shape=like((rows, n + parts[0].shape[1]), BF16),
        scratch_shapes=room(arrays),
        compiler_params=params(),
        cost_estimate=took(2),
        name="join",
    )(*arrays)


def finish_kernel(*refs, mid, q_cols, cols, fold):
    parts, outs = refs[:-6], refs[-6:]
    query_ref, narrow_ref, widen_ref, kv_ref, one_ref, two_ref = outs
    total = tree([p[...].astype(F32) for p in parts])
    query_ref[...] = total[:, :q_cols]
    narrow_ref[...] = total[:, q_cols : q_cols + mid]
    first = q_cols + mid
    count = widen_ref.shape[0]
    for j in range(q_cols // fold):
        widen_ref[:, j * fold : (j + 1) * fold] = total[j * count : (j + 1) * count,
                                                        first : first + fold]
    first += fold
    kv_ref[...] = total[:, first : first + cols]
    gains = total[:, first + cols :].T
    one_ref[...] = gains[0:1]
    two_ref[...] = gains[1:2]


def finish(parts, q_cols, mid, count, cols, fold):
    piece = parts[0].shape[0]
    return pl.pallas_call(
        fetched(functools.partial(finish_kernel, q_cols=q_cols, mid=mid, cols=cols, fold=fold),
                len(parts)),
        in_specs=[ANY] * len(parts),
        scratch_shapes=room(parts),
        out_specs=[VMEM] * 6,
        out_shape=[like((piece, q_cols), F32), like((piece, mid), F32), like((count, q_cols), F32),
                   like((piece, cols), F32), like((1, piece), F32), like((1, piece), F32)],
        compiler_params=params(),
        cost_estimate=took(2.5),
        name="finish",
    )(*parts)


def swap_cores(keeps, send, later=()):
    got, count = swap(send, "fsdp", 1), len(keeps)
    return add([*keeps, got], [[(k, None), (count, k)] for k in range(count)], later)


def pairs_kernel(*refs):
    parts, (keep_ref, send_ref) = refs[:-2], refs[-2:]
    for i in range(2):
        for k, ref in ((2 * i, keep_ref), (2 * i + 1, send_ref)):
            ref[i] = tree([p[k].astype(F32) for p in parts]).astype(BF16)


def sum_pairs(parts, later=()):
    count, shape = len(parts), like((2,) + parts[0].shape[1:], BF16)
    return pl.pallas_call(
        skipping(pairs_kernel, count, len(later)),
        in_specs=[VMEM] * count + [ANY] * len(later),
        out_specs=[VMEM] * 2,
        out_shape=[shape] * 2,
        compiler_params=params(),
        cost_estimate=took(2.4),
        name="sum_pairs",
    )(*parts, *later)


def cut_kernel(where, x_ref, *outs):
    part = outs[0].shape[1]
    for s, out in enumerate(outs):
        at = pl.multiple_of((where[1] ^ s) * part, part)
        out[...] = x_ref[:, pl.ds(at, part)]


def cut_parts(where, x, later=()):
    span = lax.axis_size("seq")
    rows, part = x.shape[0], x.shape[1] // span
    cut = pl.pallas_call(
        skipping(cut_kernel, 2, len(later)),
        in_specs=[SMEM, VMEM] + [ANY] * len(later),
        out_specs=[VMEM] * span,
        out_shape=[like((rows, part), x.dtype)] * span,
        compiler_params=params(),
        cost_estimate=took(2),
        name="cut",
    )(where, x, *later)
    return cut


def halves_kernel(*refs):
    out_ref = refs[-1]
    n = refs[0].shape[1]
    out_ref[:, :n] = tree([r[...].astype(F32) for r in refs[:-3]]).astype(BF16)
    out_ref[:, n:] = tree([r[...].astype(F32) for r in refs[-3:-1]]).astype(BF16)


def halves(left, right, later=()):
    count = len(left) + 2
    shape = (left[0].shape[0], left[0].shape[1] + right[0].shape[1])
    return pl.pallas_call(
        skipping(halves_kernel, count, len(later)),
        in_specs=[VMEM] * count + [ANY] * len(later),
        out_specs=VMEM,
        out_shape=like(shape, BF16),
        compiler_params=params(),
        cost_estimate=cost(LONG, 2e6),
        name="halves",
    )(*left, *right, *later)


def lay_kernel(where, *refs, n, k):
    parts = refs[:-6]
    span = len(parts)
    gate_ref, up_ref, down_ref, out_ref, tall_ref, tall2_ref = refs[-6:]
    piece = parts[0].shape[0]
    half = span // 2
    wide = gate_ref.shape[1] // half
    per = (parts[0].shape[1] - wide) // (n + k)
    for s, ref in enumerate(parts):
        q = where[1] ^ s
        for i, out in enumerate((gate_ref, up_ref)):
            @pl.when(q // half == i)
            def _():
                at = pl.multiple_of((q % half) * wide, wide)
                out[:, pl.ds(at, wide)] = ref[:, :wide].astype(F32)
        for i in range(per):
            at = pl.ds(pl.multiple_of((q * per + i) * piece, piece), piece)
            first = wide + i * n
            tall_ref[at, :] = ref[:, first : first + n].astype(F32)
            first = wide + per * n + i * k
            tall2_ref[at, :] = ref[:, first : first + k].astype(F32)
    down_ref[...] = tall_ref[...].T
    out_ref[...] = tall2_ref[...].T


def lay(where, parts, hidden, n, k, later=()):
    piece = parts[0].shape[0]
    width = piece * lax.axis_size("fsdp")
    return pl.pallas_call(
        skipping(functools.partial(lay_kernel, n=n, k=k), 1 + len(parts), len(later)),
        in_specs=[SMEM] + [VMEM] * len(parts) + [ANY] * len(later),
        out_specs=[VMEM] * 4,
        out_shape=[like((piece, hidden), F32)] * 2 + [like((n, width), F32), like((k, width), F32)],
        scratch_shapes=[pltpu.VMEM((width, n), F32), pltpu.VMEM((width, k), F32)],
        compiler_params=params(),
        cost_estimate=took(3),
        name="lay",
    )(where, *parts, *later)


def begin_of(index, lengths):
    ends = [lengths[0]]
    for n in lengths[1:]:
        ends.append(ends[-1] + n)
    begin = index
    for d in reversed(range(len(lengths))):
        begin = jnp.where(index < ends[d], ends[d] - lengths[d], begin)
    return begin


def local(tokens, document_lengths, cotangent, attention_gain, query_projection, narrowing_factor,
          widening_factor, key_value_projection, output_projection, feedforward_gain,
          gate_projection, up_projection, down_projection):
    batches, _, rows, width = tokens.shape
    head_dim = key_value_projection.shape[1] // 2
    q_cols = query_projection.shape[1]
    mid = narrowing_factor.shape[1]
    hidden = gate_projection.shape[1]
    kv_cols = 2 * head_dim
    scale = head_dim ** (-0.5)
    parts, span = lax.axis_size("fsdp"), lax.axis_size("seq")
    place = lax.axis_index("seq")
    tile = block = math.gcd(rows, 512)
    where = jnp.stack([lax.axis_index("fsdp"), place]).astype(jnp.int32)
    piece = width // parts
    direct = piece % 16 == 0
    fold = 512
    folds = q_cols // fold

    lengths = document_lengths[:, 0]
    half = head_dim // 2
    index = place * rows + lax.broadcasted_iota(jnp.int32, (batches, rows, half), 1)
    begin = begin_of(index, [lengths[:, d][:, None, None] for d in range(lengths.shape[1])])
    freqs = THETA ** (-(lax.broadcasted_iota(jnp.int32, (1, half), 1).astype(F32) * 2.0 / head_dim))
    angles = ((index - begin).astype(F32) * freqs).reshape(batches * rows, half)
    cos, sin = jnp.cos(angles), jnp.sin(angles)

    if direct:
        first = Shards(pack_pair(key_value_projection, attention_gain, feedforward_gain))
        third = pack(where, gate_projection, up_projection, down_projection, output_projection,
                     span, [cos, sin, first.arrays[parts - 2]])
        held = Tiled(third, 2 * hidden, down_projection, output_projection)
        weights = None
    else:
        def gather(x):
            return lax.all_gather(x, "fsdp", axis=0, tiled=True)

        first = jnp.concatenate(
            [key_value_projection,
             jnp.pad(jnp.stack([attention_gain, feedforward_gain], axis=1), ((0, 0), (0, 126)))],
            axis=1)
        turned = jnp.concatenate(
            [widening_factor[:, j * fold : (j + 1) * fold] for j in range(folds)])
        turned = jnp.pad(turned, ((0, piece - turned.shape[0]), (0, 0)))
        second = jnp.concatenate([query_projection, narrowing_factor, turned], axis=1)
        first, second = Whole(gather(first)), Whole(gather(second))
        second.rows = piece
        held = None
        weights = [gather(jnp.concatenate([gate_projection, up_projection], axis=1)),
                   gather(down_projection), gather(output_projection)]

    x = tokens.reshape(batches * rows, width)
    grad = cotangent.reshape(batches * rows, width)
    normed, kv, w_pair, gains = project_kv(where, x, cos, sin, first, head_dim)
    kvs = Group(kv, batches)
    if direct:
        second = Shards(pack_query(query_projection, narrowing_factor, widening_factor, fold,
                                   [kv]), True)
    lora_mid, q, w_query, ww = project_q(where, normed, cos, sin, second, head_dim, q_cols, mid,
                                         scale, [])
    attended, lse = attend(where, lengths, q, kvs, head_dim, tile, block)
    (output, mid_grad, branch, attn_grad, delta, ffn_low, hidden_low, lift_grads,
     gain_two_grad) = middle_part(x, attended, grad, gains, held, weights, head_dim)

    if direct:
        keep, send = column_grads(where, grad, hidden_low, branch, attended, parts, span)
        got = swap(send, "fsdp", 1)
        lifts = weight_grad(ffn_low, lift_grads, 1024, [keep])
        lifts_sum = lax.psum_scatter(lifts, "fsdp", scatter_dimension=0, tiled=True)
        columns = add([keep, got], [[(0, s), (1, s)] for s in range(span)], [lifts])
        there = exchange(columns)
    dq, owns, others = None, [], []
    for m in range(batches):
        later = []
        if direct and m == 0:
            later = columns
        if direct and m == 1:
            keep, send = sum_pairs(there, [dq])
            got = swap(send, "fsdp", 2)
            later = [keep]
        dq, own, *sends = attend_back(where, lengths, lse, delta, q, attn_grad, kvs, cos, sin,
                                      head_dim, block, scale, m, dq, later)
        owns.append(own)
        others.append(exchange([own, *sends])[1:])
    if direct:
        queries, lora_grad = query_side(dq, ww, normed, lora_mid, parts, fold, [])
        queries_sum = lax.psum_scatter(queries, "fsdp", scatter_dimension=0, tiled=True)
        back, pair, in_grad, one, near, far = first_side(
            dq, w_query, lora_grad, owns[0], others[0], w_pair, x, mid_grad, gains, cos, sin, keep,
            got, head_dim, batches, [queries, lifts_sum])
        in_grad, send, *keeps = pair_side(where, owns[1], others[1], w_pair, back, x, mid_grad,
                                          normed, pair, gains, cos, sin, one, gain_two_grad,
                                          in_grad, head_dim, parts)

        def share(x):
            return exchange([x] * span)

        lifts_cut = cut_parts(where, lifts_sum, [pair])
        lifts_parts = exchange(lifts_cut)
        mine = halves(lifts_parts, [near, swap(far, "fsdp", 4)], [send])
        laid = share(mine)
        shards = swap_cores(keeps, send, [mine])
        mine = join(queries_sum, [shards[0]] + [
            swap(a, "fsdp", 2 * k) for k, a in enumerate(shards) if k > 0])
        last = share(mine)
        gate_grad, up_grad, down_grad, out_grad = lay(
            where, laid, hidden, hidden // parts, q_cols // parts, [mine])
        query_grad, narrow_grad, widen_grad, key_value_grad, one, two = finish(
            last, q_cols, mid, mid // parts, kv_cols, fold)
        gain_one_grad, gain_two_grad = one.reshape(piece), two.reshape(piece)
    else:
        lora_grad, back = query_back(dq, w_query, ww)
        in_grad, pairs, ones = None, [], []
        for m in range(batches):
            pair, in_grad, one = pair_back(x, gains, cos, sin, w_pair, owns[m], others[m], back,
                                           mid_grad, head_dim, m, batches, in_grad)
            pairs.append(pair)
            ones.append(one)

        def scatter(x):
            part = lax.psum_scatter(x.astype(BF16), "fsdp", scatter_dimension=0, tiled=True)
            return lax.psum(part, "seq").astype(F32)

        pair_grad = jnp.concatenate(pairs)
        gain_one_grad = sum(ones)
        down_grad = scatter(weight_grad(grad, hidden_low).T)
        out_grad = scatter(weight_grad(branch, attended).T)
        lift_w = scatter(weight_grad(ffn_low, lift_grads))
        gate_grad, up_grad = lift_w[:, :hidden], lift_w[:, hidden:]
        query_grad = scatter(weight_grad(normed, dq))
        narrow_grad = scatter(weight_grad(normed, lora_grad))
        widen_grad = scatter(weight_grad(lora_mid, dq))
        key_value_grad = scatter(weight_grad(normed, pair_grad))
        gains_grad = scatter(jnp.concatenate([gain_one_grad, gain_two_grad]).T)
        gain_one_grad, gain_two_grad = gains_grad[:, 0], gains_grad[:, 1]
    return (output.reshape(batches, 1, rows, width), in_grad.reshape(batches, 1, rows, width),
            gain_one_grad, query_grad, narrow_grad, widen_grad, key_value_grad, out_grad,
            gain_two_grad, gate_grad, up_grad, down_grad)


def solution(mesh):
    rows = P(None, "fsdp", "seq", None)
    vector, matrix = P("fsdp"), P("fsdp", None)
    in_specs = (rows, P(None, "fsdp", None), rows, vector) + (matrix,) * 5 + (vector,) + (matrix,) * 3
    out_specs = (rows, rows, vector) + (matrix,) * 5 + (vector,) + (matrix,) * 3
    return jax.shard_map(local, mesh=mesh, in_specs=in_specs, out_specs=out_specs, check_vma=False)
```

```python
import functools
import math

import jax
import jax.numpy as jnp
from jax import lax
from jax.experimental import pallas as pl
from jax.experimental.pallas import tpu as pltpu
from jax.sharding import PartitionSpec as P

EPSILON = 1e-06
THETA = 10000.0
F32 = jnp.float32
BF16 = jnp.bfloat16
GELU_C = math.sqrt(2.0 / math.pi)
GELU_A = 0.044715
LOWEST = -1e30
VMEM_LIMIT = 60 * 1024 * 1024
ANY = pl.BlockSpec(memory_space=pltpu.HBM)
VMEM = pl.BlockSpec(memory_space=pltpu.VMEM)
SMEM = pl.BlockSpec(memory_space=pltpu.SMEM)


def mm(left, right):
    return lax.dot_general(left, right, (((1,), (0,)), ((), ())), preferred_element_type=F32)


def mm_tn(left, right):
    return lax.dot_general(left, right, (((0,), (0,)), ((), ())), preferred_element_type=F32)


def mm_nt(left, right):
    return lax.dot_general(left, right, (((1,), (1,)), ((), ())), preferred_element_type=F32)


def full(shape):
    return pl.BlockSpec(shape, lambda i: (0,) * len(shape))


def rows_of(tile, cols):
    return pl.BlockSpec((tile, cols), lambda i: (i, 0))


def params(**more):
    return pltpu.CompilerParams(vmem_limit_bytes=VMEM_LIMIT, **more)


def cost(flops, bytes_accessed, transcendentals=0):
    return pl.CostEstimate(
        flops=int(flops), bytes_accessed=int(bytes_accessed), transcendentals=int(transcendentals)
    )


def took(us):
    return cost(us * 1.1e9, 1)


LONG = 10**12


def like(shape, dtype):
    return jax.ShapeDtypeStruct(tuple(shape), dtype)


def swap(x, axis, by):
    return lax.ppermute(x, axis, [(i, i ^ by) for i in range(lax.axis_size(axis))])


def exchange(arrays):
    got = {s: swap(arrays[s], "seq", s) for s in reversed(range(1, len(arrays)))}
    return [arrays[0]] + [got[s] for s in range(1, len(arrays))]


def skipping(kernel, first, count):
    return lambda *refs: kernel(*refs[:first], *refs[first + count :])


def tree(values):
    while len(values) > 1:
        values = [values[i] + values[i + 1] for i in range(0, len(values), 2)]
    return values[0]


class Fetch:
    def __init__(self, pairs, sem):
        self.copies = [pltpu.make_async_copy(a, b, sem.at[i]) for i, (a, b) in enumerate(pairs)]
        for c in self.copies:
            c.start()

    def wait(self, *which):
        for i in which:
            self.copies[i].wait()


def fetched(kernel, count):
    def run(*refs):
        held, sem = refs[-1 - count : -1], refs[-1]
        Fetch(list(zip(refs[:count], held)), sem).wait(*range(count))
        kernel(*held, *refs[count : -1 - count])

    return run


def room(arrays):
    return [pltpu.VMEM(a.shape, a.dtype) for a in arrays] + [
        pltpu.SemaphoreType.DMA((len(arrays),))]


def add_kernel(*refs, count, groups):
    for out, group in zip(refs[count:], groups):
        values = [refs[i][...] if k is None else refs[i][k] for i, k in group]
        out[...] = tree([v.astype(F32) for v in values]).astype(out.dtype)


def add(arrays, groups, later=()):
    shapes = [arrays[g[0][0]].shape if g[0][1] is None else arrays[g[0][0]].shape[1:]
              for g in groups]
    count = len(arrays)
    later = list(later)
    kernel = fetched(functools.partial(add_kernel, count=count, groups=groups), count)
    return list(pl.pallas_call(
        skipping(kernel, count, len(later)),
        in_specs=[ANY] * (count + len(later)),
        out_specs=[VMEM] * len(groups),
        out_shape=[like(s, BF16) for s in shapes],
        scratch_shapes=room(arrays),
        compiler_params=params(),
        cost_estimate=took(3.5),
        name="add",
    )(*arrays, *later))


class Whole:
    def __init__(self, array):
        self.arrays = [array]
        self.shape = array.shape
        self.count = 1

    def copies(self, where, refs, dst):
        return [(refs[0], dst)]


class Shards:
    def __init__(self, x, relay=False):
        parts = lax.axis_size("fsdp")
        got = {0: x}
        for r in range(2, parts, 2):
            low = r & -r
            near = relay and r != low
            got[r] = swap(got[r - low], "fsdp", low) if near else swap(x, "fsdp", r)
        for r in range(0, parts, 2):
            got[r + 1] = swap(got[r], "fsdp", 1)
        self.arrays = [got[r] for r in range(parts)]
        self.rows = x.shape[0]
        self.shape = (parts * x.shape[0], x.shape[1])
        self.count = parts

    def copies(self, where, refs, dst):
        out = []
        for r, ref in enumerate(refs):
            at = pl.multiple_of((where[0] ^ r) * self.rows, self.rows)
            out.append((ref, dst.at[pl.ds(at, self.rows), :]))
        return out


def pack_pair_kernel(kv_ref, one_ref, two_ref, out_ref):
    piece, kv_cols = kv_ref.shape
    out_ref[:, :kv_cols] = kv_ref[...]
    pad = jnp.zeros((126, piece), F32)
    gains = jnp.concatenate([one_ref[...].astype(F32), two_ref[...].astype(F32), pad], axis=0)
    out_ref[:, kv_cols:] = gains.T.astype(BF16)


def pack_pair(kv, one, two):
    piece = kv.shape[0]
    return pl.pallas_call(
        pack_pair_kernel,
        in_specs=[VMEM] * 3,
        out_specs=VMEM,
        out_shape=like((piece, kv.shape[1] + 128), BF16),
        compiler_params=params(),
        cost_estimate=took(1.6),
        name="pack_pair",
    )(kv, one.reshape(1, piece), two.reshape(1, piece))


def pack_kernel(where, gate_ref, up_ref, down_ref, out_ref, third_ref, *, span):
    piece = gate_ref.shape[0]
    hidden = gate_ref.shape[1]
    part = 2 * hidden // span
    for s in range(span):
        ref, at = (gate_ref, s * part) if s * part < hidden else (up_ref, s * part - hidden)

        @pl.when(where[1] == s)
        def _():
            third_ref[:, :part] = ref[:, at : at + part]

    col = part
    for ref in (down_ref, out_ref):
        n = ref.shape[0] // span
        for i in range(n // 16):
            row = pl.ds(pl.multiple_of(where[1] * n + 16 * i, 16), 16)
            for j in range(ref.shape[1] // 128):
                third_ref[16 * j : 16 * j + 16, col : col + 128] = ref[row, j * 128 : (j + 1) * 128]
            col += 128


def pack(where, gate, up, down, out, span, later):
    piece = gate.shape[0]
    third = (gate.shape[1] * 2 * piece + (down.shape[0] + out.shape[0]) * down.shape[1]) // span
    return pl.pallas_call(
        skipping(functools.partial(pack_kernel, span=span), 5, len(later)),
        in_specs=[SMEM] + [VMEM] * 4 + [ANY] * len(later),
        out_specs=VMEM,
        out_shape=like((piece, third // piece), BF16),
        compiler_params=params(),
        cost_estimate=took(2),
        name="pack",
    )(where, gate, up, down, out, *later)


def pack_query_kernel(q_ref, narrow_ref, widen_ref, out_ref, *, fold):
    q_cols, mid, count = q_ref.shape[1], narrow_ref.shape[1], widen_ref.shape[0]
    out_ref[:, :q_cols] = q_ref[...]
    out_ref[:, q_cols : q_cols + mid] = narrow_ref[...]
    folds = q_cols // fold
    for j in range(folds):
        out_ref[j * count : (j + 1) * count, q_cols + mid :] = widen_ref[
            :, j * fold : (j + 1) * fold]
    rest = out_ref.shape[0] - folds * count
    out_ref[folds * count :, q_cols + mid :] = jnp.zeros((rest, fold), BF16)


def pack_query(q, narrow, widen, fold, later):
    return pl.pallas_call(
        skipping(functools.partial(pack_query_kernel, fold=fold), 3, len(later)),
        in_specs=[VMEM] * 3 + [ANY] * len(later),
        out_specs=VMEM,
        out_shape=like((q.shape[0], q.shape[1] + narrow.shape[1] + fold), BF16),
        compiler_params=params(),
        cost_estimate=took(1.7),
        name="pack_query",
    )(q, narrow, widen, *later)


class Tiled:
    def __init__(self, packed, gate_up, *tall):
        parts, span = lax.axis_size("fsdp"), lax.axis_size("seq")
        piece = packed.shape[0]
        self.piece, self.part, self.parts, self.span = piece, gate_up // span, parts, span
        self.heights = [t.shape[0] // span for t in tall]
        self.up, self.across = sum(self.heights) // 16, tall[0].shape[1] // 128
        self.array = lax.all_gather(packed, ("seq", "fsdp"), axis=0, tiled=True)
        self.shape = (parts * piece, gate_up)
        self.shapes = [(parts * t.shape[0], t.shape[1]) for t in tall]
        self.scratch = (span, parts * piece, self.up * 128)

    def copies(self, ref, dst, rest):
        height = self.parts * self.piece
        rows = [pl.ds(s * height, height) for s in range(self.span)]
        return [(ref.at[at, pl.ds(self.part, self.up * 128)], rest.at[s])
                for s, at in enumerate(rows)] + [
            (ref.at[at, pl.ds(0, self.part)], dst.at[:, pl.ds(s * self.part, self.part)])
            for s, at in enumerate(rows)]

    def unfold(self, rest, dsts):
        starts, tops = [], 0
        for n in self.heights:
            starts.append(tops)
            tops += n // 16

        def shard(d, carry):
            for s in range(self.span):
                for n, first, dst in zip(self.heights, starts, dsts):
                    if dst is None:
                        continue
                    for i in range(n // 16):
                        at = pl.ds(pl.multiple_of(d * n * self.span + s * n + i * 16, 16), 16)
                        for j in range(self.across):
                            row = pl.ds(pl.multiple_of(d * self.piece + 16 * j, 16), 16)
                            col = (first + i) * 128
                            dst[at, j * 128 : (j + 1) * 128] = rest[s, row, col : col + 128]
            return carry

        lax.fori_loop(0, self.parts, shard, 0)


def carry_out(copies, sem):
    made = [pltpu.make_async_copy(src, dst, sem.at[i]) for i, (src, dst) in enumerate(copies)]
    for c in made:
        c.start()
    for c in made:
        c.wait()


def normalize(x_ref, gains_ref):
    x = x_ref[...].astype(F32)
    inv = lax.rsqrt(jnp.mean(x * x, axis=-1, keepdims=True) + EPSILON)
    return (x * inv * gains_ref[0:1, :]).astype(BF16)


def put_pair(kv_ref, pair, cos, sin, head_dim):
    half = head_dim // 2
    a, b = pair[:, :half], pair[:, half:head_dim]
    kv_ref[:, :half] = (a * cos - b * sin).astype(BF16)
    kv_ref[:, half:head_dim] = (b * cos + a * sin).astype(BF16)
    kv_ref[:, head_dim:] = pair[:, head_dim:].astype(BF16)


def project_kv_kernel(*refs, held, head_dim):
    where, x_ref, cos_ref, sin_ref = refs[:4]
    pieces = refs[4 : 4 + len(held.arrays)]
    normed_ref, kv_ref, w_ref, gains_ref, sem = refs[4 + len(held.arrays) :]
    kv_cols = 2 * head_dim

    @pl.when(pl.program_id(0) == 0)
    def _():
        carry_out(held.copies(where, pieces, w_ref), sem)
        gains_ref[...] = w_ref[:, kv_cols:].astype(F32).T[:8]

    normed = normalize(x_ref, gains_ref)
    normed_ref[...] = normed
    put_pair(kv_ref, mm(normed, w_ref[:, :kv_cols]), cos_ref[...], sin_ref[...], head_dim)


def project_kv(where, x, cos, sin, held, head_dim):
    rows, width = x.shape
    tile = math.gcd(rows, 512)
    half = head_dim // 2
    return pl.pallas_call(
        functools.partial(project_kv_kernel, held=held, head_dim=head_dim),
        grid=(rows // tile,),
        in_specs=[SMEM, rows_of(tile, width), rows_of(tile, half), rows_of(tile, half)]
        + [ANY] * len(held.arrays),
        out_specs=[rows_of(tile, width), rows_of(tile, 2 * head_dim), full(held.shape),
                   full((8, width))],
        out_shape=[like((rows, width), BF16), like((rows, 2 * head_dim), BF16),
                   like(held.shape, BF16), like((8, width), F32)],
        scratch_shapes=[pltpu.SemaphoreType.DMA((held.count,))],
        compiler_params=params(),
        cost_estimate=took(5),
        name="project_kv",
    )(where, x, cos, sin, *held.arrays)


def project_q_kernel(*refs, held, head_dim, q_cols, mid, scale):
    where, normed_ref, cos_ref, sin_ref = refs[:4]
    pieces = refs[4 : 4 + len(held.arrays)]
    lora_ref, q_ref, w_ref, ww_ref, sem = refs[4 + len(held.arrays) :]
    half = head_dim // 2
    fold = held.shape[1] - q_cols - mid
    parts = q_cols // fold

    @pl.when(pl.program_id(0) == 0)
    def _():
        carry_out(held.copies(where, pieces, w_ref), sem)
        shards = held.shape[0] // held.rows
        count = mid // shards
        for d in range(shards):
            for j in range(parts):
                ww_ref[d * count : (d + 1) * count, j * fold : (j + 1) * fold] = w_ref[
                    d * held.rows + j * count : d * held.rows + (j + 1) * count, q_cols + mid :]

    normed = normed_ref[...]
    cos, sin = cos_ref[...], sin_ref[...]
    low = mm(normed, w_ref[:, q_cols : q_cols + mid]).astype(BF16)
    lora_ref[...] = low
    query = mm(normed, w_ref[:, :q_cols]) + mm(low, ww_ref[...])
    for h in range(q_cols // head_dim):
        c = h * head_dim
        a, b = query[:, c : c + half], query[:, c + half : c + head_dim]
        q_ref[:, c : c + half] = ((a * cos - b * sin) * scale).astype(BF16)
        q_ref[:, c + half : c + head_dim] = ((b * cos + a * sin) * scale).astype(BF16)


def project_q(where, normed, cos, sin, held, head_dim, q_cols, mid, scale, later):
    rows, width = normed.shape
    tile = math.gcd(rows, 256)
    half = head_dim // 2
    count = 4 + len(held.arrays)
    return pl.pallas_call(
        skipping(functools.partial(project_q_kernel, held=held, head_dim=head_dim, q_cols=q_cols,
                                   mid=mid, scale=scale), count, len(later)),
        grid=(rows // tile,),
        in_specs=[SMEM, rows_of(tile, width), rows_of(tile, half), rows_of(tile, half)]
        + [ANY] * (len(held.arrays) + len(later)),
        out_specs=[rows_of(tile, mid), rows_of(tile, q_cols), full(held.shape),
                   full((mid, q_cols))],
        out_shape=[like((rows, mid), BF16), like((rows, q_cols), BF16), like(held.shape, BF16),
                   like((mid, q_cols), BF16)],
        scratch_shapes=[pltpu.SemaphoreType.DMA((held.count,))],
        compiler_params=params(),
        cost_estimate=cost(1, 1),
        name="project_q",
    )(where, normed, cos, sin, *held.arrays, *later)


class Group:
    def __init__(self, kv, batches):
        self.rows = kv.shape[0] // batches
        span = lax.axis_size("seq")
        self.span = span
        self.relay = span == 4 and batches == 2
        if self.relay:
            one, two = swap(kv, "seq", 1), swap(kv, "seq", 2)
            self.arrays = [kv, one, two, swap(one[: self.rows], "seq", 2),
                           swap(two[self.rows :], "seq", 1)]
        else:
            self.arrays = [kv] + [swap(kv, "seq", s) for s in range(1, span)]

    def at(self, n, s):
        return (3 + n, 0) if self.relay and s == 3 else (s, n * self.rows)

    def copy(self, refs, n, s, place, dst, sem):
        i, row = self.at(n, s)
        to = pl.multiple_of((place ^ s) * self.rows, self.rows)
        return pltpu.make_async_copy(refs[i].at[pl.ds(row, self.rows)],
                                     dst.at[pl.ds(to, self.rows), :], sem)


def attend_kernel(*refs, group, head_dim, tile, block):
    where, lengths_ref, q_ref = refs[:3]
    kvs = refs[3 : 3 + len(group.arrays)]
    span = group.span
    o_ref, lse_ref, kv_ref, vt_ref, acc_ref, sem = refs[-6:]
    heads = q_ref.shape[1] // head_dim
    rows = q_ref.shape[0]
    m = pl.program_id(0)
    place = where[1]
    base = place * rows
    lengths = [lengths_ref[m, d] for d in range(lengths_ref.shape[1])]

    def first(t):
        return lax.div(begin_of(base + t * tile, lengths), block)

    def copy(n, s):
        return group.copy(kvs, n, s, place, kv_ref.at[n], sem.at[n, s])

    @pl.when(m == 0)
    def _():
        for n in range(kv_ref.shape[0]):
            for s in range(span):
                pl.when((place ^ s) <= place)(lambda n=n, s=s: copy(n, s).start())

    for n in range(kv_ref.shape[0]):
        for s in range(span):
            pl.when((m == n) & ((place ^ s) <= place))(lambda n=n, s=s: copy(n, s).wait())

    def flip(kb, carry):
        at = pl.ds(pl.multiple_of(kb * block, block), block)
        vt_ref[:, at] = kv_ref[m, at, head_dim:].T
        return carry

    lax.fori_loop(first(0), lax.div(base + rows + block - 1, block), flip, 0)
    for t in range(rows // tile):
        q_rows = slice(t * tile, (t + 1) * tile)
        high = base + t * tile + lax.broadcasted_iota(jnp.int32, (1, tile), 1)
        low = begin_of(high, lengths)
        acc_ref[...] = jnp.zeros_like(acc_ref)

        def visit(kb, carry):
            at = pl.ds(pl.multiple_of(kb * block, block), block)
            keys = kv_ref[m, at, :head_dim]
            vt = vt_ref[:, at]
            index = kb * block + lax.broadcasted_iota(jnp.int32, (block, tile), 0)
            mask = (index >= low) & (index <= high)
            out = []
            for h in range(heads):
                peak, total = carry[h]
                s = mm_nt(keys, q_ref[q_rows, h * head_dim : (h + 1) * head_dim])
                s = jnp.where(mask, s, -jnp.inf)
                new_peak = jnp.maximum(peak, jnp.max(s, axis=0, keepdims=True))
                factor = jnp.exp(peak - new_peak)
                p = jnp.exp(s - new_peak)
                total = total * factor + jnp.sum(p, axis=0, keepdims=True)
                acc_ref[h] = acc_ref[h] * factor + mm(vt, p.astype(BF16))
                out.append((new_peak, total))
            return tuple(out)

        start = tuple(
            (jnp.full((1, tile), LOWEST, F32), jnp.zeros((1, tile), F32)) for _ in range(heads)
        )
        stats = lax.fori_loop(first(t), lax.div(base + (t + 1) * tile + block - 1, block), visit,
                              start)
        for h in range(heads):
            peak, total = stats[h]
            o_ref[q_rows, h * head_dim : (h + 1) * head_dim] = (acc_ref[h] / total).T.astype(BF16)
            lse_ref[0, h : h + 1, q_rows] = peak + jnp.log(total)


def attend(where, lengths, q, group, head_dim, tile, block):
    total, q_cols = q.shape
    batches = lengths.shape[0]
    rows = total // batches
    heads = q_cols // head_dim
    span = group.span
    return pl.pallas_call(
        functools.partial(attend_kernel, group=group, head_dim=head_dim, tile=tile, block=block),
        grid=(batches,),
        in_specs=[SMEM, SMEM, rows_of(rows, q_cols)] + [ANY] * len(group.arrays),
        out_specs=[rows_of(rows, q_cols), pl.BlockSpec((1, heads, rows), lambda i: (i, 0, 0))],
        out_shape=[like(q.shape, BF16), like((batches, heads, rows), F32)],
        scratch_shapes=[pltpu.VMEM((batches, span * rows, 2 * head_dim), BF16),
                        pltpu.VMEM((head_dim, span * rows), BF16),
                        pltpu.VMEM((heads, head_dim, tile), F32),
                        pltpu.SemaphoreType.DMA((batches, span))],
        compiler_params=params(),
        cost_estimate=took(18),
        name="attend",
    )(where, lengths, q, *group.arrays)


def middle_kernel(*refs, held, head_dim, chunk):
    x_ref, attn_ref, g_ref, gains_ref = refs[:4]
    if held is None:
        w_ref, wd_ref, wo_ref = refs[4:7]
    else:
        w_ref, wd_ref, wo_ref, rest_ref, sem = refs[-5:]
    (out_ref, mid_grad_ref, branch_ref, attn_grad_ref, delta_ref, low_ref, hidden_ref, grads_ref,
     gain_grad_ref) = refs[5:14] if held is not None else refs[7:16]

    @pl.when(pl.program_id(0) == 0)
    def _():
        if held is not None:
            f = Fetch(held.copies(refs[4], w_ref, rest_ref), sem)
            f.wait(*range(held.span))
            held.unfold(rest_ref, [None, wo_ref])
        gain_grad_ref[...] = jnp.zeros_like(gain_grad_ref)

    gain = gains_ref[1:2, :]
    attn = attn_ref[...]
    middle = x_ref[...].astype(F32) + mm(attn, wo_ref[...])
    inv = lax.rsqrt(jnp.mean(middle * middle, axis=-1, keepdims=True) + EPSILON)
    unit = middle * inv
    low = (unit * gain).astype(BF16)
    low_ref[...] = low
    if held is not None:
        @pl.when(pl.program_id(0) == 0)
        def _():
            held.unfold(rest_ref, [wd_ref, None])
            copies = held.copies(refs[4], w_ref, rest_ref)
            for i in range(held.span, 2 * held.span):
                pltpu.make_async_copy(*copies[i], sem.at[i]).wait()

    grad = g_ref[...]
    result = middle
    back = jnp.zeros_like(middle)
    wide = wd_ref.shape[0]
    for c in range(wide // chunk):
        at = slice(c * chunk, (c + 1) * chunk)
        to = slice(wide + c * chunk, wide + (c + 1) * chunk)
        gate = mm(low, w_ref[:, at])
        lift = mm(low, w_ref[:, to])
        square = gate * gate
        bend = jnp.tanh(GELU_C * gate * (1.0 + GELU_A * square))
        cdf = 0.5 * (1.0 + bend)
        gelu = gate * cdf
        hidden = (gelu * lift).astype(BF16)
        hidden_ref[:, at] = hidden
        result = result + mm(hidden, wd_ref[at, :])
        hidden_grad = mm_nt(grad, wd_ref[at, :])
        slope = cdf + (0.5 * GELU_C) * gate * (1.0 - bend * bend) * (1.0 + 3.0 * GELU_A * square)
        gate_grad = (hidden_grad * lift * slope).astype(BF16)
        lift_grad = (hidden_grad * gelu).astype(BF16)
        grads_ref[:, at] = gate_grad
        grads_ref[:, to] = lift_grad
        back = back + mm_nt(gate_grad, w_ref[:, at]) + mm_nt(lift_grad, w_ref[:, to])
    out_ref[...] = result.astype(BF16)
    gain_grad_ref[...] += jnp.sum(unit * back, axis=0, keepdims=True)
    scaled = back * gain
    mid_grad = grad.astype(F32) + inv * (
        scaled - unit * jnp.mean(unit * scaled, axis=-1, keepdims=True)
    )
    mid_grad_ref[...] = mid_grad
    branch = mid_grad.astype(BF16)
    branch_ref[...] = branch
    attn_grad = mm_nt(branch, wo_ref[...]).astype(BF16)
    attn_grad_ref[...] = attn_grad
    product = attn_grad.astype(F32) * attn.astype(F32)
    half = head_dim // 2
    for h in range(attn.shape[1] // head_dim):
        c = h * head_dim
        folded = product[:, c : c + half] + product[:, c + half : c + head_dim]
        delta_ref[h : h + 1, :] = jnp.sum(folded.T, axis=0, keepdims=True)


def middle_part(x, attn, grad, gains, held, weights, head_dim):
    rows, width = x.shape
    q_cols = attn.shape[1]
    hidden = (weights[0].shape if held is None else held.shape)[1] // 2
    heads = q_cols // head_dim
    tile = math.gcd(rows, 512)
    if held is None:
        more, specs, scratch = weights, [full(w.shape) for w in weights], []
    else:
        more, specs = [held.array], [ANY]
        scratch = [pltpu.VMEM(held.shape, BF16)] + [pltpu.VMEM(s, BF16) for s in held.shapes]
        scratch += [pltpu.VMEM(held.scratch, BF16), pltpu.SemaphoreType.DMA((2 * held.span,))]
    return pl.pallas_call(
        functools.partial(middle_kernel, held=held, head_dim=head_dim, chunk=512),
        grid=(rows // tile,),
        in_specs=[rows_of(tile, width), rows_of(tile, q_cols), rows_of(tile, width),
                  full(gains.shape)] + specs,
        out_specs=[rows_of(tile, width), rows_of(tile, width), rows_of(tile, width),
                   rows_of(tile, q_cols), pl.BlockSpec((heads, tile), lambda i: (0, i)),
                   rows_of(tile, width), rows_of(tile, hidden), rows_of(tile, 2 * hidden),
                   full((1, width))],
        out_shape=[like((rows, width), BF16), like((rows, width), F32), like((rows, width), BF16),
                   like((rows, q_cols), BF16), like((heads, rows), F32),
                   like((rows, width), BF16), like((rows, hidden), BF16),
                   like((rows, 2 * hidden), BF16), like((1, width), F32)],
        scratch_shapes=scratch,
        compiler_params=params(),
        cost_estimate=took(39),
        name="middle",
    )(x, attn, grad, gains, *more)


def attend_back_kernel(*refs, group, head_dim, block, scale, m):
    where, lengths_ref, lse_ref, delta_ref, q_ref, do_ref, cos_ref, sin_ref = refs[:8]
    kvs, span = refs[8 : 8 + len(group.arrays)], group.span
    kv_ref, kt_ref, acc_ref, sem = refs[-4:]
    sends = refs[-4 - (span - 1) : -4]
    dq_ref, own_ref = refs[-4 - span - 1 : -4 - span + 1]
    heads = q_ref.shape[1] // head_dim
    half = head_dim // 2
    rows = q_ref.shape[0]
    place = where[1]
    base = place * rows
    lengths = [lengths_ref[m, d] for d in range(lengths_ref.shape[1])]

    def copy(s):
        return group.copy(kvs, m, s, place, kv_ref, sem.at[s])

    for s in range(span):
        pl.when((place ^ s) <= place)(lambda s=s: copy(s).start())
    acc_ref[...] = jnp.zeros_like(acc_ref)
    for s in range(span):
        pl.when((place ^ s) <= place)(lambda s=s: copy(s).wait())
    index = lax.broadcasted_iota(jnp.int32, (block, rows), 0)
    high = base + lax.broadcasted_iota(jnp.int32, (1, rows), 1)
    low = begin_of(high, lengths)
    count = rows // block

    def visit(kb, carry):
        at = pl.ds(pl.multiple_of(kb * block, block), block)
        keys = kv_ref[at, :head_dim]
        vals = kv_ref[at, head_dim:]
        kt_ref[...] = keys.T
        here = kb * block + index
        mask = (here >= low) & (here <= high)
        dk = jnp.zeros((block, head_dim), F32)
        dv = jnp.zeros((block, head_dim), F32)
        for h in range(heads):
            cols = slice(h * head_dim, (h + 1) * head_dim)
            q = q_ref[:, cols]
            do = do_ref[:, cols]
            s = mm_nt(keys, q)
            p = jnp.where(mask, jnp.exp(s - lse_ref[0, h : h + 1, :]), 0.0)
            dv = dv + mm(p.astype(BF16), do)
            ds = (p * (mm_nt(vals, do) - delta_ref[h : h + 1, :])).astype(BF16)
            dk = dk + mm(ds, q)
            acc_ref[h] += mm(kt_ref[...], ds)
        owner = lax.div(kb, count)
        to = pl.ds(pl.multiple_of((kb - owner * count) * block, block), block)

        def put(ref):
            ref[to, :head_dim] = dk.astype(ref.dtype)
            ref[to, head_dim:] = dv.astype(ref.dtype)

        pl.when(owner == place)(lambda: put(own_ref))
        for s, ref in enumerate(sends, 1):
            pl.when(owner == (place ^ s))(lambda ref=ref: put(ref))
        return carry

    begin = lax.div(begin_of(base, lengths), block)
    for s, ref in enumerate([own_ref, *sends]):
        @pl.when(((place ^ s) > place) | ((place ^ s) * count < begin))
        def _():
            ref[...] = jnp.zeros_like(ref)

    lax.fori_loop(begin, (place + 1) * count, visit, 0)
    cos, sin = cos_ref[...], sin_ref[...]
    for h in range(heads):
        c = h * head_dim
        dq = acc_ref[h].T * scale
        a, b = dq[:, :half], dq[:, half:]
        dq_ref[:, c : c + half] = (a * cos + b * sin).astype(BF16)
        dq_ref[:, c + half : c + head_dim] = (b * cos - a * sin).astype(BF16)


def attend_back(where, lengths, lse, delta, q, do, group, cos, sin, head_dim, block, scale, m,
                before, later):
    q_cols = q.shape[1]
    rows = q.shape[0] // lengths.shape[0]
    heads = q_cols // head_dim
    span, n = group.span, len(group.arrays)
    tokens = span * rows
    half = head_dim // 2
    here = pl.BlockSpec((rows, q_cols), lambda i: (m, 0))
    angle = pl.BlockSpec((rows, half), lambda i: (m, 0))
    more = ([] if before is None else [before]) + later
    return pl.pallas_call(
        functools.partial(attend_back_kernel, group=group, head_dim=head_dim, block=block,
                          scale=scale, m=m),
        grid=(1,),
        in_specs=[SMEM, SMEM, pl.BlockSpec((1, heads, rows), lambda i: (m, 0, 0)),
                  pl.BlockSpec((heads, rows), lambda i: (0, m)), here, here, angle, angle]
        + [ANY] * (n + len(more)),
        out_specs=[here] + [VMEM] * span,
        out_shape=[like(q.shape, BF16), like((rows, 2 * head_dim), F32)]
        + [like((rows, 2 * head_dim), BF16)] * (span - 1),
        scratch_shapes=[pltpu.VMEM((tokens, 2 * head_dim), BF16),
                        pltpu.VMEM((head_dim, block), BF16),
                        pltpu.VMEM((heads, head_dim, rows), F32),
                        pltpu.SemaphoreType.DMA((span,))],
        input_output_aliases={} if before is None else {8 + n: 0},
        compiler_params=params(),
        cost_estimate=cost(LONG, 1),
        name="attend_back",
    )(where, lengths, lse, delta, q, do, cos, sin, *group.arrays, *more)


def query_back_kernel(dq_ref, w_ref, ww_ref, lora_grad_ref, back_ref, *, q_cols, mid):
    dq = dq_ref[...]
    lora_grad = mm_nt(dq, ww_ref[...]).astype(BF16)
    lora_grad_ref[...] = lora_grad
    back_ref[...] = (mm_nt(dq, w_ref[:, :q_cols])
                     + mm_nt(lora_grad, w_ref[:, q_cols : q_cols + mid]))


def query_back(dq, w, ww, later=()):
    rows, q_cols = dq.shape
    mid, width = ww.shape[0], w.shape[0]
    tile = math.gcd(rows, 256)
    return pl.pallas_call(
        skipping(functools.partial(query_back_kernel, q_cols=q_cols, mid=mid), 3, len(later)),
        grid=(rows // tile,),
        in_specs=[rows_of(tile, q_cols), full(w.shape), full(ww.shape)] + [ANY] * len(later),
        out_specs=[rows_of(tile, mid), rows_of(tile, width)],
        out_shape=[like((rows, mid), BF16), like((rows, width), F32)],
        compiler_params=params(),
        cost_estimate=cost(2 * rows * (width * (q_cols + mid) + mid * q_cols), 9e6),
        name="query_back",
    )(dq, w, ww, *later)


def pair_back_kernel(*refs, head_dim, others):
    x_ref, gains_ref, cos_ref, sin_ref, w_ref, back_ref, mid_grad_ref, own_ref = refs[:8]
    pair_grad_ref, in_grad_ref, gain_grad_ref = refs[-3:]

    @pl.when(pl.program_id(0) == 0)
    def _():
        gain_grad_ref[...] = jnp.zeros_like(gain_grad_ref)

    half = head_dim // 2
    gain = gains_ref[0:1, :]
    cos, sin = cos_ref[...], sin_ref[...]
    dkv = own_ref[...]
    for ref in refs[8 : 8 + others]:
        dkv = dkv + ref[...].astype(F32)
    a, b = dkv[:, :half], dkv[:, half:head_dim]
    pair_grad_ref[:, :half] = (a * cos + b * sin).astype(BF16)
    pair_grad_ref[:, half:head_dim] = (b * cos - a * sin).astype(BF16)
    pair_grad_ref[:, head_dim:] = dkv[:, head_dim:].astype(BF16)
    back = back_ref[...] + mm_nt(pair_grad_ref[...], w_ref[:, : 2 * head_dim])
    x = x_ref[...].astype(F32)
    inv = lax.rsqrt(jnp.mean(x * x, axis=-1, keepdims=True) + EPSILON)
    unit = x * inv
    gain_grad_ref[...] += jnp.sum(unit * back, axis=0, keepdims=True)
    scaled = back * gain
    in_grad_ref[...] = mid_grad_ref[...] + inv * (
        scaled - unit * jnp.mean(unit * scaled, axis=-1, keepdims=True)
    )


def pair_back(x, gains, cos, sin, w, own, others, back, mid_grad, head_dim, m, batches, before=None,
              later=()):
    width = x.shape[1]
    rows = x.shape[0] // batches
    tile = math.gcd(rows, 256)
    half, cols = head_dim // 2, 2 * head_dim
    count = rows // tile

    def here(n):
        return pl.BlockSpec((tile, n), lambda i: (m * count + i, 0))

    more = ([] if before is None else [before]) + list(later)
    return pl.pallas_call(
        functools.partial(pair_back_kernel, head_dim=head_dim, others=len(others)),
        grid=(count,),
        in_specs=[here(width), full(gains.shape), here(half), here(half), full(w.shape),
                  here(width), here(width)] + [rows_of(tile, cols)] * (1 + len(others))
        + [ANY] * len(more),
        out_specs=[rows_of(tile, cols), here(width), full((1, width))],
        out_shape=[like((rows, cols), BF16), like(x.shape, F32), like((1, width), F32)],
        input_output_aliases={} if before is None else {8 + len(others): 1},
        compiler_params=params(),
        cost_estimate=cost(2 * rows * width * cols, 7e6),
        name="pair_back",
    )(x, gains, cos, sin, w, back, mid_grad, own, *others, *more)


def weight_grad_kernel(x_ref, y_ref, out_ref):
    out_ref[...] = mm_tn(x_ref[...], y_ref[...]).astype(BF16)


def weight_grad(x, y, tile=256, later=()):
    rows, width = x.shape
    cols = y.shape[1]
    tile = math.gcd(cols, tile)
    return pl.pallas_call(
        skipping(weight_grad_kernel, 2, len(later)),
        grid=(cols // tile,),
        in_specs=[full(x.shape), pl.BlockSpec((rows, tile), lambda i: (0, i))] + [ANY] * len(later),
        out_specs=pl.BlockSpec((width, tile), lambda i: (0, i)),
        out_shape=like((width, cols), BF16),
        compiler_params=params(),
        cost_estimate=took(10),
        name="weight_grad",
    )(x, y, *later)


def turn(x_ref, flat_ref, xt_ref, me, parts):
    flat_ref[...] = x_ref[...].T
    piece = flat_ref.shape[0] // parts
    for r in range(parts):
        at = pl.multiple_of((me ^ r) * piece, piece)
        to = (r % 2) * (parts // 2) + r // 2
        xt_ref[to * piece : (to + 1) * piece, :] = flat_ref[pl.ds(at, piece), :]


def column_grads_kernel(where, g_in, hidden_in, b_in, attn_in, keep_ref, send_ref, g_ref, hidden_ref,
                        b_ref, attn_ref, sem, *, parts):
    f = Fetch([(g_in, g_ref), (hidden_in, hidden_ref), (b_in, b_ref), (attn_in, attn_ref)], sem)
    span, _, piece, _ = keep_ref.shape
    per = parts // span
    col = 0
    for pair, x_ref, y_ref in (((0, 1), g_ref, hidden_ref), ((2, 3), b_ref, attn_ref)):
        n = y_ref.shape[1] // parts
        f.wait(pair[0])
        f.wait(pair[1])
        for r in range(parts):
            at = pl.multiple_of((where[0] ^ r) * n, n)
            out = mm_tn(x_ref[...], y_ref[:, pl.ds(at, n)]).astype(BF16)
            ref = send_ref if r % 2 else keep_ref
            for s in range(span):
                for i in range(per):
                    ref[s ^ where[1], r // 2, :, col + i * n : col + (i + 1) * n] = out[
                        (s * per + i) * piece : (s * per + i + 1) * piece]
        col += per * n


def column_grads(where, grad, hidden, branch, attn, parts, span):
    rows, width = grad.shape
    piece = width // parts
    cols = (hidden.shape[1] + attn.shape[1]) // span
    shape = like((span, parts // 2, piece, cols), BF16)
    arrays = (grad, hidden, branch, attn)
    return pl.pallas_call(
        functools.partial(column_grads_kernel, parts=parts),
        in_specs=[SMEM] + [ANY] * 4,
        out_specs=[VMEM] * 2,
        out_shape=[shape, shape],
        scratch_shapes=[pltpu.VMEM(a.shape, BF16) for a in arrays]
        + [pltpu.SemaphoreType.DMA((4,))],
        compiler_params=params(),
        cost_estimate=took(9),
        name="column_grads",
    )(where, *arrays)


def unrotate(dkv, cos, sin, head_dim):
    half = head_dim // 2
    a, b = dkv[:, :half], dkv[:, half:head_dim]
    return jnp.concatenate([a * cos + b * sin, b * cos - a * sin, dkv[:, head_dim:]],
                           axis=1).astype(BF16)


def norm_back(x, gain, back, rest):
    inv = lax.rsqrt(jnp.mean(x * x, axis=-1, keepdims=True) + EPSILON)
    unit = x * inv
    scaled = back * gain
    return (rest + inv * (scaled - unit * jnp.mean(unit * scaled, axis=-1, keepdims=True)),
            jnp.sum(unit * back, axis=0, keepdims=True))


def fold_rows(out_ref, value, first, parts, piece, fold, j):
    count = value.shape[0] // parts
    for d in range(parts):
        at = d * piece + j * count
        out_ref[at : at + count, first : first + fold] = value[d * count : (d + 1) * count]


def query_side_kernel(dq_in, ww_in, normed_in, lora_in, queries_ref, lora_grad_ref, dq, ww, normed,
                      lora, sem, *, parts, fold):
    f = Fetch([(dq_in, dq), (ww_in, ww), (normed_in, normed), (lora_in, lora)], sem)
    q_cols, mid = dq.shape[1], lora.shape[1]
    f.wait(0, 1)
    lora_grad = mm_nt(dq[...], ww[...]).astype(BF16)
    lora_grad_ref[...] = lora_grad
    f.wait(2, 3)
    step = math.gcd(q_cols, 512)
    turned = normed[...].T
    for c in range(0, q_cols, step):
        queries_ref[:, c : c + step] = mm(turned, dq[:, c : c + step]).astype(BF16)
    queries_ref[:, q_cols : q_cols + mid] = mm(turned, lora_grad).astype(BF16)
    piece, count = normed.shape[1] // parts, mid // parts
    turned = lora[...].T
    for j in range(q_cols // fold):
        out = mm(turned, dq[:, j * fold : (j + 1) * fold]).astype(BF16)
        fold_rows(queries_ref, out, q_cols + mid, parts, piece, fold, j)
    rest = (q_cols // fold) * count
    for d in range(parts):
        queries_ref[d * piece + rest : (d + 1) * piece, q_cols + mid :] = jnp.zeros(
            (piece - rest, fold), BF16)


def query_side(dq, ww, normed, lora_mid, parts, fold, later):
    total, q_cols = dq.shape
    width, mid = normed.shape[1], lora_mid.shape[1]
    arrays = (dq, ww, normed, lora_mid)
    return pl.pallas_call(
        skipping(functools.partial(query_side_kernel, parts=parts, fold=fold), 4, len(later)),
        in_specs=[ANY] * (4 + len(later)),
        out_specs=[VMEM] * 2,
        out_shape=[like((width, q_cols + mid + fold), BF16), like((total, mid), BF16)],
        scratch_shapes=[pltpu.VMEM(a.shape, BF16) for a in arrays]
        + [pltpu.SemaphoreType.DMA((4,))],
        compiler_params=params(),
        cost_estimate=cost(LONG, 1),
        name="query_side",
    )(*arrays, *later)


def first_side_kernel(*refs, head_dim, others):
    (dq_in, w_in, lora_in, own_in, wp_in, x_in, mg_in, gains_ref, cos_ref, sin_ref, keep_ref,
     got_ref) = refs[:12]
    others_in = refs[12 : 12 + others]
    (back_ref, pair_ref, in_grad_ref, one_ref, near_ref, far_ref,
     dq, w, lora, own, wp, x, mg, there, hold, sem) = refs[12 + others :]
    rows = x.shape[0]
    f = Fetch([(dq_in, dq), (w_in, w), (lora_in, lora), (own_in, own), (wp_in, wp),
               (x_in.at[pl.ds(0, rows)], x), (mg_in.at[pl.ds(0, rows)], mg)]
              + [(r, there.at[i]) for i, r in enumerate(others_in)], sem)
    near_ref[...] = (keep_ref[0].astype(F32) + got_ref[0].astype(F32)).astype(BF16)
    far_ref[...] = (keep_ref[1].astype(F32) + got_ref[1].astype(F32)).astype(BF16)
    q_cols, mid = dq.shape[1], lora.shape[1]
    f.wait(0, 1, 2)
    for m in range(dq.shape[0] // rows):
        at = slice(m * rows, (m + 1) * rows)
        back = mm_nt(dq[at, :], w[:, :q_cols]) + mm_nt(lora[at, :], w[:, q_cols : q_cols + mid])
        if m == 0:
            hold[...] = back
        else:
            back_ref[(m - 1) * rows : m * rows] = back
    f.wait(*range(3, 7 + others))
    dkv = own[...]
    for i in range(others):
        dkv = dkv + there[i].astype(F32)
    pair = unrotate(dkv, cos_ref[...], sin_ref[...], head_dim)
    pair_ref[...] = pair
    back = hold[...] + mm_nt(pair, wp[:, : 2 * head_dim])
    in_grad_ref[...], one_ref[...] = norm_back(x[...].astype(F32), gains_ref[0:1, :], back, mg[...])


def first_side(dq, w, lora_grad, own, others, w_pair, x, mid_grad, gains, cos, sin, keep, got,
               head_dim, batches, later):
    total = dq.shape[0]
    rows = total // batches
    width, mid = x.shape[1], lora_grad.shape[1]
    half, cols = head_dim // 2, 2 * head_dim
    angle = pl.BlockSpec((rows, half), lambda i: (0, 0))
    n = len(others)
    return pl.pallas_call(
        skipping(functools.partial(first_side_kernel, head_dim=head_dim, others=n), 12 + n,
                 len(later)),
        grid=(1,),
        in_specs=[ANY] * 7 + [VMEM, angle, angle, VMEM, VMEM] + [ANY] * (n + len(later)),
        out_specs=[VMEM] * 2 + [pl.BlockSpec((rows, width), lambda i: (0, 0))] + [VMEM] * 3,
        out_shape=[like((total - rows, width), F32), like((rows, cols), BF16),
                   like((total, width), F32), like((1, width), F32)]
        + [like(keep.shape[1:], BF16)] * 2,
        scratch_shapes=[pltpu.VMEM(dq.shape, BF16), pltpu.VMEM(w.shape, BF16),
                        pltpu.VMEM(lora_grad.shape, BF16), pltpu.VMEM((rows, cols), F32),
                        pltpu.VMEM(w_pair.shape, BF16), pltpu.VMEM((rows, width), BF16),
                        pltpu.VMEM((rows, width), F32), pltpu.VMEM((n, rows, cols), BF16),
                        pltpu.VMEM((rows, width), F32), pltpu.SemaphoreType.DMA((7 + n,))],
        compiler_params=params(),
        cost_estimate=cost(1, 1),
        name="first_side",
    )(dq, w, lora_grad, own, w_pair, x, mid_grad, gains, cos, sin, keep, got, *others, *later)


def pair_side_kernel(*refs, head_dim, parts, others):
    (where, own_in, wp_in, back_in, x_in, mg_in, normed_in, first_in, gains_ref, cos_ref, sin_ref,
     one_ref, two_ref) = refs[:13]
    others_in = refs[13 : 13 + others]
    outs = refs[14 + others :]
    in_grad_ref, send_ref = outs[:2]
    keeps = outs[2 : 2 + parts // 2]
    (own, wp, back, x, mg, normed, pair_ref, there, flat_ref, xt_ref, gain_ref,
     sem) = outs[2 + parts // 2 :]
    rows = x.shape[0]
    f = Fetch([(normed_in, normed), (own_in, own)]
              + [(r, there.at[i]) for i, r in enumerate(others_in)]
              + [(first_in, pair_ref.at[pl.ds(0, rows)]), (wp_in, wp), (back_in, back),
                 (x_in.at[pl.ds(rows, rows)], x), (mg_in.at[pl.ds(rows, rows)], mg)], sem)
    f.wait(0)
    turn(normed, flat_ref, xt_ref, where[0], parts)
    f.wait(*range(1, 2 + others))
    dkv = own[...]
    for i in range(others):
        dkv = dkv + there[i].astype(F32)
    pair = unrotate(dkv, cos_ref[...], sin_ref[...], head_dim)
    pair_ref[rows:, :] = pair
    f.wait(*range(2 + others, 7 + others))
    grads = back[...] + mm_nt(pair, wp[:, : 2 * head_dim])
    in_grad_ref[...], one = norm_back(x[...].astype(F32), gains_ref[0:1, :], grads, mg[...])
    width = flat_ref.shape[0]
    piece, half, cols = width // parts, parts // 2, 2 * head_dim
    out = mm(xt_ref[...], pair_ref[...]).astype(BF16)
    pad = jnp.zeros((126, width), F32)
    gain_ref[...] = jnp.concatenate([one + one_ref[...], two_ref[...], pad], axis=0).T.astype(BF16)
    for k in range(half):
        keeps[k][:, :cols] = out[k * piece : (k + 1) * piece]
        send_ref[k, :, :cols] = out[(half + k) * piece : (half + k + 1) * piece]
        at = pl.multiple_of((where[0] ^ (2 * k)) * piece, piece)
        keeps[k][:, cols:] = gain_ref[pl.ds(at, piece), :]
        at = pl.multiple_of((where[0] ^ (2 * k + 1)) * piece, piece)
        send_ref[k, :, cols:] = gain_ref[pl.ds(at, piece), :]


def pair_side(where, own, others, w_pair, back, x, mid_grad, normed, first, gains, cos, sin, one,
              two, in_grad, head_dim, parts):
    total, width = normed.shape
    rows = total // 2
    half, cols = head_dim // 2, 2 * head_dim
    piece = width // parts
    angle = pl.BlockSpec((rows, half), lambda i: (1, 0))
    n = len(others)
    return pl.pallas_call(
        functools.partial(pair_side_kernel, head_dim=head_dim, parts=parts, others=n),
        grid=(1,),
        in_specs=[SMEM] + [ANY] * 7 + [VMEM, angle, angle, VMEM, VMEM] + [ANY] * (n + 1),
        out_specs=[pl.BlockSpec((rows, width), lambda i: (1, 0))] + [VMEM] * (1 + parts // 2),
        out_shape=[like((total, width), F32), like((parts // 2, piece, cols + 128), BF16)]
        + [like((piece, cols + 128), BF16)] * (parts // 2),
        scratch_shapes=[pltpu.VMEM((rows, cols), F32), pltpu.VMEM(w_pair.shape, BF16),
                        pltpu.VMEM((rows, width), F32), pltpu.VMEM((rows, width), BF16),
                        pltpu.VMEM((rows, width), F32), pltpu.VMEM(normed.shape, BF16),
                        pltpu.VMEM((total, cols), BF16), pltpu.VMEM((n, rows, cols), BF16),
                        pltpu.VMEM((width, total), BF16), pltpu.VMEM((width, total), BF16),
                        pltpu.VMEM((width, 128), BF16), pltpu.SemaphoreType.DMA((7 + n,))],
        input_output_aliases={13 + n: 0},
        compiler_params=params(),
        cost_estimate=cost(LONG, 12e6),
        name="pair_side",
    )(where, own, w_pair, back, x, mid_grad, normed, first, gains, cos, sin, one, two, *others,
      in_grad)


def join_kernel(left_ref, *refs):
    out_ref = refs[-1]
    n = left_ref.shape[1]
    out_ref[:, :n] = left_ref[...]
    out_ref[:, n:] = tree([r[...].astype(F32) for r in refs[:-1]]).astype(BF16)


def join(left, parts):
    rows, n = left.shape
    arrays = [left, *parts]
    return pl.pallas_call(
        fetched(join_kernel, len(arrays)),
        in_specs=[ANY] * len(arrays),
        out_specs=VMEM,
        out_shape=like((rows, n + parts[0].shape[1]), BF16),
        scratch_shapes=room(arrays),
        compiler_params=params(),
        cost_estimate=took(2),
        name="join",
    )(*arrays)


def finish_kernel(*refs, mid, q_cols, cols, fold):
    parts, outs = refs[:-6], refs[-6:]
    query_ref, narrow_ref, widen_ref, kv_ref, one_ref, two_ref = outs
    total = tree([p[...].astype(F32) for p in parts])
    query_ref[...] = total[:, :q_cols]
    narrow_ref[...] = total[:, q_cols : q_cols + mid]
    first = q_cols + mid
    count = widen_ref.shape[0]
    for j in range(q_cols // fold):
        widen_ref[:, j * fold : (j + 1) * fold] = total[j * count : (j + 1) * count,
                                                        first : first + fold]
    first += fold
    kv_ref[...] = total[:, first : first + cols]
    gains = total[:, first + cols :].T
    one_ref[...] = gains[0:1]
    two_ref[...] = gains[1:2]


def finish(parts, q_cols, mid, count, cols, fold):
    piece = parts[0].shape[0]
    return pl.pallas_call(
        fetched(functools.partial(finish_kernel, q_cols=q_cols, mid=mid, cols=cols, fold=fold),
                len(parts)),
        in_specs=[ANY] * len(parts),
        scratch_shapes=room(parts),
        out_specs=[VMEM] * 6,
        out_shape=[like((piece, q_cols), F32), like((piece, mid), F32), like((count, q_cols), F32),
                   like((piece, cols), F32), like((1, piece), F32), like((1, piece), F32)],
        compiler_params=params(),
        cost_estimate=took(2.5),
        name="finish",
    )(*parts)


def swap_cores(keeps, send, later=()):
    got, count = swap(send, "fsdp", 1), len(keeps)
    return add([*keeps, got], [[(k, None), (count, k)] for k in range(count)], later)


def pairs_kernel(*refs):
    parts, (keep_ref, send_ref) = refs[:-2], refs[-2:]
    for i in range(2):
        for k, ref in ((2 * i, keep_ref), (2 * i + 1, send_ref)):
            ref[i] = tree([p[k].astype(F32) for p in parts]).astype(BF16)


def sum_pairs(parts, later=()):
    count, shape = len(parts), like((2,) + parts[0].shape[1:], BF16)
    return pl.pallas_call(
        skipping(pairs_kernel, count, len(later)),
        in_specs=[VMEM] * count + [ANY] * len(later),
        out_specs=[VMEM] * 2,
        out_shape=[shape] * 2,
        compiler_params=params(),
        cost_estimate=took(2.4),
        name="sum_pairs",
    )(*parts, *later)


def cut_kernel(where, x_ref, *outs):
    part = outs[0].shape[1]
    for s, out in enumerate(outs):
        at = pl.multiple_of((where[1] ^ s) * part, part)
        out[...] = x_ref[:, pl.ds(at, part)]


def cut_parts(where, x, later=()):
    span = lax.axis_size("seq")
    rows, part = x.shape[0], x.shape[1] // span
    cut = pl.pallas_call(
        skipping(cut_kernel, 2, len(later)),
        in_specs=[SMEM, VMEM] + [ANY] * len(later),
        out_specs=[VMEM] * span,
        out_shape=[like((rows, part), x.dtype)] * span,
        compiler_params=params(),
        cost_estimate=took(2),
        name="cut",
    )(where, x, *later)
    return cut


def halves_kernel(*refs):
    out_ref = refs[-1]
    n = refs[0].shape[1]
    out_ref[:, :n] = tree([r[...].astype(F32) for r in refs[:-3]]).astype(BF16)
    out_ref[:, n:] = tree([r[...].astype(F32) for r in refs[-3:-1]]).astype(BF16)


def halves(left, right, later=()):
    count = len(left) + 2
    shape = (left[0].shape[0], left[0].shape[1] + right[0].shape[1])
    return pl.pallas_call(
        skipping(halves_kernel, count, len(later)),
        in_specs=[VMEM] * count + [ANY] * len(later),
        out_specs=VMEM,
        out_shape=like(shape, BF16),
        compiler_params=params(),
        cost_estimate=cost(LONG, 2e6),
        name="halves",
    )(*left, *right, *later)


def lay_kernel(where, *refs, n, k):
    parts = refs[:-6]
    span = len(parts)
    gate_ref, up_ref, down_ref, out_ref, tall_ref, tall2_ref = refs[-6:]
    piece = parts[0].shape[0]
    half = span // 2
    wide = gate_ref.shape[1] // half
    per = (parts[0].shape[1] - wide) // (n + k)
    for s, ref in enumerate(parts):
        q = where[1] ^ s
        for i, out in enumerate((gate_ref, up_ref)):
            @pl.when(q // half == i)
            def _():
                at = pl.multiple_of((q % half) * wide, wide)
                out[:, pl.ds(at, wide)] = ref[:, :wide].astype(F32)
        for i in range(per):
            at = pl.ds(pl.multiple_of((q * per + i) * piece, piece), piece)
            first = wide + i * n
            tall_ref[at, :] = ref[:, first : first + n].astype(F32)
            first = wide + per * n + i * k
            tall2_ref[at, :] = ref[:, first : first + k].astype(F32)
    down_ref[...] = tall_ref[...].T
    out_ref[...] = tall2_ref[...].T


def lay(where, parts, hidden, n, k, later=()):
    piece = parts[0].shape[0]
    width = piece * lax.axis_size("fsdp")
    return pl.pallas_call(
        skipping(functools.partial(lay_kernel, n=n, k=k), 1 + len(parts), len(later)),
        in_specs=[SMEM] + [VMEM] * len(parts) + [ANY] * len(later),
        out_specs=[VMEM] * 4,
        out_shape=[like((piece, hidden), F32)] * 2 + [like((n, width), F32), like((k, width), F32)],
        scratch_shapes=[pltpu.VMEM((width, n), F32), pltpu.VMEM((width, k), F32)],
        compiler_params=params(),
        cost_estimate=took(3),
        name="lay",
    )(where, *parts, *later)


def begin_of(index, lengths):
    ends = [lengths[0]]
    for n in lengths[1:]:
        ends.append(ends[-1] + n)
    begin = index
    for d in reversed(range(len(lengths))):
        begin = jnp.where(index < ends[d], ends[d] - lengths[d], begin)
    return begin


def local(tokens, document_lengths, cotangent, attention_gain, query_projection, narrowing_factor,
          widening_factor, key_value_projection, output_projection, feedforward_gain,
          gate_projection, up_projection, down_projection):
    batches, _, rows, width = tokens.shape
    head_dim = key_value_projection.shape[1] // 2
    q_cols = query_projection.shape[1]
    mid = narrowing_factor.shape[1]
    hidden = gate_projection.shape[1]
    kv_cols = 2 * head_dim
    scale = head_dim ** (-0.5)
    parts, span = lax.axis_size("fsdp"), lax.axis_size("seq")
    place = lax.axis_index("seq")
    tile = block = math.gcd(rows, 512)
    where = jnp.stack([lax.axis_index("fsdp"), place]).astype(jnp.int32)
    piece = width // parts
    direct = piece % 16 == 0
    fold = 512
    folds = q_cols // fold

    lengths = document_lengths[:, 0]
    half = head_dim // 2
    index = place * rows + lax.broadcasted_iota(jnp.int32, (batches, rows, half), 1)
    begin = begin_of(index, [lengths[:, d][:, None, None] for d in range(lengths.shape[1])])
    freqs = THETA ** (-(lax.broadcasted_iota(jnp.int32, (1, half), 1).astype(F32) * 2.0 / head_dim))
    angles = ((index - begin).astype(F32) * freqs).reshape(batches * rows, half)
    cos, sin = jnp.cos(angles), jnp.sin(angles)

    if direct:
        first = Shards(pack_pair(key_value_projection, attention_gain, feedforward_gain))
        third = pack(where, gate_projection, up_projection, down_projection, output_projection,
                     span, [cos, sin, first.arrays[parts - 2]])
        held = Tiled(third, 2 * hidden, down_projection, output_projection)
        weights = None
    else:
        def gather(x):
            return lax.all_gather(x, "fsdp", axis=0, tiled=True)

        first = jnp.concatenate(
            [key_value_projection,
             jnp.pad(jnp.stack([attention_gain, feedforward_gain], axis=1), ((0, 0), (0, 126)))],
            axis=1)
        turned = jnp.concatenate(
            [widening_factor[:, j * fold : (j + 1) * fold] for j in range(folds)])
        turned = jnp.pad(turned, ((0, piece - turned.shape[0]), (0, 0)))
        second = jnp.concatenate([query_projection, narrowing_factor, turned], axis=1)
        first, second = Whole(gather(first)), Whole(gather(second))
        second.rows = piece
        held = None
        weights = [gather(jnp.concatenate([gate_projection, up_projection], axis=1)),
                   gather(down_projection), gather(output_projection)]

    x = tokens.reshape(batches * rows, width)
    grad = cotangent.reshape(batches * rows, width)
    normed, kv, w_pair, gains = project_kv(where, x, cos, sin, first, head_dim)
    kvs = Group(kv, batches)
    if direct:
        second = Shards(pack_query(query_projection, narrowing_factor, widening_factor, fold,
                                   [kv]), True)
    lora_mid, q, w_query, ww = project_q(where, normed, cos, sin, second, head_dim, q_cols, mid,
                                         scale, [])
    attended, lse = attend(where, lengths, q, kvs, head_dim, tile, block)
    (output, mid_grad, branch, attn_grad, delta, ffn_low, hidden_low, lift_grads,
     gain_two_grad) = middle_part(x, attended, grad, gains, held, weights, head_dim)

    if direct:
        keep, send = column_grads(where, grad, hidden_low, branch, attended, parts, span)
        got = swap(send, "fsdp", 1)
        lifts = weight_grad(ffn_low, lift_grads, 1024, [keep])
        lifts_sum = lax.psum_scatter(lifts, "fsdp", scatter_dimension=0, tiled=True)
        columns = add([keep, got], [[(0, s), (1, s)] for s in range(span)], [lifts])
        there = exchange(columns)
    dq, owns, others = None, [], []
    for m in range(batches):
        later = []
        if direct and m == 0:
            later = columns
        if direct and m == 1:
            keep, send = sum_pairs(there, [dq])
            got = swap(send, "fsdp", 2)
            later = [keep]
        dq, own, *sends = attend_back(where, lengths, lse, delta, q, attn_grad, kvs, cos, sin,
                                      head_dim, block, scale, m, dq, later)
        owns.append(own)
        others.append(exchange([own, *sends])[1:])
    if direct:
        queries, lora_grad = query_side(dq, ww, normed, lora_mid, parts, fold, [])
        queries_sum = lax.psum_scatter(queries, "fsdp", scatter_dimension=0, tiled=True)
        back, pair, in_grad, one, near, far = first_side(
            dq, w_query, lora_grad, owns[0], others[0], w_pair, x, mid_grad, gains, cos, sin, keep,
            got, head_dim, batches, [queries, lifts_sum])
        in_grad, send, *keeps = pair_side(where, owns[1], others[1], w_pair, back, x, mid_grad,
                                          normed, pair, gains, cos, sin, one, gain_two_grad,
                                          in_grad, head_dim, parts)

        def share(x):
            return exchange([x] * span)

        lifts_cut = cut_parts(where, lifts_sum, [pair])
        lifts_parts = exchange(lifts_cut)
        mine = halves(lifts_parts, [near, swap(far, "fsdp", 4)], [send])
        laid = share(mine)
        shards = swap_cores(keeps, send, [mine])
        mine = join(queries_sum, [shards[0]] + [
            swap(a, "fsdp", 2 * k) for k, a in enumerate(shards) if k > 0])
        last = share(mine)
        gate_grad, up_grad, down_grad, out_grad = lay(
            where, laid, hidden, hidden // parts, q_cols // parts, [mine])
        query_grad, narrow_grad, widen_grad, key_value_grad, one, two = finish(
            last, q_cols, mid, mid // parts, kv_cols, fold)
        gain_one_grad, gain_two_grad = one.reshape(piece), two.reshape(piece)
    else:
        lora_grad, back = query_back(dq, w_query, ww)
        in_grad, pairs, ones = None, [], []
        for m in range(batches):
            pair, in_grad, one = pair_back(x, gains, cos, sin, w_pair, owns[m], others[m], back,
                                           mid_grad, head_dim, m, batches, in_grad)
            pairs.append(pair)
            ones.append(one)

        def scatter(x):
            part = lax.psum_scatter(x.astype(BF16), "fsdp", scatter_dimension=0, tiled=True)
            return lax.psum(part, "seq").astype(F32)

        pair_grad = jnp.concatenate(pairs)
        gain_one_grad = sum(ones)
        down_grad = scatter(weight_grad(grad, hidden_low).T)
        out_grad = scatter(weight_grad(branch, attended).T)
        lift_w = scatter(weight_grad(ffn_low, lift_grads))
        gate_grad, up_grad = lift_w[:, :hidden], lift_w[:, hidden:]
        query_grad = scatter(weight_grad(normed, dq))
        narrow_grad = scatter(weight_grad(normed, lora_grad))
        widen_grad = scatter(weight_grad(lora_mid, dq))
        key_value_grad = scatter(weight_grad(normed, pair_grad))
        gains_grad = scatter(jnp.concatenate([gain_one_grad, gain_two_grad]).T)
        gain_one_grad, gain_two_grad = gains_grad[:, 0], gains_grad[:, 1]
    return (output.reshape(batches, 1, rows, width), in_grad.reshape(batches, 1, rows, width),
            gain_one_grad, query_grad, narrow_grad, widen_grad, key_value_grad, out_grad,
            gain_two_grad, gate_grad, up_grad, down_grad)


def solution(mesh):
    rows = P(None, "fsdp", "seq", None)
    vector, matrix = P("fsdp"), P("fsdp", None)
    in_specs = (rows, P(None, "fsdp", None), rows, vector) + (matrix,) * 5 + (vector,) + (matrix,) * 3
    out_specs = (rows, rows, vector) + (matrix,) * 5 + (vector,) + (matrix,) * 3
    return jax.shard_map(local, mesh=mesh, in_specs=in_specs, out_specs=out_specs, check_vma=False)
```

```python
import functools
import math

import jax
import jax.numpy as jnp
from jax import lax
from jax.experimental import pallas as pl
from jax.experimental.pallas import tpu as pltpu
from jax.sharding import PartitionSpec as P

EPSILON = 1e-06
THETA = 10000.0
F32 = jnp.float32
BF16 = jnp.bfloat16
GELU_C = math.sqrt(2.0 / math.pi)
GELU_A = 0.044715
LOWEST = -1e30
VMEM_LIMIT = 60 * 1024 * 1024
ANY = pl.BlockSpec(memory_space=pl.ANY)
VMEM = pl.BlockSpec(memory_space=pltpu.VMEM)
SMEM = pl.BlockSpec(memory_space=pltpu.SMEM)


def mm(left, right):
    return lax.dot_general(left, right, (((1,), (0,)), ((), ())), preferred_element_type=F32)


def mm_tn(left, right):
    return lax.dot_general(left, right, (((0,), (0,)), ((), ())), preferred_element_type=F32)


def mm_nt(left, right):
    return lax.dot_general(left, right, (((1,), (1,)), ((), ())), preferred_element_type=F32)


def full(shape):
    return pl.BlockSpec(shape, lambda i: (0,) * len(shape))


def rows_of(tile, cols):
    return pl.BlockSpec((tile, cols), lambda i: (i, 0))


def params(**more):
    return pltpu.CompilerParams(vmem_limit_bytes=VMEM_LIMIT, **more)


def cost(flops, bytes_accessed, transcendentals=0):
    return pl.CostEstimate(
        flops=int(flops), bytes_accessed=int(bytes_accessed), transcendentals=int(transcendentals)
    )


def took(us):
    return cost(us * 1.1e9, 1)


LONG = 10**12


def like(shape, dtype):
    return jax.ShapeDtypeStruct(tuple(shape), dtype)


def swap(x, axis, by):
    return lax.ppermute(x, axis, [(i, i ^ by) for i in range(lax.axis_size(axis))])


def exchange(arrays):
    got = {s: swap(arrays[s], "seq", s) for s in reversed(range(1, len(arrays)))}
    return [arrays[0]] + [got[s] for s in range(1, len(arrays))]


def skipping(kernel, first, count):
    return lambda *refs: kernel(*refs[:first], *refs[first + count :])


def tree(values):
    while len(values) > 1:
        values = [values[i] + values[i + 1] for i in range(0, len(values), 2)]
    return values[0]


class Fetch:
    def __init__(self, pairs, sem):
        self.copies = [pltpu.make_async_copy(a, b, sem.at[i]) for i, (a, b) in enumerate(pairs)]
        for c in self.copies:
            c.start()

    def wait(self, *which):
        for i in which:
            self.copies[i].wait()


def fetched(kernel, count):
    def run(*refs):
        held, sem = refs[-1 - count : -1], refs[-1]
        Fetch(list(zip(refs[:count], held)), sem).wait(*range(count))
        kernel(*held, *refs[count : -1 - count])

    return run


def room(arrays):
    return [pltpu.VMEM(a.shape, a.dtype) for a in arrays] + [
        pltpu.SemaphoreType.DMA((len(arrays),))]


def add_kernel(*refs, count, groups):
    for out, group in zip(refs[count:], groups):
        values = [refs[i][...] if k is None else refs[i][k] for i, k in group]
        out[...] = tree([v.astype(F32) for v in values]).astype(out.dtype)


def add(arrays, groups, later=()):
    shapes = [arrays[g[0][0]].shape if g[0][1] is None else arrays[g[0][0]].shape[1:]
              for g in groups]
    count = len(arrays)
    later = list(later)
    kernel = fetched(functools.partial(add_kernel, count=count, groups=groups), count)
    return list(pl.pallas_call(
        skipping(kernel, count, len(later)),
        in_specs=[ANY] * (count + len(later)),
        out_specs=[VMEM] * len(groups),
        out_shape=[like(s, BF16) for s in shapes],
        scratch_shapes=room(arrays),
        compiler_params=params(),
        cost_estimate=took(3.5),
        name="add",
    )(*arrays, *later))


class Whole:
    def __init__(self, array):
        self.arrays = [array]
        self.shape = array.shape
        self.count = 1

    def copies(self, where, refs, dst):
        return [(refs[0], dst)]


class Shards:
    def __init__(self, x, relay=False):
        parts = lax.axis_size("fsdp")
        got = {0: x}
        for r in range(2, parts, 2):
            low = r & -r
            near = relay and r != low
            got[r] = swap(got[r - low], "fsdp", low) if near else swap(x, "fsdp", r)
        for r in range(0, parts, 2):
            got[r + 1] = swap(got[r], "fsdp", 1)
        self.arrays = [got[r] for r in range(parts)]
        self.rows = x.shape[0]
        self.shape = (parts * x.shape[0], x.shape[1])
        self.count = parts

    def copies(self, where, refs, dst):
        out = []
        for r, ref in enumerate(refs):
            at = pl.multiple_of((where[0] ^ r) * self.rows, self.rows)
            out.append((ref, dst.at[pl.ds(at, self.rows), :]))
        return out


def pack_pair_kernel(kv_ref, one_ref, two_ref, out_ref):
    piece, kv_cols = kv_ref.shape
    out_ref[:, :kv_cols] = kv_ref[...]
    pad = jnp.zeros((126, piece), F32)
    gains = jnp.concatenate([one_ref[...].astype(F32), two_ref[...].astype(F32), pad], axis=0)
    out_ref[:, kv_cols:] = gains.T.astype(BF16)


def pack_pair(kv, one, two):
    piece = kv.shape[0]
    return pl.pallas_call(
        pack_pair_kernel,
        in_specs=[VMEM] * 3,
        out_specs=VMEM,
        out_shape=like((piece, kv.shape[1] + 128), BF16),
        compiler_params=params(),
        cost_estimate=took(1.6),
        name="pack_pair",
    )(kv, one.reshape(1, piece), two.reshape(1, piece))


def pack_kernel(where, gate_ref, up_ref, down_ref, out_ref, third_ref, *, span):
    piece = gate_ref.shape[0]
    hidden = gate_ref.shape[1]
    part = 2 * hidden // span
    for s in range(span):
        ref, at = (gate_ref, s * part) if s * part < hidden else (up_ref, s * part - hidden)

        @pl.when(where[1] == s)
        def _():
            third_ref[:, :part] = ref[:, at : at + part]

    col = part
    for ref in (down_ref, out_ref):
        n = ref.shape[0] // span
        for i in range(n // 16):
            row = pl.ds(pl.multiple_of(where[1] * n + 16 * i, 16), 16)
            for j in range(ref.shape[1] // 128):
                third_ref[16 * j : 16 * j + 16, col : col + 128] = ref[row, j * 128 : (j + 1) * 128]
            col += 128


def pack(where, gate, up, down, out, span, later):
    piece = gate.shape[0]
    third = (gate.shape[1] * 2 * piece + (down.shape[0] + out.shape[0]) * down.shape[1]) // span
    return pl.pallas_call(
        skipping(functools.partial(pack_kernel, span=span), 5, len(later)),
        in_specs=[SMEM] + [VMEM] * 4 + [ANY] * len(later),
        out_specs=VMEM,
        out_shape=like((piece, third // piece), BF16),
        compiler_params=params(),
        cost_estimate=took(2),
        name="pack",
    )(where, gate, up, down, out, *later)


def pack_query_kernel(q_ref, narrow_ref, widen_ref, out_ref, *, fold):
    q_cols, mid, count = q_ref.shape[1], narrow_ref.shape[1], widen_ref.shape[0]
    out_ref[:, :q_cols] = q_ref[...]
    out_ref[:, q_cols : q_cols + mid] = narrow_ref[...]
    folds = q_cols // fold
    for j in range(folds):
        out_ref[j * count : (j + 1) * count, q_cols + mid :] = widen_ref[
            :, j * fold : (j + 1) * fold]
    rest = out_ref.shape[0] - folds * count
    out_ref[folds * count :, q_cols + mid :] = jnp.zeros((rest, fold), BF16)


def pack_query(q, narrow, widen, fold, later):
    return pl.pallas_call(
        skipping(functools.partial(pack_query_kernel, fold=fold), 3, len(later)),
        in_specs=[VMEM] * 3 + [ANY] * len(later),
        out_specs=VMEM,
        out_shape=like((q.shape[0], q.shape[1] + narrow.shape[1] + fold), BF16),
        compiler_params=params(),
        cost_estimate=took(1.7),
        name="pack_query",
    )(q, narrow, widen, *later)


class Tiled:
    def __init__(self, packed, gate_up, *tall):
        parts, span = lax.axis_size("fsdp"), lax.axis_size("seq")
        piece = packed.shape[0]
        self.piece, self.part, self.parts, self.span = piece, gate_up // span, parts, span
        self.heights = [t.shape[0] // span for t in tall]
        self.up, self.across = sum(self.heights) // 16, tall[0].shape[1] // 128
        self.array = lax.all_gather(packed, ("seq", "fsdp"), axis=0, tiled=True)
        self.shape = (parts * piece, gate_up)
        self.shapes = [(parts * t.shape[0], t.shape[1]) for t in tall]
        self.scratch = (span, parts * piece, self.up * 128)

    def copies(self, ref, dst, rest):
        height = self.parts * self.piece
        rows = [pl.ds(s * height, height) for s in range(self.span)]
        return [(ref.at[at, pl.ds(self.part, self.up * 128)], rest.at[s])
                for s, at in enumerate(rows)] + [
            (ref.at[at, pl.ds(0, self.part)], dst.at[:, pl.ds(s * self.part, self.part)])
            for s, at in enumerate(rows)]

    def unfold(self, rest, dsts):
        starts, tops = [], 0
        for n in self.heights:
            starts.append(tops)
            tops += n // 16

        def shard(d, carry):
            for s in range(self.span):
                for n, first, dst in zip(self.heights, starts, dsts):
                    if dst is None:
                        continue
                    for i in range(n // 16):
                        at = pl.ds(pl.multiple_of(d * n * self.span + s * n + i * 16, 16), 16)
                        for j in range(self.across):
                            row = pl.ds(pl.multiple_of(d * self.piece + 16 * j, 16), 16)
                            col = (first + i) * 128
                            dst[at, j * 128 : (j + 1) * 128] = rest[s, row, col : col + 128]
            return carry

        lax.fori_loop(0, self.parts, shard, 0)


def carry_out(copies, sem):
    made = [pltpu.make_async_copy(src, dst, sem.at[i]) for i, (src, dst) in enumerate(copies)]
    for c in made:
        c.start()
    for c in made:
        c.wait()


def normalize(x_ref, gains_ref):
    x = x_ref[...].astype(F32)
    inv = lax.rsqrt(jnp.mean(x * x, axis=-1, keepdims=True) + EPSILON)
    return (x * inv * gains_ref[0:1, :]).astype(BF16)


def put_pair(kv_ref, pair, cos, sin, head_dim):
    half = head_dim // 2
    a, b = pair[:, :half], pair[:, half:head_dim]
    kv_ref[:, :half] = (a * cos - b * sin).astype(BF16)
    kv_ref[:, half:head_dim] = (b * cos + a * sin).astype(BF16)
    kv_ref[:, head_dim:] = pair[:, head_dim:].astype(BF16)


def project_kv_kernel(*refs, held, head_dim):
    where, x_ref, cos_ref, sin_ref = refs[:4]
    pieces = refs[4 : 4 + len(held.arrays)]
    normed_ref, kv_ref, w_ref, gains_ref, sem = refs[4 + len(held.arrays) :]
    kv_cols = 2 * head_dim

    @pl.when(pl.program_id(0) == 0)
    def _():
        carry_out(held.copies(where, pieces, w_ref), sem)
        gains_ref[...] = w_ref[:, kv_cols:].astype(F32).T[:8]

    normed = normalize(x_ref, gains_ref)
    normed_ref[...] = normed
    put_pair(kv_ref, mm(normed, w_ref[:, :kv_cols]), cos_ref[...], sin_ref[...], head_dim)


def project_kv(where, x, cos, sin, held, head_dim):
    rows, width = x.shape
    tile = math.gcd(rows, 512)
    half = head_dim // 2
    return pl.pallas_call(
        functools.partial(project_kv_kernel, held=held, head_dim=head_dim),
        grid=(rows // tile,),
        in_specs=[SMEM, rows_of(tile, width), rows_of(tile, half), rows_of(tile, half)]
        + [ANY] * len(held.arrays),
        out_specs=[rows_of(tile, width), rows_of(tile, 2 * head_dim), full(held.shape),
                   full((8, width))],
        out_shape=[like((rows, width), BF16), like((rows, 2 * head_dim), BF16),
                   like(held.shape, BF16), like((8, width), F32)],
        scratch_shapes=[pltpu.SemaphoreType.DMA((held.count,))],
        compiler_params=params(),
        cost_estimate=took(5),
        name="project_kv",
    )(where, x, cos, sin, *held.arrays)


def project_q_kernel(*refs, held, head_dim, q_cols, mid, scale):
    where, normed_ref, cos_ref, sin_ref = refs[:4]
    pieces = refs[4 : 4 + len(held.arrays)]
    lora_ref, q_ref, w_ref, ww_ref, sem = refs[4 + len(held.arrays) :]
    half = head_dim // 2
    fold = held.shape[1] - q_cols - mid
    parts = q_cols // fold

    @pl.when(pl.program_id(0) == 0)
    def _():
        carry_out(held.copies(where, pieces, w_ref), sem)
        shards = held.shape[0] // held.rows
        count = mid // shards
        for d in range(shards):
            for j in range(parts):
                ww_ref[d * count : (d + 1) * count, j * fold : (j + 1) * fold] = w_ref[
                    d * held.rows + j * count : d * held.rows + (j + 1) * count, q_cols + mid :]

    normed = normed_ref[...]
    cos, sin = cos_ref[...], sin_ref[...]
    low = mm(normed, w_ref[:, q_cols : q_cols + mid]).astype(BF16)
    lora_ref[...] = low
    query = mm(normed, w_ref[:, :q_cols]) + mm(low, ww_ref[...])
    for h in range(q_cols // head_dim):
        c = h * head_dim
        a, b = query[:, c : c + half], query[:, c + half : c + head_dim]
        q_ref[:, c : c + half] = ((a * cos - b * sin) * scale).astype(BF16)
        q_ref[:, c + half : c + head_dim] = ((b * cos + a * sin) * scale).astype(BF16)


def project_q(where, normed, cos, sin, held, head_dim, q_cols, mid, scale, later):
    rows, width = normed.shape
    tile = math.gcd(rows, 256)
    half = head_dim // 2
    count = 4 + len(held.arrays)
    return pl.pallas_call(
        skipping(functools.partial(project_q_kernel, held=held, head_dim=head_dim, q_cols=q_cols,
                                   mid=mid, scale=scale), count, len(later)),
        grid=(rows // tile,),
        in_specs=[SMEM, rows_of(tile, width), rows_of(tile, half), rows_of(tile, half)]
        + [ANY] * (len(held.arrays) + len(later)),
        out_specs=[rows_of(tile, mid), rows_of(tile, q_cols), full(held.shape),
                   full((mid, q_cols))],
        out_shape=[like((rows, mid), BF16), like((rows, q_cols), BF16), like(held.shape, BF16),
                   like((mid, q_cols), BF16)],
        scratch_shapes=[pltpu.SemaphoreType.DMA((held.count,))],
        compiler_params=params(),
        cost_estimate=cost(1, 1),
        name="project_q",
    )(where, normed, cos, sin, *held.arrays, *later)


class Group:
    def __init__(self, kv, batches):
        self.rows = kv.shape[0] // batches
        span = lax.axis_size("seq")
        self.span = span
        self.relay = span == 4 and batches == 2
        if self.relay:
            one, two = swap(kv, "seq", 1), swap(kv, "seq", 2)
            self.arrays = [kv, one, two, swap(one[: self.rows], "seq", 2),
                           swap(two[self.rows :], "seq", 1)]
        else:
            self.arrays = [kv] + [swap(kv, "seq", s) for s in range(1, span)]

    def at(self, n, s):
        return (3 + n, 0) if self.relay and s == 3 else (s, n * self.rows)

    def copy(self, refs, n, s, place, dst, sem):
        i, row = self.at(n, s)
        to = pl.multiple_of((place ^ s) * self.rows, self.rows)
        return pltpu.make_async_copy(refs[i].at[pl.ds(row, self.rows)],
                                     dst.at[pl.ds(to, self.rows), :], sem)


def attend_kernel(*refs, group, head_dim, tile, block):
    where, lengths_ref, q_ref = refs[:3]
    kvs = refs[3 : 3 + len(group.arrays)]
    span = group.span
    o_ref, lse_ref, kv_ref, vt_ref, acc_ref, sem = refs[-6:]
    heads = q_ref.shape[1] // head_dim
    rows = q_ref.shape[0]
    m = pl.program_id(0)
    place = where[1]
    base = place * rows
    lengths = [lengths_ref[m, d] for d in range(lengths_ref.shape[1])]

    def first(t):
        return lax.div(begin_of(base + t * tile, lengths), block)

    def copy(n, s):
        return group.copy(kvs, n, s, place, kv_ref.at[n], sem.at[n, s])

    @pl.when(m == 0)
    def _():
        for n in range(kv_ref.shape[0]):
            for s in range(span):
                pl.when((place ^ s) <= place)(lambda n=n, s=s: copy(n, s).start())

    for n in range(kv_ref.shape[0]):
        for s in range(span):
            pl.when((m == n) & ((place ^ s) <= place))(lambda n=n, s=s: copy(n, s).wait())

    def flip(kb, carry):
        at = pl.ds(pl.multiple_of(kb * block, block), block)
        vt_ref[:, at] = kv_ref[m, at, head_dim:].T
        return carry

    lax.fori_loop(first(0), lax.div(base + rows + block - 1, block), flip, 0)
    for t in range(rows // tile):
        q_rows = slice(t * tile, (t + 1) * tile)
        high = base + t * tile + lax.broadcasted_iota(jnp.int32, (1, tile), 1)
        low = begin_of(high, lengths)
        acc_ref[...] = jnp.zeros_like(acc_ref)

        def visit(kb, carry):
            at = pl.ds(pl.multiple_of(kb * block, block), block)
            keys = kv_ref[m, at, :head_dim]
            vt = vt_ref[:, at]
            index = kb * block + lax.broadcasted_iota(jnp.int32, (block, tile), 0)
            mask = (index >= low) & (index <= high)
            out = []
            for h in range(heads):
                peak, total = carry[h]
                s = mm_nt(keys, q_ref[q_rows, h * head_dim : (h + 1) * head_dim])
                s = jnp.where(mask, s, -jnp.inf)
                new_peak = jnp.maximum(peak, jnp.max(s, axis=0, keepdims=True))
                factor = jnp.exp(peak - new_peak)
                p = jnp.exp(s - new_peak)
                total = total * factor + jnp.sum(p, axis=0, keepdims=True)
                acc_ref[h] = acc_ref[h] * factor + mm(vt, p.astype(BF16))
                out.append((new_peak, total))
            return tuple(out)

        start = tuple(
            (jnp.full((1, tile), LOWEST, F32), jnp.zeros((1, tile), F32)) for _ in range(heads)
        )
        stats = lax.fori_loop(first(t), lax.div(base + (t + 1) * tile + block - 1, block), visit,
                              start)
        for h in range(heads):
            peak, total = stats[h]
            o_ref[q_rows, h * head_dim : (h + 1) * head_dim] = (acc_ref[h] / total).T.astype(BF16)
            lse_ref[0, h : h + 1, q_rows] = peak + jnp.log(total)


def attend(where, lengths, q, group, head_dim, tile, block):
    total, q_cols = q.shape
    batches = lengths.shape[0]
    rows = total // batches
    heads = q_cols // head_dim
    span = group.span
    return pl.pallas_call(
        functools.partial(attend_kernel, group=group, head_dim=head_dim, tile=tile, block=block),
        grid=(batches,),
        in_specs=[SMEM, SMEM, rows_of(rows, q_cols)] + [ANY] * len(group.arrays),
        out_specs=[rows_of(rows, q_cols), pl.BlockSpec((1, heads, rows), lambda i: (i, 0, 0))],
        out_shape=[like(q.shape, BF16), like((batches, heads, rows), F32)],
        scratch_shapes=[pltpu.VMEM((batches, span * rows, 2 * head_dim), BF16),
                        pltpu.VMEM((head_dim, span * rows), BF16),
                        pltpu.VMEM((heads, head_dim, tile), F32),
                        pltpu.SemaphoreType.DMA((batches, span))],
        compiler_params=params(),
        cost_estimate=took(18),
        name="attend",
    )(where, lengths, q, *group.arrays)


def middle_kernel(*refs, held, head_dim, chunk):
    x_ref, attn_ref, g_ref, gains_ref = refs[:4]
    if held is None:
        w_ref, wd_ref, wo_ref = refs[4:7]
    else:
        w_ref, wd_ref, wo_ref, rest_ref, sem = refs[-5:]
    (out_ref, mid_grad_ref, branch_ref, attn_grad_ref, delta_ref, low_ref, hidden_ref, grads_ref,
     gain_grad_ref) = refs[5:14] if held is not None else refs[7:16]

    @pl.when(pl.program_id(0) == 0)
    def _():
        if held is not None:
            f = Fetch(held.copies(refs[4], w_ref, rest_ref), sem)
            f.wait(*range(held.span))
            held.unfold(rest_ref, [None, wo_ref])
        gain_grad_ref[...] = jnp.zeros_like(gain_grad_ref)

    gain = gains_ref[1:2, :]
    attn = attn_ref[...]
    middle = x_ref[...].astype(F32) + mm(attn, wo_ref[...])
    inv = lax.rsqrt(jnp.mean(middle * middle, axis=-1, keepdims=True) + EPSILON)
    unit = middle * inv
    low = (unit * gain).astype(BF16)
    low_ref[...] = low
    if held is not None:
        @pl.when(pl.program_id(0) == 0)
        def _():
            held.unfold(rest_ref, [wd_ref, None])
            copies = held.copies(refs[4], w_ref, rest_ref)
            for i in range(held.span, 2 * held.span):
                pltpu.make_async_copy(*copies[i], sem.at[i]).wait()

    grad = g_ref[...]
    result = middle
    back = jnp.zeros_like(middle)
    wide = wd_ref.shape[0]
    for c in range(wide // chunk):
        at = slice(c * chunk, (c + 1) * chunk)
        to = slice(wide + c * chunk, wide + (c + 1) * chunk)
        gate = mm(low, w_ref[:, at])
        lift = mm(low, w_ref[:, to])
        square = gate * gate
        bend = jnp.tanh(GELU_C * gate * (1.0 + GELU_A * square))
        cdf = 0.5 * (1.0 + bend)
        gelu = gate * cdf
        hidden = (gelu * lift).astype(BF16)
        hidden_ref[:, at] = hidden
        result = result + mm(hidden, wd_ref[at, :])
        hidden_grad = mm_nt(grad, wd_ref[at, :])
        slope = cdf + (0.5 * GELU_C) * gate * (1.0 - bend * bend) * (1.0 + 3.0 * GELU_A * square)
        gate_grad = (hidden_grad * lift * slope).astype(BF16)
        lift_grad = (hidden_grad * gelu).astype(BF16)
        grads_ref[:, at] = gate_grad
        grads_ref[:, to] = lift_grad
        back = back + mm_nt(gate_grad, w_ref[:, at]) + mm_nt(lift_grad, w_ref[:, to])
    out_ref[...] = result.astype(BF16)
    gain_grad_ref[...] += jnp.sum(unit * back, axis=0, keepdims=True)
    scaled = back * gain
    mid_grad = grad.astype(F32) + inv * (
        scaled - unit * jnp.mean(unit * scaled, axis=-1, keepdims=True)
    )
    mid_grad_ref[...] = mid_grad
    branch = mid_grad.astype(BF16)
    branch_ref[...] = branch
    attn_grad = mm_nt(branch, wo_ref[...]).astype(BF16)
    attn_grad_ref[...] = attn_grad
    product = attn_grad.astype(F32) * attn.astype(F32)
    half = head_dim // 2
    for h in range(attn.shape[1] // head_dim):
        c = h * head_dim
        folded = product[:, c : c + half] + product[:, c + half : c + head_dim]
        delta_ref[h : h + 1, :] = jnp.sum(folded.T, axis=0, keepdims=True)


def middle_part(x, attn, grad, gains, held, weights, head_dim):
    rows, width = x.shape
    q_cols = attn.shape[1]
    hidden = (weights[0].shape if held is None else held.shape)[1] // 2
    heads = q_cols // head_dim
    tile = math.gcd(rows, 512)
    if held is None:
        more, specs, scratch = weights, [full(w.shape) for w in weights], []
    else:
        more, specs = [held.array], [ANY]
        scratch = [pltpu.VMEM(held.shape, BF16)] + [pltpu.VMEM(s, BF16) for s in held.shapes]
        scratch += [pltpu.VMEM(held.scratch, BF16), pltpu.SemaphoreType.DMA((2 * held.span,))]
    return pl.pallas_call(
        functools.partial(middle_kernel, held=held, head_dim=head_dim, chunk=512),
        grid=(rows // tile,),
        in_specs=[rows_of(tile, width), rows_of(tile, q_cols), rows_of(tile, width),
                  full(gains.shape)] + specs,
        out_specs=[rows_of(tile, width), rows_of(tile, width), rows_of(tile, width),
                   rows_of(tile, q_cols), pl.BlockSpec((heads, tile), lambda i: (0, i)),
                   rows_of(tile, width), rows_of(tile, hidden), rows_of(tile, 2 * hidden),
                   full((1, width))],
        out_shape=[like((rows, width), BF16), like((rows, width), F32), like((rows, width), BF16),
                   like((rows, q_cols), BF16), like((heads, rows), F32),
                   like((rows, width), BF16), like((rows, hidden), BF16),
                   like((rows, 2 * hidden), BF16), like((1, width), F32)],
        scratch_shapes=scratch,
        compiler_params=params(),
        cost_estimate=took(39),
        name="middle",
    )(x, attn, grad, gains, *more)


def attend_back_kernel(*refs, group, head_dim, block, scale, m):
    where, lengths_ref, lse_ref, delta_ref, q_ref, do_ref, cos_ref, sin_ref = refs[:8]
    kvs, span = refs[8 : 8 + len(group.arrays)], group.span
    kv_ref, kt_ref, acc_ref, sem = refs[-4:]
    sends = refs[-4 - (span - 1) : -4]
    dq_ref, own_ref = refs[-4 - span - 1 : -4 - span + 1]
    heads = q_ref.shape[1] // head_dim
    half = head_dim // 2
    rows = q_ref.shape[0]
    place = where[1]
    base = place * rows
    lengths = [lengths_ref[m, d] for d in range(lengths_ref.shape[1])]

    def copy(s):
        return group.copy(kvs, m, s, place, kv_ref, sem.at[s])

    for s in range(span):
        pl.when((place ^ s) <= place)(lambda s=s: copy(s).start())
    acc_ref[...] = jnp.zeros_like(acc_ref)
    for s in range(span):
        pl.when((place ^ s) <= place)(lambda s=s: copy(s).wait())
    index = lax.broadcasted_iota(jnp.int32, (block, rows), 0)
    high = base + lax.broadcasted_iota(jnp.int32, (1, rows), 1)
    low = begin_of(high, lengths)
    count = rows // block

    def visit(kb, carry):
        at = pl.ds(pl.multiple_of(kb * block, block), block)
        keys = kv_ref[at, :head_dim]
        vals = kv_ref[at, head_dim:]
        kt_ref[...] = keys.T
        here = kb * block + index
        mask = (here >= low) & (here <= high)
        dk = jnp.zeros((block, head_dim), F32)
        dv = jnp.zeros((block, head_dim), F32)
        for h in range(heads):
            cols = slice(h * head_dim, (h + 1) * head_dim)
            q = q_ref[:, cols]
            do = do_ref[:, cols]
            s = mm_nt(keys, q)
            p = jnp.where(mask, jnp.exp(s - lse_ref[0, h : h + 1, :]), 0.0)
            dv = dv + mm(p.astype(BF16), do)
            ds = (p * (mm_nt(vals, do) - delta_ref[h : h + 1, :])).astype(BF16)
            dk = dk + mm(ds, q)
            acc_ref[h] += mm(kt_ref[...], ds)
        owner = lax.div(kb, count)
        to = pl.ds(pl.multiple_of((kb - owner * count) * block, block), block)

        def put(ref):
            ref[to, :head_dim] = dk.astype(ref.dtype)
            ref[to, head_dim:] = dv.astype(ref.dtype)

        pl.when(owner == place)(lambda: put(own_ref))
        for s, ref in enumerate(sends, 1):
            pl.when(owner == (place ^ s))(lambda ref=ref: put(ref))
        return carry

    begin = lax.div(begin_of(base, lengths), block)
    for s, ref in enumerate([own_ref, *sends]):
        @pl.when(((place ^ s) > place) | ((place ^ s) * count < begin))
        def _():
            ref[...] = jnp.zeros_like(ref)

    lax.fori_loop(begin, (place + 1) * count, visit, 0)
    cos, sin = cos_ref[...], sin_ref[...]
    for h in range(heads):
        c = h * head_dim
        dq = acc_ref[h].T * scale
        a, b = dq[:, :half], dq[:, half:]
        dq_ref[:, c : c + half] = (a * cos + b * sin).astype(BF16)
        dq_ref[:, c + half : c + head_dim] = (b * cos - a * sin).astype(BF16)


def attend_back(where, lengths, lse, delta, q, do, group, cos, sin, head_dim, block, scale, m,
                before, later):
    q_cols = q.shape[1]
    rows = q.shape[0] // lengths.shape[0]
    heads = q_cols // head_dim
    span, n = group.span, len(group.arrays)
    tokens = span * rows
    half = head_dim // 2
    here = pl.BlockSpec((rows, q_cols), lambda i: (m, 0))
    angle = pl.BlockSpec((rows, half), lambda i: (m, 0))
    more = ([] if before is None else [before]) + later
    return pl.pallas_call(
        functools.partial(attend_back_kernel, group=group, head_dim=head_dim, block=block,
                          scale=scale, m=m),
        grid=(1,),
        in_specs=[SMEM, SMEM, pl.BlockSpec((1, heads, rows), lambda i: (m, 0, 0)),
                  pl.BlockSpec((heads, rows), lambda i: (0, m)), here, here, angle, angle]
        + [ANY] * (n + len(more)),
        out_specs=[here] + [VMEM] * span,
        out_shape=[like(q.shape, BF16), like((rows, 2 * head_dim), F32)]
        + [like((rows, 2 * head_dim), BF16)] * (span - 1),
        scratch_shapes=[pltpu.VMEM((tokens, 2 * head_dim), BF16),
                        pltpu.VMEM((head_dim, block), BF16),
                        pltpu.VMEM((heads, head_dim, rows), F32),
                        pltpu.SemaphoreType.DMA((span,))],
        input_output_aliases={} if before is None else {8 + n: 0},
        compiler_params=params(),
        cost_estimate=cost(LONG, 1),
        name="attend_back",
    )(where, lengths, lse, delta, q, do, cos, sin, *group.arrays, *more)


def query_back_kernel(dq_ref, w_ref, ww_ref, lora_grad_ref, back_ref, *, q_cols, mid):
    dq = dq_ref[...]
    lora_grad = mm_nt(dq, ww_ref[...]).astype(BF16)
    lora_grad_ref[...] = lora_grad
    back_ref[...] = (mm_nt(dq, w_ref[:, :q_cols])
                     + mm_nt(lora_grad, w_ref[:, q_cols : q_cols + mid]))


def query_back(dq, w, ww, later=()):
    rows, q_cols = dq.shape
    mid, width = ww.shape[0], w.shape[0]
    tile = math.gcd(rows, 256)
    return pl.pallas_call(
        skipping(functools.partial(query_back_kernel, q_cols=q_cols, mid=mid), 3, len(later)),
        grid=(rows // tile,),
        in_specs=[rows_of(tile, q_cols), full(w.shape), full(ww.shape)] + [ANY] * len(later),
        out_specs=[rows_of(tile, mid), rows_of(tile, width)],
        out_shape=[like((rows, mid), BF16), like((rows, width), F32)],
        compiler_params=params(),
        cost_estimate=cost(2 * rows * (width * (q_cols + mid) + mid * q_cols), 9e6),
        name="query_back",
    )(dq, w, ww, *later)


def pair_back_kernel(*refs, head_dim, others):
    x_ref, gains_ref, cos_ref, sin_ref, w_ref, back_ref, mid_grad_ref, own_ref = refs[:8]
    pair_grad_ref, in_grad_ref, gain_grad_ref = refs[-3:]

    @pl.when(pl.program_id(0) == 0)
    def _():
        gain_grad_ref[...] = jnp.zeros_like(gain_grad_ref)

    half = head_dim // 2
    gain = gains_ref[0:1, :]
    cos, sin = cos_ref[...], sin_ref[...]
    dkv = own_ref[...]
    for ref in refs[8 : 8 + others]:
        dkv = dkv + ref[...].astype(F32)
    a, b = dkv[:, :half], dkv[:, half:head_dim]
    pair_grad_ref[:, :half] = (a * cos + b * sin).astype(BF16)
    pair_grad_ref[:, half:head_dim] = (b * cos - a * sin).astype(BF16)
    pair_grad_ref[:, head_dim:] = dkv[:, head_dim:].astype(BF16)
    back = back_ref[...] + mm_nt(pair_grad_ref[...], w_ref[:, : 2 * head_dim])
    x = x_ref[...].astype(F32)
    inv = lax.rsqrt(jnp.mean(x * x, axis=-1, keepdims=True) + EPSILON)
    unit = x * inv
    gain_grad_ref[...] += jnp.sum(unit * back, axis=0, keepdims=True)
    scaled = back * gain
    in_grad_ref[...] = mid_grad_ref[...] + inv * (
        scaled - unit * jnp.mean(unit * scaled, axis=-1, keepdims=True)
    )


def pair_back(x, gains, cos, sin, w, own, others, back, mid_grad, head_dim, m, batches, before=None,
              later=()):
    width = x.shape[1]
    rows = x.shape[0] // batches
    tile = math.gcd(rows, 256)
    half, cols = head_dim // 2, 2 * head_dim
    count = rows // tile

    def here(n):
        return pl.BlockSpec((tile, n), lambda i: (m * count + i, 0))

    more = ([] if before is None else [before]) + list(later)
    return pl.pallas_call(
        functools.partial(pair_back_kernel, head_dim=head_dim, others=len(others)),
        grid=(count,),
        in_specs=[here(width), full(gains.shape), here(half), here(half), full(w.shape),
                  here(width), here(width)] + [rows_of(tile, cols)] * (1 + len(others))
        + [ANY] * len(more),
        out_specs=[rows_of(tile, cols), here(width), full((1, width))],
        out_shape=[like((rows, cols), BF16), like(x.shape, F32), like((1, width), F32)],
        input_output_aliases={} if before is None else {8 + len(others): 1},
        compiler_params=params(),
        cost_estimate=cost(2 * rows * width * cols, 7e6),
        name="pair_back",
    )(x, gains, cos, sin, w, back, mid_grad, own, *others, *more)


def weight_grad_kernel(x_ref, y_ref, out_ref):
    out_ref[...] = mm_tn(x_ref[...], y_ref[...]).astype(BF16)


def weight_grad(x, y, tile=256, later=()):
    rows, width = x.shape
    cols = y.shape[1]
    tile = math.gcd(cols, tile)
    return pl.pallas_call(
        skipping(weight_grad_kernel, 2, len(later)),
        grid=(cols // tile,),
        in_specs=[full(x.shape), pl.BlockSpec((rows, tile), lambda i: (0, i))] + [ANY] * len(later),
        out_specs=pl.BlockSpec((width, tile), lambda i: (0, i)),
        out_shape=like((width, cols), BF16),
        compiler_params=params(),
        cost_estimate=took(10),
        name="weight_grad",
    )(x, y, *later)


def turn(x_ref, flat_ref, xt_ref, me, parts):
    flat_ref[...] = x_ref[...].T
    piece = flat_ref.shape[0] // parts
    for r in range(parts):
        at = pl.multiple_of((me ^ r) * piece, piece)
        to = (r % 2) * (parts // 2) + r // 2
        xt_ref[to * piece : (to + 1) * piece, :] = flat_ref[pl.ds(at, piece), :]


def column_grads_kernel(where, g_in, hidden_in, b_in, attn_in, keep_ref, send_ref, g_ref, hidden_ref,
                        b_ref, attn_ref, sem, *, parts):
    f = Fetch([(g_in, g_ref), (hidden_in, hidden_ref), (b_in, b_ref), (attn_in, attn_ref)], sem)
    span, _, piece, _ = keep_ref.shape
    per = parts // span
    col = 0
    for pair, x_ref, y_ref in (((0, 1), g_ref, hidden_ref), ((2, 3), b_ref, attn_ref)):
        n = y_ref.shape[1] // parts
        f.wait(pair[0])
        f.wait(pair[1])
        for r in range(parts):
            at = pl.multiple_of((where[0] ^ r) * n, n)
            out = mm_tn(x_ref[...], y_ref[:, pl.ds(at, n)]).astype(BF16)
            ref = send_ref if r % 2 else keep_ref
            for s in range(span):
                for i in range(per):
                    ref[s ^ where[1], r // 2, :, col + i * n : col + (i + 1) * n] = out[
                        (s * per + i) * piece : (s * per + i + 1) * piece]
        col += per * n


def column_grads(where, grad, hidden, branch, attn, parts, span):
    rows, width = grad.shape
    piece = width // parts
    cols = (hidden.shape[1] + attn.shape[1]) // span
    shape = like((span, parts // 2, piece, cols), BF16)
    arrays = (grad, hidden, branch, attn)
    return pl.pallas_call(
        functools.partial(column_grads_kernel, parts=parts),
        in_specs=[SMEM] + [ANY] * 4,
        out_specs=[VMEM] * 2,
        out_shape=[shape, shape],
        scratch_shapes=[pltpu.VMEM(a.shape, BF16) for a in arrays]
        + [pltpu.SemaphoreType.DMA((4,))],
        compiler_params=params(),
        cost_estimate=took(9),
        name="column_grads",
    )(where, *arrays)


def unrotate(dkv, cos, sin, head_dim):
    half = head_dim // 2
    a, b = dkv[:, :half], dkv[:, half:head_dim]
    return jnp.concatenate([a * cos + b * sin, b * cos - a * sin, dkv[:, head_dim:]],
                           axis=1).astype(BF16)


def norm_back(x, gain, back, rest):
    inv = lax.rsqrt(jnp.mean(x * x, axis=-1, keepdims=True) + EPSILON)
    unit = x * inv
    scaled = back * gain
    return (rest + inv * (scaled - unit * jnp.mean(unit * scaled, axis=-1, keepdims=True)),
            jnp.sum(unit * back, axis=0, keepdims=True))


def fold_rows(out_ref, value, first, parts, piece, fold, j):
    count = value.shape[0] // parts
    for d in range(parts):
        at = d * piece + j * count
        out_ref[at : at + count, first : first + fold] = value[d * count : (d + 1) * count]


def query_side_kernel(dq_in, ww_in, normed_in, lora_in, queries_ref, lora_grad_ref, dq, ww, normed,
                      lora, sem, *, parts, fold):
    f = Fetch([(dq_in, dq), (ww_in, ww), (normed_in, normed), (lora_in, lora)], sem)
    q_cols, mid = dq.shape[1], lora.shape[1]
    f.wait(0, 1)
    lora_grad = mm_nt(dq[...], ww[...]).astype(BF16)
    lora_grad_ref[...] = lora_grad
    f.wait(2, 3)
    step = math.gcd(q_cols, 512)
    turned = normed[...].T
    for c in range(0, q_cols, step):
        queries_ref[:, c : c + step] = mm(turned, dq[:, c : c + step]).astype(BF16)
    queries_ref[:, q_cols : q_cols + mid] = mm(turned, lora_grad).astype(BF16)
    piece, count = normed.shape[1] // parts, mid // parts
    turned = lora[...].T
    for j in range(q_cols // fold):
        out = mm(turned, dq[:, j * fold : (j + 1) * fold]).astype(BF16)
        fold_rows(queries_ref, out, q_cols + mid, parts, piece, fold, j)
    rest = (q_cols // fold) * count
    for d in range(parts):
        queries_ref[d * piece + rest : (d + 1) * piece, q_cols + mid :] = jnp.zeros(
            (piece - rest, fold), BF16)


def query_side(dq, ww, normed, lora_mid, parts, fold, later):
    total, q_cols = dq.shape
    width, mid = normed.shape[1], lora_mid.shape[1]
    arrays = (dq, ww, normed, lora_mid)
    return pl.pallas_call(
        skipping(functools.partial(query_side_kernel, parts=parts, fold=fold), 4, len(later)),
        in_specs=[ANY] * (4 + len(later)),
        out_specs=[VMEM] * 2,
        out_shape=[like((width, q_cols + mid + fold), BF16), like((total, mid), BF16)],
        scratch_shapes=[pltpu.VMEM(a.shape, BF16) for a in arrays]
        + [pltpu.SemaphoreType.DMA((4,))],
        compiler_params=params(),
        cost_estimate=cost(LONG, 1),
        name="query_side",
    )(*arrays, *later)


def first_side_kernel(*refs, head_dim, others):
    (dq_in, w_in, lora_in, own_in, wp_in, x_in, mg_in, gains_ref, cos_ref, sin_ref, keep_ref,
     got_ref) = refs[:12]
    others_in = refs[12 : 12 + others]
    (back_ref, pair_ref, in_grad_ref, one_ref, near_ref, far_ref,
     dq, w, lora, own, wp, x, mg, there, hold, sem) = refs[12 + others :]
    rows = x.shape[0]
    f = Fetch([(dq_in, dq), (w_in, w), (lora_in, lora), (own_in, own), (wp_in, wp),
               (x_in.at[pl.ds(0, rows)], x), (mg_in.at[pl.ds(0, rows)], mg)]
              + [(r, there.at[i]) for i, r in enumerate(others_in)], sem)
    near_ref[...] = (keep_ref[0].astype(F32) + got_ref[0].astype(F32)).astype(BF16)
    far_ref[...] = (keep_ref[1].astype(F32) + got_ref[1].astype(F32)).astype(BF16)
    q_cols, mid = dq.shape[1], lora.shape[1]
    f.wait(0, 1, 2)
    for m in range(dq.shape[0] // rows):
        at = slice(m * rows, (m + 1) * rows)
        back = mm_nt(dq[at, :], w[:, :q_cols]) + mm_nt(lora[at, :], w[:, q_cols : q_cols + mid])
        if m == 0:
            hold[...] = back
        else:
            back_ref[(m - 1) * rows : m * rows] = back
    f.wait(*range(3, 7 + others))
    dkv = own[...]
    for i in range(others):
        dkv = dkv + there[i].astype(F32)
    pair = unrotate(dkv, cos_ref[...], sin_ref[...], head_dim)
    pair_ref[...] = pair
    back = hold[...] + mm_nt(pair, wp[:, : 2 * head_dim])
    in_grad_ref[...], one_ref[...] = norm_back(x[...].astype(F32), gains_ref[0:1, :], back, mg[...])


def first_side(dq, w, lora_grad, own, others, w_pair, x, mid_grad, gains, cos, sin, keep, got,
               head_dim, batches, later):
    total = dq.shape[0]
    rows = total // batches
    width, mid = x.shape[1], lora_grad.shape[1]
    half, cols = head_dim // 2, 2 * head_dim
    angle = pl.BlockSpec((rows, half), lambda i: (0, 0))
    n = len(others)
    return pl.pallas_call(
        skipping(functools.partial(first_side_kernel, head_dim=head_dim, others=n), 12 + n,
                 len(later)),
        grid=(1,),
        in_specs=[ANY] * 7 + [VMEM, angle, angle, VMEM, VMEM] + [ANY] * (n + len(later)),
        out_specs=[VMEM] * 2 + [pl.BlockSpec((rows, width), lambda i: (0, 0))] + [VMEM] * 3,
        out_shape=[like((total - rows, width), F32), like((rows, cols), BF16),
                   like((total, width), F32), like((1, width), F32)]
        + [like(keep.shape[1:], BF16)] * 2,
        scratch_shapes=[pltpu.VMEM(dq.shape, BF16), pltpu.VMEM(w.shape, BF16),
                        pltpu.VMEM(lora_grad.shape, BF16), pltpu.VMEM((rows, cols), F32),
                        pltpu.VMEM(w_pair.shape, BF16), pltpu.VMEM((rows, width), BF16),
                        pltpu.VMEM((rows, width), F32), pltpu.VMEM((n, rows, cols), BF16),
                        pltpu.VMEM((rows, width), F32), pltpu.SemaphoreType.DMA((7 + n,))],
        compiler_params=params(),
        cost_estimate=cost(1, 1),
        name="first_side",
    )(dq, w, lora_grad, own, w_pair, x, mid_grad, gains, cos, sin, keep, got, *others, *later)


def pair_side_kernel(*refs, head_dim, parts, others):
    (where, own_in, wp_in, back_in, x_in, mg_in, normed_in, first_in, gains_ref, cos_ref, sin_ref,
     one_ref, two_ref) = refs[:13]
    others_in = refs[13 : 13 + others]
    outs = refs[14 + others :]
    in_grad_ref, send_ref = outs[:2]
    keeps = outs[2 : 2 + parts // 2]
    (own, wp, back, x, mg, normed, pair_ref, there, flat_ref, xt_ref, gain_ref,
     sem) = outs[2 + parts // 2 :]
    rows = x.shape[0]
    f = Fetch([(normed_in, normed), (own_in, own)]
              + [(r, there.at[i]) for i, r in enumerate(others_in)]
              + [(first_in, pair_ref.at[pl.ds(0, rows)]), (wp_in, wp), (back_in, back),
                 (x_in.at[pl.ds(rows, rows)], x), (mg_in.at[pl.ds(rows, rows)], mg)], sem)
    f.wait(0)
    turn(normed, flat_ref, xt_ref, where[0], parts)
    f.wait(*range(1, 2 + others))
    dkv = own[...]
    for i in range(others):
        dkv = dkv + there[i].astype(F32)
    pair = unrotate(dkv, cos_ref[...], sin_ref[...], head_dim)
    pair_ref[rows:, :] = pair
    f.wait(*range(2 + others, 7 + others))
    grads = back[...] + mm_nt(pair, wp[:, : 2 * head_dim])
    in_grad_ref[...], one = norm_back(x[...].astype(F32), gains_ref[0:1, :], grads, mg[...])
    width = flat_ref.shape[0]
    piece, half, cols = width // parts, parts // 2, 2 * head_dim
    out = mm(xt_ref[...], pair_ref[...]).astype(BF16)
    pad = jnp.zeros((126, width), F32)
    gain_ref[...] = jnp.concatenate([one + one_ref[...], two_ref[...], pad], axis=0).T.astype(BF16)
    for k in range(half):
        keeps[k][:, :cols] = out[k * piece : (k + 1) * piece]
        send_ref[k, :, :cols] = out[(half + k) * piece : (half + k + 1) * piece]
        at = pl.multiple_of((where[0] ^ (2 * k)) * piece, piece)
        keeps[k][:, cols:] = gain_ref[pl.ds(at, piece), :]
        at = pl.multiple_of((where[0] ^ (2 * k + 1)) * piece, piece)
        send_ref[k, :, cols:] = gain_ref[pl.ds(at, piece), :]


def pair_side(where, own, others, w_pair, back, x, mid_grad, normed, first, gains, cos, sin, one,
              two, in_grad, head_dim, parts):
    total, width = normed.shape
    rows = total // 2
    half, cols = head_dim // 2, 2 * head_dim
    piece = width // parts
    angle = pl.BlockSpec((rows, half), lambda i: (1, 0))
    n = len(others)
    return pl.pallas_call(
        functools.partial(pair_side_kernel, head_dim=head_dim, parts=parts, others=n),
        grid=(1,),
        in_specs=[SMEM] + [ANY] * 7 + [VMEM, angle, angle, VMEM, VMEM] + [ANY] * (n + 1),
        out_specs=[pl.BlockSpec((rows, width), lambda i: (1, 0))] + [VMEM] * (1 + parts // 2),
        out_shape=[like((total, width), F32), like((parts // 2, piece, cols + 128), BF16)]
        + [like((piece, cols + 128), BF16)] * (parts // 2),
        scratch_shapes=[pltpu.VMEM((rows, cols), F32), pltpu.VMEM(w_pair.shape, BF16),
                        pltpu.VMEM((rows, width), F32), pltpu.VMEM((rows, width), BF16),
                        pltpu.VMEM((rows, width), F32), pltpu.VMEM(normed.shape, BF16),
                        pltpu.VMEM((total, cols), BF16), pltpu.VMEM((n, rows, cols), BF16),
                        pltpu.VMEM((width, total), BF16), pltpu.VMEM((width, total), BF16),
                        pltpu.VMEM((width, 128), BF16), pltpu.SemaphoreType.DMA((7 + n,))],
        input_output_aliases={13 + n: 0},
        compiler_params=params(),
        cost_estimate=cost(LONG, 12e6),
        name="pair_side",
    )(where, own, w_pair, back, x, mid_grad, normed, first, gains, cos, sin, one, two, *others,
      in_grad)


def join_kernel(left_ref, *refs):
    out_ref = refs[-1]
    n = left_ref.shape[1]
    out_ref[:, :n] = left_ref[...]
    out_ref[:, n:] = tree([r[...].astype(F32) for r in refs[:-1]]).astype(BF16)


def join(left, parts):
    rows, n = left.shape
    arrays = [left, *parts]
    return pl.pallas_call(
        fetched(join_kernel, len(arrays)),
        in_specs=[ANY] * len(arrays),
        out_specs=VMEM,
        out_shape=like((rows, n + parts[0].shape[1]), BF16),
        scratch_shapes=room(arrays),
        compiler_params=params(),
        cost_estimate=took(2),
        name="join",
    )(*arrays)


def finish_kernel(*refs, mid, q_cols, cols, fold):
    parts, outs = refs[:-6], refs[-6:]
    query_ref, narrow_ref, widen_ref, kv_ref, one_ref, two_ref = outs
    total = tree([p[...].astype(F32) for p in parts])
    query_ref[...] = total[:, :q_cols]
    narrow_ref[...] = total[:, q_cols : q_cols + mid]
    first = q_cols + mid
    count = widen_ref.shape[0]
    for j in range(q_cols // fold):
        widen_ref[:, j * fold : (j + 1) * fold] = total[j * count : (j + 1) * count,
                                                        first : first + fold]
    first += fold
    kv_ref[...] = total[:, first : first + cols]
    gains = total[:, first + cols :].T
    one_ref[...] = gains[0:1]
    two_ref[...] = gains[1:2]


def finish(parts, q_cols, mid, count, cols, fold):
    piece = parts[0].shape[0]
    return pl.pallas_call(
        fetched(functools.partial(finish_kernel, q_cols=q_cols, mid=mid, cols=cols, fold=fold),
                len(parts)),
        in_specs=[ANY] * len(parts),
        scratch_shapes=room(parts),
        out_specs=[VMEM] * 6,
        out_shape=[like((piece, q_cols), F32), like((piece, mid), F32), like((count, q_cols), F32),
                   like((piece, cols), F32), like((1, piece), F32), like((1, piece), F32)],
        compiler_params=params(),
        cost_estimate=took(2.5),
        name="finish",
    )(*parts)


def swap_cores(keeps, send, later=()):
    got, count = swap(send, "fsdp", 1), len(keeps)
    return add([*keeps, got], [[(k, None), (count, k)] for k in range(count)], later)


def pairs_kernel(*refs):
    parts, (keep_ref, send_ref) = refs[:-2], refs[-2:]
    for i in range(2):
        for k, ref in ((2 * i, keep_ref), (2 * i + 1, send_ref)):
            ref[i] = tree([p[k].astype(F32) for p in parts]).astype(BF16)


def sum_pairs(parts, later=()):
    count, shape = len(parts), like((2,) + parts[0].shape[1:], BF16)
    return pl.pallas_call(
        skipping(pairs_kernel, count, len(later)),
        in_specs=[VMEM] * count + [ANY] * len(later),
        out_specs=[VMEM] * 2,
        out_shape=[shape] * 2,
        compiler_params=params(),
        cost_estimate=took(2.4),
        name="sum_pairs",
    )(*parts, *later)


def cut_kernel(where, x_ref, *outs):
    part = outs[0].shape[1]
    for s, out in enumerate(outs):
        at = pl.multiple_of((where[1] ^ s) * part, part)
        out[...] = x_ref[:, pl.ds(at, part)]


def cut_parts(where, x, later=()):
    span = lax.axis_size("seq")
    rows, part = x.shape[0], x.shape[1] // span
    cut = pl.pallas_call(
        skipping(cut_kernel, 2, len(later)),
        in_specs=[SMEM, VMEM] + [ANY] * len(later),
        out_specs=[VMEM] * span,
        out_shape=[like((rows, part), x.dtype)] * span,
        compiler_params=params(),
        cost_estimate=took(2),
        name="cut",
    )(where, x, *later)
    return cut


def halves_kernel(*refs):
    out_ref = refs[-1]
    n = refs[0].shape[1]
    out_ref[:, :n] = tree([r[...].astype(F32) for r in refs[:-3]]).astype(BF16)
    out_ref[:, n:] = tree([r[...].astype(F32) for r in refs[-3:-1]]).astype(BF16)


def halves(left, right, later=()):
    count = len(left) + 2
    shape = (left[0].shape[0], left[0].shape[1] + right[0].shape[1])
    return pl.pallas_call(
        skipping(halves_kernel, count, len(later)),
        in_specs=[VMEM] * count + [ANY] * len(later),
        out_specs=VMEM,
        out_shape=like(shape, BF16),
        compiler_params=params(),
        cost_estimate=cost(LONG, 2e6),
        name="halves",
    )(*left, *right, *later)


def lay_kernel(where, *refs, n, k):
    parts = refs[:-6]
    span = len(parts)
    gate_ref, up_ref, down_ref, out_ref, tall_ref, tall2_ref = refs[-6:]
    piece = parts[0].shape[0]
    half = span // 2
    wide = gate_ref.shape[1] // half
    per = (parts[0].shape[1] - wide) // (n + k)
    for s, ref in enumerate(parts):
        q = where[1] ^ s
        for i, out in enumerate((gate_ref, up_ref)):
            @pl.when(q // half == i)
            def _():
                at = pl.multiple_of((q % half) * wide, wide)
                out[:, pl.ds(at, wide)] = ref[:, :wide].astype(F32)
        for i in range(per):
            at = pl.ds(pl.multiple_of((q * per + i) * piece, piece), piece)
            first = wide + i * n
            tall_ref[at, :] = ref[:, first : first + n].astype(F32)
            first = wide + per * n + i * k
            tall2_ref[at, :] = ref[:, first : first + k].astype(F32)
    down_ref[...] = tall_ref[...].T
    out_ref[...] = tall2_ref[...].T


def lay(where, parts, hidden, n, k, later=()):
    piece = parts[0].shape[0]
    width = piece * lax.axis_size("fsdp")
    return pl.pallas_call(
        skipping(functools.partial(lay_kernel, n=n, k=k), 1 + len(parts), len(later)),
        in_specs=[SMEM] + [VMEM] * len(parts) + [ANY] * len(later),
        out_specs=[VMEM] * 4,
        out_shape=[like((piece, hidden), F32)] * 2 + [like((n, width), F32), like((k, width), F32)],
        scratch_shapes=[pltpu.VMEM((width, n), F32), pltpu.VMEM((width, k), F32)],
        compiler_params=params(),
        cost_estimate=took(3),
        name="lay",
    )(where, *parts, *later)


def begin_of(index, lengths):
    ends = [lengths[0]]
    for n in lengths[1:]:
        ends.append(ends[-1] + n)
    begin = index
    for d in reversed(range(len(lengths))):
        begin = jnp.where(index < ends[d], ends[d] - lengths[d], begin)
    return begin


def local(tokens, document_lengths, cotangent, attention_gain, query_projection, narrowing_factor,
          widening_factor, key_value_projection, output_projection, feedforward_gain,
          gate_projection, up_projection, down_projection):
    batches, _, rows, width = tokens.shape
    head_dim = key_value_projection.shape[1] // 2
    q_cols = query_projection.shape[1]
    mid = narrowing_factor.shape[1]
    hidden = gate_projection.shape[1]
    kv_cols = 2 * head_dim
    scale = head_dim ** (-0.5)
    parts, span = lax.axis_size("fsdp"), lax.axis_size("seq")
    place = lax.axis_index("seq")
    tile = block = math.gcd(rows, 512)
    where = jnp.stack([lax.axis_index("fsdp"), place]).astype(jnp.int32)
    piece = width // parts
    direct = piece % 16 == 0
    fold = 512
    folds = q_cols // fold

    lengths = document_lengths[:, 0]
    half = head_dim // 2
    index = place * rows + lax.broadcasted_iota(jnp.int32, (batches, rows, half), 1)
    begin = begin_of(index, [lengths[:, d][:, None, None] for d in range(lengths.shape[1])])
    freqs = THETA ** (-(lax.broadcasted_iota(jnp.int32, (1, half), 1).astype(F32) * 2.0 / head_dim))
    angles = ((index - begin).astype(F32) * freqs).reshape(batches * rows, half)
    cos, sin = jnp.cos(angles), jnp.sin(angles)

    if direct:
        first = Shards(pack_pair(key_value_projection, attention_gain, feedforward_gain))
        third = pack(where, gate_projection, up_projection, down_projection, output_projection,
                     span, [cos, sin, first.arrays[parts - 2]])
        held = Tiled(third, 2 * hidden, down_projection, output_projection)
        weights = None
    else:
        def gather(x):
            return lax.all_gather(x, "fsdp", axis=0, tiled=True)

        first = jnp.concatenate(
            [key_value_projection,
             jnp.pad(jnp.stack([attention_gain, feedforward_gain], axis=1), ((0, 0), (0, 126)))],
            axis=1)
        turned = jnp.concatenate(
            [widening_factor[:, j * fold : (j + 1) * fold] for j in range(folds)])
        turned = jnp.pad(turned, ((0, piece - turned.shape[0]), (0, 0)))
        second = jnp.concatenate([query_projection, narrowing_factor, turned], axis=1)
        first, second = Whole(gather(first)), Whole(gather(second))
        second.rows = piece
        held = None
        weights = [gather(jnp.concatenate([gate_projection, up_projection], axis=1)),
                   gather(down_projection), gather(output_projection)]

    x = tokens.reshape(batches * rows, width)
    grad = cotangent.reshape(batches * rows, width)
    normed, kv, w_pair, gains = project_kv(where, x, cos, sin, first, head_dim)
    kvs = Group(kv, batches)
    if direct:
        second = Shards(pack_query(query_projection, narrowing_factor, widening_factor, fold,
                                   [kv]), True)
    lora_mid, q, w_query, ww = project_q(where, normed, cos, sin, second, head_dim, q_cols, mid,
                                         scale, [])
    attended, lse = attend(where, lengths, q, kvs, head_dim, tile, block)
    (output, mid_grad, branch, attn_grad, delta, ffn_low, hidden_low, lift_grads,
     gain_two_grad) = middle_part(x, attended, grad, gains, held, weights, head_dim)

    if direct:
        keep, send = column_grads(where, grad, hidden_low, branch, attended, parts, span)
        got = swap(send, "fsdp", 1)
        lifts = weight_grad(ffn_low, lift_grads, 1024, [keep])
        lifts_sum = lax.psum_scatter(lifts, "fsdp", scatter_dimension=0, tiled=True)
        columns = add([keep, got], [[(0, s), (1, s)] for s in range(span)], [lifts])
        there = exchange(columns)
    dq, owns, others = None, [], []
    for m in range(batches):
        later = []
        if direct and m == 0:
            later = columns
        if direct and m == 1:
            keep, send = sum_pairs(there, [dq])
            got = swap(send, "fsdp", 2)
            later = [keep]
        dq, own, *sends = attend_back(where, lengths, lse, delta, q, attn_grad, kvs, cos, sin,
                                      head_dim, block, scale, m, dq, later)
        owns.append(own)
        others.append(exchange([own, *sends])[1:])
    if direct:
        queries, lora_grad = query_side(dq, ww, normed, lora_mid, parts, fold, [])
        queries_sum = lax.psum_scatter(queries, "fsdp", scatter_dimension=0, tiled=True)
        back, pair, in_grad, one, near, far = first_side(
            dq, w_query, lora_grad, owns[0], others[0], w_pair, x, mid_grad, gains, cos, sin, keep,
            got, head_dim, batches, [queries, lifts_sum])
        in_grad, send, *keeps = pair_side(where, owns[1], others[1], w_pair, back, x, mid_grad,
                                          normed, pair, gains, cos, sin, one, gain_two_grad,
                                          in_grad, head_dim, parts)

        def share(x):
            return exchange([x] * span)

        lifts_cut = cut_parts(where, lifts_sum, [pair])
        lifts_parts = exchange(lifts_cut)
        mine = halves(lifts_parts, [near, swap(far, "fsdp", 4)], [send])
        laid = share(mine)
        shards = swap_cores(keeps, send, [mine])
        mine = join(queries_sum, [shards[0]] + [
            swap(a, "fsdp", 2 * k) for k, a in enumerate(shards) if k > 0])
        last = share(mine)
        gate_grad, up_grad, down_grad, out_grad = lay(
            where, laid, hidden, hidden // parts, q_cols // parts, [mine])
        query_grad, narrow_grad, widen_grad, key_value_grad, one, two = finish(
            last, q_cols, mid, mid // parts, kv_cols, fold)
        gain_one_grad, gain_two_grad = one.reshape(piece), two.reshape(piece)
    else:
        lora_grad, back = query_back(dq, w_query, ww)
        in_grad, pairs, ones = None, [], []
        for m in range(batches):
            pair, in_grad, one = pair_back(x, gains, cos, sin, w_pair, owns[m], others[m], back,
                                           mid_grad, head_dim, m, batches, in_grad)
            pairs.append(pair)
            ones.append(one)

        def scatter(x):
            part = lax.psum_scatter(x.astype(BF16), "fsdp", scatter_dimension=0, tiled=True)
            return lax.psum(part, "seq").astype(F32)

        pair_grad = jnp.concatenate(pairs)
        gain_one_grad = sum(ones)
        down_grad = scatter(weight_grad(grad, hidden_low).T)
        out_grad = scatter(weight_grad(branch, attended).T)
        lift_w = scatter(weight_grad(ffn_low, lift_grads))
        gate_grad, up_grad = lift_w[:, :hidden], lift_w[:, hidden:]
        query_grad = scatter(weight_grad(normed, dq))
        narrow_grad = scatter(weight_grad(normed, lora_grad))
        widen_grad = scatter(weight_grad(lora_mid, dq))
        key_value_grad = scatter(weight_grad(normed, pair_grad))
        gains_grad = scatter(jnp.concatenate([gain_one_grad, gain_two_grad]).T)
        gain_one_grad, gain_two_grad = gains_grad[:, 0], gains_grad[:, 1]
    return (output.reshape(batches, 1, rows, width), in_grad.reshape(batches, 1, rows, width),
            gain_one_grad, query_grad, narrow_grad, widen_grad, key_value_grad, out_grad,
            gain_two_grad, gate_grad, up_grad, down_grad)


def solution(mesh):
    rows = P(None, "fsdp", "seq", None)
    vector, matrix = P("fsdp"), P("fsdp", None)
    in_specs = (rows, P(None, "fsdp", None), rows, vector) + (matrix,) * 5 + (vector,) + (matrix,) * 3
    out_specs = (rows, rows, vector) + (matrix,) * 5 + (vector,) + (matrix,) * 3
    return jax.shard_map(local, mesh=mesh, in_specs=in_specs, out_specs=out_specs, check_vma=False)
```
